32 devices in a mesh: band: 8 (over z, x), rep: 4 (over y, core).
Axes of the slice: x: 2, y: 2, z: 4, core: 2. Of those that a mesh axis runs over, the one named last changes fastest.
Arguments:
- patches: bfloat16 [8, 4, 80, 8, 768], P('rep', None, None, 'band'), may hold values from -6 to 6
- variable_group_index: int32 [5], replicated, may hold values from 0 to 2, as said below
- frozen_patch_weight: bfloat16 [3, 16, 512], replicated, may hold values from -0.625 to 0.625
- adapter_down: bfloat16 [80, 16], P('rep'), may hold values from -0.625 to 0.625
- adapter_up: bfloat16 [16, 512], P(None, 'rep'), may hold values from -1.5 to 1.5
- level_merge_weight: bfloat16 [4, 512, 512], replicated, may hold values from -0.125 to 0.125
- window_patch_mixer: bfloat16 [96, 96], replicated, may hold values from -0.625 to 0.625
- column_block_owner: int32 [8], replicated, may hold values from 0 to 7, each once
- mixed_token_gradient: bfloat16 [8, 8, 8, 96, 512], P('rep', 'band'), may hold values from -0.03125 to 0.03125
Outputs:
- mixed: bfloat16 [8, 8, 8, 96, 512], P('rep', 'band')
- first_factor_gradient: float32 [80, 16], P('rep')
- second_factor_gradient: float32 [16, 512], P(None, 'rep')
The draws below stay inside these ranges and needn't reach their ends.
Inputs may be any that keep to these rules, and one draw needn't show every extreme that they name: Column block j goes to the band device column_block_owner[j]; each device owns one block. `variable_group_index`: every one of the 3 groups holds at least one variable.
All inputs are finite; a program needn't handle non-finite values.
Results may differ from the reference program's by a relative error of at most 0.01.
Values may be sent and summed in bfloat16 or wider, within the bound.
No kernel may reach another device: no remote copies, remote signals or barrier semaphores. Data moves between devices by JAX's collectives and lax.ppermute only.
A program may use at most 128 MiB of HBM per device.

```python
import jax
import jax.numpy as jnp
from jax import lax

EMBED_WIDTH = 512
VARS = 5
PIX = 16
LEV = 4
ADAPTER_RANK = 16
G = 3
WLAT = 8
WLON = 12
COLS = 768
LEVEL_CHANNELS = 80
WT = 96
LAT = 8
BLOCKS = 8
BW = 96
NS = 8
N_BAND = 8


def draw_variable_group_index(key, part):
    base_key = jax.random.fold_in(key, 7)
    first_key, second_key = jax.random.split(base_key)
    groups_drawn = jax.random.randint(first_key, (VARS,), 0, G, dtype=jnp.int32)
    order = jax.random.permutation(second_key, VARS)
    forced = groups_drawn.at[order[:G]].set(jnp.arange(G, dtype=jnp.int32))
    return forced.astype(jnp.int32)


def steps_of(rng, extent, cuts, least, high):
    level = 1.0
    for axis_at, parts in cuts:
        steps = jax.random.uniform(jax.random.fold_in(jax.random.fold_in(rng, 6), axis_at), (parts,), jnp.float32, least / len(cuts), high / len(cuts))
        level = level * jnp.repeat(jnp.exp(steps), extent[axis_at] // parts).reshape((-1,) + (1,) * (len(extent) - 1 - axis_at))
    return level


def bell_draw(stream_key, dims, scale, bound, cuts=(), kind=jnp.bfloat16):
    values = jax.random.normal(stream_key, dims, jnp.float32) * scale
    if len(cuts) > 0:
        values = steps_of(stream_key, dims, cuts, -0.22, 0.18) * values
    return jnp.clip(values, min=-bound, max=bound).astype(kind)


def setup_inputs(seed: int = 0) -> dict:
    arg_keys = jax.random.split(jax.random.key(seed), 10)
    return {
        "patches": bell_draw(arg_keys[0], (NS, LEV, LEVEL_CHANNELS, LAT, COLS), 1.0, 6.0, ((0, 4), (3, 8))),
        "variable_group_index": draw_variable_group_index(jax.random.fold_in(arg_keys[9], 71), 0),
        "frozen_patch_weight": bell_draw(arg_keys[2], (G, PIX, EMBED_WIDTH), LEVEL_CHANNELS ** -0.5, 0.625),
        "adapter_down": bell_draw(arg_keys[3], (LEVEL_CHANNELS, ADAPTER_RANK), LEVEL_CHANNELS ** -0.5, 0.625, ((0, 4),)),
        "adapter_up": bell_draw(arg_keys[4], (ADAPTER_RANK, EMBED_WIDTH), ADAPTER_RANK ** -0.5, 1.5, ((1, 4),)),
        "level_merge_weight": bell_draw(arg_keys[5], (LEV, EMBED_WIDTH, EMBED_WIDTH), (LEV * EMBED_WIDTH) ** -0.5, 0.125),
        "window_patch_mixer": bell_draw(arg_keys[6], (WT, WT), WT ** -0.5, 0.625),
        "column_block_owner": jax.random.permutation(arg_keys[7], BLOCKS).astype(jnp.int32),
        "mixed_token_gradient": bell_draw(arg_keys[8], (NS, BLOCKS, LAT, BW, EMBED_WIDTH), ((NS * LAT * COLS * LEV) ** -0.5), 0.03125, ((0, 4), (1, 8))),
    }


def gelu_exact(values):
    return jax.nn.gelu(values, approximate=False)

def reference(patches, variable_group_index, frozen_patch_weight, adapter_down, adapter_up, level_merge_weight, window_patch_mixer, column_block_owner, mixed_token_gradient):
    selector = (variable_group_index[:, None] == jnp.arange(G, dtype=jnp.int32)[None, :]).astype(jnp.float32)
    base_rows = jnp.einsum('vg,gad->vad', selector, frozen_patch_weight.astype(jnp.float32)).reshape(VARS * PIX, EMBED_WIDTH)
    rank_update = jnp.dot(adapter_down, adapter_up, preferred_element_type=jnp.float32)
    merged = (base_rows + rank_update).astype(jnp.bfloat16)
    merged_f = merged.astype(jnp.float32)
    level_f = level_merge_weight.astype(jnp.float32)
    mix_table = window_patch_mixer.astype(jnp.float32).reshape(WLAT, WLON, WLAT, WLON)
    index_row = jnp.arange(N_BAND, dtype=jnp.int32)
    inverse = lax.optimization_barrier(jnp.sum(jnp.where(column_block_owner[None, :] == index_row[:, None], index_row[None, :], 0), axis=1)).astype(jnp.int32)
    block_width = COLS // N_BAND

    def row_tokens(row_patches):
        embedded = jnp.einsum('lkc,kd->lcd', row_patches.astype(jnp.float32), merged_f).astype(jnp.bfloat16)
        return jnp.einsum('lcd,lde->ce', embedded.astype(jnp.float32), level_f).astype(jnp.bfloat16)

    def row_grad(running, row_inputs):
        row_patches, row_grad_tokens = row_inputs
        grad_embed = jnp.einsum('ce,lde->lcd', row_grad_tokens.astype(jnp.float32), level_f).astype(jnp.bfloat16)
        update = jnp.einsum('lkc,lcd->kd', row_patches.astype(jnp.float32), grad_embed.astype(jnp.float32))
        return (running + update, None)

    def one_sample(inputs):
        sample_patches, sample_grad = inputs
        by_rows = jnp.moveaxis(sample_patches, 2, 0)
        tokens = lax.map(row_tokens, by_rows)
        window_tiles = tokens.astype(jnp.float32).reshape(LAT // WLAT, WLAT, COLS // WLON, WLON, EMBED_WIDTH)
        pre_act = jnp.einsum('iwjv,ajbvd->aibwd', mix_table, window_tiles).reshape(LAT, COLS, EMBED_WIDTH)
        mixed_full = (tokens.astype(jnp.float32) + gelu_exact(pre_act)).astype(jnp.bfloat16)
        mixed_blocks = jnp.moveaxis(jnp.take(mixed_full.reshape(LAT, N_BAND, block_width, EMBED_WIDTH), inverse, axis=1), 1, 0)
        grad_full = jnp.moveaxis(jnp.take(sample_grad, column_block_owner, axis=0), 0, 1).reshape(LAT, COLS, EMBED_WIDTH).astype(jnp.float32)
        grad_pre = jax.vjp(gelu_exact, pre_act)[1](grad_full)[0].astype(jnp.bfloat16)
        grad_tiles = grad_pre.astype(jnp.float32).reshape(LAT // WLAT, WLAT, COLS // WLON, WLON, EMBED_WIDTH)
        spread = jnp.einsum('iwjv,aibwd->ajbvd', mix_table, grad_tiles).reshape(LAT, COLS, EMBED_WIDTH)
        grad_tokens = (grad_full + spread).astype(jnp.bfloat16)
        adapter_weight_gradient, unused_out = lax.scan(row_grad, jnp.zeros((VARS * PIX, EMBED_WIDTH), jnp.float32), (by_rows, grad_tokens))
        return (mixed_blocks, adapter_weight_gradient)
    mixed_all, weight_grads = lax.map(one_sample, (patches, mixed_token_gradient))
    adapter_weight_gradient = lax.optimization_barrier(jnp.sum(weight_grads, axis=0))
    first_factor_gradient = jnp.dot(adapter_weight_gradient, adapter_up.astype(jnp.float32).T, precision=lax.Precision.HIGHEST)
    second_factor_gradient = jnp.dot(adapter_down.astype(jnp.float32).T, adapter_weight_gradient, precision=lax.Precision.HIGHEST)
    return (mixed_all, first_factor_gradient, second_factor_gradient)
```

```python
import functools

import jax
import jax.numpy as jnp
from jax import lax
from jax.experimental import pallas as pl
from jax.experimental.pallas import tpu as pltpu
from jax.sharding import PartitionSpec as P

WLAT = 8
WLON = 12
LANE = 128
SUB = 16
VMEM_LIMIT = 50 * 1024 * 1024
BF16 = jnp.bfloat16
F32 = jnp.float32


def round_up(value, step):
    return -(-value // step) * step


def dot_nn(a, b):
    return lax.dot_general(a, b, (((1,), (0,)), ((), ())), preferred_element_type=F32)


def dot_nt(a, b):
    return lax.dot_general(a, b, (((1,), (1,)), ((), ())), preferred_element_type=F32)


def dot_tn(a, b):
    return lax.dot_general(a, b, (((0,), (0,)), ((), ())), preferred_element_type=F32)


def split_hi_lo(values):
    high = values.astype(BF16)
    low = (values - high.astype(F32)).astype(BF16)
    return high, low


def iota2(shape, axis):
    return lax.broadcasted_iota(jnp.int32, shape, axis)


def params(**extra):
    return pltpu.CompilerParams(vmem_limit_bytes=VMEM_LIMIT, **extra)


def send_kernel(band_count, half_width, owner_ref, x_ref, *out_refs):
    halves = len(out_refs)
    for tile in range(x_ref.shape[1] // LANE):
        rows = x_ref[:, tile * LANE : (tile + 1) * LANE].T
        start = tile * LANE
        while start < (tile + 1) * LANE:
            piece = start // half_width
            end = min((piece + 1) * half_width, (tile + 1) * LANE)
            slot = owner_ref[piece // halves]
            offset = start - piece * half_width
            out_refs[piece % halves][slot, offset : offset + end - start, :] = rows[
                start - tile * LANE : end - tile * LANE, :
            ]
            start = end


def send_blocks(pixels, owner, band_count, halves, half_width):
    features, columns = pixels.shape
    block = jax.ShapeDtypeStruct((band_count, half_width, features), BF16)
    out_spec = pl.BlockSpec((band_count, half_width, LANE), lambda f, owner: (0, 0, f))
    return pl.pallas_call(
        functools.partial(send_kernel, band_count, half_width),
        out_shape=[block] * halves,
        grid_spec=pltpu.PrefetchScalarGridSpec(
            num_scalar_prefetch=1,
            grid=(features // LANE,),
            in_specs=[pl.BlockSpec((LANE, columns), lambda f, owner: (f, 0))],
            out_specs=[out_spec] * halves,
        ),
        compiler_params=params(),
        name="send_blocks",
    )(owner, pixels)


def expand_table(table, rows, half_width_padded, half_width, transpose):
    position = iota2((rows, WLAT * WLON), 0)
    line, col = position // half_width_padded, position % half_width_padded
    target = iota2((rows, WLAT * WLON), 1)
    pick = jnp.where((target == line * WLON + col % WLON) & (col < half_width), 1.0, 0.0).astype(BF16)
    left = (dot_nt if transpose else dot_nn)(pick, table).astype(BF16)
    full = dot_nt(left, pick)
    row_window = (iota2((rows, 1), 0) % half_width_padded) // WLON
    col_window = (iota2((1, rows), 1) % half_width_padded) // WLON
    return jnp.where(row_window == col_window, full, 0.0).astype(BF16)


def prep_kernel(
    row_share,
    half_width,
    half_width_padded,
    group_ref,
    frozen_ref,
    factors_ref,
    level_ref,
    mixer_ref,
    merged_ref,
    up_ref,
    down_ref,
    mix_ref,
    mix_t_ref,
):
    reps, _, rank, share = factors_ref.shape
    levels = level_ref.shape[0]
    variables = group_ref.shape[0]
    channels = variables * frozen_ref.shape[1]
    up = jnp.concatenate([factors_ref[r, 0] for r in range(reps)], axis=1)
    source, target = iota2((share, channels), 0), iota2((share, channels), 1)
    down_t = jnp.zeros((rank, channels), F32)
    for r in range(reps):
        place = jnp.where((target == source + r * row_share) & (source < row_share), 1.0, 0.0)
        down_t = down_t + dot_nn(factors_ref[r, 1], place.astype(BF16))
    down_t = down_t.astype(BF16)
    down_ref[...] = down_t
    base = jnp.concatenate([frozen_ref[group_ref[v]].astype(F32) for v in range(variables)], axis=0)
    merged = (base + dot_tn(down_t, up)).astype(BF16)
    stacked = jnp.concatenate([merged, up], axis=0)
    merged_ref[...] = jnp.zeros_like(merged_ref)
    for level in range(levels):
        through = dot_nn(stacked, level_ref[level])
        weights = through[:channels].astype(BF16)
        for s in range(merged_ref.shape[0]):
            offset = (s * levels * channels) % LANE + level * channels
            merged_ref[s, offset : offset + channels, :] = weights
        up_high, up_low = split_hi_lo(through[channels:])
        up_ref[level, :rank, :] = up_high
        up_ref[level, rank:, :] = up_low
    rows = mix_ref.shape[0]
    mix_ref[...] = expand_table(mixer_ref[...], rows, half_width_padded, half_width, False)
    mix_t_ref[...] = expand_table(mixer_ref[...], rows, half_width_padded, half_width, True)


def prepare(groups, frozen, factors, level_weight, mixer, samples, row_share, half_width, half_width_padded):
    reps, _, rank, _ = factors.shape
    levels, feature_dim, _ = level_weight.shape
    channels = groups.shape[0] * frozen.shape[1]
    reach = round_up(levels * channels + LANE // 2, LANE)
    rows = WLAT * half_width_padded
    vmem = pl.BlockSpec(memory_space=pltpu.VMEM)
    flops = 2 * levels * (channels + rank) * feature_dim * feature_dim + 4 * rows * rows * WLAT * WLON
    return pl.pallas_call(
        functools.partial(prep_kernel, row_share, half_width, half_width_padded),
        out_shape=[
            jax.ShapeDtypeStruct((samples, reach, feature_dim), BF16),
            jax.ShapeDtypeStruct((levels, 2 * rank, feature_dim), BF16),
            jax.ShapeDtypeStruct((rank, channels), BF16),
            jax.ShapeDtypeStruct((rows, rows), BF16),
            jax.ShapeDtypeStruct((rows, rows), BF16),
        ],
        in_specs=[pl.BlockSpec(memory_space=pltpu.SMEM)] + [vmem] * 4,
        out_specs=[vmem] * 5,
        compiler_params=params(),
        cost_estimate=pl.CostEstimate(flops=flops, bytes_accessed=4 * 2**20, transcendentals=0),
        name="prepare",
    )(groups, frozen, factors, level_weight, mixer)


def normal_parts(values):
    cdf = 0.5 + 0.5 * lax.erf(values * 0.7071067811865476)
    pdf = 0.3989422804014327 * jnp.exp(-0.5 * values * values)
    return cdf, pdf


def mix_kernel(chained, last, dims, *refs):
    levels, channels, rank, reps = dims
    refs = list(refs)
    arrived_ref, merged_ref, mix_ref, mix_t_ref, grad_ref = refs[:5]
    del refs[:5]
    before_ref = None
    if chained:
        before_ref = refs[1]
        del refs[:2]
    if last:
        up_ref, down_ref, level_ref = refs[:3]
        del refs[:3]
    mixed_ref, out_ref, total_ref, tokens_ref, pre_ref, grad_pre_ref = refs

    window_row, sample = pl.program_id(0), pl.program_id(1)
    samples = merged_ref.shape[0]
    reach = merged_ref.shape[1]
    width = arrived_ref.shape[1]
    rows = WLAT * width
    depth = levels * channels
    first_lane = pl.multiple_of((sample * depth) // LANE * LANE, LANE)
    pixels = arrived_ref[:, :, pl.ds(first_lane, reach)].reshape(rows, reach)
    tokens_ref[...] = dot_nn(pixels, merged_ref[sample]).astype(BF16)
    pre_ref[...] = dot_nn(mix_ref[...], tokens_ref[...])

    def line(i, carry):
        for start in range(0, width, SUB):
            at = pl.ds(pl.multiple_of(i * width + start, SUB), SUB)
            pre = pre_ref[at, :]
            cdf, pdf = normal_parts(pre)
            mixed_ref[0, i, start : start + SUB, :] = (
                tokens_ref[at, :].astype(F32) + pre * cdf
            ).astype(BF16)
            grad = grad_ref[0, i, start : start + SUB, :].astype(F32)
            grad_pre_ref[at, :] = (grad * (cdf + pre * pdf)).astype(BF16)
        return carry

    lax.fori_loop(0, WLAT, line, 0)
    feature_dim = tokens_ref.shape[1]
    grad_tokens = dot_nn(mix_t_ref[...], grad_pre_ref[...]) + grad_ref[0].reshape(
        rows, feature_dim
    ).astype(F32)
    share = dot_tn(pixels, grad_tokens.astype(BF16))

    @pl.when(window_row == 0)
    def _():
        total_ref[sample] = share

    @pl.when(window_row != 0)
    def _():
        total_ref[sample] = total_ref[sample] + share

    @pl.when((window_row == pl.num_programs(0) - 1) & (sample == samples - 1))
    def _():
        total = before_ref[...] if chained else jnp.zeros((depth, feature_dim), F32)
        for s in range(samples):
            offset = (s * depth) % LANE
            total = total + total_ref[s, offset : offset + depth, :]
        if not last:
            out_ref[...] = total
            return
        high, low = split_hi_lo(total)
        first = jnp.zeros((rank, channels), F32)
        second = jnp.zeros((2 * rank, feature_dim), F32)
        for level in range(levels):
            at = slice(level * channels, (level + 1) * channels)
            both = dot_nt(up_ref[level], high[at])
            first = first + both[:rank] + both[rank:] + dot_nt(up_ref[level, :rank, :], low[at])
            down = down_ref[...]
            through = dot_nn(down, high[at]) + dot_nn(down, low[at])
            through = jnp.concatenate(split_hi_lo(through), axis=0)
            second = second + dot_nt(through, level_ref[level])
        second = second[:rank] + second[rank:]
        col_share = feature_dim // reps
        out_ref[...] = jnp.zeros_like(out_ref)
        for r in range(reps):
            out_ref[r, :, :col_share] = second[:, r * col_share : (r + 1) * col_share]
            out_ref[r, :, col_share : col_share + channels] = first


def mix_half(half, last, arrived, merged, mix, mix_t, grad, chain, tail, reps):
    lat_rows, width, lanes = arrived.shape
    samples, _, block_width, feature_dim = grad.shape
    reach = merged.shape[1]
    rows = WLAT * width
    levels, two_rank, _ = tail[0].shape
    rank = two_rank // 2
    channels = tail[1].shape[1]
    depth = levels * channels
    whole = lambda shape: pl.BlockSpec(shape, lambda w, s: (0,) * len(shape))
    block = pl.BlockSpec((1, WLAT, width, feature_dim), lambda w, s: (s, w, half, 0))
    in_specs = [
        pl.BlockSpec((WLAT, width, lanes), lambda w, s: (w, 0, 0)),
        whole(merged.shape),
        whole(mix.shape),
        whole(mix_t.shape),
        block,
    ]
    operands = [arrived, merged, mix, mix_t, grad]
    aliases = {}
    if chain is not None:
        aliases = {len(operands): 0}
        in_specs += [pl.BlockSpec(memory_space=pl.ANY), whole(chain[1].shape)]
        operands += list(chain)
    if last:
        in_specs += [whole(array.shape) for array in tail]
        operands += list(tail)
        out_tile = (reps, rank, feature_dim // reps + round_up(channels, LANE))
    else:
        out_tile = (depth, feature_dim)
    flops = 2 * samples * lat_rows * width * feature_dim * (2 * reach + 2 * rows)
    return pl.pallas_call(
        functools.partial(mix_kernel, chain is not None, last, (levels, channels, rank, reps)),
        out_shape=[
            jax.ShapeDtypeStruct(grad.shape, BF16),
            jax.ShapeDtypeStruct(out_tile, F32),
        ],
        grid=(lat_rows // WLAT, samples),
        in_specs=in_specs,
        out_specs=[block, whole(out_tile)],
        scratch_shapes=[
            pltpu.VMEM((samples, reach, feature_dim), F32),
            pltpu.VMEM((rows, feature_dim), BF16),
            pltpu.VMEM((rows, feature_dim), F32),
            pltpu.VMEM((rows, feature_dim), BF16),
        ],
        input_output_aliases=aliases,
        compiler_params=params(dimension_semantics=("arbitrary", "arbitrary")),
        cost_estimate=pl.CostEstimate(
            flops=flops, bytes_accessed=8 * 2**20, transcendentals=samples * lat_rows * width * feature_dim
        ),
        name="mix_half",
    )(*operands)


def on_device(
    patches,
    variable_group_index,
    frozen_patch_weight,
    adapter_down,
    adapter_up,
    level_merge_weight,
    window_patch_mixer,
    column_block_owner,
    mixed_token_gradient,
):
    band_count, reps = lax.axis_size("band"), lax.axis_size("rep")
    samples, levels, channels, row_count, col_count = patches.shape
    feature_dim = frozen_patch_weight.shape[2]
    rank, col_share = adapter_up.shape
    row_share = adapter_down.shape[0]
    lat_rows = band_count * row_count
    block_width = col_count // band_count
    halves = 2 if block_width % (2 * SUB * WLON // 4) == 0 else 1
    half_width = block_width // halves
    half_padded = round_up(half_width, SUB)
    features = samples * levels * channels

    pixels = patches.reshape(features, col_count)
    if half_padded == half_width and features % LANE == 0 and col_count % LANE == 0:
        outgoing = send_blocks(pixels, column_block_owner, band_count, halves, half_width)
    else:
        block_ids = jnp.arange(band_count, dtype=jnp.int32)
        inverse = jnp.sum(
            jnp.where(column_block_owner[None, :] == block_ids[:, None], block_ids[None, :], 0), axis=1
        )
        by_block = jnp.take(pixels.T.reshape(band_count, block_width, features), inverse, axis=0)
        outgoing = [
            jnp.pad(
                by_block[:, h * half_width : (h + 1) * half_width],
                ((0, 0), (0, half_padded - half_width), (0, 0)),
            )
            for h in range(halves)
        ]
    arrived = [lax.all_to_all(part, "band", split_axis=0, concat_axis=0, tiled=True) for part in outgoing]

    pack_width = round_up(max(row_share, col_share), LANE)
    pack = jnp.stack(
        [
            jnp.pad(adapter_up, ((0, 0), (0, pack_width - col_share))),
            jnp.pad(adapter_down.T, ((0, 0), (0, pack_width - row_share))),
        ]
    )
    factors = lax.all_gather(pack, "rep", axis=0, tiled=False)
    merged, up_through, down_t, mix, mix_t = prepare(
        variable_group_index,
        frozen_patch_weight,
        factors,
        level_merge_weight,
        window_patch_mixer,
        samples,
        row_share,
        half_width,
        half_padded,
    )
    tail = (up_through, down_t, level_merge_weight)

    grad = mixed_token_gradient.reshape(samples, lat_rows, block_width, feature_dim)
    if half_padded != half_width:
        grad = jnp.pad(grad, ((0, 0), (0, 0), (0, half_padded - half_width), (0, 0)))
    chain = None
    for half in range(halves):
        chain = mix_half(
            half, half == halves - 1, arrived[half], merged, mix, mix_t, grad, chain, tail, reps
        )
    mixed, shares = chain
    if half_padded != half_width:
        mixed = mixed[:, :, :block_width]

    mine = jnp.sum(lax.all_to_all(shares, "rep", split_axis=0, concat_axis=0, tiled=True), axis=0)
    summed = jnp.sum(lax.all_gather(mine, "band", axis=0, tiled=False), axis=0)
    first_t = lax.dynamic_slice_in_dim(summed, col_share + lax.axis_index("rep") * row_share, row_share, 1)
    return (
        mixed.reshape(mixed_token_gradient.shape),
        first_t.T,
        summed[:, :col_share],
    )


def solution(mesh):
    in_specs = (
        P("rep", None, None, "band", None),
        P(),
        P(),
        P("rep", None),
        P(None, "rep"),
        P(),
        P(),
        P(),
        P("rep", "band", None, None, None),
    )
    out_specs = (P("rep", "band", None, None, None), P("rep", None), P(None, "rep"))
    return jax.shard_map(
        on_device, mesh=mesh, in_specs=in_specs, out_specs=out_specs, check_vma=False
    )
```

```python
import functools

import jax
import jax.numpy as jnp
from jax import lax
from jax.experimental import pallas as pl
from jax.experimental.pallas import tpu as pltpu
from jax.sharding import PartitionSpec as P

WLAT = 8
WLON = 12
LANE = 128
SUB = 16
VMEM_LIMIT = 24 * 1024 * 1024
MAX_PERMUTES = 8
BF16 = jnp.bfloat16
F32 = jnp.float32


def round_up(value, step):
    return -(-value // step) * step


def dot_nn(a, b):
    return lax.dot_general(a, b, (((1,), (0,)), ((), ())), preferred_element_type=F32)


def dot_nt(a, b):
    return lax.dot_general(a, b, (((1,), (1,)), ((), ())), preferred_element_type=F32)


def dot_tn(a, b):
    return lax.dot_general(a, b, (((0,), (0,)), ((), ())), preferred_element_type=F32)


def split_hi_lo(values):
    high = values.astype(BF16)
    low = (values - high.astype(F32)).astype(BF16)
    return high, low


def iota2(shape, axis):
    return lax.broadcasted_iota(jnp.int32, shape, axis)


def params(**extra):
    return pltpu.CompilerParams(vmem_limit_bytes=VMEM_LIMIT, **extra)


def send_kernel(band_count, halves, half_width, owner_ref, x_ref, *refs):
    out_refs, turned_ref = refs[:-1], refs[-1]
    me = lax.axis_index("band")
    for tile in range(x_ref.shape[1] // LANE):
        at = slice(tile * LANE, (tile + 1) * LANE)
        turned_ref[at, :] = x_ref[:, at].T
    for k in range(band_count):
        target = jnp.bitwise_xor(me, k)
        block = 0
        for j in range(1, band_count):
            block = jnp.where(owner_ref[j] == target, j, block)
        for half in range(halves):
            start = pl.multiple_of((block * halves + half) * half_width, SUB)
            out_refs[half * band_count + k][...] = turned_ref[pl.ds(start, half_width), :]


def send_blocks(pixels, owner, band_count, halves, half_width):
    features, columns = pixels.shape
    count = band_count * halves
    block = jax.ShapeDtypeStruct((half_width, features), BF16)
    out_spec = pl.BlockSpec((half_width, LANE), lambda f, owner: (0, f))
    pieces = pl.pallas_call(
        functools.partial(send_kernel, band_count, halves, half_width),
        out_shape=[block] * count,
        grid_spec=pltpu.PrefetchScalarGridSpec(
            num_scalar_prefetch=1,
            grid=(features // LANE,),
            in_specs=[pl.BlockSpec((LANE, columns), lambda f, owner: (f, 0))],
            out_specs=[out_spec] * count,
            scratch_shapes=[pltpu.VMEM((columns, LANE), BF16)],
        ),
        compiler_params=params(),
        name="send_blocks",
    )(owner, pixels)
    return [pieces[half * band_count : (half + 1) * band_count] for half in range(halves)]


def exchange(pieces, band_count):
    arrived = [pieces[0]]
    for k in range(1, band_count):
        pairs = [(source, source ^ k) for source in range(band_count)]
        arrived.append(lax.ppermute(pieces[k], "band", pairs))
    return arrived


def expand_table(table, rows, half_width_padded, half_width, transpose):
    position = iota2((rows, WLAT * WLON), 0)
    line, col = position // half_width_padded, position % half_width_padded
    target = iota2((rows, WLAT * WLON), 1)
    pick = jnp.where((target == line * WLON + col % WLON) & (col < half_width), 1.0, 0.0).astype(BF16)
    left = (dot_nt if transpose else dot_nn)(pick, table).astype(BF16)
    full = dot_nt(left, pick)
    row_window = (iota2((rows, 1), 0) % half_width_padded) // WLON
    col_window = (iota2((1, rows), 1) % half_width_padded) // WLON
    return jnp.where(row_window == col_window, full, 0.0).astype(BF16)


def prep_kernel(
    row_share,
    half_width,
    half_width_padded,
    group_ref,
    frozen_ref,
    factors_ref,
    level_ref,
    mixer_ref,
    merged_ref,
    up_ref,
    down_ref,
    mix_ref,
    mix_t_ref,
):
    reps, _, rank, share = factors_ref.shape
    levels = level_ref.shape[0]
    variables = group_ref.shape[0]
    channels = variables * frozen_ref.shape[1]
    up = jnp.concatenate([factors_ref[r, 0] for r in range(reps)], axis=1)
    source, target = iota2((share, channels), 0), iota2((share, channels), 1)
    down_t = jnp.zeros((rank, channels), F32)
    for r in range(reps):
        place = jnp.where((target == source + r * row_share) & (source < row_share), 1.0, 0.0)
        down_t = down_t + dot_nn(factors_ref[r, 1], place.astype(BF16))
    down_t = down_t.astype(BF16)
    down_ref[...] = down_t
    base = jnp.concatenate([frozen_ref[group_ref[v]].astype(F32) for v in range(variables)], axis=0)
    merged = (base + dot_tn(down_t, up)).astype(BF16)
    stacked = jnp.concatenate([merged, up], axis=0)
    merged_ref[...] = jnp.zeros_like(merged_ref)
    for level in range(levels):
        through = dot_nn(stacked, level_ref[level])
        weights = through[:channels].astype(BF16)
        for s in range(merged_ref.shape[0]):
            offset = (s * levels * channels) % LANE + level * channels
            merged_ref[s, offset : offset + channels, :] = weights
        up_high, up_low = split_hi_lo(through[channels:])
        up_ref[level, :rank, :] = up_high
        up_ref[level, rank:, :] = up_low
    rows = mix_ref.shape[0]
    mix_ref[...] = expand_table(mixer_ref[...], rows, half_width_padded, half_width, False)
    mix_t_ref[...] = expand_table(mixer_ref[...], rows, half_width_padded, half_width, True)


def prepare(groups, frozen, factors, level_weight, mixer, samples, row_share, half_width, half_width_padded):
    reps, _, rank, _ = factors.shape
    levels, feature_dim, _ = level_weight.shape
    channels = groups.shape[0] * frozen.shape[1]
    reach = round_up(levels * channels + LANE // 2, LANE)
    rows = WLAT * half_width_padded
    vmem = pl.BlockSpec(memory_space=pltpu.VMEM)
    flops = 2 * levels * (channels + rank) * feature_dim * feature_dim + 4 * rows * rows * WLAT * WLON
    return pl.pallas_call(
        functools.partial(prep_kernel, row_share, half_width, half_width_padded),
        out_shape=[
            jax.ShapeDtypeStruct((samples, reach, feature_dim), BF16),
            jax.ShapeDtypeStruct((levels, 2 * rank, feature_dim), BF16),
            jax.ShapeDtypeStruct((rank, channels), BF16),
            jax.ShapeDtypeStruct((rows, rows), BF16),
            jax.ShapeDtypeStruct((rows, rows), BF16),
        ],
        in_specs=[pl.BlockSpec(memory_space=pltpu.SMEM)] + [vmem] * 4,
        out_specs=[vmem] * 5,
        compiler_params=params(),
        cost_estimate=pl.CostEstimate(flops=flops, bytes_accessed=4 * 2**20, transcendentals=0),
        name="prepare",
    )(groups, frozen, factors, level_weight, mixer)


def normal_parts(values):
    cdf = 0.5 + 0.5 * lax.erf(values * 0.7071067811865476)
    pdf = 0.3989422804014327 * jnp.exp(-0.5 * values * values)
    return cdf, pdf


def mix_kernel(chained, last, pieces, dims, *refs):
    levels, channels, rank, reps = dims
    refs = list(refs)
    piece_refs = refs[:pieces]
    del refs[:pieces]
    merged_ref, mix_ref, mix_t_ref, grad_ref = refs[:4]
    del refs[:4]
    before_ref = None
    if chained:
        before_ref = refs[1]
        del refs[:2]
    if last:
        up_ref, down_ref, level_ref = refs[:3]
        del refs[:3]
    mixed_ref, out_ref, total_ref, tokens_ref, pre_ref, grad_pre_ref = refs[:6]
    arrived_ref = piece_refs[0] if pieces == 1 else refs[6]

    window_row, sample = pl.program_id(0), pl.program_id(1)
    samples = merged_ref.shape[0]
    reach = merged_ref.shape[1]
    width = arrived_ref.shape[1]
    rows = WLAT * width
    depth = levels * channels
    if pieces > 1:

        @pl.when(sample == 0)
        def _():
            me = lax.axis_index("band")
            for k in range(pieces):
                arrived_ref[jnp.bitwise_xor(me, k)] = piece_refs[k][...]

    first_lane = pl.multiple_of((sample * depth) // LANE * LANE, LANE)
    pixels = arrived_ref[:, :, pl.ds(first_lane, reach)].reshape(rows, reach)
    tokens_ref[...] = dot_nn(pixels, merged_ref[sample]).astype(BF16)
    pre_ref[...] = dot_nn(mix_ref[...], tokens_ref[...])

    def line(i, carry):
        for start in range(0, width, SUB):
            at = pl.ds(pl.multiple_of(i * width + start, SUB), SUB)
            pre = pre_ref[at, :]
            cdf, pdf = normal_parts(pre)
            mixed_ref[0, i, start : start + SUB, :] = (
                tokens_ref[at, :].astype(F32) + pre * cdf
            ).astype(BF16)
            grad = grad_ref[0, i, start : start + SUB, :].astype(F32)
            grad_pre_ref[at, :] = (grad * (cdf + pre * pdf)).astype(BF16)
        return carry

    lax.fori_loop(0, WLAT, line, 0)
    feature_dim = tokens_ref.shape[1]
    grad_tokens = dot_nn(mix_t_ref[...], grad_pre_ref[...]) + grad_ref[0].reshape(
        rows, feature_dim
    ).astype(F32)
    share = dot_tn(pixels, grad_tokens.astype(BF16))

    @pl.when(window_row == 0)
    def _():
        total_ref[sample] = share

    @pl.when(window_row != 0)
    def _():
        total_ref[sample] = total_ref[sample] + share

    @pl.when((window_row == pl.num_programs(0) - 1) & (sample == samples - 1))
    def _():
        total = before_ref[...] if chained else jnp.zeros((depth, feature_dim), F32)
        for s in range(samples):
            offset = (s * depth) % LANE
            total = total + total_ref[s, offset : offset + depth, :]
        if not last:
            out_ref[...] = total
            return
        high, low = split_hi_lo(total)
        first = jnp.zeros((rank, channels), F32)
        second = jnp.zeros((2 * rank, feature_dim), F32)
        for level in range(levels):
            at = slice(level * channels, (level + 1) * channels)
            both = dot_nt(up_ref[level], high[at])
            first = first + both[:rank] + both[rank:] + dot_nt(up_ref[level, :rank, :], low[at])
            down = down_ref[...]
            through = dot_nn(down, high[at]) + dot_nn(down, low[at])
            through = jnp.concatenate(split_hi_lo(through), axis=0)
            second = second + dot_nt(through, level_ref[level])
        second = second[:rank] + second[rank:]
        col_share = feature_dim // reps
        out_ref[...] = jnp.zeros_like(out_ref)
        for r in range(reps):
            out_ref[r, :, :col_share] = second[:, r * col_share : (r + 1) * col_share].astype(BF16)
            out_ref[r, :, col_share : col_share + channels] = first.astype(BF16)


def mix_half(half, last, arrived, merged, mix, mix_t, grad, chain, tail, reps):
    samples, lat_rows, _, feature_dim = grad.shape
    width, lanes = arrived[0].shape[-2:]
    reach = merged.shape[1]
    rows = WLAT * width
    levels, two_rank, _ = tail[0].shape
    rank = two_rank // 2
    channels = tail[1].shape[1]
    depth = levels * channels
    whole = lambda shape: pl.BlockSpec(shape, lambda w, s: (0,) * len(shape))
    block = pl.BlockSpec((1, WLAT, width, feature_dim), lambda w, s: (s, w, half, 0))
    scratch = [
        pltpu.VMEM((samples, reach, feature_dim), F32),
        pltpu.VMEM((rows, feature_dim), BF16),
        pltpu.VMEM((rows, feature_dim), F32),
        pltpu.VMEM((rows, feature_dim), BF16),
    ]
    if len(arrived) > 1:
        arrived_specs = [whole(piece.shape) for piece in arrived]
        scratch.append(pltpu.VMEM((WLAT, width, lanes), BF16))
    else:
        arrived_specs = [pl.BlockSpec((WLAT, width, lanes), lambda w, s: (w, 0, 0))]
    in_specs = arrived_specs + [
        whole(merged.shape),
        whole(mix.shape),
        whole(mix_t.shape),
        block,
    ]
    operands = list(arrived) + [merged, mix, mix_t, grad]
    aliases = {}
    if chain is not None:
        aliases = {len(operands): 0}
        in_specs += [pl.BlockSpec(memory_space=pl.ANY), whole(chain[1].shape)]
        operands += list(chain)
    if last:
        in_specs += [whole(array.shape) for array in tail]
        operands += list(tail)
        out_tile, out_type = (reps, rank, feature_dim // reps + round_up(channels, LANE)), BF16
    else:
        out_tile, out_type = (depth, feature_dim), F32
    flops = 2 * samples * lat_rows * width * feature_dim * (2 * reach + 2 * rows)
    return pl.pallas_call(
        functools.partial(mix_kernel, chain is not None, last, len(arrived), (levels, channels, rank, reps)),
        out_shape=[
            jax.ShapeDtypeStruct(grad.shape, BF16),
            jax.ShapeDtypeStruct(out_tile, out_type),
        ],
        grid=(lat_rows // WLAT, samples),
        in_specs=in_specs,
        out_specs=[block, whole(out_tile)],
        scratch_shapes=scratch,
        input_output_aliases=aliases,
        compiler_params=params(dimension_semantics=("arbitrary", "arbitrary")),
        cost_estimate=pl.CostEstimate(
            flops=flops, bytes_accessed=8 * 2**20, transcendentals=samples * lat_rows * width * feature_dim
        ),
        name="mix_half",
    )(*operands)


def on_device(
    patches,
    variable_group_index,
    frozen_patch_weight,
    adapter_down,
    adapter_up,
    level_merge_weight,
    window_patch_mixer,
    column_block_owner,
    mixed_token_gradient,
):
    band_count, reps = lax.axis_size("band"), lax.axis_size("rep")
    samples, levels, channels, row_count, col_count = patches.shape
    feature_dim = frozen_patch_weight.shape[2]
    rank, col_share = adapter_up.shape
    row_share = adapter_down.shape[0]
    lat_rows = band_count * row_count
    block_width = col_count // band_count
    halves = 2 if block_width % (2 * SUB * WLON // 4) == 0 else 1
    half_width = block_width // halves
    half_padded = round_up(half_width, SUB)
    features = samples * levels * channels

    pixels = patches.reshape(features, col_count)
    direct = band_count <= MAX_PERMUTES and lat_rows == WLAT and half_padded == half_width
    if direct and features % LANE == 0 and col_count % LANE == 0:
        outgoing = send_blocks(pixels, column_block_owner, band_count, halves, half_width)
        arrived = [exchange(pieces, band_count) for pieces in outgoing]
    else:
        block_ids = jnp.arange(band_count, dtype=jnp.int32)
        inverse = jnp.sum(
            jnp.where(column_block_owner[None, :] == block_ids[:, None], block_ids[None, :], 0), axis=1
        )
        by_block = jnp.take(pixels.T.reshape(band_count, block_width, features), inverse, axis=0)
        outgoing = [
            jnp.pad(
                by_block[:, h * half_width : (h + 1) * half_width],
                ((0, 0), (0, half_padded - half_width), (0, 0)),
            )
            for h in range(halves)
        ]
        arrived = [
            [lax.all_to_all(part, "band", split_axis=0, concat_axis=0, tiled=True)] for part in outgoing
        ]

    pack_width = round_up(max(row_share, col_share), LANE)
    pack = jnp.stack(
        [
            jnp.pad(adapter_up, ((0, 0), (0, pack_width - col_share))),
            jnp.pad(adapter_down.T, ((0, 0), (0, pack_width - row_share))),
        ]
    )
    factors = lax.all_gather(pack, "rep", axis=0, tiled=False)
    merged, up_through, down_t, mix, mix_t = prepare(
        variable_group_index,
        frozen_patch_weight,
        factors,
        level_merge_weight,
        window_patch_mixer,
        samples,
        row_share,
        half_width,
        half_padded,
    )
    tail = (up_through, down_t, level_merge_weight)

    grad = mixed_token_gradient.reshape(samples, lat_rows, block_width, feature_dim)
    if half_padded != half_width:
        grad = jnp.pad(grad, ((0, 0), (0, 0), (0, half_padded - half_width), (0, 0)))
    chain = None
    for half in range(halves):
        chain = mix_half(
            half, half == halves - 1, arrived[half], merged, mix, mix_t, grad, chain, tail, reps
        )
    mixed, shares = chain
    if half_padded != half_width:
        mixed = mixed[:, :, :block_width]

    shares = jnp.broadcast_to(shares[None], (band_count,) + shares.shape).reshape((-1,) + shares.shape[1:])
    parts = lax.all_to_all(shares, ("band", "rep"), split_axis=0, concat_axis=0, tiled=True)
    summed = jnp.sum(parts.astype(F32), axis=0)
    first_t = lax.dynamic_slice_in_dim(summed, col_share + lax.axis_index("rep") * row_share, row_share, 1)
    return (
        mixed.reshape(mixed_token_gradient.shape),
        first_t.T,
        summed[:, :col_share],
    )


def solution(mesh):
    in_specs = (
        P("rep", None, None, "band", None),
        P(),
        P(),
        P("rep", None),
        P(None, "rep"),
        P(),
        P(),
        P(),
        P("rep", "band", None, None, None),
    )
    out_specs = (P("rep", "band", None, None, None), P("rep", None), P(None, "rep"))
    return jax.shard_map(
        on_device, mesh=mesh, in_specs=in_specs, out_specs=out_specs, check_vma=False
    )
```

```python
import functools

import jax
import jax.numpy as jnp
from jax import lax
from jax.experimental import pallas as pl
from jax.experimental.pallas import tpu as pltpu
from jax.sharding import PartitionSpec as P

WLAT = 8
WLON = 12
LANE = 128
SUB = 16
VMEM_LIMIT = 24 * 1024 * 1024
SEND_VMEM_LIMIT = 60 * 1024 * 1024
BF16 = jnp.bfloat16
F32 = jnp.float32


def round_up(value, step):
    return -(-value // step) * step


def dot_nn(a, b):
    return lax.dot_general(a, b, (((1,), (0,)), ((), ())), preferred_element_type=F32)


def dot_nt(a, b):
    return lax.dot_general(a, b, (((1,), (1,)), ((), ())), preferred_element_type=F32)


def dot_tn(a, b):
    return lax.dot_general(a, b, (((0,), (0,)), ((), ())), preferred_element_type=F32)


def split_hi_lo(values):
    high = values.astype(BF16)
    low = (values - high.astype(F32)).astype(BF16)
    return high, low


def iota2(shape, axis):
    return lax.broadcasted_iota(jnp.int32, shape, axis)


def params(limit=VMEM_LIMIT, **extra):
    return pltpu.CompilerParams(vmem_limit_bytes=limit, **extra)


def send_kernel(owner_ref, x_ref, out_ref):
    band_count, width, _ = out_ref.shape
    for tile in range(x_ref.shape[1] // LANE):
        first, past = tile * LANE, (tile + 1) * LANE
        rows = x_ref[:, first:past].T
        start = first
        while start < past:
            block = start // width
            end = min((block + 1) * width, past)
            inside = slice(start - block * width, end - block * width)
            out_ref[owner_ref[block], inside, :] = rows[start - first : end - first, :]
            start = end


def send_blocks(pixels, owner, band_count, width):
    features, columns = pixels.shape
    return pl.pallas_call(
        send_kernel,
        out_shape=jax.ShapeDtypeStruct((band_count, width, features), BF16),
        grid_spec=pltpu.PrefetchScalarGridSpec(
            num_scalar_prefetch=1,
            grid=(features // LANE,),
            in_specs=[pl.BlockSpec((LANE, columns), lambda f, owner: (f, 0))],
            out_specs=pl.BlockSpec((band_count, width, LANE), lambda f, owner: (0, 0, f)),
        ),
        compiler_params=params(SEND_VMEM_LIMIT),
        name="send_blocks",
    )(owner, pixels)


def expand_table(table, rows, half_width_padded, half_width, transpose):
    position = iota2((rows, WLAT * WLON), 0)
    line, col = position // half_width_padded, position % half_width_padded
    target = iota2((rows, WLAT * WLON), 1)
    pick = jnp.where((target == line * WLON + col % WLON) & (col < half_width), 1.0, 0.0).astype(BF16)
    left = (dot_nt if transpose else dot_nn)(pick, table).astype(BF16)
    full = dot_nt(left, pick)
    row_window = (iota2((rows, 1), 0) % half_width_padded) // WLON
    col_window = (iota2((1, rows), 1) % half_width_padded) // WLON
    return jnp.where(row_window == col_window, full, 0.0).astype(BF16)


def prep_kernel(
    row_share,
    half_width,
    half_width_padded,
    group_ref,
    frozen_ref,
    factors_ref,
    level_ref,
    mixer_ref,
    merged_ref,
    up_ref,
    down_ref,
    mix_ref,
    mix_t_ref,
):
    reps, _, rank, share = factors_ref.shape
    levels = level_ref.shape[0]
    variables = group_ref.shape[0]
    channels = variables * frozen_ref.shape[1]
    up = jnp.concatenate([factors_ref[r, 0] for r in range(reps)], axis=1)
    source, target = iota2((share, channels), 0), iota2((share, channels), 1)
    down_t = jnp.zeros((rank, channels), F32)
    for r in range(reps):
        place = jnp.where((target == source + r * row_share) & (source < row_share), 1.0, 0.0)
        down_t = down_t + dot_nn(factors_ref[r, 1], place.astype(BF16))
    down_t = down_t.astype(BF16)
    down_ref[...] = down_t
    base = jnp.concatenate([frozen_ref[group_ref[v]].astype(F32) for v in range(variables)], axis=0)
    merged = (base + dot_tn(down_t, up)).astype(BF16)
    stacked = jnp.concatenate([merged, up], axis=0)
    merged_ref[...] = jnp.zeros_like(merged_ref)
    for level in range(levels):
        through = dot_nn(stacked, level_ref[level])
        weights = through[:channels].astype(BF16)
        for s in range(merged_ref.shape[0]):
            offset = (s * levels * channels) % LANE + level * channels
            merged_ref[s, offset : offset + channels, :] = weights
        up_high, up_low = split_hi_lo(through[channels:])
        up_ref[level, :rank, :] = up_high
        up_ref[level, rank:, :] = up_low
    rows = mix_ref.shape[0]
    mix_ref[...] = expand_table(mixer_ref[...], rows, half_width_padded, half_width, False)
    mix_t_ref[...] = expand_table(mixer_ref[...], rows, half_width_padded, half_width, True)


def prepare(groups, frozen, factors, level_weight, mixer, samples, row_share, half_width, half_width_padded):
    reps, _, rank, _ = factors.shape
    levels, feature_dim, _ = level_weight.shape
    channels = groups.shape[0] * frozen.shape[1]
    reach = round_up(levels * channels + LANE // 2, LANE)
    rows = WLAT * half_width_padded
    vmem = pl.BlockSpec(memory_space=pltpu.VMEM)
    flops = 2 * levels * (channels + rank) * feature_dim * feature_dim + 4 * rows * rows * WLAT * WLON
    return pl.pallas_call(
        functools.partial(prep_kernel, row_share, half_width, half_width_padded),
        out_shape=[
            jax.ShapeDtypeStruct((samples, reach, feature_dim), BF16),
            jax.ShapeDtypeStruct((levels, 2 * rank, feature_dim), BF16),
            jax.ShapeDtypeStruct((rank, channels), BF16),
            jax.ShapeDtypeStruct((rows, rows), BF16),
            jax.ShapeDtypeStruct((rows, rows), BF16),
        ],
        in_specs=[pl.BlockSpec(memory_space=pltpu.SMEM)] + [vmem] * 4,
        out_specs=[vmem] * 5,
        compiler_params=params(),
        cost_estimate=pl.CostEstimate(flops=flops, bytes_accessed=4 * 2**20, transcendentals=0),
        name="prepare",
    )(groups, frozen, factors, level_weight, mixer)


def normal_parts(values):
    bell = jnp.exp(-0.5 * values * values)
    t = 1.0 / (1.0 + 0.23164189 * jnp.abs(values))
    tail = t * (
        0.127414796 + t * (-0.142248368 + t * (0.7107068705 + t * (-0.7265760135 + t * 0.5307027145)))
    )
    tail = tail * bell
    return jnp.where(values < 0.0, tail, 1.0 - tail), 0.3989422804014327 * bell


def factor_shares(total, up_ref, down_ref, level_ref):
    levels, two_rank, feature_dim = up_ref.shape
    rank, channels = down_ref.shape
    high, low = split_hi_lo(total)
    down = down_ref[...]
    first = jnp.zeros((rank, channels), F32)
    second = jnp.zeros((two_rank, feature_dim), F32)
    for level in range(levels):
        at = slice(level * channels, (level + 1) * channels)
        both = dot_nt(up_ref[level], high[at])
        first = first + both[:rank] + both[rank:] + dot_nt(up_ref[level, :rank, :], low[at])
        through = dot_nn(down, high[at]) + dot_nn(down, low[at])
        through = jnp.concatenate(split_hi_lo(through), axis=0)
        second = second + dot_nt(through, level_ref[level])
    return first, second[:rank] + second[rank:]


def mix_kernel(
    arrived_ref,
    merged_ref,
    mix_ref,
    mix_t_ref,
    grad_ref,
    up_ref,
    down_ref,
    level_ref,
    mixed_ref,
    share_ref,
    total_ref,
    pre_ref,
    tokens_ref,
    grad_pre_ref,
    second_ref,
):
    samples, reach, feature_dim = merged_ref.shape
    _, width, features = arrived_ref.shape
    depth = features // samples
    rows = WLAT * width
    step = pl.program_id(0) * pl.num_programs(1) + pl.program_id(1)

    def forward(s):
        lane = s * depth // LANE * LANE
        pixels = arrived_ref[:, :, lane : lane + reach].reshape(rows, reach)
        tokens = dot_nn(pixels, merged_ref[s]).astype(BF16)
        tokens_ref[s] = tokens
        pre_ref[s] = dot_nn(mix_ref[...], tokens)
        return pixels

    def pointwise(s):
        for line in range(WLAT):
            for start in range(0, width, SUB):
                at, within = pl.ds(line * width + start, SUB), pl.ds(start, SUB)
                pre = pre_ref[s, at, :]
                cdf, pdf = normal_parts(pre)
                tokens = tokens_ref[s, at, :].astype(F32)
                mixed_ref[s, line, within, :] = (tokens + pre * cdf).astype(BF16)
                grad = grad_ref[s, line, within, :].astype(F32)
                grad_pre_ref[s, at, :] = (grad * (cdf + pre * pdf)).astype(BF16)

    def backward(s, pixels):
        direct = grad_ref[s].reshape(rows, feature_dim).astype(F32)
        grad_tokens = dot_nn(mix_t_ref[...], grad_pre_ref[s]) + direct
        offset = s * depth % LANE
        return dot_tn(pixels, grad_tokens.astype(BF16))[offset : offset + depth]

    pixels = [forward(s) for s in range(samples)]
    share = jnp.zeros((depth, feature_dim), F32)
    for s in range(samples):
        pointwise(s)
        share = share + backward(s, pixels[s])

    @pl.when(step == 0)
    def _():
        total_ref[...] = share

    @pl.when(step != 0)
    def _():
        total_ref[...] = total_ref[...] + share

    @pl.when(step == pl.num_programs(0) * pl.num_programs(1) - 1)
    def _():
        first, second = factor_shares(total_ref[...], up_ref, down_ref, level_ref)
        second_ref[...] = second
        reps, channels = share_ref.shape[0], down_ref.shape[1]
        columns = feature_dim // reps
        me = lax.axis_index("rep")
        share_ref[...] = jnp.zeros_like(share_ref)
        for k in range(reps):
            lane = pl.multiple_of(jnp.bitwise_xor(me, k) * columns, LANE)
            share_ref[k, :, :columns] = second_ref[:, pl.ds(lane, columns)]
            share_ref[k, :, columns : columns + channels] = first


def mix_blocks(halves, arrived, merged, mix, mix_t, grad, up_through, down_t, level_weight, reps):
    samples, lat_rows, block_width, feature_dim = grad.shape
    width = block_width // halves
    lanes = arrived.shape[2]
    reach = merged.shape[1]
    rows = WLAT * width
    rank, channels = down_t.shape

    def whole(shape):
        return pl.BlockSpec(shape, lambda w, h: (0,) * len(shape))

    block = pl.BlockSpec((samples, WLAT, width, feature_dim), lambda w, h: (0, w, h, 0))
    share_shape = (reps, rank, feature_dim // reps + round_up(channels, LANE))
    flops = 2 * samples * lat_rows * block_width * feature_dim * (2 * reach + 2 * rows)
    constants = [up_through, down_t, level_weight]
    return pl.pallas_call(
        mix_kernel,
        out_shape=[
            jax.ShapeDtypeStruct(grad.shape, BF16),
            jax.ShapeDtypeStruct(share_shape, F32),
        ],
        grid=(lat_rows // WLAT, halves),
        in_specs=[
            pl.BlockSpec((WLAT, width, lanes), lambda w, h: (w, h, 0)),
            whole(merged.shape),
            whole(mix.shape),
            whole(mix_t.shape),
            block,
        ]
        + [whole(array.shape) for array in constants],
        out_specs=[block, whole(share_shape)],
        scratch_shapes=[
            pltpu.VMEM((lanes // samples, feature_dim), F32),
            pltpu.VMEM((samples, rows, feature_dim), F32),
            pltpu.VMEM((samples, rows, feature_dim), BF16),
            pltpu.VMEM((samples, rows, feature_dim), BF16),
            pltpu.VMEM((rank, feature_dim), F32),
        ],
        compiler_params=params(dimension_semantics=("arbitrary", "arbitrary")),
        cost_estimate=pl.CostEstimate(
            flops=flops,
            bytes_accessed=12 * 2**20,
            transcendentals=samples * lat_rows * block_width * feature_dim,
        ),
        name="mix_blocks",
    )(arrived, merged, mix, mix_t, grad, *constants)


def swap(values, axis, distance):
    count = lax.axis_size(axis)
    return lax.ppermute(values, axis, [(source, source ^ distance) for source in range(count)])


def sum_shares(shares):
    half = shares.shape[0] // 2
    while half >= 1:
        shares = shares[:half] + swap(shares[half:], "rep", half)
        half //= 2
    total = shares[0]
    distance = 1
    while distance < lax.axis_size("band"):
        total = total + swap(total, "band", distance)
        distance *= 2
    return total


def on_device(
    patches,
    variable_group_index,
    frozen_patch_weight,
    adapter_down,
    adapter_up,
    level_merge_weight,
    window_patch_mixer,
    column_block_owner,
    mixed_token_gradient,
):
    band_count, reps = lax.axis_size("band"), lax.axis_size("rep")
    samples, levels, channels, row_count, col_count = patches.shape
    feature_dim = frozen_patch_weight.shape[2]
    rank, col_share = adapter_up.shape
    row_share = adapter_down.shape[0]
    lat_rows = band_count * row_count
    block_width = col_count // band_count
    halves = 2 if block_width % (2 * SUB * WLON // 4) == 0 else 1
    half_width = block_width // halves
    half_padded = round_up(half_width, SUB)
    padded_width = halves * half_padded
    features = samples * levels * channels

    pixels = patches.reshape(features, col_count)
    if half_padded == half_width and features % LANE == 0 and col_count % LANE == 0:
        outgoing = send_blocks(pixels, column_block_owner, band_count, block_width)
    else:
        block_ids = jnp.arange(band_count, dtype=jnp.int32)
        inverse = jnp.sum(
            jnp.where(column_block_owner[None, :] == block_ids[:, None], block_ids[None, :], 0), axis=1
        )
        outgoing = jnp.take(pixels.T.reshape(band_count, block_width, features), inverse, axis=0)
        outgoing = jnp.pad(outgoing, ((0, 0), (0, padded_width - block_width), (0, 0)))
    arrived = lax.all_to_all(outgoing, "band", split_axis=0, concat_axis=0, tiled=True)

    pack_width = round_up(max(row_share, col_share), LANE)
    pack = jnp.stack(
        [
            jnp.pad(adapter_up, ((0, 0), (0, pack_width - col_share))),
            jnp.pad(adapter_down.T, ((0, 0), (0, pack_width - row_share))),
        ]
    )
    factors = lax.all_gather(pack, "rep", axis=0, tiled=False)
    merged, up_through, down_t, mix, mix_t = prepare(
        variable_group_index,
        frozen_patch_weight,
        factors,
        level_merge_weight,
        window_patch_mixer,
        samples,
        row_share,
        half_width,
        half_padded,
    )
    grad = mixed_token_gradient.reshape(samples, lat_rows, block_width, feature_dim)
    if padded_width != block_width:
        grad = jnp.pad(grad, ((0, 0), (0, 0), (0, padded_width - block_width), (0, 0)))
    mixed, shares = mix_blocks(
        halves, arrived, merged, mix, mix_t, grad, up_through, down_t, level_merge_weight, reps
    )
    if padded_width != block_width:
        mixed = mixed[:, :, :block_width]

    summed = sum_shares(shares)
    first_t = lax.dynamic_slice_in_dim(summed, col_share + lax.axis_index("rep") * row_share, row_share, 1)
    return (
        mixed.reshape(mixed_token_gradient.shape),
        first_t.T,
        summed[:, :col_share],
    )


def solution(mesh):
    in_specs = (
        P("rep", None, None, "band", None),
        P(),
        P(),
        P("rep", None),
        P(None, "rep"),
        P(),
        P(),
        P(),
        P("rep", "band", None, None, None),
    )
    out_specs = (P("rep", "band", None, None, None), P("rep", None), P(None, "rep"))
    return jax.shard_map(
        on_device, mesh=mesh, in_specs=in_specs, out_specs=out_specs, check_vma=False
    )
```

```python
import functools

import jax
import jax.numpy as jnp
from jax import lax
from jax.experimental import pallas as pl
from jax.experimental.pallas import tpu as pltpu
from jax.sharding import PartitionSpec as P

WLAT = 8
WLON = 12
LANE = 128
SUB = 16
VMEM_LIMIT = 24 * 1024 * 1024
MAX_PERMUTES = 8
BF16 = jnp.bfloat16
F32 = jnp.float32


def round_up(value, step):
    return -(-value // step) * step


def dot_nn(a, b):
    return lax.dot_general(a, b, (((1,), (0,)), ((), ())), preferred_element_type=F32)


def dot_nt(a, b):
    return lax.dot_general(a, b, (((1,), (1,)), ((), ())), preferred_element_type=F32)


def dot_tn(a, b):
    return lax.dot_general(a, b, (((0,), (0,)), ((), ())), preferred_element_type=F32)


def split_hi_lo(values):
    high = values.astype(BF16)
    low = (values - high.astype(F32)).astype(BF16)
    return high, low


def iota2(shape, axis):
    return lax.broadcasted_iota(jnp.int32, shape, axis)


def params(**extra):
    return pltpu.CompilerParams(vmem_limit_bytes=VMEM_LIMIT, **extra)


def in_hbm(values):
    return pltpu.with_memory_space_constraint(values, pltpu.HBM)


def swap(values, axis, distance):
    count = lax.axis_size(axis)
    return lax.ppermute(values, axis, [(source, source ^ distance) for source in range(count)])


def send_kernel(owner_hbm_ref, x_hbm_ref, *refs):
    out_refs, (owner_ref, x_ref, turned_ref, owner_sem, x_sems) = refs[:-5], refs[-5:]
    band_count, width = len(out_refs), out_refs[0].shape[0]
    features, columns = x_ref.shape
    copies = [pltpu.make_async_copy(owner_hbm_ref, owner_ref, owner_sem)]
    parts = [slice(start, start + LANE) for start in range(0, features, LANE)]
    for n, part in enumerate(parts):
        copies.append(pltpu.make_async_copy(x_hbm_ref.at[part, :], x_ref.at[part, :], x_sems.at[n]))
    for copy in copies:
        copy.start()
    for n, part in enumerate(parts):
        copies[n + 1].wait()
        for start in range(0, columns, LANE):
            at = slice(start, start + LANE)
            turned_ref[at, part] = x_ref[part, at].T
    copies[0].wait()
    me = lax.axis_index("band")
    for k, out_ref in enumerate(out_refs):
        target = jnp.bitwise_xor(me, k)
        block = 0
        for j in range(1, band_count):
            block = jnp.where(owner_ref[j] == target, j, block)
        out_ref[...] = turned_ref[pl.ds(pl.multiple_of(block * width, SUB), width), :]


def send_blocks(pixels, owner, band_count, width):
    features, columns = pixels.shape
    any_space = pl.BlockSpec(memory_space=pl.ANY)
    return pl.pallas_call(
        send_kernel,
        out_shape=[jax.ShapeDtypeStruct((width, features), BF16)] * band_count,
        in_specs=[any_space, any_space],
        out_specs=[pl.BlockSpec(memory_space=pltpu.VMEM)] * band_count,
        scratch_shapes=[
            pltpu.SMEM(owner.shape, jnp.int32),
            pltpu.VMEM((features, columns), BF16),
            pltpu.VMEM((columns, features), BF16),
            pltpu.SemaphoreType.DMA,
            pltpu.SemaphoreType.DMA((features // LANE,)),
        ],
        compiler_params=params(),
        name="send_blocks",
    )(in_hbm(owner), in_hbm(pixels))


def exchange(pieces):
    arrived = list(pieces)
    for k in reversed(range(1, len(pieces))):
        arrived[k] = swap(pieces[k], "band", k)
    return arrived


def expand_table(table, rows, half_width_padded, half_width, transpose):
    position = iota2((rows, WLAT * WLON), 0)
    line, col = position // half_width_padded, position % half_width_padded
    target = iota2((rows, WLAT * WLON), 1)
    pick = jnp.where((target == line * WLON + col % WLON) & (col < half_width), 1.0, 0.0).astype(BF16)
    left = (dot_nt if transpose else dot_nn)(pick, table).astype(BF16)
    full = dot_nt(left, pick)
    row_window = (iota2((rows, 1), 0) % half_width_padded) // WLON
    col_window = (iota2((1, rows), 1) % half_width_padded) // WLON
    return jnp.where(row_window == col_window, full, 0.0).astype(BF16)


def prep_kernel(
    row_share,
    half_width,
    half_width_padded,
    group_ref,
    frozen_ref,
    factors_ref,
    level_ref,
    mixer_ref,
    merged_ref,
    up_ref,
    down_ref,
    mix_ref,
    mix_t_ref,
):
    reps, _, rank, share = factors_ref.shape
    levels = level_ref.shape[0]
    variables = group_ref.shape[0]
    channels = variables * frozen_ref.shape[1]
    up = jnp.concatenate([factors_ref[r, 0] for r in range(reps)], axis=1)
    source, target = iota2((share, channels), 0), iota2((share, channels), 1)
    down_t = jnp.zeros((rank, channels), F32)
    for r in range(reps):
        place = jnp.where((target == source + r * row_share) & (source < row_share), 1.0, 0.0)
        down_t = down_t + dot_nn(factors_ref[r, 1], place.astype(BF16))
    down_t = down_t.astype(BF16)
    down_ref[...] = down_t
    base = jnp.concatenate([frozen_ref[group_ref[v]].astype(F32) for v in range(variables)], axis=0)
    merged = (base + dot_tn(down_t, up)).astype(BF16)
    stacked = jnp.concatenate([merged, up], axis=0)
    merged_ref[...] = jnp.zeros_like(merged_ref)
    for level in range(levels):
        through = dot_nn(stacked, level_ref[level])
        weights = through[:channels].astype(BF16)
        for s in range(merged_ref.shape[0]):
            offset = (s * levels * channels) % LANE + level * channels
            merged_ref[s, offset : offset + channels, :] = weights
        up_high, up_low = split_hi_lo(through[channels:])
        up_ref[level, :rank, :] = up_high
        up_ref[level, rank:, :] = up_low
    rows = mix_ref.shape[0]
    mix_ref[...] = expand_table(mixer_ref[...], rows, half_width_padded, half_width, False)
    mix_t_ref[...] = expand_table(mixer_ref[...], rows, half_width_padded, half_width, True)


def prepare(groups, frozen, factors, level_weight, mixer, samples, row_share, half_width, half_width_padded):
    reps, _, rank, _ = factors.shape
    levels, feature_dim, _ = level_weight.shape
    channels = groups.shape[0] * frozen.shape[1]
    reach = round_up(levels * channels + LANE // 2, LANE)
    rows = WLAT * half_width_padded
    vmem = pl.BlockSpec(memory_space=pltpu.VMEM)
    flops = 2 * levels * (channels + rank) * feature_dim * feature_dim + 4 * rows * rows * WLAT * WLON
    return pl.pallas_call(
        functools.partial(prep_kernel, row_share, half_width, half_width_padded),
        out_shape=[
            jax.ShapeDtypeStruct((samples, reach, feature_dim), BF16),
            jax.ShapeDtypeStruct((levels, 2 * rank, feature_dim), BF16),
            jax.ShapeDtypeStruct((rank, channels), BF16),
            jax.ShapeDtypeStruct((rows, rows), BF16),
            jax.ShapeDtypeStruct((rows, rows), BF16),
        ],
        in_specs=[pl.BlockSpec(memory_space=pltpu.SMEM)] + [vmem] * 4,
        out_specs=[vmem] * 5,
        compiler_params=params(),
        cost_estimate=pl.CostEstimate(flops=flops, bytes_accessed=4 * 2**20, transcendentals=0),
        name="prepare",
    )(groups, in_hbm(frozen), factors, in_hbm(level_weight), in_hbm(mixer))


def normal_parts(values):
    bell = jnp.exp(-0.5 * values * values)
    t = 1.0 / (1.0 + 0.23164189 * jnp.abs(values))
    tail = t * (
        0.127414796 + t * (-0.142248368 + t * (0.7107068705 + t * (-0.7265760135 + t * 0.5307027145)))
    )
    tail = tail * bell
    return jnp.where(values < 0.0, tail, 1.0 - tail), 0.3989422804014327 * bell


def factor_shares(total, up_ref, down_ref, level_ref):
    levels, two_rank, feature_dim = up_ref.shape
    rank, channels = down_ref.shape
    high, low = split_hi_lo(total)
    down = down_ref[...]
    first = jnp.zeros((rank, channels), F32)
    second = jnp.zeros((two_rank, feature_dim), F32)
    for level in range(levels):
        at = slice(level * channels, (level + 1) * channels)
        both = dot_nt(up_ref[level], high[at])
        first = first + both[:rank] + both[rank:] + dot_nt(up_ref[level, :rank, :], low[at])
        through = dot_nn(down, high[at]) + dot_nn(down, low[at])
        through = jnp.concatenate(split_hi_lo(through), axis=0)
        second = second + dot_nt(through, level_ref[level])
    return first, second[:rank] + second[rank:]


def mix_kernel(
    piece_refs,
    merged_ref,
    mix_ref,
    mix_t_ref,
    grad_ref,
    up_ref,
    down_ref,
    level_ref,
    mixed_ref,
    share_ref,
    total_ref,
    pre_ref,
    tokens_ref,
    grad_pre_ref,
    second_ref,
    arrived_ref,
):
    samples, reach, feature_dim = merged_ref.shape
    _, _, width, features = arrived_ref.shape
    depth = features // samples
    rows = WLAT * width
    half = pl.program_id(1)
    step = pl.program_id(0) * pl.num_programs(1) + half

    @pl.when(half == 0)
    def _():
        for h in range(arrived_ref.shape[0]):
            within = slice(h * width, (h + 1) * width)
            if len(piece_refs) == 1:
                arrived_ref[h] = piece_refs[0][:, within, :]
            else:
                me = lax.axis_index("band")
                for k, piece_ref in enumerate(piece_refs):
                    arrived_ref[h, jnp.bitwise_xor(me, k)] = piece_ref[within, :]

    def forward(s):
        lane = s * depth // LANE * LANE
        pixels = arrived_ref[half, :, :, lane : lane + reach].reshape(rows, reach)
        tokens = dot_nn(pixels, merged_ref[s]).astype(BF16)
        tokens_ref[s] = tokens
        pre_ref[s] = dot_nn(mix_ref[...], tokens)
        return pixels

    def pointwise(s):
        for line in range(WLAT):
            for start in range(0, width, SUB):
                at, within = pl.ds(line * width + start, SUB), pl.ds(start, SUB)
                pre = pre_ref[s, at, :]
                cdf, pdf = normal_parts(pre)
                tokens = tokens_ref[s, at, :].astype(F32)
                mixed_ref[s, line, within, :] = (tokens + pre * cdf).astype(BF16)
                grad = grad_ref[s, line, within, :].astype(F32)
                grad_pre_ref[s, at, :] = (grad * (cdf + pre * pdf)).astype(BF16)

    def backward(s, pixels):
        direct = grad_ref[s].reshape(rows, feature_dim).astype(F32)
        grad_tokens = dot_nn(mix_t_ref[...], grad_pre_ref[s]) + direct
        offset = s * depth % LANE
        return dot_tn(pixels, grad_tokens.astype(BF16))[offset : offset + depth]

    pixels = [forward(s) for s in range(samples)]
    share = jnp.zeros((depth, feature_dim), F32)
    for s in range(samples):
        pointwise(s)
        share = share + backward(s, pixels[s])

    @pl.when(step == 0)
    def _():
        total_ref[...] = share

    @pl.when(step != 0)
    def _():
        total_ref[...] = total_ref[...] + share

    @pl.when(step == pl.num_programs(0) * pl.num_programs(1) - 1)
    def _():
        first, second = factor_shares(total_ref[...], up_ref, down_ref, level_ref)
        second_ref[...] = second
        reps, channels = share_ref.shape[0], down_ref.shape[1]
        columns = feature_dim // reps
        me = lax.axis_index("rep")
        share_ref[...] = jnp.zeros_like(share_ref)
        for k in range(reps):
            lane = pl.multiple_of(jnp.bitwise_xor(me, k) * columns, LANE)
            share_ref[k, :, :columns] = second_ref[:, pl.ds(lane, columns)]
            share_ref[k, :, columns : columns + channels] = first


def mix_blocks(halves, arrived, merged, mix, mix_t, grad, up_through, down_t, level_weight, reps):
    samples, lat_rows, block_width, feature_dim = grad.shape
    width = block_width // halves
    lanes = arrived[0].shape[-1]
    reach = merged.shape[1]
    rows = WLAT * width
    rank, channels = down_t.shape

    def whole(shape):
        return pl.BlockSpec(shape, lambda w, h: (0,) * len(shape))

    block = pl.BlockSpec((samples, WLAT, width, feature_dim), lambda w, h: (0, w, h, 0))
    if len(arrived) == 1:
        arrived_specs = [pl.BlockSpec((WLAT, block_width, lanes), lambda w, h: (w, 0, 0))]
    else:
        arrived_specs = [whole(piece.shape) for piece in arrived]
    share_shape = (reps, rank, feature_dim // reps + round_up(channels, LANE))
    flops = 2 * samples * lat_rows * block_width * feature_dim * (2 * reach + 2 * rows)
    constants = [up_through, down_t, level_weight]
    return pl.pallas_call(
        lambda *refs: mix_kernel(refs[: len(arrived)], *refs[len(arrived) :]),
        out_shape=[
            jax.ShapeDtypeStruct(grad.shape, BF16),
            jax.ShapeDtypeStruct(share_shape, F32),
        ],
        grid=(lat_rows // WLAT, halves),
        in_specs=arrived_specs
        + [
            whole(merged.shape),
            whole(mix.shape),
            whole(mix_t.shape),
            block,
        ]
        + [whole(array.shape) for array in constants],
        out_specs=[block, whole(share_shape)],
        scratch_shapes=[
            pltpu.VMEM((lanes // samples, feature_dim), F32),
            pltpu.VMEM((samples, rows, feature_dim), F32),
            pltpu.VMEM((samples, rows, feature_dim), BF16),
            pltpu.VMEM((samples, rows, feature_dim), BF16),
            pltpu.VMEM((rank, feature_dim), F32),
            pltpu.VMEM((halves, WLAT, width, lanes), BF16),
        ],
        compiler_params=params(dimension_semantics=("arbitrary", "arbitrary")),
        cost_estimate=pl.CostEstimate(
            flops=flops,
            bytes_accessed=12 * 2**20,
            transcendentals=samples * lat_rows * block_width * feature_dim,
        ),
        name="mix_blocks",
    )(*arrived, merged, mix, mix_t, in_hbm(grad), *constants)


def sum_shares(shares):
    half = shares.shape[0] // 2
    while half >= 1:
        shares = shares[:half] + swap(shares[half:], "rep", half)
        half //= 2
    copies = jnp.broadcast_to(shares, (lax.axis_size("band"),) + shares.shape[1:])
    return jnp.sum(lax.all_to_all(copies, "band", split_axis=0, concat_axis=0, tiled=True), axis=0)


def on_device(
    patches,
    variable_group_index,
    frozen_patch_weight,
    adapter_down,
    adapter_up,
    level_merge_weight,
    window_patch_mixer,
    column_block_owner,
    mixed_token_gradient,
):
    band_count, reps = lax.axis_size("band"), lax.axis_size("rep")
    samples, levels, channels, row_count, col_count = patches.shape
    feature_dim = frozen_patch_weight.shape[2]
    rank, col_share = adapter_up.shape
    row_share = adapter_down.shape[0]
    lat_rows = band_count * row_count
    block_width = col_count // band_count
    halves = 2 if block_width % (2 * SUB * WLON // 4) == 0 else 1
    half_width = block_width // halves
    half_padded = round_up(half_width, SUB)
    padded_width = halves * half_padded
    features = samples * levels * channels

    pixels = patches.reshape(features, col_count)
    direct = band_count <= MAX_PERMUTES and lat_rows == WLAT and half_padded == half_width
    if direct and features % LANE == 0 and col_count % LANE == 0:
        arrived = exchange(send_blocks(pixels, column_block_owner, band_count, block_width))
    else:
        block_ids = jnp.arange(band_count, dtype=jnp.int32)
        inverse = jnp.sum(
            jnp.where(column_block_owner[None, :] == block_ids[:, None], block_ids[None, :], 0), axis=1
        )
        outgoing = jnp.take(pixels.T.reshape(band_count, block_width, features), inverse, axis=0)
        outgoing = jnp.pad(outgoing, ((0, 0), (0, padded_width - block_width), (0, 0)))
        arrived = [lax.all_to_all(outgoing, "band", split_axis=0, concat_axis=0, tiled=True)]

    pack_width = round_up(max(row_share, col_share), LANE)
    pack = jnp.stack(
        [
            jnp.pad(adapter_up, ((0, 0), (0, pack_width - col_share))),
            jnp.pad(adapter_down.T, ((0, 0), (0, pack_width - row_share))),
        ]
    )
    factors = lax.all_gather(pack, "rep", axis=0, tiled=False)
    merged, up_through, down_t, mix, mix_t = prepare(
        variable_group_index,
        frozen_patch_weight,
        factors,
        level_merge_weight,
        window_patch_mixer,
        samples,
        row_share,
        half_width,
        half_padded,
    )
    grad = mixed_token_gradient.reshape(samples, lat_rows, block_width, feature_dim)
    if padded_width != block_width:
        grad = jnp.pad(grad, ((0, 0), (0, 0), (0, padded_width - block_width), (0, 0)))
    mixed, shares = mix_blocks(
        halves, arrived, merged, mix, mix_t, grad, up_through, down_t, level_merge_weight, reps
    )
    if padded_width != block_width:
        mixed = mixed[:, :, :block_width]

    summed = sum_shares(shares)
    first_t = lax.dynamic_slice_in_dim(summed, col_share + lax.axis_index("rep") * row_share, row_share, 1)
    return (
        mixed.reshape(mixed_token_gradient.shape),
        first_t.T,
        summed[:, :col_share],
    )


def solution(mesh):
    in_specs = (
        P("rep", None, None, "band", None),
        P(),
        P(),
        P("rep", None),
        P(None, "rep"),
        P(),
        P(),
        P(),
        P("rep", "band", None, None, None),
    )
    out_specs = (P("rep", "band", None, None, None), P("rep", None), P(None, "rep"))
    return jax.shard_map(
        on_device, mesh=mesh, in_specs=in_specs, out_specs=out_specs, check_vma=False
    )
```

```python
import functools

import jax
import jax.numpy as jnp
from jax import lax
from jax.experimental import pallas as pl
from jax.experimental.pallas import tpu as pltpu
from jax.sharding import PartitionSpec as P

WLAT = 8
WLON = 12
LANE = 128
SUB = 16
VMEM_LIMIT = 24 * 1024 * 1024
MAX_PERMUTES = 8
FOLDS = 2
BF16 = jnp.bfloat16
F32 = jnp.float32


def round_up(value, step):
    return -(-value // step) * step


def dot_nn(a, b):
    return lax.dot_general(a, b, (((1,), (0,)), ((), ())), preferred_element_type=F32)


def dot_nt(a, b):
    return lax.dot_general(a, b, (((1,), (1,)), ((), ())), preferred_element_type=F32)


def dot_tn(a, b):
    return lax.dot_general(a, b, (((0,), (0,)), ((), ())), preferred_element_type=F32)


def split_hi_lo(values):
    high = values.astype(BF16)
    low = (values - high.astype(F32)).astype(BF16)
    return high, low


def iota2(shape, axis):
    return lax.broadcasted_iota(jnp.int32, shape, axis)


def params(**extra):
    return pltpu.CompilerParams(vmem_limit_bytes=VMEM_LIMIT, **extra)


def in_hbm(values):
    return pltpu.with_memory_space_constraint(values, pltpu.HBM)


def swap(values, axis, distance):
    count = lax.axis_size(axis)
    return lax.ppermute(values, axis, [(source, source ^ distance) for source in range(count)])


def distances(band_count):
    half = band_count // 2
    return [0] + [k for pair in zip(range(half, band_count), range(1, half)) for k in pair] + [band_count - 1]


def send_kernel(owner_hbm_ref, x_hbm_ref, *refs):
    out_refs, (owner_ref, x_ref, turned_ref, owner_sem, x_sems) = refs[:-5], refs[-5:]
    band_count, width = len(out_refs), out_refs[0].shape[0]
    features, columns = x_ref.shape
    copies = [pltpu.make_async_copy(owner_hbm_ref, owner_ref, owner_sem)]
    parts = [slice(start, start + LANE) for start in range(0, features, LANE)]
    for n, part in enumerate(parts):
        copies.append(pltpu.make_async_copy(x_hbm_ref.at[part, :], x_ref.at[part, :], x_sems.at[n]))
    for copy in copies:
        copy.start()
    for n, part in enumerate(parts):
        copies[n + 1].wait()
        for start in range(0, columns, LANE):
            at = slice(start, start + LANE)
            turned_ref[at, part] = x_ref[part, at].T
    copies[0].wait()
    me = lax.axis_index("band")
    for k, out_ref in zip(distances(band_count), out_refs):
        target = jnp.bitwise_xor(me, k)
        block = 0
        for j in range(1, band_count):
            block = jnp.where(owner_ref[j] == target, j, block)
        out_ref[...] = turned_ref[pl.ds(pl.multiple_of(block * width, SUB), width), :]


def send_blocks(pixels, owner, band_count, width):
    features, columns = pixels.shape
    any_space = pl.BlockSpec(memory_space=pl.ANY)
    return pl.pallas_call(
        send_kernel,
        out_shape=[jax.ShapeDtypeStruct((width, features), BF16)] * band_count,
        in_specs=[any_space, any_space],
        out_specs=[pl.BlockSpec(memory_space=pltpu.VMEM)] * band_count,
        scratch_shapes=[
            pltpu.SMEM(owner.shape, jnp.int32),
            pltpu.VMEM((features, columns), BF16),
            pltpu.VMEM((columns, features), BF16),
            pltpu.SemaphoreType.DMA,
            pltpu.SemaphoreType.DMA((features // LANE,)),
        ],
        compiler_params=params(),
        name="send_blocks",
    )(in_hbm(owner), in_hbm(pixels))


def exchange(pieces):
    return [piece if k == 0 else swap(piece, "band", k) for k, piece in zip(distances(len(pieces)), pieces)]


def expand_table(table, rows, half_width_padded, half_width, transpose):
    position = iota2((rows, WLAT * WLON), 0)
    line, col = position // half_width_padded, position % half_width_padded
    target = iota2((rows, WLAT * WLON), 1)
    pick = jnp.where((target == line * WLON + col % WLON) & (col < half_width), 1.0, 0.0).astype(BF16)
    left = (dot_nt if transpose else dot_nn)(pick, table).astype(BF16)
    full = dot_nt(left, pick)
    row_window = (iota2((rows, 1), 0) % half_width_padded) // WLON
    col_window = (iota2((1, rows), 1) % half_width_padded) // WLON
    return jnp.where(row_window == col_window, full, 0.0).astype(BF16)


def prep_kernel(
    row_share,
    half_width,
    half_width_padded,
    group_ref,
    frozen_ref,
    factors_ref,
    level_ref,
    mixer_ref,
    merged_ref,
    up_ref,
    down_ref,
    mix_ref,
    mix_t_ref,
):
    reps, _, rank, share = factors_ref.shape
    levels = level_ref.shape[0]
    variables = group_ref.shape[0]
    channels = variables * frozen_ref.shape[1]
    up = jnp.concatenate([factors_ref[r, 0] for r in range(reps)], axis=1)
    source, target = iota2((share, channels), 0), iota2((share, channels), 1)
    down_t = jnp.zeros((rank, channels), F32)
    for r in range(reps):
        place = jnp.where((target == source + r * row_share) & (source < row_share), 1.0, 0.0)
        down_t = down_t + dot_nn(factors_ref[r, 1], place.astype(BF16))
    down_t = down_t.astype(BF16)
    down_ref[...] = down_t
    base = jnp.concatenate([frozen_ref[group_ref[v]].astype(F32) for v in range(variables)], axis=0)
    merged = (base + dot_tn(down_t, up)).astype(BF16)
    stacked = jnp.concatenate([merged, up], axis=0)
    merged_ref[...] = jnp.zeros_like(merged_ref)
    for level in range(levels):
        through = dot_nn(stacked, level_ref[level])
        weights = through[:channels].astype(BF16)
        for s in range(merged_ref.shape[0]):
            offset = (s * levels * channels) % LANE + level * channels
            merged_ref[s, offset : offset + channels, :] = weights
        up_high, up_low = split_hi_lo(through[channels:])
        up_ref[level, :rank, :] = up_high
        up_ref[level, rank:, :] = up_low
    rows = mix_ref.shape[0]
    mix_ref[...] = expand_table(mixer_ref[...], rows, half_width_padded, half_width, False)
    mix_t_ref[...] = expand_table(mixer_ref[...], rows, half_width_padded, half_width, True)


def prepare(groups, frozen, factors, level_weight, mixer, samples, row_share, half_width, half_width_padded):
    reps, _, rank, _ = factors.shape
    levels, feature_dim, _ = level_weight.shape
    channels = groups.shape[0] * frozen.shape[1]
    reach = round_up(levels * channels + LANE // 2, LANE)
    rows = WLAT * half_width_padded
    vmem = pl.BlockSpec(memory_space=pltpu.VMEM)
    flops = 2 * levels * (channels + rank) * feature_dim * feature_dim + 4 * rows * rows * WLAT * WLON
    return pl.pallas_call(
        functools.partial(prep_kernel, row_share, half_width, half_width_padded),
        out_shape=[
            jax.ShapeDtypeStruct((samples, reach, feature_dim), BF16),
            jax.ShapeDtypeStruct((levels, 2 * rank, feature_dim), BF16),
            jax.ShapeDtypeStruct((rank, channels), BF16),
            jax.ShapeDtypeStruct((rows, rows), BF16),
            jax.ShapeDtypeStruct((rows, rows), BF16),
        ],
        in_specs=[pl.BlockSpec(memory_space=pltpu.SMEM)] + [vmem] * 4,
        out_specs=[vmem] * 5,
        compiler_params=params(),
        cost_estimate=pl.CostEstimate(flops=flops, bytes_accessed=4 * 2**20, transcendentals=0),
        name="prepare",
    )(groups, in_hbm(frozen), factors, in_hbm(level_weight), in_hbm(mixer))


def normal_parts(values):
    bell = jnp.exp2(values * values * -0.7213475204444817)
    scaled = 1.0 + 0.23164189 * jnp.abs(values)
    t = pl.reciprocal(scaled, approx=True)
    t = t * (2.0 - scaled * t)
    tail = t * (
        0.127414796 + t * (-0.142248368 + t * (0.7107068705 + t * (-0.7265760135 + t * 0.5307027145)))
    )
    tail = tail * bell
    return jnp.where(values < 0.0, tail, 1.0 - tail), 0.3989422804014327 * bell


def factor_shares(total, up_ref, down_ref, level_ref):
    levels, two_rank, feature_dim = up_ref.shape
    rank, channels = down_ref.shape
    high, low = split_hi_lo(total)
    down = down_ref[...]
    first = jnp.zeros((rank, channels), F32)
    second = jnp.zeros((two_rank, feature_dim), F32)
    for level in range(levels):
        at = slice(level * channels, (level + 1) * channels)
        both = dot_nt(up_ref[level], high[at])
        first = first + both[:rank] + both[rank:] + dot_nt(up_ref[level, :rank, :], low[at])
        through = dot_nn(down, high[at]) + dot_nn(down, low[at])
        through = jnp.concatenate(split_hi_lo(through), axis=0)
        second = second + dot_nt(through, level_ref[level])
    return first, second[:rank] + second[rank:]


def mix_kernel(
    piece_refs,
    merged_ref,
    mix_ref,
    mix_t_ref,
    grad_ref,
    up_ref,
    down_ref,
    level_ref,
    mixed_ref,
    share_ref,
    total_ref,
    pre_ref,
    tokens_ref,
    grad_pre_ref,
    arrived_ref,
):
    samples, reach, feature_dim = merged_ref.shape
    _, _, width, features = arrived_ref.shape
    depth = features // samples
    rows = WLAT * width
    half = pl.program_id(1)
    step = pl.program_id(0) * pl.num_programs(1) + half

    @pl.when(half == 0)
    def _():
        for h in range(arrived_ref.shape[0]):
            within = slice(h * width, (h + 1) * width)
            if len(piece_refs) == 1:
                arrived_ref[h] = piece_refs[0][:, within, :]
            else:
                me = lax.axis_index("band")
                for k, piece_ref in zip(distances(len(piece_refs)), piece_refs):
                    arrived_ref[h, jnp.bitwise_xor(me, k)] = piece_ref[within, :]

    def forward(s):
        lane = s * depth // LANE * LANE
        pixels = arrived_ref[half, :, :, lane : lane + reach].reshape(rows, reach)
        tokens = dot_nn(pixels, merged_ref[s]).astype(BF16)
        tokens_ref[s] = tokens
        pre_ref[s] = dot_nn(mix_ref[...], tokens)
        return pixels

    def pointwise(s):
        for line in range(WLAT):
            for start in range(0, width, SUB):
                at, within = pl.ds(line * width + start, SUB), pl.ds(start, SUB)
                pre = pre_ref[s, at, :]
                cdf, pdf = normal_parts(pre)
                tokens = tokens_ref[s, at, :].astype(F32)
                mixed_ref[s, line, within, :] = (tokens + pre * cdf).astype(BF16)
                grad = grad_ref[s, line, within, :].astype(F32)
                grad_pre_ref[s, at, :] = (grad * (cdf + pre * pdf)).astype(BF16)

    def backward(s, pixels):
        direct = grad_ref[s].reshape(rows, feature_dim).astype(F32)
        grad_tokens = dot_nn(mix_t_ref[...], grad_pre_ref[s]) + direct
        offset = s * depth % LANE
        return dot_tn(pixels, grad_tokens.astype(BF16))[offset : offset + depth]

    pixels = [forward(s) for s in range(samples)]
    share = jnp.zeros((depth, feature_dim), F32)
    for s in range(samples):
        pointwise(s)
        share = share + backward(s, pixels[s])

    @pl.when(step == 0)
    def _():
        total_ref[...] = share

    @pl.when(step != 0)
    def _():
        total_ref[...] = total_ref[...] + share

    @pl.when(step == pl.num_programs(0) * pl.num_programs(1) - 1)
    def _():
        first, second = factor_shares(total_ref[...], up_ref, down_ref, level_ref)
        rank, channels = down_ref.shape
        columns = share_ref.shape[2]
        reps = feature_dim // columns
        folds = rank // (share_ref.shape[1] - rank)
        depth_rows, fold_lanes, row_share = rank // folds, columns // folds, channels // reps
        packed = jnp.zeros((depth_rows, feature_dim), F32)
        row, lane = iota2((channels, feature_dim), 0), iota2((channels, feature_dim), 1)
        rep, lane = lane // columns, lane % columns
        for fold in range(folds):
            inside = lane - fold * fold_lanes
            pick = (row == inside + rep * row_share) & (inside >= 0) & (inside < row_share)
            pick = jnp.where(pick, 1.0, 0.0).astype(BF16)
            packed = packed + dot_nn(
                first[fold * depth_rows : (fold + 1) * depth_rows].astype(BF16), pick
            )
        payload = jnp.concatenate([second, packed], axis=0).astype(BF16)
        for slot in range(share_ref.shape[0]):
            at = slot % reps * columns
            share_ref[slot] = payload[:, at : at + columns]


def mix_blocks(halves, arrived, merged, mix, mix_t, grad, up_through, down_t, level_weight, band_count, reps):
    samples, lat_rows, block_width, feature_dim = grad.shape
    width = block_width // halves
    lanes = arrived[0].shape[-1]
    reach = merged.shape[1]
    rows = WLAT * width
    rank, channels = down_t.shape

    def whole(shape):
        return pl.BlockSpec(shape, lambda w, h: (0,) * len(shape))

    block = pl.BlockSpec((samples, WLAT, width, feature_dim), lambda w, h: (0, w, h, 0))
    if len(arrived) == 1:
        arrived_specs = [pl.BlockSpec((WLAT, block_width, lanes), lambda w, h: (w, 0, 0))]
    else:
        arrived_specs = [whole(piece.shape) for piece in arrived]
    share_shape = (band_count * reps, rank + rank // FOLDS, feature_dim // reps)
    flops = 2 * samples * lat_rows * block_width * feature_dim * (2 * reach + 2 * rows)
    constants = [up_through, down_t, level_weight]
    return pl.pallas_call(
        lambda *refs: mix_kernel(refs[: len(arrived)], *refs[len(arrived) :]),
        out_shape=[
            jax.ShapeDtypeStruct(grad.shape, BF16),
            jax.ShapeDtypeStruct(share_shape, BF16),
        ],
        grid=(lat_rows // WLAT, halves),
        in_specs=arrived_specs
        + [
            whole(merged.shape),
            whole(mix.shape),
            whole(mix_t.shape),
            block,
        ]
        + [whole(array.shape) for array in constants],
        out_specs=[block, whole(share_shape)],
        scratch_shapes=[
            pltpu.VMEM((lanes // samples, feature_dim), F32),
            pltpu.VMEM((samples, rows, feature_dim), F32),
            pltpu.VMEM((samples, rows, feature_dim), BF16),
            pltpu.VMEM((samples, rows, feature_dim), BF16),
            pltpu.VMEM((halves, WLAT, width, lanes), BF16),
        ],
        compiler_params=params(dimension_semantics=("arbitrary", "arbitrary")),
        cost_estimate=pl.CostEstimate(
            flops=flops,
            bytes_accessed=12 * 2**20,
            transcendentals=samples * lat_rows * block_width * feature_dim,
        ),
        name="mix_blocks",
    )(*arrived, merged, mix, mix_t, in_hbm(grad), *constants)


def sum_kernel(parts_ref, first_ref, second_ref):
    rank, row_share = first_ref.shape
    total = parts_ref[0].astype(F32)
    for n in range(1, parts_ref.shape[0]):
        total = total + parts_ref[n].astype(F32)
    second_ref[...] = total[:rank]
    depth_rows = total.shape[0] - rank
    for fold in range(rank // depth_rows):
        lane = fold * depth_rows * total.shape[1] // rank
        first_ref[fold * depth_rows : (fold + 1) * depth_rows, :] = total[rank:, lane : lane + row_share]


def sum_shares(shares, rank, row_share):
    parts = lax.all_to_all(shares, ("band", "rep"), split_axis=0, concat_axis=0, tiled=True)
    return pl.pallas_call(
        sum_kernel,
        out_shape=[
            jax.ShapeDtypeStruct((rank, row_share), F32),
            jax.ShapeDtypeStruct((rank, shares.shape[2]), F32),
        ],
        compiler_params=params(),
        name="sum_shares",
    )(parts)


def on_device(
    patches,
    variable_group_index,
    frozen_patch_weight,
    adapter_down,
    adapter_up,
    level_merge_weight,
    window_patch_mixer,
    column_block_owner,
    mixed_token_gradient,
):
    band_count, reps = lax.axis_size("band"), lax.axis_size("rep")
    samples, levels, channels, row_count, col_count = patches.shape
    feature_dim = frozen_patch_weight.shape[2]
    rank, col_share = adapter_up.shape
    row_share = adapter_down.shape[0]
    lat_rows = band_count * row_count
    block_width = col_count // band_count
    halves = 2 if block_width % (2 * SUB * WLON // 4) == 0 else 1
    half_width = block_width // halves
    half_padded = round_up(half_width, SUB)
    padded_width = halves * half_padded
    features = samples * levels * channels

    pixels = patches.reshape(features, col_count)
    direct = band_count <= MAX_PERMUTES and lat_rows == WLAT and half_padded == half_width
    if direct and features % LANE == 0 and col_count % LANE == 0:
        arrived = exchange(send_blocks(pixels, column_block_owner, band_count, block_width))
    else:
        block_ids = jnp.arange(band_count, dtype=jnp.int32)
        inverse = jnp.sum(
            jnp.where(column_block_owner[None, :] == block_ids[:, None], block_ids[None, :], 0), axis=1
        )
        outgoing = jnp.take(pixels.T.reshape(band_count, block_width, features), inverse, axis=0)
        outgoing = jnp.pad(outgoing, ((0, 0), (0, padded_width - block_width), (0, 0)))
        arrived = [lax.all_to_all(outgoing, "band", split_axis=0, concat_axis=0, tiled=True)]

    pack_width = round_up(max(row_share, col_share), LANE)
    pack = jnp.stack(
        [
            jnp.pad(adapter_up, ((0, 0), (0, pack_width - col_share))),
            jnp.pad(adapter_down.T, ((0, 0), (0, pack_width - row_share))),
        ]
    )
    factors = lax.all_gather(pack, "rep", axis=0, tiled=False)
    merged, up_through, down_t, mix, mix_t = prepare(
        variable_group_index,
        frozen_patch_weight,
        factors,
        level_merge_weight,
        window_patch_mixer,
        samples,
        row_share,
        half_width,
        half_padded,
    )
    grad = mixed_token_gradient.reshape(samples, lat_rows, block_width, feature_dim)
    if padded_width != block_width:
        grad = jnp.pad(grad, ((0, 0), (0, 0), (0, padded_width - block_width), (0, 0)))
    mixed, shares = mix_blocks(
        halves, arrived, merged, mix, mix_t, grad, up_through, down_t, level_merge_weight, band_count, reps
    )
    if padded_width != block_width:
        mixed = mixed[:, :, :block_width]
    first_t, second = sum_shares(shares, rank, row_share)
    return mixed.reshape(mixed_token_gradient.shape), first_t.T, second


def solution(mesh):
    in_specs = (
        P("rep", None, None, "band", None),
        P(),
        P(),
        P("rep", None),
        P(None, "rep"),
        P(),
        P(),
        P(),
        P("rep", "band", None, None, None),
    )
    out_specs = (P("rep", "band", None, None, None), P("rep", None), P(None, "rep"))
    return jax.shard_map(
        on_device, mesh=mesh, in_specs=in_specs, out_specs=out_specs, check_vma=False
    )
```

```python
import functools

import jax
import jax.numpy as jnp
from jax import lax
from jax.experimental import pallas as pl
from jax.experimental.pallas import tpu as pltpu
from jax.sharding import PartitionSpec as P

WLAT = 8
WLON = 12
LANE = 128
SUB = 16
VMEM_LIMIT = 24 * 1024 * 1024
MAX_PERMUTES = 8
FOLDS = 2
BF16 = jnp.bfloat16
F32 = jnp.float32


def round_up(value, step):
    return -(-value // step) * step


def dot_nn(a, b):
    return lax.dot_general(a, b, (((1,), (0,)), ((), ())), preferred_element_type=F32)


def dot_nt(a, b):
    return lax.dot_general(a, b, (((1,), (1,)), ((), ())), preferred_element_type=F32)


def dot_tn(a, b):
    return lax.dot_general(a, b, (((0,), (0,)), ((), ())), preferred_element_type=F32)


def split_hi_lo(values):
    high = values.astype(BF16)
    low = (values - high.astype(F32)).astype(BF16)
    return high, low


def iota2(shape, axis):
    return lax.broadcasted_iota(jnp.int32, shape, axis)


def params(**extra):
    return pltpu.CompilerParams(vmem_limit_bytes=VMEM_LIMIT, **extra)


def in_hbm(values):
    return pltpu.with_memory_space_constraint(values, pltpu.HBM)


def swap(values, axis, distance):
    count = lax.axis_size(axis)
    return lax.ppermute(values, axis, [(source, source ^ distance) for source in range(count)])


def distances(band_count):
    half = band_count // 2
    return [0] + list(range(half, band_count)) + list(range(2, half)) + [1]


def send_kernel(owner_hbm_ref, x_hbm_ref, *refs):
    out_refs, (owner_ref, x_ref, turned_ref, owner_sem, x_sems) = refs[:-5], refs[-5:]
    band_count, width = len(out_refs), out_refs[0].shape[0]
    features, columns = x_ref.shape
    copies = [pltpu.make_async_copy(owner_hbm_ref, owner_ref, owner_sem)]
    parts = [slice(start, start + LANE) for start in range(0, features, LANE)]
    for n, part in enumerate(parts):
        copies.append(pltpu.make_async_copy(x_hbm_ref.at[part, :], x_ref.at[part, :], x_sems.at[n]))
    for copy in copies:
        copy.start()
    for n, part in enumerate(parts):
        copies[n + 1].wait()
        for start in range(0, columns, LANE):
            at = slice(start, start + LANE)
            turned_ref[at, part] = x_ref[part, at].T
    copies[0].wait()
    me = lax.axis_index("band")
    for k, out_ref in zip(distances(band_count), out_refs):
        target = jnp.bitwise_xor(me, k)
        block = 0
        for j in range(1, band_count):
            block = jnp.where(owner_ref[j] == target, j, block)
        out_ref[...] = turned_ref[pl.ds(pl.multiple_of(block * width, SUB), width), :]


def send_blocks(pixels, owner, band_count, width):
    features, columns = pixels.shape
    any_space = pl.BlockSpec(memory_space=pl.ANY)
    return pl.pallas_call(
        send_kernel,
        out_shape=[jax.ShapeDtypeStruct((width, features), BF16)] * band_count,
        in_specs=[any_space, any_space],
        out_specs=[pl.BlockSpec(memory_space=pltpu.VMEM)] * band_count,
        scratch_shapes=[
            pltpu.SMEM(owner.shape, jnp.int32),
            pltpu.VMEM((features, columns), BF16),
            pltpu.VMEM((columns, features), BF16),
            pltpu.SemaphoreType.DMA,
            pltpu.SemaphoreType.DMA((features // LANE,)),
        ],
        compiler_params=params(),
        name="send_blocks",
    )(in_hbm(owner), in_hbm(pixels))


def exchange(pieces, factors):
    far = len(pieces) - 2
    late = lax.optimization_barrier((factors, *pieces[far:]))
    factors, pieces = late[0], list(pieces[:far]) + list(late[1:])
    return factors, [
        piece if k == 0 else swap(piece, "band", k) for k, piece in zip(distances(len(pieces)), pieces)
    ]


def expand_table(table, rows, half_width_padded, half_width, transpose):
    position = iota2((rows, WLAT * WLON), 0)
    line, col = position // half_width_padded, position % half_width_padded
    target = iota2((rows, WLAT * WLON), 1)
    pick = jnp.where((target == line * WLON + col % WLON) & (col < half_width), 1.0, 0.0).astype(BF16)
    left = (dot_nt if transpose else dot_nn)(pick, table).astype(BF16)
    full = dot_nt(left, pick)
    row_window = (iota2((rows, 1), 0) % half_width_padded) // WLON
    col_window = (iota2((1, rows), 1) % half_width_padded) // WLON
    return jnp.where(row_window == col_window, full, 0.0).astype(BF16)


def prep_kernel(
    row_share,
    half_width,
    half_width_padded,
    group_ref,
    frozen_ref,
    factors_ref,
    level_ref,
    mixer_ref,
    merged_ref,
    up_ref,
    down_ref,
    mix_ref,
    mix_t_ref,
):
    reps, _, rank, share = factors_ref.shape
    levels = level_ref.shape[0]
    variables = group_ref.shape[0]
    channels = variables * frozen_ref.shape[1]
    up = jnp.concatenate([factors_ref[r, 0] for r in range(reps)], axis=1)
    source, target = iota2((share, channels), 0), iota2((share, channels), 1)
    down_t = jnp.zeros((rank, channels), F32)
    for r in range(reps):
        place = jnp.where((target == source + r * row_share) & (source < row_share), 1.0, 0.0)
        down_t = down_t + dot_nn(factors_ref[r, 1], place.astype(BF16))
    down_t = down_t.astype(BF16)
    down_ref[...] = down_t
    base = jnp.concatenate([frozen_ref[group_ref[v]].astype(F32) for v in range(variables)], axis=0)
    merged = (base + dot_tn(down_t, up)).astype(BF16)
    stacked = jnp.concatenate([merged, up], axis=0)
    merged_ref[...] = jnp.zeros_like(merged_ref)
    for level in range(levels):
        through = dot_nn(stacked, level_ref[level])
        weights = through[:channels].astype(BF16)
        for s in range(merged_ref.shape[0]):
            offset = (s * levels * channels) % LANE + level * channels
            merged_ref[s, offset : offset + channels, :] = weights
        up_high, up_low = split_hi_lo(through[channels:])
        up_ref[level, :rank, :] = up_high
        up_ref[level, rank:, :] = up_low
    rows = mix_ref.shape[0]
    mix_ref[...] = expand_table(mixer_ref[...], rows, half_width_padded, half_width, False)
    mix_t_ref[...] = expand_table(mixer_ref[...], rows, half_width_padded, half_width, True)


def prepare(groups, frozen, factors, level_weight, mixer, samples, row_share, half_width, half_width_padded):
    reps, _, rank, _ = factors.shape
    levels, feature_dim, _ = level_weight.shape
    channels = groups.shape[0] * frozen.shape[1]
    reach = round_up(levels * channels + LANE // 2, LANE)
    rows = WLAT * half_width_padded
    vmem = pl.BlockSpec(memory_space=pltpu.VMEM)
    flops = 2 * levels * (channels + rank) * feature_dim * feature_dim + 4 * rows * rows * WLAT * WLON
    return pl.pallas_call(
        functools.partial(prep_kernel, row_share, half_width, half_width_padded),
        out_shape=[
            jax.ShapeDtypeStruct((samples, reach, feature_dim), BF16),
            jax.ShapeDtypeStruct((levels, 2 * rank, feature_dim), BF16),
            jax.ShapeDtypeStruct((rank, channels), BF16),
            jax.ShapeDtypeStruct((rows, rows), BF16),
            jax.ShapeDtypeStruct((rows, rows), BF16),
        ],
        in_specs=[pl.BlockSpec(memory_space=pltpu.SMEM)] + [vmem] * 4,
        out_specs=[vmem] * 5,
        compiler_params=params(),
        cost_estimate=pl.CostEstimate(flops=flops, bytes_accessed=4 * 2**20, transcendentals=0),
        name="prepare",
    )(groups, in_hbm(frozen), factors, in_hbm(level_weight), in_hbm(mixer))


def normal_parts(values):
    bell = jnp.exp2(values * values * -0.7213475204444817)
    scaled = 1.0 + 0.23164189 * jnp.abs(values)
    t = pl.reciprocal(scaled, approx=True)
    t = t * (2.0 - scaled * t)
    tail = t * (
        0.127414796 + t * (-0.142248368 + t * (0.7107068705 + t * (-0.7265760135 + t * 0.5307027145)))
    )
    tail = tail * bell
    return jnp.where(values < 0.0, tail, 1.0 - tail), 0.3989422804014327 * bell


def factor_shares(total, up_ref, down_ref, level_ref):
    levels, two_rank, feature_dim = up_ref.shape
    rank, channels = down_ref.shape
    high, low = split_hi_lo(total)
    down = down_ref[...]
    first = jnp.zeros((rank, channels), F32)
    second = jnp.zeros((two_rank, feature_dim), F32)
    for level in range(levels):
        at = slice(level * channels, (level + 1) * channels)
        both = dot_nt(up_ref[level], high[at])
        first = first + both[:rank] + both[rank:] + dot_nt(up_ref[level, :rank, :], low[at])
        through = dot_nn(down, high[at]) + dot_nn(down, low[at])
        through = jnp.concatenate(split_hi_lo(through), axis=0)
        second = second + dot_nt(through, level_ref[level])
    return first, second[:rank] + second[rank:]


def mix_kernel(
    piece_refs,
    merged_ref,
    mix_ref,
    mix_t_ref,
    up_ref,
    down_ref,
    grad_hbm_ref,
    level_hbm_ref,
    mixed_hbm_ref,
    share_ref,
    arrived_ref,
    grad_ref,
    mixed_ref,
    level_ref,
    total_ref,
    pre_ref,
    tokens_ref,
    grad_pre_ref,
    grad_sems,
    mixed_sems,
    level_sem,
):
    samples, reach, feature_dim = merged_ref.shape
    chunk_count, _, width, _ = grad_ref.shape
    halves = piece_refs[0].shape[-2] // width
    depth = piece_refs[0].shape[-1] // samples
    rows = WLAT * width

    def place(n):
        window_row, half, s = n // (halves * samples), n // samples % halves, n % samples
        lines, columns = pl.ds(window_row * WLAT, WLAT), pl.ds(half * width, width)
        return window_row, half, s, (s, lines, columns)

    loads = [
        pltpu.make_async_copy(grad_hbm_ref.at[place(n)[3]], grad_ref.at[n], grad_sems.at[n])
        for n in range(chunk_count)
    ]
    stores = [
        pltpu.make_async_copy(mixed_ref.at[n], mixed_hbm_ref.at[place(n)[3]], mixed_sems.at[n])
        for n in range(chunk_count)
    ]
    level_load = pltpu.make_async_copy(level_hbm_ref, level_ref, level_sem)
    for load in loads:
        load.start()
    level_load.start()
    if len(piece_refs) > 1:
        me = lax.axis_index("band")
        for k, piece_ref in zip(distances(len(piece_refs)), piece_refs):
            for half in range(halves):
                within = slice(half * width, (half + 1) * width)
                arrived_ref[half, jnp.bitwise_xor(me, k)] = piece_ref[within, :]

    def pixels_of(n):
        window_row, half, s, _ = place(n)
        lanes = slice(s * depth // LANE * LANE, s * depth // LANE * LANE + reach)
        if len(piece_refs) > 1:
            block = arrived_ref[half, :, :, lanes]
        else:
            lines = slice(window_row * WLAT, (window_row + 1) * WLAT)
            block = piece_refs[0][lines, half * width : (half + 1) * width, lanes]
        return block.reshape(rows, reach)

    def forward(n):
        tokens = dot_nn(pixels_of(n), merged_ref[n % samples]).astype(BF16)
        tokens_ref[n] = tokens
        pre_ref[n] = dot_nn(mix_ref[...], tokens)

    def pointwise(n):
        loads[n].wait()
        for line in range(WLAT):
            for start in range(0, width, SUB):
                at, within = pl.ds(line * width + start, SUB), pl.ds(start, SUB)
                pre = pre_ref[n, at, :]
                cdf, pdf = normal_parts(pre)
                tokens = tokens_ref[n, at, :].astype(F32)
                mixed_ref[n, line, within, :] = (tokens + pre * cdf).astype(BF16)
                grad = grad_ref[n, line, within, :].astype(F32)
                grad_pre_ref[n, at, :] = (grad * (cdf + pre * pdf)).astype(BF16)
        stores[n].start()

    def backward(n):
        direct = grad_ref[n].reshape(rows, feature_dim).astype(F32)
        grad_tokens = dot_nn(mix_t_ref[...], grad_pre_ref[n]) + direct
        offset = n % samples * depth % LANE
        share = dot_tn(pixels_of(n), grad_tokens.astype(BF16))[offset : offset + depth]
        total_ref[...] = share if n == 0 else total_ref[...] + share

    forward(0)
    for n in range(chunk_count):
        if n + 1 < chunk_count:
            forward(n + 1)
        pointwise(n)
        backward(n)

    level_load.wait()
    first, second = factor_shares(total_ref[...], up_ref, down_ref, level_ref)
    rank, channels = down_ref.shape
    columns = share_ref.shape[2]
    reps = feature_dim // columns
    folds = rank // (share_ref.shape[1] - rank)
    depth_rows, fold_lanes, row_share = rank // folds, columns // folds, channels // reps
    packed = jnp.zeros((depth_rows, feature_dim), F32)
    row, lane = iota2((channels, feature_dim), 0), iota2((channels, feature_dim), 1)
    rep, lane = lane // columns, lane % columns
    for fold in range(folds):
        inside = lane - fold * fold_lanes
        pick = (row == inside + rep * row_share) & (inside >= 0) & (inside < row_share)
        pick = jnp.where(pick, 1.0, 0.0).astype(BF16)
        part = first[fold * depth_rows : (fold + 1) * depth_rows].astype(BF16)
        packed = packed + dot_nn(part, pick)
    payload = jnp.concatenate([second, packed], axis=0).astype(BF16)
    for slot in range(share_ref.shape[0]):
        at = slot % reps * columns
        share_ref[slot] = payload[:, at : at + columns]
    for store in stores:
        store.wait()


def mix_blocks(halves, arrived, merged, mix, mix_t, grad, up_through, down_t, level_weight, band_count, reps):
    samples, lat_rows, block_width, feature_dim = grad.shape
    width = block_width // halves
    lanes = arrived[0].shape[-1]
    reach = merged.shape[1]
    rows = WLAT * width
    rank = down_t.shape[0]
    chunks = lat_rows // WLAT * halves * samples
    share_shape = (band_count * reps, rank + rank // FOLDS, feature_dim // reps)
    flops = 2 * samples * lat_rows * block_width * feature_dim * (2 * reach + 2 * rows)
    vmem = pl.BlockSpec(memory_space=pltpu.VMEM)
    any_space = pl.BlockSpec(memory_space=pl.ANY)
    local = [*arrived, merged, mix, mix_t, up_through, down_t]
    return pl.pallas_call(
        lambda *refs: mix_kernel(refs[: len(arrived)], *refs[len(arrived) :]),
        out_shape=[
            jax.ShapeDtypeStruct(grad.shape, BF16),
            jax.ShapeDtypeStruct(share_shape, BF16),
        ],
        in_specs=[vmem] * len(local) + [any_space, any_space],
        out_specs=[any_space, vmem],
        scratch_shapes=[
            pltpu.VMEM((halves, WLAT, width, lanes), BF16),
            pltpu.VMEM((chunks, WLAT, width, feature_dim), BF16),
            pltpu.VMEM((chunks, WLAT, width, feature_dim), BF16),
            pltpu.VMEM(level_weight.shape, BF16),
            pltpu.VMEM((lanes // samples, feature_dim), F32),
            pltpu.VMEM((chunks, rows, feature_dim), F32),
            pltpu.VMEM((chunks, rows, feature_dim), BF16),
            pltpu.VMEM((chunks, rows, feature_dim), BF16),
            pltpu.SemaphoreType.DMA((chunks,)),
            pltpu.SemaphoreType.DMA((chunks,)),
            pltpu.SemaphoreType.DMA,
        ],
        compiler_params=params(),
        cost_estimate=pl.CostEstimate(
            flops=flops,
            bytes_accessed=12 * 2**20,
            transcendentals=samples * lat_rows * block_width * feature_dim,
        ),
        name="mix_blocks",
    )(*local, in_hbm(grad), in_hbm(level_weight))


def sum_kernel(parts_ref, first_ref, second_ref):
    rank, row_share = first_ref.shape
    total = parts_ref[0].astype(F32)
    for n in range(1, parts_ref.shape[0]):
        total = total + parts_ref[n].astype(F32)
    second_ref[...] = total[:rank]
    depth_rows = total.shape[0] - rank
    for fold in range(rank // depth_rows):
        lane = fold * depth_rows * total.shape[1] // rank
        first_ref[fold * depth_rows : (fold + 1) * depth_rows, :] = total[rank:, lane : lane + row_share]


def sum_shares(shares, rank, row_share):
    parts = lax.all_to_all(shares, ("band", "rep"), split_axis=0, concat_axis=0, tiled=True)
    return pl.pallas_call(
        sum_kernel,
        out_shape=[
            jax.ShapeDtypeStruct((rank, row_share), F32),
            jax.ShapeDtypeStruct((rank, shares.shape[2]), F32),
        ],
        compiler_params=params(),
        name="sum_shares",
    )(parts)


def on_device(
    patches,
    variable_group_index,
    frozen_patch_weight,
    adapter_down,
    adapter_up,
    level_merge_weight,
    window_patch_mixer,
    column_block_owner,
    mixed_token_gradient,
):
    band_count, reps = lax.axis_size("band"), lax.axis_size("rep")
    samples, levels, channels, row_count, col_count = patches.shape
    feature_dim = frozen_patch_weight.shape[2]
    rank, col_share = adapter_up.shape
    row_share = adapter_down.shape[0]
    lat_rows = band_count * row_count
    block_width = col_count // band_count
    halves = 2 if block_width % (2 * SUB * WLON // 4) == 0 else 1
    half_width = block_width // halves
    half_padded = round_up(half_width, SUB)
    padded_width = halves * half_padded
    features = samples * levels * channels

    pack_width = round_up(max(row_share, col_share), LANE)
    pack = jnp.stack(
        [
            jnp.pad(adapter_up, ((0, 0), (0, pack_width - col_share))),
            jnp.pad(adapter_down.T, ((0, 0), (0, pack_width - row_share))),
        ]
    )
    factors = lax.all_gather(pack, "rep", axis=0, tiled=False)

    pixels = patches.reshape(features, col_count)
    direct = band_count <= MAX_PERMUTES and lat_rows == WLAT and half_padded == half_width
    if direct and features % LANE == 0 and col_count % LANE == 0:
        pieces = send_blocks(pixels, column_block_owner, band_count, block_width)
        factors, arrived = exchange(pieces, factors)
    else:
        block_ids = jnp.arange(band_count, dtype=jnp.int32)
        inverse = jnp.sum(
            jnp.where(column_block_owner[None, :] == block_ids[:, None], block_ids[None, :], 0), axis=1
        )
        outgoing = jnp.take(pixels.T.reshape(band_count, block_width, features), inverse, axis=0)
        outgoing = jnp.pad(outgoing, ((0, 0), (0, padded_width - block_width), (0, 0)))
        arrived = [lax.all_to_all(outgoing, "band", split_axis=0, concat_axis=0, tiled=True)]

    merged, up_through, down_t, mix, mix_t = prepare(
        variable_group_index,
        frozen_patch_weight,
        factors,
        level_merge_weight,
        window_patch_mixer,
        samples,
        row_share,
        half_width,
        half_padded,
    )
    grad = mixed_token_gradient.reshape(samples, lat_rows, block_width, feature_dim)
    if padded_width != block_width:
        grad = jnp.pad(grad, ((0, 0), (0, 0), (0, padded_width - block_width), (0, 0)))
    mixed, shares = mix_blocks(
        halves, arrived, merged, mix, mix_t, grad, up_through, down_t, level_merge_weight, band_count, reps
    )
    if padded_width != block_width:
        mixed = mixed[:, :, :block_width]
    first_t, second = sum_shares(shares, rank, row_share)
    return mixed.reshape(mixed_token_gradient.shape), first_t.T, second


def solution(mesh):
    in_specs = (
        P("rep", None, None, "band", None),
        P(),
        P(),
        P("rep", None),
        P(None, "rep"),
        P(),
        P(),
        P(),
        P("rep", "band", None, None, None),
    )
    out_specs = (P("rep", "band", None, None, None), P("rep", None), P(None, "rep"))
    return jax.shard_map(
        on_device, mesh=mesh, in_specs=in_specs, out_specs=out_specs, check_vma=False
    )
```

```python
import functools

import jax
import jax.numpy as jnp
from jax import lax
from jax.experimental import pallas as pl
from jax.experimental.pallas import tpu as pltpu
from jax.sharding import PartitionSpec as P

WLAT = 8
WLON = 12
LANE = 128
SUB = 16
VMEM_LIMIT = 24 * 1024 * 1024
MAX_PERMUTES = 8
FOLDS = 2
COLUMNS = 256
BF16 = jnp.bfloat16
F32 = jnp.float32


def round_up(value, step):
    return -(-value // step) * step


def dot_nn(a, b):
    return lax.dot_general(a, b, (((1,), (0,)), ((), ())), preferred_element_type=F32)


def dot_nt(a, b):
    return lax.dot_general(a, b, (((1,), (1,)), ((), ())), preferred_element_type=F32)


def dot_tn(a, b):
    return lax.dot_general(a, b, (((0,), (0,)), ((), ())), preferred_element_type=F32)


def split_hi_lo(values):
    high = values.astype(BF16)
    low = (values - high.astype(F32)).astype(BF16)
    return high, low


def iota2(shape, axis):
    return lax.broadcasted_iota(jnp.int32, shape, axis)


def params(**extra):
    return pltpu.CompilerParams(vmem_limit_bytes=VMEM_LIMIT, **extra)


def in_hbm(values):
    return pltpu.with_memory_space_constraint(values, pltpu.HBM)


def swap(values, axis, distance):
    count = lax.axis_size(axis)
    return lax.ppermute(values, axis, [(source, source ^ distance) for source in range(count)])


def distances(band_count):
    half = band_count // 2
    return [0, 1] + list(range(half, band_count)) + list(range(2, half))


def send_kernel(owner_hbm_ref, x_hbm_ref, *refs):
    out_refs, (owner_ref, x_ref, turned_ref, owner_sem, x_sems) = refs[:-5], refs[-5:]
    band_count, width = len(out_refs), out_refs[0].shape[0]
    features, columns = x_ref.shape
    copies = [pltpu.make_async_copy(owner_hbm_ref, owner_ref, owner_sem)]
    parts = [slice(start, start + LANE) for start in range(0, features, LANE)]
    for n, part in enumerate(parts):
        copies.append(pltpu.make_async_copy(x_hbm_ref.at[part, :], x_ref.at[part, :], x_sems.at[n]))
    for copy in copies:
        copy.start()
    for n, part in enumerate(parts):
        copies[n + 1].wait()
        for start in range(0, columns, LANE):
            at = slice(start, start + LANE)
            turned_ref[at, part] = x_ref[part, at].T
    copies[0].wait()
    me = lax.axis_index("band")
    for k, out_ref in zip(distances(band_count), out_refs):
        target = jnp.bitwise_xor(me, k)
        block = 0
        for j in range(1, band_count):
            block = jnp.where(owner_ref[j] == target, j, block)
        out_ref[...] = turned_ref[pl.ds(pl.multiple_of(block * width, SUB), width), :]


def send_blocks(pixels, owner, band_count, width):
    features, columns = pixels.shape
    any_space = pl.BlockSpec(memory_space=pl.ANY)
    return pl.pallas_call(
        send_kernel,
        out_shape=[jax.ShapeDtypeStruct((width, features), BF16)] * band_count,
        in_specs=[any_space, any_space],
        out_specs=[pl.BlockSpec(memory_space=pltpu.VMEM)] * band_count,
        scratch_shapes=[
            pltpu.SMEM(owner.shape, jnp.int32),
            pltpu.VMEM((features, columns), BF16),
            pltpu.VMEM((columns, features), BF16),
            pltpu.SemaphoreType.DMA,
            pltpu.SemaphoreType.DMA((features // LANE,)),
        ],
        compiler_params=params(),
        name="send_blocks",
    )(in_hbm(owner), in_hbm(pixels))


def exchange(pieces, pack):
    order = distances(len(pieces))
    near = swap(pieces[1], "band", order[1])
    near, pack = lax.optimization_barrier((near, pack))
    factors = lax.all_gather(pack, "rep", axis=0, tiled=False)
    first_late = 2 + len(pieces) // 2
    far = [swap(piece, "band", k) for k, piece in zip(order[2:first_late], pieces[2:first_late])]
    factors, *late = lax.optimization_barrier((factors, *pieces[first_late:]))
    late = [swap(piece, "band", k) for k, piece in zip(order[first_late:], late)]
    return [pieces[0], near, *far, *late], factors


def expand_table(table, rows, half_width_padded, half_width, transpose):
    position = iota2((rows, WLAT * WLON), 0)
    line, col = position // half_width_padded, position % half_width_padded
    target = iota2((rows, WLAT * WLON), 1)
    pick = jnp.where((target == line * WLON + col % WLON) & (col < half_width), 1.0, 0.0).astype(BF16)
    left = (dot_nt if transpose else dot_nn)(pick, table).astype(BF16)
    full = dot_nt(left, pick)
    row_window = (iota2((rows, 1), 0) % half_width_padded) // WLON
    col_window = (iota2((1, rows), 1) % half_width_padded) // WLON
    return jnp.where(row_window == col_window, full, 0.0).astype(BF16)


def prep_kernel(
    row_share,
    half_width,
    half_width_padded,
    group_ref,
    frozen_ref,
    factors_ref,
    level_ref,
    mixer_ref,
    merged_ref,
    up_ref,
    down_ref,
    mix_ref,
    mix_t_ref,
):
    reps, _, rank, share = factors_ref.shape
    levels = level_ref.shape[0]
    variables = group_ref.shape[0]
    channels = variables * frozen_ref.shape[1]
    up = jnp.concatenate([factors_ref[r, 0] for r in range(reps)], axis=1)
    source, target = iota2((share, channels), 0), iota2((share, channels), 1)
    down_t = jnp.zeros((rank, channels), F32)
    for r in range(reps):
        place = jnp.where((target == source + r * row_share) & (source < row_share), 1.0, 0.0)
        down_t = down_t + dot_nn(factors_ref[r, 1], place.astype(BF16))
    down_t = down_t.astype(BF16)
    down_ref[...] = down_t
    base = jnp.concatenate([frozen_ref[group_ref[v]].astype(F32) for v in range(variables)], axis=0)
    merged = (base + dot_tn(down_t, up)).astype(BF16)
    stacked = jnp.concatenate([merged, up], axis=0)
    merged_ref[...] = jnp.zeros_like(merged_ref)
    for level in range(levels):
        through = dot_nn(stacked, level_ref[level])
        weights = through[:channels].astype(BF16)
        for s in range(merged_ref.shape[0]):
            offset = (s * levels * channels) % LANE + level * channels
            merged_ref[s, offset : offset + channels, :] = weights
        up_high, up_low = split_hi_lo(through[channels:])
        up_ref[level, :rank, :] = up_high
        up_ref[level, rank:, :] = up_low
    rows = mix_ref.shape[0]
    mix_ref[...] = expand_table(mixer_ref[...], rows, half_width_padded, half_width, False)
    mix_t_ref[...] = expand_table(mixer_ref[...], rows, half_width_padded, half_width, True)


def prepare(groups, frozen, factors, level_weight, mixer, samples, row_share, half_width, half_width_padded):
    reps, _, rank, _ = factors.shape
    levels, feature_dim, _ = level_weight.shape
    channels = groups.shape[0] * frozen.shape[1]
    reach = round_up(levels * channels + LANE // 2, LANE)
    rows = WLAT * half_width_padded
    vmem = pl.BlockSpec(memory_space=pltpu.VMEM)
    flops = 2 * levels * (channels + rank) * feature_dim * feature_dim + 4 * rows * rows * WLAT * WLON
    return pl.pallas_call(
        functools.partial(prep_kernel, row_share, half_width, half_width_padded),
        out_shape=[
            jax.ShapeDtypeStruct((samples, reach, feature_dim), BF16),
            jax.ShapeDtypeStruct((levels, 2 * rank, feature_dim), BF16),
            jax.ShapeDtypeStruct((rank, channels), BF16),
            jax.ShapeDtypeStruct((rows, rows), BF16),
            jax.ShapeDtypeStruct((rows, rows), BF16),
        ],
        in_specs=[pl.BlockSpec(memory_space=pltpu.SMEM)] + [vmem] * 4,
        out_specs=[vmem] * 5,
        compiler_params=params(),
        cost_estimate=pl.CostEstimate(flops=flops, bytes_accessed=4 * 2**20, transcendentals=0),
        name="prepare",
    )(groups, in_hbm(frozen), factors, in_hbm(level_weight), in_hbm(mixer))


def normal_parts(values):
    bell = jnp.exp2(values * values * -0.7213475204444817)
    scaled = 1.0 + 0.23164189 * jnp.abs(values)
    t = pl.reciprocal(scaled, approx=True)
    t = t * (2.0 - scaled * t)
    tail = t * (
        0.127414796 + t * (-0.142248368 + t * (0.7107068705 + t * (-0.7265760135 + t * 0.5307027145)))
    )
    tail = tail * bell
    return jnp.where(values < 0.0, tail, 1.0 - tail), 0.3989422804014327 * bell


def factor_shares(total, up_ref, down_ref, level_ref):
    levels, two_rank, feature_dim = up_ref.shape
    rank, channels = down_ref.shape
    high, low = split_hi_lo(total)
    down = down_ref[...]
    first = jnp.zeros((rank, channels), F32)
    second = jnp.zeros((two_rank, feature_dim), F32)
    for level in range(levels):
        at = slice(level * channels, (level + 1) * channels)
        both = dot_nt(up_ref[level], high[at])
        first = first + both[:rank] + both[rank:] + dot_nt(up_ref[level, :rank, :], low[at])
        through = dot_nn(down, high[at]) + dot_nn(down, low[at])
        through = jnp.concatenate(split_hi_lo(through), axis=0)
        second = second + dot_nt(through, level_ref[level])
    return first, second[:rank] + second[rank:]


def mix_kernel(
    piece_refs,
    merged_ref,
    mix_ref,
    mix_t_ref,
    up_ref,
    down_ref,
    grad_hbm_ref,
    level_hbm_ref,
    mixed_hbm_ref,
    share_ref,
    arrived_ref,
    grad_ref,
    mixed_ref,
    level_ref,
    total_ref,
    pre_ref,
    tokens_ref,
    grad_pre_ref,
    grad_tokens_ref,
    turned_ref,
    grad_sems,
    mixed_sems,
    level_sem,
):
    samples, reach, feature_dim = merged_ref.shape
    chunk_count, _, width, _ = grad_ref.shape
    halves = piece_refs[0].shape[-2] // width
    depth = piece_refs[0].shape[-1] // samples
    rows = WLAT * width

    def place(n):
        window_row, half, s = n // (halves * samples), n // samples % halves, n % samples
        lines, columns = pl.ds(window_row * WLAT, WLAT), pl.ds(half * width, width)
        return window_row, half, s, (s, lines, columns)

    loads = [
        pltpu.make_async_copy(grad_hbm_ref.at[place(n)[3]], grad_ref.at[n], grad_sems.at[n])
        for n in range(chunk_count)
    ]
    stores = [
        pltpu.make_async_copy(mixed_ref.at[n], mixed_hbm_ref.at[place(n)[3]], mixed_sems.at[n])
        for n in range(chunk_count)
    ]
    level_load = pltpu.make_async_copy(level_hbm_ref, level_ref, level_sem)
    for load in loads:
        load.start()
    level_load.start()
    if len(piece_refs) > 1:
        me = lax.axis_index("band")
        for k, piece_ref in zip(distances(len(piece_refs)), piece_refs):
            for half in range(halves):
                within = slice(half * width, (half + 1) * width)
                arrived_ref[half, jnp.bitwise_xor(me, k)] = piece_ref[within, :]

    def pixels_of(n, lanes):
        window_row, half, _, _ = place(n)
        if len(piece_refs) > 1:
            block = arrived_ref[half, :, :, lanes]
        else:
            lines = slice(window_row * WLAT, (window_row + 1) * WLAT)
            block = piece_refs[0][lines, half * width : (half + 1) * width, lanes]
        return block.reshape(rows, lanes.stop - lanes.start)

    def turn(n):
        def part(lanes):
            turned_ref[n // samples, lanes, :] = pixels_of(n, lanes).T

        starts = range(0, samples * depth, LANE)
        return [functools.partial(part, slice(start, start + LANE)) for start in starts]

    def forward(n, columns):
        s = n % samples
        lane = s * depth // LANE * LANE

        def embed():
            pixels = pixels_of(n, slice(lane, lane + reach))
            tokens_ref[n, :, columns] = dot_nn(pixels, merged_ref[s, :, columns]).astype(BF16)

        def mixing():
            pre_ref[n, :, columns] = dot_nn(mix_ref[...], tokens_ref[n, :, columns])

        return [embed, mixing]

    def pointwise(n, columns):
        def part(line):
            for start in range(0, width, SUB):
                at, within = pl.ds(line * width + start, SUB), pl.ds(start, SUB)
                pre = pre_ref[n, at, columns]
                cdf, pdf = normal_parts(pre)
                tokens = tokens_ref[n, at, columns].astype(F32)
                mixed_ref[n, line, within, columns] = (tokens + pre * cdf).astype(BF16)
                grad = grad_ref[n, line, within, columns].astype(F32)
                grad_pre_ref[n, at, columns] = (grad * (cdf + pre * pdf)).astype(BF16)

        return [functools.partial(part, line) for line in range(WLAT)]

    def backward(n, columns):
        def spread():
            direct = grad_ref[n, :, :, columns].reshape(rows, COLUMNS).astype(F32)
            through = dot_nn(mix_t_ref[...], grad_pre_ref[n, :, columns])
            grad_tokens_ref[n, :, columns] = (through + direct).astype(BF16)

        def share():
            s = n % samples
            turned = turned_ref[n // samples, s * depth : (s + 1) * depth, :]
            part = dot_nn(turned, grad_tokens_ref[n, :, columns])
            total_ref[:, columns] = part if n == 0 else total_ref[:, columns] + part

        return [spread, share]

    units = [
        (n, slice(start, start + COLUMNS))
        for n in range(chunk_count)
        for start in range(0, feature_dim, COLUMNS)
    ]
    for step in forward(*units[0]):
        step()
    for load in loads:
        load.wait()
    for i, unit in enumerate(units):
        n, columns = unit
        others = []
        if i + 1 < len(units):
            others += forward(*units[i + 1])
        if columns.start == 0 and n % samples == 0:
            others += turn(n)
        if i > 0:
            others += backward(*units[i - 1])
        lines = pointwise(*unit)
        for line, vector_step in enumerate(lines):
            vector_step()
            for step in others[line * len(others) // len(lines) : (line + 1) * len(others) // len(lines)]:
                step()
        if columns.stop == feature_dim:
            stores[n].start()
    for step in backward(*units[-1]):
        step()

    level_load.wait()
    first, second = factor_shares(total_ref[...], up_ref, down_ref, level_ref)
    rank, channels = down_ref.shape
    columns = share_ref.shape[2]
    reps = feature_dim // columns
    folds = rank // (share_ref.shape[1] - rank)
    depth_rows, fold_lanes, row_share = rank // folds, columns // folds, channels // reps
    packed = jnp.zeros((depth_rows, feature_dim), F32)
    row, lane = iota2((channels, feature_dim), 0), iota2((channels, feature_dim), 1)
    rep, lane = lane // columns, lane % columns
    for fold in range(folds):
        inside = lane - fold * fold_lanes
        pick = (row == inside + rep * row_share) & (inside >= 0) & (inside < row_share)
        pick = jnp.where(pick, 1.0, 0.0).astype(BF16)
        part = first[fold * depth_rows : (fold + 1) * depth_rows].astype(BF16)
        packed = packed + dot_nn(part, pick)
    payload = jnp.concatenate([second, packed], axis=0).astype(BF16)
    for slot in range(share_ref.shape[0]):
        at = slot % reps * columns
        share_ref[slot] = payload[:, at : at + columns]
    for store in stores:
        store.wait()


def mix_blocks(halves, arrived, merged, mix, mix_t, grad, up_through, down_t, level_weight, band_count, reps):
    samples, lat_rows, block_width, feature_dim = grad.shape
    width = block_width // halves
    lanes = arrived[0].shape[-1]
    reach = merged.shape[1]
    rows = WLAT * width
    rank = down_t.shape[0]
    chunks = lat_rows // WLAT * halves * samples
    share_shape = (band_count * reps, rank + rank // FOLDS, feature_dim // reps)
    flops = 2 * samples * lat_rows * block_width * feature_dim * (2 * reach + 2 * rows)
    vmem = pl.BlockSpec(memory_space=pltpu.VMEM)
    any_space = pl.BlockSpec(memory_space=pl.ANY)
    local = [*arrived, merged, mix, mix_t, up_through, down_t]
    return pl.pallas_call(
        lambda *refs: mix_kernel(refs[: len(arrived)], *refs[len(arrived) :]),
        out_shape=[
            jax.ShapeDtypeStruct(grad.shape, BF16),
            jax.ShapeDtypeStruct(share_shape, BF16),
        ],
        in_specs=[vmem] * len(local) + [any_space, any_space],
        out_specs=[any_space, vmem],
        scratch_shapes=[
            pltpu.VMEM((halves, WLAT, width, lanes), BF16),
            pltpu.VMEM((chunks, WLAT, width, feature_dim), BF16),
            pltpu.VMEM((chunks, WLAT, width, feature_dim), BF16),
            pltpu.VMEM(level_weight.shape, BF16),
            pltpu.VMEM((lanes // samples, feature_dim), F32),
            pltpu.VMEM((chunks, rows, feature_dim), F32),
            pltpu.VMEM((chunks, rows, feature_dim), BF16),
            pltpu.VMEM((chunks, rows, feature_dim), BF16),
            pltpu.VMEM((chunks, rows, feature_dim), BF16),
            pltpu.VMEM((chunks // samples, lanes, rows), BF16),
            pltpu.SemaphoreType.DMA((chunks,)),
            pltpu.SemaphoreType.DMA((chunks,)),
            pltpu.SemaphoreType.DMA,
        ],
        compiler_params=params(),
        cost_estimate=pl.CostEstimate(
            flops=flops,
            bytes_accessed=12 * 2**20,
            transcendentals=samples * lat_rows * block_width * feature_dim,
        ),
        name="mix_blocks",
    )(*local, in_hbm(grad), in_hbm(level_weight))


def sum_kernel(parts_ref, first_ref, second_ref):
    rank, row_share = first_ref.shape
    total = parts_ref[0].astype(F32)
    for n in range(1, parts_ref.shape[0]):
        total = total + parts_ref[n].astype(F32)
    second_ref[...] = total[:rank]
    depth_rows = total.shape[0] - rank
    for fold in range(rank // depth_rows):
        lane = fold * depth_rows * total.shape[1] // rank
        first_ref[fold * depth_rows : (fold + 1) * depth_rows, :] = total[rank:, lane : lane + row_share]


def sum_shares(shares, rank, row_share):
    parts = lax.all_to_all(shares, ("band", "rep"), split_axis=0, concat_axis=0, tiled=True)
    return pl.pallas_call(
        sum_kernel,
        out_shape=[
            jax.ShapeDtypeStruct((rank, row_share), F32),
            jax.ShapeDtypeStruct((rank, shares.shape[2]), F32),
        ],
        compiler_params=params(),
        name="sum_shares",
    )(parts)


def on_device(
    patches,
    variable_group_index,
    frozen_patch_weight,
    adapter_down,
    adapter_up,
    level_merge_weight,
    window_patch_mixer,
    column_block_owner,
    mixed_token_gradient,
):
    band_count, reps = lax.axis_size("band"), lax.axis_size("rep")
    samples, levels, channels, row_count, col_count = patches.shape
    feature_dim = frozen_patch_weight.shape[2]
    rank, col_share = adapter_up.shape
    row_share = adapter_down.shape[0]
    lat_rows = band_count * row_count
    block_width = col_count // band_count
    halves = 2 if block_width % (2 * SUB * WLON // 4) == 0 else 1
    half_width = block_width // halves
    half_padded = round_up(half_width, SUB)
    padded_width = halves * half_padded
    features = samples * levels * channels

    pack_width = round_up(max(row_share, col_share), LANE)
    pack = jnp.stack(
        [
            jnp.pad(adapter_up, ((0, 0), (0, pack_width - col_share))),
            jnp.pad(adapter_down.T, ((0, 0), (0, pack_width - row_share))),
        ]
    )

    pixels = patches.reshape(features, col_count)
    direct = band_count <= MAX_PERMUTES and lat_rows == WLAT and half_padded == half_width
    if direct and features % LANE == 0 and col_count % LANE == 0:
        pieces = send_blocks(pixels, column_block_owner, band_count, block_width)
        arrived, factors = exchange(pieces, pack)
    else:
        block_ids = jnp.arange(band_count, dtype=jnp.int32)
        inverse = jnp.sum(
            jnp.where(column_block_owner[None, :] == block_ids[:, None], block_ids[None, :], 0), axis=1
        )
        outgoing = jnp.take(pixels.T.reshape(band_count, block_width, features), inverse, axis=0)
        outgoing = jnp.pad(outgoing, ((0, 0), (0, padded_width - block_width), (0, 0)))
        arrived = [lax.all_to_all(outgoing, "band", split_axis=0, concat_axis=0, tiled=True)]
        factors = lax.all_gather(pack, "rep", axis=0, tiled=False)

    merged, up_through, down_t, mix, mix_t = prepare(
        variable_group_index,
        frozen_patch_weight,
        factors,
        level_merge_weight,
        window_patch_mixer,
        samples,
        row_share,
        half_width,
        half_padded,
    )
    grad = mixed_token_gradient.reshape(samples, lat_rows, block_width, feature_dim)
    if padded_width != block_width:
        grad = jnp.pad(grad, ((0, 0), (0, 0), (0, padded_width - block_width), (0, 0)))
    mixed, shares = mix_blocks(
        halves, arrived, merged, mix, mix_t, grad, up_through, down_t, level_merge_weight, band_count, reps
    )
    if padded_width != block_width:
        mixed = mixed[:, :, :block_width]
    first_t, second = sum_shares(shares, rank, row_share)
    return mixed.reshape(mixed_token_gradient.shape), first_t.T, second


def solution(mesh):
    in_specs = (
        P("rep", None, None, "band", None),
        P(),
        P(),
        P("rep", None),
        P(None, "rep"),
        P(),
        P(),
        P(),
        P("rep", "band", None, None, None),
    )
    out_specs = (P("rep", "band", None, None, None), P("rep", None), P(None, "rep"))
    return jax.shard_map(
        on_device, mesh=mesh, in_specs=in_specs, out_specs=out_specs, check_vma=False
    )
```

```python
import functools

import jax
import jax.numpy as jnp
from jax import lax
from jax.experimental import pallas as pl
from jax.experimental.pallas import tpu as pltpu
from jax.sharding import PartitionSpec as P

WLAT = 8
WLON = 12
LANE = 128
SUB = 16
VMEM_LIMIT = 24 * 1024 * 1024
BANDS = 8
FOLDS = 2
COLUMNS = 256
BF16 = jnp.bfloat16
F32 = jnp.float32


def round_up(value, step):
    return -(-value // step) * step


def dot_nn(a, b):
    return lax.dot_general(a, b, (((1,), (0,)), ((), ())), preferred_element_type=F32)


def dot_nt(a, b):
    return lax.dot_general(a, b, (((1,), (1,)), ((), ())), preferred_element_type=F32)


def dot_tn(a, b):
    return lax.dot_general(a, b, (((0,), (0,)), ((), ())), preferred_element_type=F32)


def split_hi_lo(values):
    high = values.astype(BF16)
    low = (values - high.astype(F32)).astype(BF16)
    return high, low


def iota2(shape, axis):
    return lax.broadcasted_iota(jnp.int32, shape, axis)


def params(**extra):
    return pltpu.CompilerParams(vmem_limit_bytes=VMEM_LIMIT, **extra)


def in_hbm(values):
    return pltpu.with_memory_space_constraint(values, pltpu.HBM)


def swap(values, axis, distance):
    count = lax.axis_size(axis)
    return lax.ppermute(values, axis, [(source, source ^ distance) for source in range(count)])


def send_kernel(owner_hbm_ref, up_hbm_ref, down_hbm_ref, x_hbm_ref, own_ref, near_ref, beside_ref, *refs):
    far_refs, pack_ref, scratch = refs[:-8], refs[-8], refs[-7:]
    owner_ref, up_ref, down_ref, x_ref, turned_ref, small_sems, x_sems = scratch
    width = own_ref.shape[0]
    features, columns = x_ref.shape
    small = [
        pltpu.make_async_copy(source, target, small_sems.at[n])
        for n, (source, target) in enumerate(
            [(owner_hbm_ref, owner_ref), (up_hbm_ref, up_ref), (down_hbm_ref, down_ref)]
        )
    ]
    parts = [slice(start, start + LANE) for start in range(0, features, LANE)]
    large = [
        pltpu.make_async_copy(x_hbm_ref.at[part, :], x_ref.at[part, :], x_sems.at[n])
        for n, part in enumerate(parts)
    ]
    for copy in large + small:
        copy.start()
    for copy, part in zip(large, parts):
        copy.wait()
        for start in range(0, columns, LANE):
            at = slice(start, start + LANE)
            turned_ref[at, part] = x_ref[part, at].T
    for copy in small:
        copy.wait()
    pack_ref[...] = jnp.zeros_like(pack_ref)
    pack_ref[0, :, : up_ref.shape[1]] = up_ref[...]
    pack_ref[1, :, : down_ref.shape[1]] = down_ref[...]
    me = lax.axis_index("band")

    def block_of(distance):
        target = jnp.bitwise_xor(me, distance)
        block = 0
        for j in range(1, owner_ref.shape[0]):
            block = jnp.where(owner_ref[j] == target, j, block)
        return turned_ref[pl.ds(pl.multiple_of(block * width, SUB), width), :]

    own_ref[...] = block_of(0)
    near_ref[0] = block_of(2)
    near_ref[1] = block_of(3)
    beside_ref[0] = block_of(1)
    for n, far_ref in enumerate(far_refs):
        far_ref[...] = block_of(BANDS // 2 + n)


def send_blocks(pixels, owner, up, down_t, width, pack_shape):
    features, columns = pixels.shape
    any_space = pl.BlockSpec(memory_space=pl.ANY)
    vmem = pl.BlockSpec(memory_space=pltpu.VMEM)
    blocks = [(width, features), (2, width, features), (1, width, features)]
    blocks += [(width, features)] * (BANDS // 2)
    own, near, beside, *far, pack = pl.pallas_call(
        send_kernel,
        out_shape=[jax.ShapeDtypeStruct(shape, BF16) for shape in [*blocks, pack_shape]],
        in_specs=[any_space] * 4,
        out_specs=[vmem] * (len(blocks) + 1),
        scratch_shapes=[
            pltpu.SMEM(owner.shape, jnp.int32),
            pltpu.VMEM(up.shape, BF16),
            pltpu.VMEM(down_t.shape, BF16),
            pltpu.VMEM((features, columns), BF16),
            pltpu.VMEM((columns, features), BF16),
            pltpu.SemaphoreType.DMA((3,)),
            pltpu.SemaphoreType.DMA((features // LANE,)),
        ],
        compiler_params=params(),
        name="send_blocks",
    )(in_hbm(owner), in_hbm(up), in_hbm(down_t), in_hbm(pixels))
    return own, near, beside, far, pack


def exchange(own, near, beside, far, pack):
    by_z = swap(near, "band", 2)
    by_z, pack = lax.optimization_barrier((by_z, pack))
    arrived_far = [swap(piece, "band", BANDS // 2 + n) for n, piece in enumerate(far)]
    factors = lax.all_gather(pack, "rep", axis=0, tiled=False)
    joined, factors = lax.optimization_barrier((jnp.concatenate([beside, by_z[1:]], axis=0), factors))
    return [own, by_z, swap(joined, "band", 1), *arrived_far], factors


def expand_table(table, rows, half_width_padded, half_width, transpose):
    position = iota2((rows, WLAT * WLON), 0)
    line, col = position // half_width_padded, position % half_width_padded
    target = iota2((rows, WLAT * WLON), 1)
    pick = jnp.where((target == line * WLON + col % WLON) & (col < half_width), 1.0, 0.0).astype(BF16)
    left = (dot_nt if transpose else dot_nn)(pick, table).astype(BF16)
    full = dot_nt(left, pick)
    row_window = (iota2((rows, 1), 0) % half_width_padded) // WLON
    col_window = (iota2((1, rows), 1) % half_width_padded) // WLON
    return jnp.where(row_window == col_window, full, 0.0).astype(BF16)


def prep_kernel(
    row_share,
    half_width,
    half_width_padded,
    group_hbm_ref,
    frozen_ref,
    factors_ref,
    level_ref,
    mixer_ref,
    merged_ref,
    up_ref,
    down_ref,
    mix_ref,
    mix_t_ref,
    group_ref,
    group_sem,
):
    load = pltpu.make_async_copy(group_hbm_ref, group_ref, group_sem)
    load.start()
    reps, _, rank, share = factors_ref.shape
    levels = level_ref.shape[0]
    variables = group_ref.shape[0]
    channels = variables * frozen_ref.shape[1]
    up = jnp.concatenate([factors_ref[r, 0] for r in range(reps)], axis=1)
    source, target = iota2((share, channels), 0), iota2((share, channels), 1)
    down_t = jnp.zeros((rank, channels), F32)
    for r in range(reps):
        place = jnp.where((target == source + r * row_share) & (source < row_share), 1.0, 0.0)
        down_t = down_t + dot_nn(factors_ref[r, 1], place.astype(BF16))
    down_t = down_t.astype(BF16)
    down_ref[...] = down_t
    load.wait()
    base = jnp.concatenate([frozen_ref[group_ref[v]].astype(F32) for v in range(variables)], axis=0)
    merged = (base + dot_tn(down_t, up)).astype(BF16)
    stacked = jnp.concatenate([merged, up], axis=0)
    merged_ref[...] = jnp.zeros_like(merged_ref)
    for level in range(levels):
        through = dot_nn(stacked, level_ref[level])
        weights = through[:channels].astype(BF16)
        for s in range(merged_ref.shape[0]):
            offset = (s * levels * channels) % LANE + level * channels
            merged_ref[s, offset : offset + channels, :] = weights
        up_high, up_low = split_hi_lo(through[channels:])
        up_ref[level, :rank, :] = up_high
        up_ref[level, rank:, :] = up_low
    rows = mix_ref.shape[0]
    mix_ref[...] = expand_table(mixer_ref[...], rows, half_width_padded, half_width, False)
    mix_t_ref[...] = expand_table(mixer_ref[...], rows, half_width_padded, half_width, True)


def prepare(groups, frozen, factors, level_weight, mixer, samples, row_share, half_width, half_width_padded):
    reps, _, rank, _ = factors.shape
    levels, feature_dim, _ = level_weight.shape
    channels = groups.shape[0] * frozen.shape[1]
    reach = round_up(levels * channels + LANE // 2, LANE)
    rows = WLAT * half_width_padded
    vmem = pl.BlockSpec(memory_space=pltpu.VMEM)
    flops = 2 * levels * (channels + rank) * feature_dim * feature_dim + 4 * rows * rows * WLAT * WLON
    return pl.pallas_call(
        functools.partial(prep_kernel, row_share, half_width, half_width_padded),
        out_shape=[
            jax.ShapeDtypeStruct((samples, reach, feature_dim), BF16),
            jax.ShapeDtypeStruct((levels, 2 * rank, feature_dim), BF16),
            jax.ShapeDtypeStruct((rank, channels), BF16),
            jax.ShapeDtypeStruct((rows, rows), BF16),
            jax.ShapeDtypeStruct((rows, rows), BF16),
        ],
        in_specs=[pl.BlockSpec(memory_space=pl.ANY)] + [vmem] * 4,
        out_specs=[vmem] * 5,
        scratch_shapes=[pltpu.SMEM(groups.shape, jnp.int32), pltpu.SemaphoreType.DMA],
        compiler_params=params(),
        cost_estimate=pl.CostEstimate(flops=flops, bytes_accessed=4 * 2**20, transcendentals=0),
        name="prepare",
    )(in_hbm(groups), in_hbm(frozen), factors, in_hbm(level_weight), in_hbm(mixer))


def normal_parts(values):
    bell = jnp.exp2(values * values * -0.7213475204444817)
    scaled = 1.0 + 0.23164189 * jnp.abs(values)
    t = pl.reciprocal(scaled, approx=True)
    t = t * (2.0 - scaled * t)
    tail = t * (
        0.127414796 + t * (-0.142248368 + t * (0.7107068705 + t * (-0.7265760135 + t * 0.5307027145)))
    )
    tail = tail * bell
    return jnp.where(values < 0.0, tail, 1.0 - tail), 0.3989422804014327 * bell


def factor_shares(total, up_ref, down_ref, level_ref):
    levels, two_rank, feature_dim = up_ref.shape
    rank, channels = down_ref.shape
    high, low = split_hi_lo(total)
    down = down_ref[...]
    first = jnp.zeros((rank, channels), F32)
    second = jnp.zeros((two_rank, feature_dim), F32)
    for level in range(levels):
        at = slice(level * channels, (level + 1) * channels)
        both = dot_nt(up_ref[level], high[at])
        first = first + both[:rank] + both[rank:] + dot_nt(up_ref[level, :rank, :], low[at])
        through = dot_nn(down, high[at]) + dot_nn(down, low[at])
        through = jnp.concatenate(split_hi_lo(through), axis=0)
        second = second + dot_nt(through, level_ref[level])
    return first, second[:rank] + second[rank:]


def mix_kernel(
    piece_refs,
    merged_ref,
    mix_ref,
    mix_t_ref,
    up_ref,
    down_ref,
    grad_hbm_ref,
    level_hbm_ref,
    mixed_hbm_ref,
    share_ref,
    arrived_ref,
    grad_ref,
    mixed_ref,
    level_ref,
    total_ref,
    pre_ref,
    tokens_ref,
    grad_pre_ref,
    grad_tokens_ref,
    turned_ref,
    grad_sems,
    mixed_sems,
    level_sem,
):
    samples, reach, feature_dim = merged_ref.shape
    chunk_count, _, width, _ = grad_ref.shape
    halves = piece_refs[0].shape[-2] // width
    arrived_directly = len(piece_refs) > 1
    depth = piece_refs[0].shape[-1] // samples
    rows = WLAT * width

    def place(n):
        window_row, half, s = n // (halves * samples), n // samples % halves, n % samples
        lines, columns = pl.ds(window_row * WLAT, WLAT), pl.ds(half * width, width)
        return window_row, half, s, (s, lines, columns)

    loads = [
        pltpu.make_async_copy(grad_hbm_ref.at[place(n)[3]], grad_ref.at[n], grad_sems.at[n])
        for n in range(chunk_count)
    ]
    stores = [
        pltpu.make_async_copy(mixed_ref.at[n], mixed_hbm_ref.at[place(n)[3]], mixed_sems.at[n])
        for n in range(chunk_count)
    ]
    level_load = pltpu.make_async_copy(level_hbm_ref, level_ref, level_sem)
    for load in loads:
        load.start()
    level_load.start()
    if arrived_directly:
        own_ref, by_z_ref, by_x_ref, *far_refs = piece_refs
        sources = {0: own_ref, 1: by_x_ref.at[0], 2: by_z_ref.at[0], 3: by_x_ref.at[1]}
        sources |= {BANDS // 2 + n: far_ref for n, far_ref in enumerate(far_refs)}
        me = lax.axis_index("band")
        for distance, piece_ref in sources.items():
            for half in range(halves):
                within = slice(half * width, (half + 1) * width)
                arrived_ref[half, jnp.bitwise_xor(me, distance)] = piece_ref[within, :]

    def pixels_of(n, lanes):
        window_row, half, _, _ = place(n)
        if arrived_directly:
            block = arrived_ref[half, :, :, lanes]
        else:
            lines = slice(window_row * WLAT, (window_row + 1) * WLAT)
            block = piece_refs[0][lines, half * width : (half + 1) * width, lanes]
        return block.reshape(rows, lanes.stop - lanes.start)

    def turn(n):
        def part(lanes):
            turned_ref[n // samples, lanes, :] = pixels_of(n, lanes).T

        starts = range(0, samples * depth, LANE)
        return [functools.partial(part, slice(start, start + LANE)) for start in starts]

    def forward(n, columns):
        s = n % samples
        lane = s * depth // LANE * LANE

        def embed():
            pixels = pixels_of(n, slice(lane, lane + reach))
            tokens_ref[n, :, columns] = dot_nn(pixels, merged_ref[s, :, columns]).astype(BF16)

        def mixing():
            pre_ref[n, :, columns] = dot_nn(mix_ref[...], tokens_ref[n, :, columns])

        return [embed, mixing]

    def pointwise(n, columns):
        def part(line):
            for start in range(0, width, SUB):
                at, within = pl.ds(line * width + start, SUB), pl.ds(start, SUB)
                pre = pre_ref[n, at, columns]
                cdf, pdf = normal_parts(pre)
                tokens = tokens_ref[n, at, columns].astype(F32)
                mixed_ref[n, line, within, columns] = (tokens + pre * cdf).astype(BF16)
                grad = grad_ref[n, line, within, columns].astype(F32)
                grad_pre_ref[n, at, columns] = (grad * (cdf + pre * pdf)).astype(BF16)

        return [functools.partial(part, line) for line in range(WLAT)]

    def backward(n, columns):
        def spread():
            direct = grad_ref[n, :, :, columns].reshape(rows, COLUMNS).astype(F32)
            through = dot_nn(mix_t_ref[...], grad_pre_ref[n, :, columns])
            grad_tokens_ref[n, :, columns] = (through + direct).astype(BF16)

        def share():
            s = n % samples
            turned = turned_ref[n // samples, s * depth : (s + 1) * depth, :]
            part = dot_nn(turned, grad_tokens_ref[n, :, columns])
            total_ref[:, columns] = part if n == 0 else total_ref[:, columns] + part

        return [spread, share]

    units = [
        (n, slice(start, start + COLUMNS))
        for n in range(chunk_count)
        for start in range(0, feature_dim, COLUMNS)
    ]
    for step in forward(*units[0]):
        step()
    for load in loads:
        load.wait()
    for i, unit in enumerate(units):
        n, columns = unit
        others = []
        if i + 1 < len(units):
            others += forward(*units[i + 1])
        if columns.start == 0 and n % samples == 0:
            others += turn(n)
        if i > 0:
            others += backward(*units[i - 1])
        lines = pointwise(*unit)
        for line, vector_step in enumerate(lines):
            vector_step()
            for step in others[line * len(others) // len(lines) : (line + 1) * len(others) // len(lines)]:
                step()
        if columns.stop == feature_dim:
            stores[n].start()
    for step in backward(*units[-1]):
        step()

    level_load.wait()
    first, second = factor_shares(total_ref[...], up_ref, down_ref, level_ref)
    rank, channels = down_ref.shape
    columns = share_ref.shape[2]
    reps = feature_dim // columns
    folds = rank // (share_ref.shape[1] - rank)
    depth_rows, fold_lanes, row_share = rank // folds, columns // folds, channels // reps
    packed = jnp.zeros((depth_rows, feature_dim), F32)
    row, lane = iota2((channels, feature_dim), 0), iota2((channels, feature_dim), 1)
    rep, lane = lane // columns, lane % columns
    for fold in range(folds):
        inside = lane - fold * fold_lanes
        pick = (row == inside + rep * row_share) & (inside >= 0) & (inside < row_share)
        pick = jnp.where(pick, 1.0, 0.0).astype(BF16)
        part = first[fold * depth_rows : (fold + 1) * depth_rows].astype(BF16)
        packed = packed + dot_nn(part, pick)
    payload = jnp.concatenate([second, packed], axis=0).astype(BF16)
    for slot in range(share_ref.shape[0]):
        at = slot % reps * columns
        share_ref[slot] = payload[:, at : at + columns]
    for store in stores:
        store.wait()


def mix_blocks(halves, arrived, merged, mix, mix_t, grad, up_through, down_t, level_weight, band_count, reps):
    samples, lat_rows, block_width, feature_dim = grad.shape
    width = block_width // halves
    lanes = arrived[0].shape[-1]
    reach = merged.shape[1]
    rows = WLAT * width
    rank = down_t.shape[0]
    chunks = lat_rows // WLAT * halves * samples
    share_shape = (band_count * reps, rank + rank // FOLDS, feature_dim // reps)
    flops = 2 * samples * lat_rows * block_width * feature_dim * (2 * reach + 2 * rows)
    vmem = pl.BlockSpec(memory_space=pltpu.VMEM)
    any_space = pl.BlockSpec(memory_space=pl.ANY)
    local = [*arrived, merged, mix, mix_t, up_through, down_t]
    return pl.pallas_call(
        lambda *refs: mix_kernel(refs[: len(arrived)], *refs[len(arrived) :]),
        out_shape=[
            jax.ShapeDtypeStruct(grad.shape, BF16),
            jax.ShapeDtypeStruct(share_shape, BF16),
        ],
        in_specs=[vmem] * len(local) + [any_space, any_space],
        out_specs=[any_space, vmem],
        scratch_shapes=[
            pltpu.VMEM((halves, WLAT, width, lanes), BF16),
            pltpu.VMEM((chunks, WLAT, width, feature_dim), BF16),
            pltpu.VMEM((chunks, WLAT, width, feature_dim), BF16),
            pltpu.VMEM(level_weight.shape, BF16),
            pltpu.VMEM((lanes // samples, feature_dim), F32),
            pltpu.VMEM((chunks, rows, feature_dim), F32),
            pltpu.VMEM((chunks, rows, feature_dim), BF16),
            pltpu.VMEM((chunks, rows, feature_dim), BF16),
            pltpu.VMEM((chunks, rows, feature_dim), BF16),
            pltpu.VMEM((chunks // samples, lanes, rows), BF16),
            pltpu.SemaphoreType.DMA((chunks,)),
            pltpu.SemaphoreType.DMA((chunks,)),
            pltpu.SemaphoreType.DMA,
        ],
        compiler_params=params(),
        cost_estimate=pl.CostEstimate(
            flops=flops,
            bytes_accessed=12 * 2**20,
            transcendentals=samples * lat_rows * block_width * feature_dim,
        ),
        name="mix_blocks",
    )(*local, in_hbm(grad), in_hbm(level_weight))


def sum_kernel(parts_ref, first_ref, second_ref):
    rank, row_share = first_ref.shape
    total = parts_ref[0].astype(F32)
    for n in range(1, parts_ref.shape[0]):
        total = total + parts_ref[n].astype(F32)
    second_ref[...] = total[:rank]
    depth_rows = total.shape[0] - rank
    for fold in range(rank // depth_rows):
        lane = fold * depth_rows * total.shape[1] // rank
        first_ref[fold * depth_rows : (fold + 1) * depth_rows, :] = total[rank:, lane : lane + row_share]


def sum_shares(shares, rank, row_share):
    parts = lax.all_to_all(shares, ("band", "rep"), split_axis=0, concat_axis=0, tiled=True)
    return pl.pallas_call(
        sum_kernel,
        out_shape=[
            jax.ShapeDtypeStruct((rank, row_share), F32),
            jax.ShapeDtypeStruct((rank, shares.shape[2]), F32),
        ],
        compiler_params=params(),
        name="sum_shares",
    )(parts)


def on_device(
    patches,
    variable_group_index,
    frozen_patch_weight,
    adapter_down,
    adapter_up,
    level_merge_weight,
    window_patch_mixer,
    column_block_owner,
    mixed_token_gradient,
):
    band_count, reps = lax.axis_size("band"), lax.axis_size("rep")
    samples, levels, channels, row_count, col_count = patches.shape
    feature_dim = frozen_patch_weight.shape[2]
    rank, col_share = adapter_up.shape
    row_share = adapter_down.shape[0]
    lat_rows = band_count * row_count
    block_width = col_count // band_count
    halves = 2 if block_width % (2 * SUB * WLON // 4) == 0 else 1
    half_width = block_width // halves
    half_padded = round_up(half_width, SUB)
    padded_width = halves * half_padded
    features = samples * levels * channels

    pixels = patches.reshape(features, col_count)
    pack_shape = (2, rank, round_up(max(row_share, col_share), LANE))
    direct = band_count == BANDS and lat_rows == WLAT and half_padded == half_width
    if direct and features % LANE == 0 and col_count % LANE == 0:
        pieces = send_blocks(
            pixels, column_block_owner, adapter_up, adapter_down.T, block_width, pack_shape
        )
        arrived, factors = exchange(*pieces)
    else:
        block_ids = jnp.arange(band_count, dtype=jnp.int32)
        inverse = jnp.sum(
            jnp.where(column_block_owner[None, :] == block_ids[:, None], block_ids[None, :], 0), axis=1
        )
        outgoing = jnp.take(pixels.T.reshape(band_count, block_width, features), inverse, axis=0)
        outgoing = jnp.pad(outgoing, ((0, 0), (0, padded_width - block_width), (0, 0)))
        arrived = [lax.all_to_all(outgoing, "band", split_axis=0, concat_axis=0, tiled=True)]
        pack = jnp.stack(
            [
                jnp.pad(array, ((0, 0), (0, pack_shape[2] - array.shape[1])))
                for array in (adapter_up, adapter_down.T)
            ]
        )
        factors = lax.all_gather(pack, "rep", axis=0, tiled=False)

    merged, up_through, down_t, mix, mix_t = prepare(
        variable_group_index,
        frozen_patch_weight,
        factors,
        level_merge_weight,
        window_patch_mixer,
        samples,
        row_share,
        half_width,
        half_padded,
    )
    grad = mixed_token_gradient.reshape(samples, lat_rows, block_width, feature_dim)
    if padded_width != block_width:
        grad = jnp.pad(grad, ((0, 0), (0, 0), (0, padded_width - block_width), (0, 0)))
    mixed, shares = mix_blocks(
        halves, arrived, merged, mix, mix_t, grad, up_through, down_t, level_merge_weight, band_count, reps
    )
    if padded_width != block_width:
        mixed = mixed[:, :, :block_width]
    first_t, second = sum_shares(shares, rank, row_share)
    return mixed.reshape(mixed_token_gradient.shape), first_t.T, second


def solution(mesh):
    in_specs = (
        P("rep", None, None, "band", None),
        P(),
        P(),
        P("rep", None),
        P(None, "rep"),
        P(),
        P(),
        P(),
        P("rep", "band", None, None, None),
    )
    out_specs = (P("rep", "band", None, None, None), P("rep", None), P(None, "rep"))
    return jax.shard_map(
        on_device, mesh=mesh, in_specs=in_specs, out_specs=out_specs, check_vma=False
    )
```

```python
import functools

import jax
import jax.numpy as jnp
from jax import lax
from jax.experimental import pallas as pl
from jax.experimental.pallas import tpu as pltpu
from jax.sharding import PartitionSpec as P

WLAT = 8
WLON = 12
LANE = 128
SUB = 16
VMEM_LIMIT = 24 * 1024 * 1024
BANDS = 8
FOLDS = 2
COLUMNS = 256
BF16 = jnp.bfloat16
F32 = jnp.float32


def round_up(value, step):
    return -(-value // step) * step


def dot_nn(a, b):
    return lax.dot_general(a, b, (((1,), (0,)), ((), ())), preferred_element_type=F32)


def dot_nt(a, b):
    return lax.dot_general(a, b, (((1,), (1,)), ((), ())), preferred_element_type=F32)


def dot_tn(a, b):
    return lax.dot_general(a, b, (((0,), (0,)), ((), ())), preferred_element_type=F32)


def split_hi_lo(values):
    high = values.astype(BF16)
    low = (values - high.astype(F32)).astype(BF16)
    return high, low


def iota2(shape, axis):
    return lax.broadcasted_iota(jnp.int32, shape, axis)


def params(**extra):
    return pltpu.CompilerParams(vmem_limit_bytes=VMEM_LIMIT, **extra)


def in_hbm(values):
    return pltpu.with_memory_space_constraint(values, pltpu.HBM)


def swap(values, axis, distance):
    count = lax.axis_size(axis)
    return lax.ppermute(values, axis, [(source, source ^ distance) for source in range(count)])


def send_kernel(owner_hbm_ref, up_hbm_ref, down_hbm_ref, x_hbm_ref, own_ref, near_ref, beside_ref, *refs):
    far_refs, pack_ref, scratch = refs[:-8], refs[-8], refs[-7:]
    owner_ref, up_ref, down_ref, x_ref, turned_ref, small_sems, x_sems = scratch
    width = own_ref.shape[0]
    features, columns = x_ref.shape
    small = [
        pltpu.make_async_copy(source, target, small_sems.at[n])
        for n, (source, target) in enumerate(
            [(owner_hbm_ref, owner_ref), (up_hbm_ref, up_ref), (down_hbm_ref, down_ref)]
        )
    ]
    parts = [slice(start, start + LANE) for start in range(0, features, LANE)]
    large = [
        pltpu.make_async_copy(x_hbm_ref.at[part, :], x_ref.at[part, :], x_sems.at[n])
        for n, part in enumerate(parts)
    ]
    for copy in large + small:
        copy.start()
    for copy, part in zip(large, parts):
        copy.wait()
        for start in range(0, columns, LANE):
            at = slice(start, start + LANE)
            turned_ref[at, part] = x_ref[part, at].T
    for copy in small:
        copy.wait()
    pack_ref[...] = jnp.zeros_like(pack_ref)
    pack_ref[0, :, : up_ref.shape[1]] = up_ref[...]
    pack_ref[1, :, : down_ref.shape[1]] = down_ref[...]
    me = lax.axis_index("band")

    def block_of(distance):
        target = jnp.bitwise_xor(me, distance)
        block = 0
        for j in range(1, owner_ref.shape[0]):
            block = jnp.where(owner_ref[j] == target, j, block)
        return turned_ref[pl.ds(pl.multiple_of(block * width, SUB), width), :]

    own_ref[...] = block_of(0)
    near_ref[0] = block_of(2)
    near_ref[1] = block_of(3)
    beside_ref[...] = block_of(1)
    for n, far_ref in enumerate(far_refs):
        far_ref[...] = block_of(BANDS // 2 + n)


def send_blocks(pixels, owner, up, down_t, width, pack_shape):
    features, columns = pixels.shape
    any_space = pl.BlockSpec(memory_space=pl.ANY)
    vmem = pl.BlockSpec(memory_space=pltpu.VMEM)
    blocks = [(width, features), (2, width, features), (width, features)]
    blocks += [(width, features)] * (BANDS // 2)
    own, near, beside, *far, pack = pl.pallas_call(
        send_kernel,
        out_shape=[jax.ShapeDtypeStruct(shape, BF16) for shape in [*blocks, pack_shape]],
        in_specs=[any_space] * 4,
        out_specs=[vmem] * (len(blocks) + 1),
        scratch_shapes=[
            pltpu.SMEM(owner.shape, jnp.int32),
            pltpu.VMEM(up.shape, BF16),
            pltpu.VMEM(down_t.shape, BF16),
            pltpu.VMEM((features, columns), BF16),
            pltpu.VMEM((columns, features), BF16),
            pltpu.SemaphoreType.DMA((3,)),
            pltpu.SemaphoreType.DMA((features // LANE,)),
        ],
        compiler_params=params(),
        name="send_blocks",
    )(in_hbm(owner), in_hbm(up), in_hbm(down_t), in_hbm(pixels))
    return own, near, beside, far, pack


def exchange(own, near, beside, far, pack):
    by_z = swap(near, "band", 2)
    by_z, pack = lax.optimization_barrier((by_z, pack))
    arrived_far = [swap(piece, "band", BANDS // 2 + n) for n, piece in enumerate(far)]
    factors = lax.all_gather(pack, "rep", axis=0, tiled=False)
    factors, beside, onward = lax.optimization_barrier((factors, beside, by_z[1]))
    return [own, by_z, *arrived_far, swap(beside, "band", 1), swap(onward, "band", 1)], factors


def expand_table(table, rows, half_width_padded, half_width, transpose):
    position = iota2((rows, WLAT * WLON), 0)
    line, col = position // half_width_padded, position % half_width_padded
    target = iota2((rows, WLAT * WLON), 1)
    pick = jnp.where((target == line * WLON + col % WLON) & (col < half_width), 1.0, 0.0).astype(BF16)
    left = (dot_nt if transpose else dot_nn)(pick, table).astype(BF16)
    full = dot_nt(left, pick)
    row_window = (iota2((rows, 1), 0) % half_width_padded) // WLON
    col_window = (iota2((1, rows), 1) % half_width_padded) // WLON
    return jnp.where(row_window == col_window, full, 0.0).astype(BF16)


def prep_kernel(
    row_share,
    half_width,
    half_width_padded,
    group_hbm_ref,
    frozen_ref,
    factors_ref,
    level_ref,
    mixer_ref,
    merged_ref,
    up_ref,
    down_ref,
    mix_ref,
    mix_t_ref,
    group_ref,
    group_sem,
):
    load = pltpu.make_async_copy(group_hbm_ref, group_ref, group_sem)
    load.start()
    reps, _, rank, share = factors_ref.shape
    levels = level_ref.shape[0]
    variables = group_ref.shape[0]
    channels = variables * frozen_ref.shape[1]
    up = jnp.concatenate([factors_ref[r, 0] for r in range(reps)], axis=1)
    source, target = iota2((share, channels), 0), iota2((share, channels), 1)
    down_t = jnp.zeros((rank, channels), F32)
    for r in range(reps):
        place = jnp.where((target == source + r * row_share) & (source < row_share), 1.0, 0.0)
        down_t = down_t + dot_nn(factors_ref[r, 1], place.astype(BF16))
    down_t = down_t.astype(BF16)
    down_ref[...] = down_t
    load.wait()
    base = jnp.concatenate([frozen_ref[group_ref[v]].astype(F32) for v in range(variables)], axis=0)
    merged = (base + dot_tn(down_t, up)).astype(BF16)
    stacked = jnp.concatenate([merged, up], axis=0)
    merged_ref[...] = jnp.zeros_like(merged_ref)
    for level in range(levels):
        through = dot_nn(stacked, level_ref[level])
        weights = through[:channels].astype(BF16)
        for s in range(merged_ref.shape[0]):
            offset = (s * levels * channels) % LANE + level * channels
            merged_ref[s, offset : offset + channels, :] = weights
        up_high, up_low = split_hi_lo(through[channels:])
        up_ref[level, :rank, :] = up_high
        up_ref[level, rank:, :] = up_low
    rows = mix_ref.shape[0]
    mix_ref[...] = expand_table(mixer_ref[...], rows, half_width_padded, half_width, False)
    mix_t_ref[...] = expand_table(mixer_ref[...], rows, half_width_padded, half_width, True)


def prepare(groups, frozen, factors, level_weight, mixer, samples, row_share, half_width, half_width_padded):
    reps, _, rank, _ = factors.shape
    levels, feature_dim, _ = level_weight.shape
    channels = groups.shape[0] * frozen.shape[1]
    reach = round_up(levels * channels + LANE // 2, LANE)
    rows = WLAT * half_width_padded
    vmem = pl.BlockSpec(memory_space=pltpu.VMEM)
    flops = 2 * levels * (channels + rank) * feature_dim * feature_dim + 4 * rows * rows * WLAT * WLON
    return pl.pallas_call(
        functools.partial(prep_kernel, row_share, half_width, half_width_padded),
        out_shape=[
            jax.ShapeDtypeStruct((samples, reach, feature_dim), BF16),
            jax.ShapeDtypeStruct((levels, 2 * rank, feature_dim), BF16),
            jax.ShapeDtypeStruct((rank, channels), BF16),
            jax.ShapeDtypeStruct((rows, rows), BF16),
            jax.ShapeDtypeStruct((rows, rows), BF16),
        ],
        in_specs=[pl.BlockSpec(memory_space=pl.ANY)] + [vmem] * 4,
        out_specs=[vmem] * 5,
        scratch_shapes=[pltpu.SMEM(groups.shape, jnp.int32), pltpu.SemaphoreType.DMA],
        compiler_params=params(),
        cost_estimate=pl.CostEstimate(flops=flops, bytes_accessed=4 * 2**20, transcendentals=0),
        name="prepare",
    )(in_hbm(groups), in_hbm(frozen), factors, in_hbm(level_weight), in_hbm(mixer))


def normal_parts(values):
    bell = jnp.exp2(values * values * -0.7213475204444817)
    scaled = 1.0 + 0.23164189 * jnp.abs(values)
    t = pl.reciprocal(scaled, approx=True)
    t = t * (2.0 - scaled * t)
    tail = t * (
        0.127414796 + t * (-0.142248368 + t * (0.7107068705 + t * (-0.7265760135 + t * 0.5307027145)))
    )
    tail = tail * bell
    return jnp.where(values < 0.0, tail, 1.0 - tail), 0.3989422804014327 * bell


def factor_shares(total, up_ref, down_ref, level_ref):
    levels, two_rank, feature_dim = up_ref.shape
    rank, channels = down_ref.shape
    high, low = split_hi_lo(total)
    down = down_ref[...]
    first = jnp.zeros((rank, channels), F32)
    second = jnp.zeros((two_rank, feature_dim), F32)
    for level in range(levels):
        at = slice(level * channels, (level + 1) * channels)
        both = dot_nt(up_ref[level], high[at])
        first = first + both[:rank] + both[rank:] + dot_nt(up_ref[level, :rank, :], low[at])
        through = dot_nn(down, high[at]) + dot_nn(down, low[at])
        through = jnp.concatenate(split_hi_lo(through), axis=0)
        second = second + dot_nt(through, level_ref[level])
    return first, second[:rank] + second[rank:]


def mix_kernel(
    piece_refs,
    merged_ref,
    mix_ref,
    mix_t_ref,
    up_ref,
    down_ref,
    grad_hbm_ref,
    level_hbm_ref,
    mixed_hbm_ref,
    share_ref,
    arrived_ref,
    grad_ref,
    mixed_ref,
    level_ref,
    total_ref,
    pre_ref,
    tokens_ref,
    grad_pre_ref,
    grad_tokens_ref,
    turned_ref,
    grad_sems,
    mixed_sems,
    level_sem,
):
    samples, reach, feature_dim = merged_ref.shape
    chunk_count, _, width, _ = grad_ref.shape
    halves = piece_refs[0].shape[-2] // width
    arrived_directly = len(piece_refs) > 1
    depth = piece_refs[0].shape[-1] // samples
    rows = WLAT * width

    def place(n):
        window_row, half, s = n // (halves * samples), n // samples % halves, n % samples
        lines, columns = pl.ds(window_row * WLAT, WLAT), pl.ds(half * width, width)
        return window_row, half, s, (s, lines, columns)

    loads = [
        pltpu.make_async_copy(grad_hbm_ref.at[place(n)[3]], grad_ref.at[n], grad_sems.at[n])
        for n in range(chunk_count)
    ]
    stores = [
        pltpu.make_async_copy(mixed_ref.at[n], mixed_hbm_ref.at[place(n)[3]], mixed_sems.at[n])
        for n in range(chunk_count)
    ]
    level_load = pltpu.make_async_copy(level_hbm_ref, level_ref, level_sem)
    for load in loads:
        load.start()
    level_load.start()
    if arrived_directly:
        own_ref, by_z_ref, *far_refs, beside_ref, onward_ref = piece_refs
        sources = {0: own_ref, 1: beside_ref, 2: by_z_ref.at[0], 3: onward_ref}
        sources |= {BANDS // 2 + n: far_ref for n, far_ref in enumerate(far_refs)}
        me = lax.axis_index("band")
        for distance, piece_ref in sources.items():
            for half in range(halves):
                within = slice(half * width, (half + 1) * width)
                arrived_ref[half, jnp.bitwise_xor(me, distance)] = piece_ref[within, :]

    def pixels_of(n, lanes):
        window_row, half, _, _ = place(n)
        if arrived_directly:
            block = arrived_ref[half, :, :, lanes]
        else:
            lines = slice(window_row * WLAT, (window_row + 1) * WLAT)
            block = piece_refs[0][lines, half * width : (half + 1) * width, lanes]
        return block.reshape(rows, lanes.stop - lanes.start)

    def turn(n):
        def part(lanes):
            turned_ref[n // samples, lanes, :] = pixels_of(n, lanes).T

        starts = range(0, samples * depth, LANE)
        return [functools.partial(part, slice(start, start + LANE)) for start in starts]

    def forward(n, columns):
        s = n % samples
        lane = s * depth // LANE * LANE

        def embed():
            pixels = pixels_of(n, slice(lane, lane + reach))
            tokens_ref[n, :, columns] = dot_nn(pixels, merged_ref[s, :, columns]).astype(BF16)

        def mixing():
            pre_ref[n, :, columns] = dot_nn(mix_ref[...], tokens_ref[n, :, columns])

        return [embed, mixing]

    def pointwise(n, columns):
        def part(line):
            for start in range(0, width, SUB):
                at, within = pl.ds(line * width + start, SUB), pl.ds(start, SUB)
                pre = pre_ref[n, at, columns]
                cdf, pdf = normal_parts(pre)
                tokens = tokens_ref[n, at, columns].astype(F32)
                mixed_ref[n, line, within, columns] = (tokens + pre * cdf).astype(BF16)
                grad = grad_ref[n, line, within, columns].astype(F32)
                grad_pre_ref[n, at, columns] = (grad * (cdf + pre * pdf)).astype(BF16)

        return [functools.partial(part, line) for line in range(WLAT)]

    def backward(n, columns):
        def spread():
            direct = grad_ref[n, :, :, columns].reshape(rows, COLUMNS).astype(F32)
            through = dot_nn(mix_t_ref[...], grad_pre_ref[n, :, columns])
            grad_tokens_ref[n, :, columns] = (through + direct).astype(BF16)

        def share():
            s = n % samples
            turned = turned_ref[n // samples, s * depth : (s + 1) * depth, :]
            part = dot_nn(turned, grad_tokens_ref[n, :, columns])
            total_ref[:, columns] = part if n == 0 else total_ref[:, columns] + part

        return [spread, share]

    units = [
        (n, slice(start, start + COLUMNS))
        for n in range(chunk_count)
        for start in range(0, feature_dim, COLUMNS)
    ]
    for step in forward(*units[0]):
        step()
    for load in loads:
        load.wait()
    for i, unit in enumerate(units):
        n, columns = unit
        others = []
        if i + 1 < len(units):
            others += forward(*units[i + 1])
        if columns.start == 0 and n % samples == 0:
            others += turn(n)
        if i > 0:
            others += backward(*units[i - 1])
        lines = pointwise(*unit)
        for line, vector_step in enumerate(lines):
            vector_step()
            for step in others[line * len(others) // len(lines) : (line + 1) * len(others) // len(lines)]:
                step()
        if columns.stop == feature_dim:
            stores[n].start()
    for step in backward(*units[-1]):
        step()

    level_load.wait()
    first, second = factor_shares(total_ref[...], up_ref, down_ref, level_ref)
    rank, channels = down_ref.shape
    columns = share_ref.shape[2]
    reps = feature_dim // columns
    folds = rank // (share_ref.shape[1] - rank)
    depth_rows, fold_lanes, row_share = rank // folds, columns // folds, channels // reps
    packed = jnp.zeros((depth_rows, feature_dim), F32)
    row, lane = iota2((channels, feature_dim), 0), iota2((channels, feature_dim), 1)
    rep, lane = lane // columns, lane % columns
    for fold in range(folds):
        inside = lane - fold * fold_lanes
        pick = (row == inside + rep * row_share) & (inside >= 0) & (inside < row_share)
        pick = jnp.where(pick, 1.0, 0.0).astype(BF16)
        part = first[fold * depth_rows : (fold + 1) * depth_rows].astype(BF16)
        packed = packed + dot_nn(part, pick)
    payload = jnp.concatenate([second, packed], axis=0).astype(BF16)
    for slot in range(share_ref.shape[0]):
        at = slot % reps * columns
        share_ref[slot] = payload[:, at : at + columns]
    for store in stores:
        store.wait()


def mix_blocks(halves, arrived, merged, mix, mix_t, grad, up_through, down_t, level_weight, band_count, reps):
    samples, lat_rows, block_width, feature_dim = grad.shape
    width = block_width // halves
    lanes = arrived[0].shape[-1]
    reach = merged.shape[1]
    rows = WLAT * width
    rank = down_t.shape[0]
    chunks = lat_rows // WLAT * halves * samples
    share_shape = (band_count * reps, rank + rank // FOLDS, feature_dim // reps)
    flops = 2 * samples * lat_rows * block_width * feature_dim * (2 * reach + 2 * rows)
    vmem = pl.BlockSpec(memory_space=pltpu.VMEM)
    any_space = pl.BlockSpec(memory_space=pl.ANY)
    local = [*arrived, merged, mix, mix_t, up_through, down_t]
    return pl.pallas_call(
        lambda *refs: mix_kernel(refs[: len(arrived)], *refs[len(arrived) :]),
        out_shape=[
            jax.ShapeDtypeStruct(grad.shape, BF16),
            jax.ShapeDtypeStruct(share_shape, BF16),
        ],
        in_specs=[vmem] * len(local) + [any_space, any_space],
        out_specs=[any_space, vmem],
        scratch_shapes=[
            pltpu.VMEM((halves, WLAT, width, lanes), BF16),
            pltpu.VMEM((chunks, WLAT, width, feature_dim), BF16),
            pltpu.VMEM((chunks, WLAT, width, feature_dim), BF16),
            pltpu.VMEM(level_weight.shape, BF16),
            pltpu.VMEM((lanes // samples, feature_dim), F32),
            pltpu.VMEM((chunks, rows, feature_dim), F32),
            pltpu.VMEM((chunks, rows, feature_dim), BF16),
            pltpu.VMEM((chunks, rows, feature_dim), BF16),
            pltpu.VMEM((chunks, rows, feature_dim), BF16),
            pltpu.VMEM((chunks // samples, lanes, rows), BF16),
            pltpu.SemaphoreType.DMA((chunks,)),
            pltpu.SemaphoreType.DMA((chunks,)),
            pltpu.SemaphoreType.DMA,
        ],
        compiler_params=params(),
        cost_estimate=pl.CostEstimate(
            flops=flops,
            bytes_accessed=12 * 2**20,
            transcendentals=samples * lat_rows * block_width * feature_dim,
        ),
        name="mix_blocks",
    )(*local, in_hbm(grad), in_hbm(level_weight))


def sum_kernel(parts_ref, first_ref, second_ref):
    rank, row_share = first_ref.shape
    total = parts_ref[0].astype(F32)
    for n in range(1, parts_ref.shape[0]):
        total = total + parts_ref[n].astype(F32)
    second_ref[...] = total[:rank]
    depth_rows = total.shape[0] - rank
    for fold in range(rank // depth_rows):
        lane = fold * depth_rows * total.shape[1] // rank
        first_ref[fold * depth_rows : (fold + 1) * depth_rows, :] = total[rank:, lane : lane + row_share]


def sum_shares(shares, rank, row_share):
    parts = lax.all_to_all(shares, ("band", "rep"), split_axis=0, concat_axis=0, tiled=True)
    return pl.pallas_call(
        sum_kernel,
        out_shape=[
            jax.ShapeDtypeStruct((rank, row_share), F32),
            jax.ShapeDtypeStruct((rank, shares.shape[2]), F32),
        ],
        compiler_params=params(),
        name="sum_shares",
    )(parts)


def on_device(
    patches,
    variable_group_index,
    frozen_patch_weight,
    adapter_down,
    adapter_up,
    level_merge_weight,
    window_patch_mixer,
    column_block_owner,
    mixed_token_gradient,
):
    band_count, reps = lax.axis_size("band"), lax.axis_size("rep")
    samples, levels, channels, row_count, col_count = patches.shape
    feature_dim = frozen_patch_weight.shape[2]
    rank, col_share = adapter_up.shape
    row_share = adapter_down.shape[0]
    lat_rows = band_count * row_count
    block_width = col_count // band_count
    halves = 2 if block_width % (2 * SUB * WLON // 4) == 0 else 1
    half_width = block_width // halves
    half_padded = round_up(half_width, SUB)
    padded_width = halves * half_padded
    features = samples * levels * channels

    pixels = patches.reshape(features, col_count)
    pack_shape = (2, rank, round_up(max(row_share, col_share), LANE))
    direct = band_count == BANDS and lat_rows == WLAT and half_padded == half_width
    if direct and features % LANE == 0 and col_count % LANE == 0:
        pieces = send_blocks(
            pixels, column_block_owner, adapter_up, adapter_down.T, block_width, pack_shape
        )
        arrived, factors = exchange(*pieces)
    else:
        block_ids = jnp.arange(band_count, dtype=jnp.int32)
        inverse = jnp.sum(
            jnp.where(column_block_owner[None, :] == block_ids[:, None], block_ids[None, :], 0), axis=1
        )
        outgoing = jnp.take(pixels.T.reshape(band_count, block_width, features), inverse, axis=0)
        outgoing = jnp.pad(outgoing, ((0, 0), (0, padded_width - block_width), (0, 0)))
        arrived = [lax.all_to_all(outgoing, "band", split_axis=0, concat_axis=0, tiled=True)]
        pack = jnp.stack(
            [
                jnp.pad(array, ((0, 0), (0, pack_shape[2] - array.shape[1])))
                for array in (adapter_up, adapter_down.T)
            ]
        )
        factors = lax.all_gather(pack, "rep", axis=0, tiled=False)

    merged, up_through, down_t, mix, mix_t = prepare(
        variable_group_index,
        frozen_patch_weight,
        factors,
        level_merge_weight,
        window_patch_mixer,
        samples,
        row_share,
        half_width,
        half_padded,
    )
    grad = mixed_token_gradient.reshape(samples, lat_rows, block_width, feature_dim)
    if padded_width != block_width:
        grad = jnp.pad(grad, ((0, 0), (0, 0), (0, padded_width - block_width), (0, 0)))
    mixed, shares = mix_blocks(
        halves, arrived, merged, mix, mix_t, grad, up_through, down_t, level_merge_weight, band_count, reps
    )
    if padded_width != block_width:
        mixed = mixed[:, :, :block_width]
    first_t, second = sum_shares(shares, rank, row_share)
    return mixed.reshape(mixed_token_gradient.shape), first_t.T, second


def solution(mesh):
    in_specs = (
        P("rep", None, None, "band", None),
        P(),
        P(),
        P("rep", None),
        P(None, "rep"),
        P(),
        P(),
        P(),
        P("rep", "band", None, None, None),
    )
    out_specs = (P("rep", "band", None, None, None), P("rep", None), P(None, "rep"))
    return jax.shard_map(
        on_device, mesh=mesh, in_specs=in_specs, out_specs=out_specs, check_vma=False
    )
```

```python
import functools

import jax
import jax.numpy as jnp
from jax import lax
from jax.experimental import pallas as pl
from jax.experimental.pallas import tpu as pltpu
from jax.sharding import PartitionSpec as P

WLAT = 8
WLON = 12
LANE = 128
SUB = 16
VMEM_LIMIT = 24 * 1024 * 1024
BANDS = 8
ORDER = (0, 4, 1, 5, 2, 6, 7, 3)
FOLDS = 2
COLUMNS = 256
PAIR = 2
BF16 = jnp.bfloat16
F32 = jnp.float32


def round_up(value, step):
    return -(-value // step) * step


def dot_nn(a, b):
    return lax.dot_general(a, b, (((1,), (0,)), ((), ())), preferred_element_type=F32)


def dot_nt(a, b):
    return lax.dot_general(a, b, (((1,), (1,)), ((), ())), preferred_element_type=F32)


def dot_tn(a, b):
    return lax.dot_general(a, b, (((0,), (0,)), ((), ())), preferred_element_type=F32)


def split_hi_lo(values):
    high = values.astype(BF16)
    low = (values - high.astype(F32)).astype(BF16)
    return high, low


def iota2(shape, axis):
    return lax.broadcasted_iota(jnp.int32, shape, axis)


def params(**extra):
    return pltpu.CompilerParams(vmem_limit_bytes=VMEM_LIMIT, **extra)


def in_hbm(values):
    return pltpu.with_memory_space_constraint(values, pltpu.HBM)


def swap(values, axis, distance):
    count = lax.axis_size(axis)
    return lax.ppermute(values, axis, [(source, source ^ distance) for source in range(count)])


def send_kernel(owner_hbm_ref, up_hbm_ref, down_hbm_ref, x_hbm_ref, *refs):
    block_refs, pack_ref, scratch = refs[:-8], refs[-8], refs[-7:]
    owner_ref, up_ref, down_ref, x_ref, turned_ref, small_sems, x_sems = scratch
    width = block_refs[0].shape[0]
    features, columns = x_ref.shape
    small = [
        pltpu.make_async_copy(source, target, small_sems.at[n])
        for n, (source, target) in enumerate(
            [(owner_hbm_ref, owner_ref), (up_hbm_ref, up_ref), (down_hbm_ref, down_ref)]
        )
    ]
    parts = [slice(start, start + LANE) for start in range(0, features, LANE)]
    large = [
        pltpu.make_async_copy(x_hbm_ref.at[part, :], x_ref.at[part, :], x_sems.at[n])
        for n, part in enumerate(parts)
    ]
    for copy in large + small:
        copy.start()
    for copy, part in zip(large, parts):
        copy.wait()
        for start in range(0, columns, LANE):
            at = slice(start, start + LANE)
            turned_ref[at, part] = x_ref[part, at].T
    for copy in small:
        copy.wait()
    pack_ref[...] = jnp.zeros_like(pack_ref)
    pack_ref[0, :, : up_ref.shape[1]] = up_ref[...]
    pack_ref[1, :, : down_ref.shape[1]] = down_ref[...]
    me = lax.axis_index("band")
    for distance, block_ref in zip(ORDER, block_refs):
        target = jnp.bitwise_xor(me, distance)
        block = 0
        for j in range(1, owner_ref.shape[0]):
            block = jnp.where(owner_ref[j] == target, j, block)
        block_ref[...] = turned_ref[pl.ds(pl.multiple_of(block * width, SUB), width), :]


def send_blocks(pixels, owner, up, down_t, width, pack_shape):
    features, columns = pixels.shape
    any_space = pl.BlockSpec(memory_space=pl.ANY)
    vmem = pl.BlockSpec(memory_space=pltpu.VMEM)
    blocks = [(width, features)] * BANDS
    *blocks, pack = pl.pallas_call(
        send_kernel,
        out_shape=[jax.ShapeDtypeStruct(shape, BF16) for shape in [*blocks, pack_shape]],
        in_specs=[any_space] * 4,
        out_specs=[vmem] * (len(blocks) + 1),
        scratch_shapes=[
            pltpu.SMEM(owner.shape, jnp.int32),
            pltpu.VMEM(up.shape, BF16),
            pltpu.VMEM(down_t.shape, BF16),
            pltpu.VMEM((features, columns), BF16),
            pltpu.VMEM((columns, features), BF16),
            pltpu.SemaphoreType.DMA((3,)),
            pltpu.SemaphoreType.DMA((features // LANE,)),
        ],
        compiler_params=params(),
        name="send_blocks",
    )(in_hbm(owner), in_hbm(up), in_hbm(down_t), in_hbm(pixels))
    return blocks, pack


def exchange(blocks):
    arrived = dict(zip(ORDER, blocks))
    for distance in ORDER[1:-2]:
        arrived[distance] = swap(arrived[distance], "band", distance)
    for distance, before in zip(ORDER[-2:], (1, 2)):
        block, arrived[before] = lax.optimization_barrier((arrived[distance], arrived[before]))
        arrived[distance] = swap(block, "band", distance)
    return [arrived[distance] for distance in ORDER]


def expand_table(table, rows, half_width_padded, half_width, transpose):
    position = iota2((rows, WLAT * WLON), 0)
    line, col = position // half_width_padded, position % half_width_padded
    target = iota2((rows, WLAT * WLON), 1)
    pick = jnp.where((target == line * WLON + col % WLON) & (col < half_width), 1.0, 0.0).astype(BF16)
    left = (dot_nt if transpose else dot_nn)(pick, table).astype(BF16)
    full = dot_nt(left, pick)
    row_window = (iota2((rows, 1), 0) % half_width_padded) // WLON
    col_window = (iota2((1, rows), 1) % half_width_padded) // WLON
    return jnp.where(row_window == col_window, full, 0.0).astype(BF16)


def prep_kernel(
    row_share,
    half_width,
    half_width_padded,
    group_hbm_ref,
    frozen_ref,
    factors_ref,
    level_ref,
    mixer_ref,
    merged_ref,
    up_ref,
    down_ref,
    mix_ref,
    mix_t_ref,
    group_ref,
    group_sem,
):
    load = pltpu.make_async_copy(group_hbm_ref, group_ref, group_sem)
    load.start()
    reps, _, rank, share = factors_ref.shape
    levels = level_ref.shape[0]
    variables = group_ref.shape[0]
    channels = variables * frozen_ref.shape[1]
    up = jnp.concatenate([factors_ref[r, 0] for r in range(reps)], axis=1)
    source, target = iota2((share, channels), 0), iota2((share, channels), 1)
    down_t = jnp.zeros((rank, channels), F32)
    for r in range(reps):
        place = jnp.where((target == source + r * row_share) & (source < row_share), 1.0, 0.0)
        down_t = down_t + dot_nn(factors_ref[r, 1], place.astype(BF16))
    down_t = down_t.astype(BF16)
    down_ref[...] = down_t
    load.wait()
    base = jnp.concatenate([frozen_ref[group_ref[v]].astype(F32) for v in range(variables)], axis=0)
    merged = (base + dot_tn(down_t, up)).astype(BF16)
    stacked = jnp.concatenate([merged, up], axis=0)
    merged_ref[...] = jnp.zeros_like(merged_ref)
    for level in range(levels):
        through = dot_nn(stacked, level_ref[level])
        weights = through[:channels].astype(BF16)
        for s in range(merged_ref.shape[0]):
            offset = (s * levels * channels) % LANE + level * channels
            merged_ref[s, offset : offset + channels, :] = weights
        up_high, up_low = split_hi_lo(through[channels:])
        up_ref[level, :rank, :] = up_high
        up_ref[level, rank:, :] = up_low
    rows = mix_ref.shape[0]
    mix_ref[...] = expand_table(mixer_ref[...], rows, half_width_padded, half_width, False)
    mix_t_ref[...] = expand_table(mixer_ref[...], rows, half_width_padded, half_width, True)


def prepare(groups, frozen, factors, level_weight, mixer, samples, row_share, half_width, half_width_padded):
    reps, _, rank, _ = factors.shape
    levels, feature_dim, _ = level_weight.shape
    channels = groups.shape[0] * frozen.shape[1]
    reach = round_up(levels * channels + LANE // 2, LANE)
    rows = WLAT * half_width_padded
    vmem = pl.BlockSpec(memory_space=pltpu.VMEM)
    flops = 2 * levels * (channels + rank) * feature_dim * feature_dim + 4 * rows * rows * WLAT * WLON
    return pl.pallas_call(
        functools.partial(prep_kernel, row_share, half_width, half_width_padded),
        out_shape=[
            jax.ShapeDtypeStruct((samples, reach, feature_dim), BF16),
            jax.ShapeDtypeStruct((levels, 2 * rank, feature_dim), BF16),
            jax.ShapeDtypeStruct((rank, channels), BF16),
            jax.ShapeDtypeStruct((rows, rows), BF16),
            jax.ShapeDtypeStruct((rows, rows), BF16),
        ],
        in_specs=[pl.BlockSpec(memory_space=pl.ANY)] + [vmem] * 4,
        out_specs=[vmem] * 5,
        scratch_shapes=[pltpu.SMEM(groups.shape, jnp.int32), pltpu.SemaphoreType.DMA],
        compiler_params=params(),
        cost_estimate=pl.CostEstimate(flops=flops, bytes_accessed=4 * 2**20, transcendentals=0),
        name="prepare",
    )(in_hbm(groups), in_hbm(frozen), factors, in_hbm(level_weight), in_hbm(mixer))


def normal_parts(values):
    bell = jnp.exp2(values * values * -0.7213475204444817)
    scaled = 1.0 + 0.23164189 * jnp.abs(values)
    t = pl.reciprocal(scaled, approx=True)
    t = t * (2.0 - scaled * t)
    tail = t * (
        0.127414796 + t * (-0.142248368 + t * (0.7107068705 + t * (-0.7265760135 + t * 0.5307027145)))
    )
    tail = tail * bell
    return jnp.where(values < 0.0, tail, 1.0 - tail), 0.3989422804014327 * bell


def factor_shares(total, up_ref, down_ref, level_ref):
    levels, two_rank, feature_dim = up_ref.shape
    rank, channels = down_ref.shape
    high, low = split_hi_lo(total)
    down = down_ref[...]
    first = jnp.zeros((rank, channels), F32)
    second = jnp.zeros((two_rank, feature_dim), F32)
    for level in range(levels):
        at = slice(level * channels, (level + 1) * channels)
        both = dot_nt(up_ref[level], high[at])
        first = first + both[:rank] + both[rank:] + dot_nt(up_ref[level, :rank, :], low[at])
        through = dot_nn(down, high[at]) + dot_nn(down, low[at])
        through = jnp.concatenate(split_hi_lo(through), axis=0)
        second = second + dot_nt(through, level_ref[level])
    return first, second[:rank] + second[rank:]


def mix_kernel(
    piece_refs,
    merged_ref,
    mix_ref,
    mix_t_ref,
    up_ref,
    down_ref,
    grad_hbm_ref,
    level_hbm_ref,
    mixed_hbm_ref,
    share_ref,
    arrived_ref,
    grad_ref,
    mixed_ref,
    level_ref,
    total_ref,
    pre_ref,
    tokens_ref,
    grad_pre_ref,
    grad_tokens_ref,
    turned_ref,
    grad_sems,
    mixed_sems,
    level_sem,
):
    samples, reach, feature_dim = merged_ref.shape
    chunk_count, _, width, _ = grad_ref.shape
    halves = piece_refs[0].shape[-2] // width
    arrived_directly = len(piece_refs) > 1
    depth = piece_refs[0].shape[-1] // samples
    rows = WLAT * width
    group_rows = mix_ref.shape[0]
    group = group_rows // WLAT
    groups = [(slice(start, start + group), slice(start * WLAT, start * WLAT + group_rows)) for start in range(0, width, group)]

    def place(n):
        window_row, half, s = n // (halves * samples), n // samples % halves, n % samples
        lines, columns = pl.ds(window_row * WLAT, WLAT), pl.ds(half * width, width)
        return window_row, half, s, (s, lines, columns)

    loads = [
        pltpu.make_async_copy(grad_hbm_ref.at[place(n)[3]], grad_ref.at[n], grad_sems.at[n])
        for n in range(chunk_count)
    ]
    stores = [
        pltpu.make_async_copy(mixed_ref.at[n], mixed_hbm_ref.at[place(n)[3]], mixed_sems.at[n])
        for n in range(chunk_count)
    ]
    level_load = pltpu.make_async_copy(level_hbm_ref, level_ref, level_sem)
    for load in loads:
        load.start()
    level_load.start()
    if arrived_directly:
        me = lax.axis_index("band")
        for distance, piece_ref in zip(ORDER, piece_refs):
            for half in range(halves):
                within = slice(half * width, (half + 1) * width)
                arrived_ref[half, jnp.bitwise_xor(me, distance)] = piece_ref[within, :]

    def pixels_of(n, lanes):
        window_row, half, _, _ = place(n)
        if arrived_directly:
            block = arrived_ref[half, :, :, lanes]
        else:
            lines = slice(window_row * WLAT, (window_row + 1) * WLAT)
            block = piece_refs[0][lines, half * width : (half + 1) * width, lanes]
        return block.reshape(rows, lanes.stop - lanes.start)

    def turn(n):
        def part(lanes):
            turned_ref[n // samples, lanes, :] = pixels_of(n, lanes).T

        starts = range(0, samples * depth, LANE)
        return [functools.partial(part, slice(start, start + LANE)) for start in starts]

    def forward(n, columns):
        s = n % samples
        lane = s * depth // LANE * LANE

        def embed():
            pixels = pixels_of(n, slice(lane, lane + reach))
            tokens = dot_nn(pixels, merged_ref[s, :, columns]).reshape(WLAT, width, COLUMNS)
            for within, at in groups:
                tokens_ref[n, at, columns] = tokens[:, within].reshape(group_rows, COLUMNS).astype(BF16)

        def mixing():
            for _, at in groups:
                pre_ref[n, at, columns] = dot_nn(mix_ref[...], tokens_ref[n, at, columns])

        return [embed, mixing]

    def pointwise(n, columns):
        def part(line, lanes):
            grads = [grad_ref[n, line + k, :, lanes].astype(F32) for k in range(PAIR)]
            mixed = []
            for within, at in groups:
                at = pl.ds(at.start + line * group, PAIR * group)
                pre = pre_ref[n, at, lanes]
                cdf, pdf = normal_parts(pre)
                mixed.append(tokens_ref[n, at, lanes].astype(F32) + pre * cdf)
                grad = jnp.concatenate([grad[within] for grad in grads], axis=0)
                grad_pre_ref[n, at, lanes] = (grad * (cdf + pre * pdf)).astype(BF16)
            for k in range(PAIR):
                rows_of_line = [values[k * group : (k + 1) * group] for values in mixed]
                mixed_ref[n, line + k, :, lanes] = jnp.concatenate(rows_of_line, axis=0).astype(BF16)

        return [
            functools.partial(part, line, slice(start, start + LANE))
            for line in range(0, WLAT, PAIR)
            for start in range(columns.start, columns.stop, LANE)
        ]

    def backward(n, columns):
        def spread():
            direct = grad_ref[n, :, :, columns].astype(F32)
            through = [
                dot_nn(mix_t_ref[...], grad_pre_ref[n, at, columns]).reshape(WLAT, group, COLUMNS)
                for _, at in groups
            ]
            total = jnp.concatenate(through, axis=1) + direct
            grad_tokens_ref[n, :, columns] = total.reshape(rows, COLUMNS).astype(BF16)

        def share():
            s = n % samples
            turned = turned_ref[n // samples, s * depth : (s + 1) * depth, :]
            part = dot_nn(turned, grad_tokens_ref[n, :, columns])
            total_ref[:, columns] = part if n == 0 else total_ref[:, columns] + part

        return [spread, share]

    units = [
        (n, slice(start, start + COLUMNS))
        for n in range(chunk_count)
        for start in range(0, feature_dim, COLUMNS)
    ]
    for step in forward(*units[0]):
        step()
    for i, unit in enumerate(units):
        n, columns = unit
        others = []
        if i + 1 < len(units):
            others += forward(*units[i + 1])
        if columns.start == 0 and n % samples == 0:
            others += turn(n)
        if i > 0:
            others += backward(*units[i - 1])
        if columns.start == 0:
            loads[n].wait()
        lines = pointwise(*unit)
        for line, vector_step in enumerate(lines):
            vector_step()
            for step in others[line * len(others) // len(lines) : (line + 1) * len(others) // len(lines)]:
                step()
        if columns.stop == feature_dim:
            stores[n].start()
    for step in backward(*units[-1]):
        step()

    level_load.wait()
    first, second = factor_shares(total_ref[...], up_ref, down_ref, level_ref)
    rank, channels = down_ref.shape
    columns = share_ref.shape[2]
    reps = feature_dim // columns
    folds = rank // (share_ref.shape[1] - rank)
    depth_rows, fold_lanes, row_share = rank // folds, columns // folds, channels // reps
    packed = jnp.zeros((depth_rows, feature_dim), F32)
    row, lane = iota2((channels, feature_dim), 0), iota2((1, feature_dim), 1)
    rep, lane = lane // columns, lane % columns
    for fold in range(folds):
        inside = lane - fold * fold_lanes
        target = jnp.where((inside >= 0) & (inside < row_share), inside + rep * row_share, -1)
        pick = jnp.where(row == target, 1.0, 0.0).astype(BF16)
        part = first[fold * depth_rows : (fold + 1) * depth_rows].astype(BF16)
        packed = packed + dot_nn(part, pick)
    payload = jnp.concatenate([second, packed], axis=0).astype(BF16)
    for slot in range(share_ref.shape[0]):
        at = slot % reps * columns
        share_ref[slot] = payload[:, at : at + columns]
    for store in stores:
        store.wait()


def mix_blocks(halves, arrived, merged, mix, mix_t, grad, up_through, down_t, level_weight, band_count, reps):
    samples, lat_rows, block_width, feature_dim = grad.shape
    width = block_width // halves
    lanes = arrived[0].shape[-1]
    reach = merged.shape[1]
    rows = WLAT * width
    rank = down_t.shape[0]
    chunks = lat_rows // WLAT * halves * samples
    share_shape = (band_count * reps, rank + rank // FOLDS, feature_dim // reps)
    flops = 2 * samples * lat_rows * block_width * feature_dim * (2 * reach + 2 * rows)
    vmem = pl.BlockSpec(memory_space=pltpu.VMEM)
    any_space = pl.BlockSpec(memory_space=pl.ANY)
    local = [*arrived, merged, mix, mix_t, up_through, down_t]
    return pl.pallas_call(
        lambda *refs: mix_kernel(refs[: len(arrived)], *refs[len(arrived) :]),
        out_shape=[
            jax.ShapeDtypeStruct(grad.shape, BF16),
            jax.ShapeDtypeStruct(share_shape, BF16),
        ],
        in_specs=[vmem] * len(local) + [any_space, any_space],
        out_specs=[any_space, vmem],
        scratch_shapes=[
            pltpu.VMEM((halves, WLAT, width, lanes), BF16),
            pltpu.VMEM((chunks, WLAT, width, feature_dim), BF16),
            pltpu.VMEM((chunks, WLAT, width, feature_dim), BF16),
            pltpu.VMEM(level_weight.shape, BF16),
            pltpu.VMEM((lanes // samples, feature_dim), F32),
            pltpu.VMEM((chunks, rows, feature_dim), F32),
            pltpu.VMEM((chunks, rows, feature_dim), BF16),
            pltpu.VMEM((chunks, rows, feature_dim), BF16),
            pltpu.VMEM((chunks, rows, feature_dim), BF16),
            pltpu.VMEM((chunks // samples, lanes, rows), BF16),
            pltpu.SemaphoreType.DMA((chunks,)),
            pltpu.SemaphoreType.DMA((chunks,)),
            pltpu.SemaphoreType.DMA,
        ],
        compiler_params=params(),
        cost_estimate=pl.CostEstimate(
            flops=flops,
            bytes_accessed=12 * 2**20,
            transcendentals=samples * lat_rows * block_width * feature_dim,
        ),
        name="mix_blocks",
    )(*local, in_hbm(grad), in_hbm(level_weight))


def sum_kernel(parts_ref, first_ref, second_ref):
    rank, row_share = first_ref.shape
    total = parts_ref[0].astype(F32)
    for n in range(1, parts_ref.shape[0]):
        total = total + parts_ref[n].astype(F32)
    second_ref[...] = total[:rank]
    depth_rows = total.shape[0] - rank
    for fold in range(rank // depth_rows):
        lane = fold * depth_rows * total.shape[1] // rank
        first_ref[fold * depth_rows : (fold + 1) * depth_rows, :] = total[rank:, lane : lane + row_share]


def sum_shares(shares, rank, row_share):
    parts = lax.all_to_all(shares, ("band", "rep"), split_axis=0, concat_axis=0, tiled=True)
    return pl.pallas_call(
        sum_kernel,
        out_shape=[
            jax.ShapeDtypeStruct((rank, row_share), F32),
            jax.ShapeDtypeStruct((rank, shares.shape[2]), F32),
        ],
        compiler_params=params(),
        name="sum_shares",
    )(parts)


def on_device(
    patches,
    variable_group_index,
    frozen_patch_weight,
    adapter_down,
    adapter_up,
    level_merge_weight,
    window_patch_mixer,
    column_block_owner,
    mixed_token_gradient,
):
    band_count, reps = lax.axis_size("band"), lax.axis_size("rep")
    samples, levels, channels, row_count, col_count = patches.shape
    feature_dim = frozen_patch_weight.shape[2]
    rank, col_share = adapter_up.shape
    row_share = adapter_down.shape[0]
    lat_rows = band_count * row_count
    block_width = col_count // band_count
    halves = 2 if block_width % (2 * SUB * WLON // 4) == 0 else 1
    half_width = block_width // halves
    half_padded = round_up(half_width, SUB)
    padded_width = halves * half_padded
    group = 2 * WLON if half_width % (2 * WLON) == 0 else half_padded
    features = samples * levels * channels

    pixels = patches.reshape(features, col_count)
    pack_shape = (2, rank, round_up(max(row_share, col_share), LANE))
    direct = band_count == BANDS and lat_rows == WLAT and half_padded == half_width
    if direct and features % LANE == 0 and col_count % LANE == 0:
        blocks, pack = send_blocks(
            pixels, column_block_owner, adapter_up, adapter_down.T, block_width, pack_shape
        )
        arrived = exchange(blocks)
    else:
        block_ids = jnp.arange(band_count, dtype=jnp.int32)
        inverse = jnp.sum(
            jnp.where(column_block_owner[None, :] == block_ids[:, None], block_ids[None, :], 0), axis=1
        )
        outgoing = jnp.take(pixels.T.reshape(band_count, block_width, features), inverse, axis=0)
        outgoing = jnp.pad(outgoing, ((0, 0), (0, padded_width - block_width), (0, 0)))
        arrived = [lax.all_to_all(outgoing, "band", split_axis=0, concat_axis=0, tiled=True)]
        pack = jnp.stack(
            [
                jnp.pad(array, ((0, 0), (0, pack_shape[2] - array.shape[1])))
                for array in (adapter_up, adapter_down.T)
            ]
        )
    factors = lax.all_gather(pack, "rep", axis=0, tiled=False)

    merged, up_through, down_t, mix, mix_t = prepare(
        variable_group_index,
        frozen_patch_weight,
        factors,
        level_merge_weight,
        window_patch_mixer,
        samples,
        row_share,
        min(half_width, group),
        group,
    )
    grad = mixed_token_gradient.reshape(samples, lat_rows, block_width, feature_dim)
    if padded_width != block_width:
        grad = jnp.pad(grad, ((0, 0), (0, 0), (0, padded_width - block_width), (0, 0)))
    mixed, shares = mix_blocks(
        halves, arrived, merged, mix, mix_t, grad, up_through, down_t, level_merge_weight, band_count, reps
    )
    if padded_width != block_width:
        mixed = mixed[:, :, :block_width]
    first_t, second = sum_shares(shares, rank, row_share)
    return mixed.reshape(mixed_token_gradient.shape), first_t.T, second


def solution(mesh):
    in_specs = (
        P("rep", None, None, "band", None),
        P(),
        P(),
        P("rep", None),
        P(None, "rep"),
        P(),
        P(),
        P(),
        P("rep", "band", None, None, None),
    )
    out_specs = (P("rep", "band", None, None, None), P("rep", None), P(None, "rep"))
    return jax.shard_map(
        on_device, mesh=mesh, in_specs=in_specs, out_specs=out_specs, check_vma=False
    )
```

```python
import functools

import jax
import jax.numpy as jnp
from jax import lax
from jax.experimental import pallas as pl
from jax.experimental.pallas import tpu as pltpu
from jax.sharding import PartitionSpec as P

WLAT = 8
WLON = 12
LANE = 128
SUB = 16
VMEM_LIMIT = 24 * 1024 * 1024
BANDS = 8
ORDER = (0, 4, 1, 5, 2, 6, 7, 3)
FOLDS = 2
COLUMNS = 256
BF16 = jnp.bfloat16
F32 = jnp.float32


def round_up(value, step):
    return -(-value // step) * step


def dot_nn(a, b):
    return lax.dot_general(a, b, (((1,), (0,)), ((), ())), preferred_element_type=F32)


def dot_nt(a, b):
    return lax.dot_general(a, b, (((1,), (1,)), ((), ())), preferred_element_type=F32)


def dot_tn(a, b):
    return lax.dot_general(a, b, (((0,), (0,)), ((), ())), preferred_element_type=F32)


def split_hi_lo(values):
    high = values.astype(BF16)
    low = (values - high.astype(F32)).astype(BF16)
    return high, low


def iota2(shape, axis):
    return lax.broadcasted_iota(jnp.int32, shape, axis)


def params(**extra):
    return pltpu.CompilerParams(vmem_limit_bytes=VMEM_LIMIT, **extra)


def in_hbm(values):
    return pltpu.with_memory_space_constraint(values, pltpu.HBM)


def swap(values, axis, distance):
    count = lax.axis_size(axis)
    return lax.ppermute(values, axis, [(source, source ^ distance) for source in range(count)])


def send_kernel(owner_hbm_ref, up_hbm_ref, down_hbm_ref, x_hbm_ref, *refs):
    block_refs, pack_ref, scratch = refs[:-8], refs[-8], refs[-7:]
    owner_ref, up_ref, down_ref, x_ref, turned_ref, small_sems, x_sems = scratch
    width = block_refs[0].shape[0]
    features, columns = x_ref.shape
    small = [
        pltpu.make_async_copy(source, target, small_sems.at[n])
        for n, (source, target) in enumerate(
            [(owner_hbm_ref, owner_ref), (up_hbm_ref, up_ref), (down_hbm_ref, down_ref)]
        )
    ]
    parts = [slice(start, start + LANE) for start in range(0, features, LANE)]
    large = [
        pltpu.make_async_copy(x_hbm_ref.at[part, :], x_ref.at[part, :], x_sems.at[n])
        for n, part in enumerate(parts)
    ]
    for copy in large + small:
        copy.start()
    for copy, part in zip(large, parts):
        copy.wait()
        for start in range(0, columns, LANE):
            at = slice(start, start + LANE)
            turned_ref[at, part] = x_ref[part, at].T
    for copy in small:
        copy.wait()
    pack_ref[...] = jnp.zeros_like(pack_ref)
    pack_ref[0, :, : up_ref.shape[1]] = up_ref[...]
    pack_ref[1, :, : down_ref.shape[1]] = down_ref[...]
    me = lax.axis_index("band")
    for distance, block_ref in zip(ORDER, block_refs):
        target = jnp.bitwise_xor(me, distance)
        block = 0
        for j in range(1, owner_ref.shape[0]):
            block = jnp.where(owner_ref[j] == target, j, block)
        block_ref[...] = turned_ref[pl.ds(pl.multiple_of(block * width, SUB), width), :]


def send_blocks(pixels, owner, up, down_t, width, pack_shape):
    features, columns = pixels.shape
    any_space = pl.BlockSpec(memory_space=pl.ANY)
    vmem = pl.BlockSpec(memory_space=pltpu.VMEM)
    blocks = [(width, features)] * BANDS
    *blocks, pack = pl.pallas_call(
        send_kernel,
        out_shape=[jax.ShapeDtypeStruct(shape, BF16) for shape in [*blocks, pack_shape]],
        in_specs=[any_space] * 4,
        out_specs=[vmem] * (len(blocks) + 1),
        scratch_shapes=[
            pltpu.SMEM(owner.shape, jnp.int32),
            pltpu.VMEM(up.shape, BF16),
            pltpu.VMEM(down_t.shape, BF16),
            pltpu.VMEM((features, columns), BF16),
            pltpu.VMEM((columns, features), BF16),
            pltpu.SemaphoreType.DMA((3,)),
            pltpu.SemaphoreType.DMA((features // LANE,)),
        ],
        compiler_params=params(),
        name="send_blocks",
    )(in_hbm(owner), in_hbm(up), in_hbm(down_t), in_hbm(pixels))
    return blocks, pack


def exchange(blocks):
    arrived = dict(zip(ORDER, blocks))
    for distance in ORDER[1:-2]:
        arrived[distance] = swap(arrived[distance], "band", distance)
    for distance, before in zip(ORDER[-2:], (1, 2)):
        block, arrived[before] = lax.optimization_barrier((arrived[distance], arrived[before]))
        arrived[distance] = swap(block, "band", distance)
    return [arrived[distance] for distance in ORDER]


def expand_table(table, rows, half_width_padded, half_width, transpose):
    position = iota2((rows, WLAT * WLON), 0)
    line, col = position // half_width_padded, position % half_width_padded
    target = iota2((rows, WLAT * WLON), 1)
    pick = jnp.where((target == line * WLON + col % WLON) & (col < half_width), 1.0, 0.0).astype(BF16)
    left = (dot_nt if transpose else dot_nn)(pick, table).astype(BF16)
    full = dot_nt(left, pick)
    row_window = (iota2((rows, 1), 0) % half_width_padded) // WLON
    col_window = (iota2((1, rows), 1) % half_width_padded) // WLON
    return jnp.where(row_window == col_window, full, 0.0).astype(BF16)


def prep_kernel(
    row_share,
    half_width,
    half_width_padded,
    group_hbm_ref,
    frozen_ref,
    factors_ref,
    level_ref,
    mixer_ref,
    merged_ref,
    up_ref,
    down_ref,
    mix_ref,
    mix_t_ref,
    group_ref,
    group_sem,
):
    load = pltpu.make_async_copy(group_hbm_ref, group_ref, group_sem)
    load.start()
    reps, _, rank, share = factors_ref.shape
    levels = level_ref.shape[0]
    variables = group_ref.shape[0]
    channels = variables * frozen_ref.shape[1]
    up = jnp.concatenate([factors_ref[r, 0] for r in range(reps)], axis=1)
    source, target = iota2((share, channels), 0), iota2((share, channels), 1)
    down_t = jnp.zeros((rank, channels), F32)
    for r in range(reps):
        place = jnp.where((target == source + r * row_share) & (source < row_share), 1.0, 0.0)
        down_t = down_t + dot_nn(factors_ref[r, 1], place.astype(BF16))
    down_t = down_t.astype(BF16)
    down_ref[...] = down_t
    load.wait()
    base = jnp.concatenate([frozen_ref[group_ref[v]].astype(F32) for v in range(variables)], axis=0)
    merged = (base + dot_tn(down_t, up)).astype(BF16)
    stacked = jnp.concatenate([merged, up], axis=0)
    merged_ref[...] = jnp.zeros_like(merged_ref)
    for level in range(levels):
        through = dot_nn(stacked, level_ref[level])
        weights = through[:channels].astype(BF16)
        for s in range(merged_ref.shape[0]):
            offset = (s * levels * channels) % LANE + level * channels
            merged_ref[s, offset : offset + channels, :] = weights
        up_high, up_low = split_hi_lo(through[channels:])
        up_ref[level, :rank, :] = up_high
        up_ref[level, rank:, :] = up_low
    rows = mix_ref.shape[0]
    mix_ref[...] = expand_table(mixer_ref[...], rows, half_width_padded, half_width, False)
    mix_t_ref[...] = expand_table(mixer_ref[...], rows, half_width_padded, half_width, True)


def prepare(groups, frozen, factors, level_weight, mixer, samples, row_share, half_width, half_width_padded):
    reps, _, rank, _ = factors.shape
    levels, feature_dim, _ = level_weight.shape
    channels = groups.shape[0] * frozen.shape[1]
    reach = round_up(levels * channels + LANE // 2, LANE)
    rows = WLAT * half_width_padded
    vmem = pl.BlockSpec(memory_space=pltpu.VMEM)
    flops = 2 * levels * (channels + rank) * feature_dim * feature_dim + 4 * rows * rows * WLAT * WLON
    return pl.pallas_call(
        functools.partial(prep_kernel, row_share, half_width, half_width_padded),
        out_shape=[
            jax.ShapeDtypeStruct((samples, reach, feature_dim), BF16),
            jax.ShapeDtypeStruct((levels, 2 * rank, feature_dim), BF16),
            jax.ShapeDtypeStruct((rank, channels), BF16),
            jax.ShapeDtypeStruct((rows, rows), BF16),
            jax.ShapeDtypeStruct((rows, rows), BF16),
        ],
        in_specs=[pl.BlockSpec(memory_space=pl.ANY)] + [vmem] * 4,
        out_specs=[vmem] * 5,
        scratch_shapes=[pltpu.SMEM(groups.shape, jnp.int32), pltpu.SemaphoreType.DMA],
        compiler_params=params(),
        cost_estimate=pl.CostEstimate(flops=flops, bytes_accessed=4 * 2**20, transcendentals=0),
        name="prepare",
    )(in_hbm(groups), in_hbm(frozen), factors, in_hbm(level_weight), in_hbm(mixer))


def normal_parts(values):
    bell = jnp.exp2(values * values * -0.7213475204444817)
    scaled = 1.0 + 0.23164189 * jnp.abs(values)
    t = pl.reciprocal(scaled, approx=True)
    t = t * (2.0 - scaled * t)
    tail = t * (
        0.127414796 + t * (-0.142248368 + t * (0.7107068705 + t * (-0.7265760135 + t * 0.5307027145)))
    )
    tail = tail * bell
    return jnp.where(values < 0.0, tail, 1.0 - tail), 0.3989422804014327 * bell


def factor_shares(total, up_ref, down_ref, level_ref):
    levels, two_rank, feature_dim = up_ref.shape
    rank, channels = down_ref.shape
    high, low = split_hi_lo(total)
    down = down_ref[...]
    first = jnp.zeros((rank, channels), F32)
    second = jnp.zeros((two_rank, feature_dim), F32)
    for level in range(levels):
        at = slice(level * channels, (level + 1) * channels)
        both = dot_nt(up_ref[level], high[at])
        first = first + both[:rank] + both[rank:] + dot_nt(up_ref[level, :rank, :], low[at])
        through = dot_nn(down, high[at]) + dot_nn(down, low[at])
        through = jnp.concatenate(split_hi_lo(through), axis=0)
        second = second + dot_nt(through, level_ref[level])
    return first, second[:rank] + second[rank:]


def mix_kernel(
    piece_refs,
    merged_ref,
    mix_ref,
    mix_t_ref,
    up_ref,
    down_ref,
    grad_hbm_ref,
    level_hbm_ref,
    mixed_hbm_ref,
    share_ref,
    arrived_refs,
    turned_refs,
    grad_refs,
    mixed_refs,
    pre_refs,
    tokens_refs,
    grad_pre_refs,
    grad_tokens_refs,
    level_ref,
    total_ref,
    grad_sems,
    mixed_sems,
    level_sem,
):
    samples, reach, feature_dim = merged_ref.shape
    chunk_count, (_, width, _) = len(grad_refs), grad_refs[0].shape
    halves = piece_refs[0].shape[-2] // width
    arrived_directly = len(piece_refs) > 1
    depth = piece_refs[0].shape[-1] // samples
    rows = WLAT * width
    group_rows = mix_ref.shape[0]
    group = group_rows // WLAT
    groups = [(slice(start, start + group), slice(start * WLAT, start * WLAT + group_rows)) for start in range(0, width, group)]

    def place(n):
        window_row, half, s = n // (halves * samples), n // samples % halves, n % samples
        lines, columns = pl.ds(window_row * WLAT, WLAT), pl.ds(half * width, width)
        return window_row, half, s, (s, lines, columns)

    loads = [
        pltpu.make_async_copy(grad_hbm_ref.at[place(n)[3]], grad_refs[n], grad_sems.at[n])
        for n in range(chunk_count)
    ]
    stores = [
        pltpu.make_async_copy(mixed_refs[n], mixed_hbm_ref.at[place(n)[3]], mixed_sems.at[n])
        for n in range(chunk_count)
    ]
    level_load = pltpu.make_async_copy(level_hbm_ref, level_ref, level_sem)
    for load in loads:
        load.start()
    level_load.start()
    if arrived_directly:
        me = lax.axis_index("band")
        for distance, piece_ref in zip(ORDER, piece_refs):
            for half in range(halves):
                within = slice(half * width, (half + 1) * width)
                arrived_refs[half][jnp.bitwise_xor(me, distance)] = piece_ref[within, :]

    def pixels_of(n, lanes):
        window_row, half, _, _ = place(n)
        if arrived_directly:
            block = arrived_refs[half][:, :, lanes]
        else:
            lines = slice(window_row * WLAT, (window_row + 1) * WLAT)
            block = piece_refs[0][lines, half * width : (half + 1) * width, lanes]
        return block.reshape(rows, lanes.stop - lanes.start)

    def turn(n):
        def part(lanes):
            turned_refs[n // samples][lanes, :] = pixels_of(n, lanes).T

        starts = range(0, samples * depth, LANE)
        return [functools.partial(part, slice(start, start + LANE)) for start in starts]

    def forward(n, columns):
        s = n % samples
        lane = s * depth // LANE * LANE

        def embed():
            pixels = pixels_of(n, slice(lane, lane + reach))
            tokens = dot_nn(pixels, merged_ref[s, :, columns]).reshape(WLAT, width, COLUMNS)
            for within, at in groups:
                tokens_refs[n][at, columns] = tokens[:, within].reshape(group_rows, COLUMNS).astype(BF16)

        def mixing():
            for _, at in groups:
                pre_refs[n][at, columns] = dot_nn(mix_ref[...], tokens_refs[n][at, columns])

        return [embed, mixing]

    pair = 1 if group % SUB == 0 else 2

    def pointwise(n, columns):
        def part(line, lanes):
            grads = [grad_refs[n][line + k, :, lanes].astype(F32) for k in range(pair)]
            mixed = []
            for within, at in groups:
                at = pl.ds(at.start + line * group, pair * group)
                pre = pre_refs[n][at, lanes]
                cdf, pdf = normal_parts(pre)
                mixed.append(tokens_refs[n][at, lanes].astype(F32) + pre * cdf)
                grad = jnp.concatenate([grad[within] for grad in grads], axis=0)
                grad_pre_refs[n][at, lanes] = (grad * (cdf + pre * pdf)).astype(BF16)
            for k in range(pair):
                rows_of_line = [values[k * group : (k + 1) * group] for values in mixed]
                mixed_refs[n][line + k, :, lanes] = jnp.concatenate(rows_of_line, axis=0).astype(BF16)

        return [
            functools.partial(part, line, slice(start, start + LANE))
            for line in range(0, WLAT, pair)
            for start in range(columns.start, columns.stop, LANE)
        ]

    def backward(n, columns):
        def spread():
            direct = grad_refs[n][:, :, columns].astype(F32)
            through = [
                dot_nn(mix_t_ref[...], grad_pre_refs[n][at, columns]).reshape(WLAT, group, COLUMNS)
                for _, at in groups
            ]
            total = jnp.concatenate(through, axis=1) + direct
            grad_tokens_refs[n][:, columns] = total.reshape(rows, COLUMNS).astype(BF16)

        def share():
            s = n % samples
            turned = turned_refs[n // samples][s * depth : (s + 1) * depth, :]
            part = dot_nn(turned, grad_tokens_refs[n][:, columns])
            total_ref[:, columns] = part if n == 0 else total_ref[:, columns] + part

        return [spread, share]

    units = [
        (n, slice(start, start + COLUMNS))
        for n in range(chunk_count)
        for start in range(0, feature_dim, COLUMNS)
    ]
    for step in forward(*units[0]):
        step()
    for load in loads:
        load.wait()
    for i, unit in enumerate(units):
        n, columns = unit
        others = []
        if i + 1 < len(units):
            others += forward(*units[i + 1])
        if columns.start == 0 and n % samples == 0:
            others += turn(n)
        if i > 0:
            others += backward(*units[i - 1])
        lines = pointwise(*unit)
        for line, vector_step in enumerate(lines):
            vector_step()
            for step in others[line * len(others) // len(lines) : (line + 1) * len(others) // len(lines)]:
                step()
    for store in stores:
        store.start()
    for step in backward(*units[-1]):
        step()

    level_load.wait()
    first, second = factor_shares(total_ref[...], up_ref, down_ref, level_ref)
    rank, channels = down_ref.shape
    columns = share_ref.shape[2]
    reps = feature_dim // columns
    folds = rank // (share_ref.shape[1] - rank)
    depth_rows, fold_lanes, row_share = rank // folds, columns // folds, channels // reps
    packed = jnp.zeros((depth_rows, feature_dim), F32)
    row, lane = iota2((channels, feature_dim), 0), iota2((1, feature_dim), 1)
    rep, lane = lane // columns, lane % columns
    for fold in range(folds):
        inside = lane - fold * fold_lanes
        target = jnp.where((inside >= 0) & (inside < row_share), inside + rep * row_share, -1)
        pick = jnp.where(row == target, 1.0, 0.0).astype(BF16)
        part = first[fold * depth_rows : (fold + 1) * depth_rows].astype(BF16)
        packed = packed + dot_nn(part, pick)
    payload = jnp.concatenate([second, packed], axis=0).astype(BF16)
    for slot in range(share_ref.shape[0]):
        at = slot % reps * columns
        share_ref[slot] = payload[:, at : at + columns]
    for store in stores:
        store.wait()


def mix_blocks(halves, arrived, merged, mix, mix_t, grad, up_through, down_t, level_weight, band_count, reps):
    samples, lat_rows, block_width, feature_dim = grad.shape
    width = block_width // halves
    lanes = arrived[0].shape[-1]
    reach = merged.shape[1]
    rows = WLAT * width
    rank = down_t.shape[0]
    chunks = lat_rows // WLAT * halves * samples
    share_shape = (band_count * reps, rank + rank // FOLDS, feature_dim // reps)
    flops = 2 * samples * lat_rows * block_width * feature_dim * (2 * reach + 2 * rows)
    vmem = pl.BlockSpec(memory_space=pltpu.VMEM)
    any_space = pl.BlockSpec(memory_space=pl.ANY)
    local = [*arrived, merged, mix, mix_t, up_through, down_t]
    return pl.pallas_call(
        lambda *refs: mix_kernel(refs[: len(arrived)], *refs[len(arrived) :]),
        out_shape=[
            jax.ShapeDtypeStruct(grad.shape, BF16),
            jax.ShapeDtypeStruct(share_shape, BF16),
        ],
        in_specs=[vmem] * len(local) + [any_space, any_space],
        out_specs=[any_space, vmem],
        scratch_shapes=[
            [pltpu.VMEM((WLAT, width, lanes), BF16)] * halves,
            [pltpu.VMEM((lanes, rows), BF16)] * (chunks // samples),
            [pltpu.VMEM((WLAT, width, feature_dim), BF16)] * chunks,
            [pltpu.VMEM((WLAT, width, feature_dim), BF16)] * chunks,
            [pltpu.VMEM((rows, feature_dim), F32)] * chunks,
            [pltpu.VMEM((rows, feature_dim), BF16)] * chunks,
            [pltpu.VMEM((rows, feature_dim), BF16)] * chunks,
            [pltpu.VMEM((rows, feature_dim), BF16)] * chunks,
            pltpu.VMEM(level_weight.shape, BF16),
            pltpu.VMEM((lanes // samples, feature_dim), F32),
            pltpu.SemaphoreType.DMA((chunks,)),
            pltpu.SemaphoreType.DMA((chunks,)),
            pltpu.SemaphoreType.DMA,
        ],
        compiler_params=params(),
        cost_estimate=pl.CostEstimate(
            flops=flops,
            bytes_accessed=12 * 2**20,
            transcendentals=samples * lat_rows * block_width * feature_dim,
        ),
        name="mix_blocks",
    )(*local, in_hbm(grad), in_hbm(level_weight))


def sum_kernel(parts_ref, first_ref, second_ref):
    rank, row_share = first_ref.shape
    total = parts_ref[0].astype(F32)
    for n in range(1, parts_ref.shape[0]):
        total = total + parts_ref[n].astype(F32)
    second_ref[...] = total[:rank]
    depth_rows = total.shape[0] - rank
    for fold in range(rank // depth_rows):
        lane = fold * depth_rows * total.shape[1] // rank
        first_ref[fold * depth_rows : (fold + 1) * depth_rows, :] = total[rank:, lane : lane + row_share]


def sum_shares(shares, rank, row_share):
    parts = lax.all_to_all(shares, ("band", "rep"), split_axis=0, concat_axis=0, tiled=True)
    return pl.pallas_call(
        sum_kernel,
        out_shape=[
            jax.ShapeDtypeStruct((rank, row_share), F32),
            jax.ShapeDtypeStruct((rank, shares.shape[2]), F32),
        ],
        compiler_params=params(),
        name="sum_shares",
    )(parts)


def on_device(
    patches,
    variable_group_index,
    frozen_patch_weight,
    adapter_down,
    adapter_up,
    level_merge_weight,
    window_patch_mixer,
    column_block_owner,
    mixed_token_gradient,
):
    band_count, reps = lax.axis_size("band"), lax.axis_size("rep")
    samples, levels, channels, row_count, col_count = patches.shape
    feature_dim = frozen_patch_weight.shape[2]
    rank, col_share = adapter_up.shape
    row_share = adapter_down.shape[0]
    lat_rows = band_count * row_count
    block_width = col_count // band_count
    halves = 2 if block_width % (2 * SUB * WLON // 4) == 0 else 1
    half_width = block_width // halves
    half_padded = round_up(half_width, SUB)
    padded_width = halves * half_padded
    features = samples * levels * channels

    pixels = patches.reshape(features, col_count)
    pack_shape = (2, rank, round_up(max(row_share, col_share), LANE))
    direct = band_count == BANDS and lat_rows == WLAT and half_padded == half_width
    if direct and features % LANE == 0 and col_count % LANE == 0:
        blocks, pack = send_blocks(
            pixels, column_block_owner, adapter_up, adapter_down.T, block_width, pack_shape
        )
        arrived = exchange(blocks)
    else:
        block_ids = jnp.arange(band_count, dtype=jnp.int32)
        inverse = jnp.sum(
            jnp.where(column_block_owner[None, :] == block_ids[:, None], block_ids[None, :], 0), axis=1
        )
        outgoing = jnp.take(pixels.T.reshape(band_count, block_width, features), inverse, axis=0)
        outgoing = jnp.pad(outgoing, ((0, 0), (0, padded_width - block_width), (0, 0)))
        arrived = [lax.all_to_all(outgoing, "band", split_axis=0, concat_axis=0, tiled=True)]
        pack = jnp.stack(
            [
                jnp.pad(array, ((0, 0), (0, pack_shape[2] - array.shape[1])))
                for array in (adapter_up, adapter_down.T)
            ]
        )
    factors = lax.all_gather(pack, "rep", axis=0, tiled=False)

    merged, up_through, down_t, mix, mix_t = prepare(
        variable_group_index,
        frozen_patch_weight,
        factors,
        level_merge_weight,
        window_patch_mixer,
        samples,
        row_share,
        half_width,
        half_padded,
    )
    grad = mixed_token_gradient.reshape(samples, lat_rows, block_width, feature_dim)
    if padded_width != block_width:
        grad = jnp.pad(grad, ((0, 0), (0, 0), (0, padded_width - block_width), (0, 0)))
    mixed, shares = mix_blocks(
        halves, arrived, merged, mix, mix_t, grad, up_through, down_t, level_merge_weight, band_count, reps
    )
    if padded_width != block_width:
        mixed = mixed[:, :, :block_width]
    first_t, second = sum_shares(shares, rank, row_share)
    return mixed.reshape(mixed_token_gradient.shape), first_t.T, second


def solution(mesh):
    in_specs = (
        P("rep", None, None, "band", None),
        P(),
        P(),
        P("rep", None),
        P(None, "rep"),
        P(),
        P(),
        P(),
        P("rep", "band", None, None, None),
    )
    out_specs = (P("rep", "band", None, None, None), P("rep", None), P(None, "rep"))
    return jax.shard_map(
        on_device, mesh=mesh, in_specs=in_specs, out_specs=out_specs, check_vma=False
    )
```

```python
import functools

import jax
import jax.numpy as jnp
from jax import lax
from jax.experimental import pallas as pl
from jax.experimental.pallas import tpu as pltpu
from jax.sharding import PartitionSpec as P

WLAT = 8
WLON = 12
LANE = 128
SUB = 16
VMEM_LIMIT = 24 * 1024 * 1024
BANDS = 8
ORDER = (0, 4, 1, 5, 2, 6, 7, 3)
FOLDS = 2
COLUMNS = 256
BF16 = jnp.bfloat16
F32 = jnp.float32


def round_up(value, step):
    return -(-value // step) * step


def dot_nn(a, b):
    return lax.dot_general(a, b, (((1,), (0,)), ((), ())), preferred_element_type=F32)


def dot_nt(a, b):
    return lax.dot_general(a, b, (((1,), (1,)), ((), ())), preferred_element_type=F32)


def dot_tn(a, b):
    return lax.dot_general(a, b, (((0,), (0,)), ((), ())), preferred_element_type=F32)


def split_hi_lo(values):
    high = values.astype(BF16)
    low = (values - high.astype(F32)).astype(BF16)
    return high, low


def iota2(shape, axis):
    return lax.broadcasted_iota(jnp.int32, shape, axis)


def params(**extra):
    return pltpu.CompilerParams(vmem_limit_bytes=VMEM_LIMIT, **extra)


def in_hbm(values):
    return pltpu.with_memory_space_constraint(values, pltpu.HBM)


def swap(values, axis, distance):
    count = lax.axis_size(axis)
    return lax.ppermute(values, axis, [(source, source ^ distance) for source in range(count)])


def send_kernel(owner_hbm_ref, up_hbm_ref, down_hbm_ref, x_hbm_ref, *refs):
    block_refs, pack_ref, scratch = refs[:-8], refs[-8], refs[-7:]
    owner_ref, up_ref, down_ref, x_ref, turned_ref, small_sems, x_sems = scratch
    width = block_refs[0].shape[0]
    features, columns = x_ref.shape
    small = [
        pltpu.make_async_copy(source, target, small_sems.at[n])
        for n, (source, target) in enumerate(
            [(owner_hbm_ref, owner_ref), (up_hbm_ref, up_ref), (down_hbm_ref, down_ref)]
        )
    ]
    parts = [slice(start, start + LANE) for start in range(0, features, LANE)]
    large = [
        pltpu.make_async_copy(x_hbm_ref.at[part, :], x_ref.at[part, :], x_sems.at[n])
        for n, part in enumerate(parts)
    ]
    for copy in large + small:
        copy.start()
    for copy, part in zip(large, parts):
        copy.wait()
        for start in range(0, columns, LANE):
            at = slice(start, start + LANE)
            turned_ref[at, part] = x_ref[part, at].T
    for copy in small:
        copy.wait()
    pack_ref[...] = jnp.zeros_like(pack_ref)
    pack_ref[0, :, : up_ref.shape[1]] = up_ref[...]
    pack_ref[1, :, : down_ref.shape[1]] = down_ref[...]
    me = lax.axis_index("band")
    for distance, block_ref in zip(ORDER, block_refs):
        target = jnp.bitwise_xor(me, distance)
        block = 0
        for j in range(1, owner_ref.shape[0]):
            block = jnp.where(owner_ref[j] == target, j, block)
        block_ref[...] = turned_ref[pl.ds(pl.multiple_of(block * width, SUB), width), :]


def send_blocks(pixels, owner, up, down_t, width, pack_shape):
    features, columns = pixels.shape
    any_space = pl.BlockSpec(memory_space=pl.ANY)
    vmem = pl.BlockSpec(memory_space=pltpu.VMEM)
    blocks = [(width, features)] * BANDS
    *blocks, pack = pl.pallas_call(
        send_kernel,
        out_shape=[jax.ShapeDtypeStruct(shape, BF16) for shape in [*blocks, pack_shape]],
        in_specs=[any_space] * 4,
        out_specs=[vmem] * (len(blocks) + 1),
        scratch_shapes=[
            pltpu.SMEM(owner.shape, jnp.int32),
            pltpu.VMEM(up.shape, BF16),
            pltpu.VMEM(down_t.shape, BF16),
            pltpu.VMEM((features, columns), BF16),
            pltpu.VMEM((columns, features), BF16),
            pltpu.SemaphoreType.DMA((3,)),
            pltpu.SemaphoreType.DMA((features // LANE,)),
        ],
        compiler_params=params(),
        name="send_blocks",
    )(in_hbm(owner), in_hbm(up), in_hbm(down_t), in_hbm(pixels))
    return blocks, pack


def exchange(blocks):
    arrived = dict(zip(ORDER, blocks))
    for distance in ORDER[1:-2]:
        arrived[distance] = swap(arrived[distance], "band", distance)
    for distance, before in zip(ORDER[-2:], (1, 2)):
        block, arrived[before] = lax.optimization_barrier((arrived[distance], arrived[before]))
        arrived[distance] = swap(block, "band", distance)
    return [arrived[distance] for distance in ORDER]


def expand_table(table, rows, half_width_padded, half_width, transpose):
    position = iota2((rows, WLAT * WLON), 0)
    line, col = position // half_width_padded, position % half_width_padded
    target = iota2((rows, WLAT * WLON), 1)
    pick = jnp.where((target == line * WLON + col % WLON) & (col < half_width), 1.0, 0.0).astype(BF16)
    left = (dot_nt if transpose else dot_nn)(pick, table).astype(BF16)
    full = dot_nt(left, pick)
    row_window = (iota2((rows, 1), 0) % half_width_padded) // WLON
    col_window = (iota2((1, rows), 1) % half_width_padded) // WLON
    return jnp.where(row_window == col_window, full, 0.0).astype(BF16)


def prep_kernel(
    row_share,
    half_width,
    half_width_padded,
    group_hbm_ref,
    frozen_ref,
    factors_ref,
    level_ref,
    mixer_ref,
    merged_ref,
    up_ref,
    down_ref,
    mix_ref,
    mix_t_ref,
    group_ref,
    group_sem,
):
    load = pltpu.make_async_copy(group_hbm_ref, group_ref, group_sem)
    load.start()
    reps, _, rank, share = factors_ref.shape
    levels = level_ref.shape[0]
    variables = group_ref.shape[0]
    channels = variables * frozen_ref.shape[1]
    up = jnp.concatenate([factors_ref[r, 0] for r in range(reps)], axis=1)
    source, target = iota2((share, channels), 0), iota2((share, channels), 1)
    down_t = jnp.zeros((rank, channels), F32)
    for r in range(reps):
        place = jnp.where((target == source + r * row_share) & (source < row_share), 1.0, 0.0)
        down_t = down_t + dot_nn(factors_ref[r, 1], place.astype(BF16))
    down_t = down_t.astype(BF16)
    down_ref[...] = down_t
    load.wait()
    base = jnp.concatenate([frozen_ref[group_ref[v]].astype(F32) for v in range(variables)], axis=0)
    merged = (base + dot_tn(down_t, up)).astype(BF16)
    stacked = jnp.concatenate([merged, up], axis=0)
    merged_ref[...] = jnp.zeros_like(merged_ref)
    for level in range(levels):
        through = dot_nn(stacked, level_ref[level])
        weights = through[:channels].astype(BF16)
        for s in range(merged_ref.shape[0]):
            offset = (s * levels * channels) % LANE + level * channels
            merged_ref[s, offset : offset + channels, :] = weights
        up_high, up_low = split_hi_lo(through[channels:])
        up_ref[level, :rank, :] = up_high
        up_ref[level, rank:, :] = up_low
    rows = mix_ref.shape[0]
    mix_ref[...] = expand_table(mixer_ref[...], rows, half_width_padded, half_width, False)
    mix_t_ref[...] = expand_table(mixer_ref[...], rows, half_width_padded, half_width, True)


def prepare(groups, frozen, factors, level_weight, mixer, samples, row_share, half_width, half_width_padded):
    reps, _, rank, _ = factors.shape
    levels, feature_dim, _ = level_weight.shape
    channels = groups.shape[0] * frozen.shape[1]
    reach = round_up(levels * channels + LANE // 2, LANE)
    rows = WLAT * half_width_padded
    vmem = pl.BlockSpec(memory_space=pltpu.VMEM)
    flops = 2 * levels * (channels + rank) * feature_dim * feature_dim + 4 * rows * rows * WLAT * WLON
    return pl.pallas_call(
        functools.partial(prep_kernel, row_share, half_width, half_width_padded),
        out_shape=[
            jax.ShapeDtypeStruct((samples, reach, feature_dim), BF16),
            jax.ShapeDtypeStruct((levels, 2 * rank, feature_dim), BF16),
            jax.ShapeDtypeStruct((rank, channels), BF16),
            jax.ShapeDtypeStruct((rows, rows), BF16),
            jax.ShapeDtypeStruct((rows, rows), BF16),
        ],
        in_specs=[pl.BlockSpec(memory_space=pl.ANY)] + [vmem] * 4,
        out_specs=[vmem] * 5,
        scratch_shapes=[pltpu.SMEM(groups.shape, jnp.int32), pltpu.SemaphoreType.DMA],
        compiler_params=params(),
        cost_estimate=pl.CostEstimate(flops=flops, bytes_accessed=4 * 2**20, transcendentals=0),
        name="prepare",
    )(in_hbm(groups), in_hbm(frozen), factors, in_hbm(level_weight), in_hbm(mixer))


def normal_parts(values):
    cdf = 0.5 + 0.5 * lax.erf(values * 0.7071067811865476)
    return cdf, 0.3989422804014327 * jnp.exp2(values * values * -0.7213475204444817)


def factor_shares(total, up_ref, down_ref, level_ref):
    levels, two_rank, feature_dim = up_ref.shape
    rank, channels = down_ref.shape
    high, low = split_hi_lo(total)
    down = down_ref[...]
    first = jnp.zeros((rank, channels), F32)
    second = jnp.zeros((two_rank, feature_dim), F32)
    for level in range(levels):
        at = slice(level * channels, (level + 1) * channels)
        both = dot_nt(up_ref[level], high[at])
        first = first + both[:rank] + both[rank:] + dot_nt(up_ref[level, :rank, :], low[at])
        through = dot_nn(down, high[at]) + dot_nn(down, low[at])
        through = jnp.concatenate(split_hi_lo(through), axis=0)
        second = second + dot_nt(through, level_ref[level])
    return first, second[:rank] + second[rank:]


def mix_kernel(
    piece_refs,
    merged_ref,
    mix_ref,
    mix_t_ref,
    up_ref,
    down_ref,
    grad_hbm_ref,
    level_hbm_ref,
    mixed_hbm_ref,
    share_ref,
    arrived_refs,
    turned_refs,
    grad_refs,
    mixed_refs,
    pre_refs,
    tokens_refs,
    grad_pre_refs,
    grad_tokens_refs,
    level_ref,
    total_ref,
    grad_sems,
    mixed_sems,
    level_sem,
):
    samples, reach, feature_dim = merged_ref.shape
    chunk_count, (_, width, _) = len(grad_refs), grad_refs[0].shape
    halves = piece_refs[0].shape[-2] // width
    arrived_directly = len(piece_refs) > 1
    depth = piece_refs[0].shape[-1] // samples
    rows = WLAT * width

    def place(n):
        window_row, half, s = n // (halves * samples), n // samples % halves, n % samples
        lines, columns = pl.ds(window_row * WLAT, WLAT), pl.ds(half * width, width)
        return window_row, half, s, (s, lines, columns)

    loads = [
        pltpu.make_async_copy(grad_hbm_ref.at[place(n)[3]], grad_refs[n], grad_sems.at[n])
        for n in range(chunk_count)
    ]
    stores = [
        pltpu.make_async_copy(mixed_refs[n], mixed_hbm_ref.at[place(n)[3]], mixed_sems.at[n])
        for n in range(chunk_count)
    ]
    level_load = pltpu.make_async_copy(level_hbm_ref, level_ref, level_sem)
    for load in loads:
        load.start()
    level_load.start()
    if arrived_directly:
        me = lax.axis_index("band")
        for distance, piece_ref in zip(ORDER, piece_refs):
            for half in range(halves):
                within = slice(half * width, (half + 1) * width)
                arrived_refs[half][jnp.bitwise_xor(me, distance)] = piece_ref[within, :]

    def pixels_of(n, lanes):
        window_row, half, _, _ = place(n)
        if arrived_directly:
            block = arrived_refs[half][:, :, lanes]
        else:
            lines = slice(window_row * WLAT, (window_row + 1) * WLAT)
            block = piece_refs[0][lines, half * width : (half + 1) * width, lanes]
        return block.reshape(rows, lanes.stop - lanes.start)

    def turn(n):
        def part(lanes):
            turned_refs[n // samples][lanes, :] = pixels_of(n, lanes).T

        starts = range(0, samples * depth, LANE)
        return [functools.partial(part, slice(start, start + LANE)) for start in starts]

    def forward(n, columns):
        s = n % samples
        lane = s * depth // LANE * LANE

        def embed():
            pixels = pixels_of(n, slice(lane, lane + reach))
            tokens_refs[n][:, columns] = dot_nn(pixels, merged_ref[s, :, columns]).astype(BF16)

        def mixing():
            pre_refs[n][:, columns] = dot_nn(mix_ref[...], tokens_refs[n][:, columns])

        return [embed, mixing]

    def pointwise(n, columns):
        def part(line):
            for start in range(0, width, SUB):
                at, within = pl.ds(line * width + start, SUB), pl.ds(start, SUB)
                pre = pre_refs[n][at, columns]
                cdf, pdf = normal_parts(pre)
                tokens = tokens_refs[n][at, columns].astype(F32)
                mixed_refs[n][line, within, columns] = (tokens + pre * cdf).astype(BF16)
                grad = grad_refs[n][line, within, columns].astype(F32)
                grad_pre_refs[n][at, columns] = (grad * (cdf + pre * pdf)).astype(BF16)

        return [functools.partial(part, line) for line in range(WLAT)]

    def backward(n, columns):
        def spread():
            direct = grad_refs[n][:, :, columns].reshape(rows, COLUMNS).astype(F32)
            through = dot_nn(mix_t_ref[...], grad_pre_refs[n][:, columns])
            grad_tokens_refs[n][:, columns] = (through + direct).astype(BF16)

        def share():
            s = n % samples
            turned = turned_refs[n // samples][s * depth : (s + 1) * depth, :]
            part = dot_nn(turned, grad_tokens_refs[n][:, columns])
            total_ref[:, columns] = part if n == 0 else total_ref[:, columns] + part

        return [spread, share]

    units = [
        (n, slice(start, start + COLUMNS))
        for n in range(chunk_count)
        for start in range(0, feature_dim, COLUMNS)
    ]
    for step in forward(*units[0]):
        step()
    for load in loads:
        load.wait()
    for i, unit in enumerate(units):
        n, columns = unit
        others = []
        if i + 1 < len(units):
            others += forward(*units[i + 1])
        if columns.start == 0 and n % samples == 0:
            others += turn(n)
        if i > 0:
            others += backward(*units[i - 1])
        lines = pointwise(*unit)
        for line, vector_step in enumerate(lines):
            vector_step()
            for step in others[line * len(others) // len(lines) : (line + 1) * len(others) // len(lines)]:
                step()
        if columns.stop == feature_dim:
            stores[n].start()
    for step in backward(*units[-1]):
        step()

    level_load.wait()
    first, second = factor_shares(total_ref[...], up_ref, down_ref, level_ref)
    rank, channels = down_ref.shape
    columns = share_ref.shape[2]
    reps = feature_dim // columns
    folds = rank // (share_ref.shape[1] - rank)
    depth_rows, fold_lanes, row_share = rank // folds, columns // folds, channels // reps
    packed = jnp.zeros((depth_rows, feature_dim), F32)
    row, lane = iota2((channels, feature_dim), 0), iota2((1, feature_dim), 1)
    rep, lane = lane // columns, lane % columns
    for fold in range(folds):
        inside = lane - fold * fold_lanes
        target = jnp.where((inside >= 0) & (inside < row_share), inside + rep * row_share, -1)
        pick = jnp.where(row == target, 1.0, 0.0).astype(BF16)
        part = first[fold * depth_rows : (fold + 1) * depth_rows].astype(BF16)
        packed = packed + dot_nn(part, pick)
    payload = jnp.concatenate([second, packed], axis=0).astype(BF16)
    for slot in range(share_ref.shape[0]):
        at = slot % reps * columns
        share_ref[slot] = payload[:, at : at + columns]
    for store in stores:
        store.wait()


def mix_blocks(halves, arrived, merged, mix, mix_t, grad, up_through, down_t, level_weight, band_count, reps):
    samples, lat_rows, block_width, feature_dim = grad.shape
    width = block_width // halves
    lanes = arrived[0].shape[-1]
    reach = merged.shape[1]
    rows = WLAT * width
    rank = down_t.shape[0]
    chunks = lat_rows // WLAT * halves * samples
    share_shape = (band_count * reps, rank + rank // FOLDS, feature_dim // reps)
    flops = 2 * samples * lat_rows * block_width * feature_dim * (2 * reach + 2 * rows)
    vmem = pl.BlockSpec(memory_space=pltpu.VMEM)
    any_space = pl.BlockSpec(memory_space=pl.ANY)
    local = [*arrived, merged, mix, mix_t, up_through, down_t]
    return pl.pallas_call(
        lambda *refs: mix_kernel(refs[: len(arrived)], *refs[len(arrived) :]),
        out_shape=[
            jax.ShapeDtypeStruct(grad.shape, BF16),
            jax.ShapeDtypeStruct(share_shape, BF16),
        ],
        in_specs=[vmem] * len(local) + [any_space, any_space],
        out_specs=[any_space, vmem],
        scratch_shapes=[
            [pltpu.VMEM((WLAT, width, lanes), BF16)] * halves,
            [pltpu.VMEM((lanes, rows), BF16)] * (chunks // samples),
            [pltpu.VMEM((WLAT, width, feature_dim), BF16)] * chunks,
            [pltpu.VMEM((WLAT, width, feature_dim), BF16)] * chunks,
            [pltpu.VMEM((rows, feature_dim), F32)] * chunks,
            [pltpu.VMEM((rows, feature_dim), BF16)] * chunks,
            [pltpu.VMEM((rows, feature_dim), BF16)] * chunks,
            [pltpu.VMEM((rows, feature_dim), BF16)] * chunks,
            pltpu.VMEM(level_weight.shape, BF16),
            pltpu.VMEM((lanes // samples, feature_dim), F32),
            pltpu.SemaphoreType.DMA((chunks,)),
            pltpu.SemaphoreType.DMA((chunks,)),
            pltpu.SemaphoreType.DMA,
        ],
        compiler_params=params(),
        cost_estimate=pl.CostEstimate(
            flops=flops,
            bytes_accessed=12 * 2**20,
            transcendentals=samples * lat_rows * block_width * feature_dim,
        ),
        name="mix_blocks",
    )(*local, in_hbm(grad), in_hbm(level_weight))


def sum_kernel(parts_ref, first_ref, second_ref):
    rank, row_share = first_ref.shape
    total = parts_ref[0].astype(F32)
    for n in range(1, parts_ref.shape[0]):
        total = total + parts_ref[n].astype(F32)
    second_ref[...] = total[:rank]
    depth_rows = total.shape[0] - rank
    for fold in range(rank // depth_rows):
        lane = fold * depth_rows * total.shape[1] // rank
        first_ref[fold * depth_rows : (fold + 1) * depth_rows, :] = total[rank:, lane : lane + row_share]


def sum_shares(shares, rank, row_share):
    parts = lax.all_to_all(shares, ("band", "rep"), split_axis=0, concat_axis=0, tiled=True)
    return pl.pallas_call(
        sum_kernel,
        out_shape=[
            jax.ShapeDtypeStruct((rank, row_share), F32),
            jax.ShapeDtypeStruct((rank, shares.shape[2]), F32),
        ],
        compiler_params=params(),
        name="sum_shares",
    )(parts)


def on_device(
    patches,
    variable_group_index,
    frozen_patch_weight,
    adapter_down,
    adapter_up,
    level_merge_weight,
    window_patch_mixer,
    column_block_owner,
    mixed_token_gradient,
):
    band_count, reps = lax.axis_size("band"), lax.axis_size("rep")
    samples, levels, channels, row_count, col_count = patches.shape
    feature_dim = frozen_patch_weight.shape[2]
    rank, col_share = adapter_up.shape
    row_share = adapter_down.shape[0]
    lat_rows = band_count * row_count
    block_width = col_count // band_count
    halves = 2 if block_width % (2 * SUB * WLON // 4) == 0 else 1
    half_width = block_width // halves
    half_padded = round_up(half_width, SUB)
    padded_width = halves * half_padded
    features = samples * levels * channels

    pixels = patches.reshape(features, col_count)
    pack_shape = (2, rank, round_up(max(row_share, col_share), LANE))
    direct = band_count == BANDS and lat_rows == WLAT and half_padded == half_width
    if direct and features % LANE == 0 and col_count % LANE == 0:
        blocks, pack = send_blocks(
            pixels, column_block_owner, adapter_up, adapter_down.T, block_width, pack_shape
        )
        arrived = exchange(blocks)
    else:
        block_ids = jnp.arange(band_count, dtype=jnp.int32)
        inverse = jnp.sum(
            jnp.where(column_block_owner[None, :] == block_ids[:, None], block_ids[None, :], 0), axis=1
        )
        outgoing = jnp.take(pixels.T.reshape(band_count, block_width, features), inverse, axis=0)
        outgoing = jnp.pad(outgoing, ((0, 0), (0, padded_width - block_width), (0, 0)))
        arrived = [lax.all_to_all(outgoing, "band", split_axis=0, concat_axis=0, tiled=True)]
        pack = jnp.stack(
            [
                jnp.pad(array, ((0, 0), (0, pack_shape[2] - array.shape[1])))
                for array in (adapter_up, adapter_down.T)
            ]
        )
    factors = lax.all_gather(pack, "rep", axis=0, tiled=False)

    merged, up_through, down_t, mix, mix_t = prepare(
        variable_group_index,
        frozen_patch_weight,
        factors,
        level_merge_weight,
        window_patch_mixer,
        samples,
        row_share,
        half_width,
        half_padded,
    )
    grad = mixed_token_gradient.reshape(samples, lat_rows, block_width, feature_dim)
    if padded_width != block_width:
        grad = jnp.pad(grad, ((0, 0), (0, 0), (0, padded_width - block_width), (0, 0)))
    mixed, shares = mix_blocks(
        halves, arrived, merged, mix, mix_t, grad, up_through, down_t, level_merge_weight, band_count, reps
    )
    if padded_width != block_width:
        mixed = mixed[:, :, :block_width]
    first_t, second = sum_shares(shares, rank, row_share)
    return mixed.reshape(mixed_token_gradient.shape), first_t.T, second


def solution(mesh):
    in_specs = (
        P("rep", None, None, "band", None),
        P(),
        P(),
        P("rep", None),
        P(None, "rep"),
        P(),
        P(),
        P(),
        P("rep", "band", None, None, None),
    )
    out_specs = (P("rep", "band", None, None, None), P("rep", None), P(None, "rep"))
    return jax.shard_map(
        on_device, mesh=mesh, in_specs=in_specs, out_specs=out_specs, check_vma=False
    )
```

```python
import functools

import jax
import jax.numpy as jnp
from jax import lax
from jax.experimental import pallas as pl
from jax.experimental.pallas import tpu as pltpu
from jax.sharding import PartitionSpec as P

WLAT = 8
WLON = 12
LANE = 128
SUB = 16
VMEM_LIMIT = 24 * 1024 * 1024
BANDS = 8
ORDER = (0, 4, 1, 5, 2, 6, 7, 3)
FOLDS = 2
COLUMNS = 256
BF16 = jnp.bfloat16
F32 = jnp.float32


def round_up(value, step):
    return -(-value // step) * step


def dot_nn(a, b):
    return lax.dot_general(a, b, (((1,), (0,)), ((), ())), preferred_element_type=F32)


def dot_nt(a, b):
    return lax.dot_general(a, b, (((1,), (1,)), ((), ())), preferred_element_type=F32)


def dot_tn(a, b):
    return lax.dot_general(a, b, (((0,), (0,)), ((), ())), preferred_element_type=F32)


def split_hi_lo(values):
    high = values.astype(BF16)
    low = (values - high.astype(F32)).astype(BF16)
    return high, low


def iota2(shape, axis):
    return lax.broadcasted_iota(jnp.int32, shape, axis)


def params(**extra):
    return pltpu.CompilerParams(vmem_limit_bytes=VMEM_LIMIT, **extra)


def in_hbm(values):
    return pltpu.with_memory_space_constraint(values, pltpu.HBM)


def swap(values, axis, distance):
    count = lax.axis_size(axis)
    return lax.ppermute(values, axis, [(source, source ^ distance) for source in range(count)])


def send_kernel(owner_hbm_ref, up_hbm_ref, down_hbm_ref, x_hbm_ref, *refs):
    block_refs, pack_ref, scratch = refs[:-8], refs[-8], refs[-7:]
    owner_ref, up_ref, down_ref, x_ref, turned_ref, small_sems, x_sems = scratch
    width = block_refs[0].shape[0]
    features, columns = x_ref.shape
    small = [
        pltpu.make_async_copy(source, target, small_sems.at[n])
        for n, (source, target) in enumerate(
            [(owner_hbm_ref, owner_ref), (up_hbm_ref, up_ref), (down_hbm_ref, down_ref)]
        )
    ]
    parts = [slice(start, start + LANE) for start in range(0, features, LANE)]
    large = [
        pltpu.make_async_copy(x_hbm_ref.at[part, :], x_ref.at[part, :], x_sems.at[n])
        for n, part in enumerate(parts)
    ]
    for copy in large + small:
        copy.start()
    for copy, part in zip(large, parts):
        copy.wait()
        for start in range(0, columns, LANE):
            at = slice(start, start + LANE)
            turned_ref[at, part] = x_ref[part, at].T
    for copy in small:
        copy.wait()
    pack_ref[...] = jnp.zeros_like(pack_ref)
    pack_ref[0, :, : up_ref.shape[1]] = up_ref[...]
    pack_ref[1, :, : down_ref.shape[1]] = down_ref[...]
    me = lax.axis_index("band")
    for distance, block_ref in zip(ORDER, block_refs):
        target = jnp.bitwise_xor(me, distance)
        block = 0
        for j in range(1, owner_ref.shape[0]):
            block = jnp.where(owner_ref[j] == target, j, block)
        block_ref[...] = turned_ref[pl.ds(pl.multiple_of(block * width, SUB), width), :]


def send_blocks(pixels, owner, up, down_t, width, pack_shape):
    features, columns = pixels.shape
    any_space = pl.BlockSpec(memory_space=pl.ANY)
    vmem = pl.BlockSpec(memory_space=pltpu.VMEM)
    blocks = [(width, features)] * BANDS
    *blocks, pack = pl.pallas_call(
        send_kernel,
        out_shape=[jax.ShapeDtypeStruct(shape, BF16) for shape in [*blocks, pack_shape]],
        in_specs=[any_space] * 4,
        out_specs=[vmem] * (len(blocks) + 1),
        scratch_shapes=[
            pltpu.SMEM(owner.shape, jnp.int32),
            pltpu.VMEM(up.shape, BF16),
            pltpu.VMEM(down_t.shape, BF16),
            pltpu.VMEM((features, columns), BF16),
            pltpu.VMEM((columns, features), BF16),
            pltpu.SemaphoreType.DMA((3,)),
            pltpu.SemaphoreType.DMA((features // LANE,)),
        ],
        compiler_params=params(),
        name="send_blocks",
    )(in_hbm(owner), in_hbm(up), in_hbm(down_t), in_hbm(pixels))
    return blocks, pack


def exchange(blocks):
    arrived = dict(zip(ORDER, blocks))
    for distance in ORDER[1:-2]:
        arrived[distance] = swap(arrived[distance], "band", distance)
    for distance, before in zip(ORDER[-2:], (1, 2)):
        block, arrived[before] = lax.optimization_barrier((arrived[distance], arrived[before]))
        arrived[distance] = swap(block, "band", distance)
    return [arrived[distance] for distance in ORDER]


def expand_table(table, rows, half_width_padded, half_width, transpose):
    position = iota2((rows, WLAT * WLON), 0)
    line, col = position // half_width_padded, position % half_width_padded
    target = iota2((rows, WLAT * WLON), 1)
    pick = jnp.where((target == line * WLON + col % WLON) & (col < half_width), 1.0, 0.0).astype(BF16)
    left = (dot_nt if transpose else dot_nn)(pick, table).astype(BF16)
    full = dot_nt(left, pick)
    row_window = (iota2((rows, 1), 0) % half_width_padded) // WLON
    col_window = (iota2((1, rows), 1) % half_width_padded) // WLON
    return jnp.where(row_window == col_window, full, 0.0).astype(BF16)


def prep_kernel(
    row_share,
    half_width,
    half_width_padded,
    group_hbm_ref,
    level_hbm_ref,
    grad_hbm_ref,
    frozen_ref,
    factors_ref,
    mixer_ref,
    merged_ref,
    up_ref,
    down_ref,
    mix_ref,
    mix_t_ref,
    level_ref,
    grad_ref,
    group_ref,
    sems,
):
    sources = [group_hbm_ref, level_hbm_ref, grad_hbm_ref]
    loads = [
        pltpu.make_async_copy(source, target, sems.at[n])
        for n, (source, target) in enumerate(zip(sources, [group_ref, level_ref, grad_ref]))
    ]
    for load in loads:
        load.start()
    rows = mix_ref.shape[0]
    mix_ref[...] = expand_table(mixer_ref[...], rows, half_width_padded, half_width, False)
    mix_t_ref[...] = expand_table(mixer_ref[...], rows, half_width_padded, half_width, True)
    reps, _, rank, share = factors_ref.shape
    levels = level_ref.shape[0]
    variables = group_ref.shape[0]
    channels = variables * frozen_ref.shape[1]
    up = jnp.concatenate([factors_ref[r, 0] for r in range(reps)], axis=1)
    source, target = iota2((share, channels), 0), iota2((share, channels), 1)
    down_t = jnp.zeros((rank, channels), F32)
    for r in range(reps):
        place = jnp.where((target == source + r * row_share) & (source < row_share), 1.0, 0.0)
        down_t = down_t + dot_nn(factors_ref[r, 1], place.astype(BF16))
    down_t = down_t.astype(BF16)
    down_ref[...] = down_t
    loads[0].wait()
    base = jnp.concatenate([frozen_ref[group_ref[v]].astype(F32) for v in range(variables)], axis=0)
    merged = (base + dot_tn(down_t, up)).astype(BF16)
    stacked = jnp.concatenate([merged, up], axis=0)
    merged_ref[...] = jnp.zeros_like(merged_ref)
    loads[1].wait()
    for level in range(levels):
        through = dot_nn(stacked, level_ref[level])
        weights = through[:channels].astype(BF16)
        for s in range(merged_ref.shape[0]):
            offset = (s * levels * channels) % LANE + level * channels
            merged_ref[s, offset : offset + channels, :] = weights
        up_high, up_low = split_hi_lo(through[channels:])
        up_ref[level, :rank, :] = up_high
        up_ref[level, rank:, :] = up_low
    loads[2].wait()


def prepare(groups, frozen, factors, level_weight, mixer, grad, row_share, half_width, half_width_padded):
    reps, _, rank, _ = factors.shape
    levels, feature_dim, _ = level_weight.shape
    channels = groups.shape[0] * frozen.shape[1]
    reach = round_up(levels * channels + LANE // 2, LANE)
    rows = WLAT * half_width_padded
    vmem = pl.BlockSpec(memory_space=pltpu.VMEM)
    flops = 2 * levels * (channels + rank) * feature_dim * feature_dim + 4 * rows * rows * WLAT * WLON
    shapes = [
        (grad.shape[0], reach, feature_dim),
        (levels, 2 * rank, feature_dim),
        (rank, channels),
        (rows, rows),
        (rows, rows),
        level_weight.shape,
        grad.shape,
    ]
    return pl.pallas_call(
        functools.partial(prep_kernel, row_share, half_width, half_width_padded),
        out_shape=[jax.ShapeDtypeStruct(shape, BF16) for shape in shapes],
        in_specs=[pl.BlockSpec(memory_space=pl.ANY)] * 3 + [vmem] * 3,
        out_specs=[vmem] * len(shapes),
        scratch_shapes=[pltpu.SMEM(groups.shape, jnp.int32), pltpu.SemaphoreType.DMA((3,))],
        compiler_params=params(),
        cost_estimate=pl.CostEstimate(flops=flops, bytes_accessed=6 * 2**20, transcendentals=0),
        name="prepare",
    )(in_hbm(groups), in_hbm(level_weight), in_hbm(grad), in_hbm(frozen), factors, in_hbm(mixer))


def normal_parts(values):
    cdf = 0.5 + 0.5 * lax.erf(values * 0.7071067811865476)
    return cdf, 0.3989422804014327 * jnp.exp2(values * values * -0.7213475204444817)


def factor_shares(total, up_ref, down_ref, level_ref):
    levels, two_rank, feature_dim = up_ref.shape
    rank, channels = down_ref.shape
    high, low = split_hi_lo(total)
    down = down_ref[...]
    first = jnp.zeros((rank, channels), F32)
    second = jnp.zeros((two_rank, feature_dim), F32)
    for level in range(levels):
        at = slice(level * channels, (level + 1) * channels)
        both = dot_nt(up_ref[level], high[at])
        first = first + both[:rank] + both[rank:] + dot_nt(up_ref[level, :rank, :], low[at])
        through = dot_nn(down, high[at]) + dot_nn(down, low[at])
        through = jnp.concatenate(split_hi_lo(through), axis=0)
        second = second + dot_nt(through, level_ref[level])
    return first, second[:rank] + second[rank:]


def mix_kernel(
    piece_refs,
    merged_ref,
    mix_ref,
    mix_t_ref,
    up_ref,
    down_ref,
    grad_ref,
    level_ref,
    mixed_hbm_ref,
    share_ref,
    arrived_refs,
    turned_refs,
    mixed_refs,
    pre_refs,
    tokens_refs,
    grad_pre_refs,
    grad_tokens_refs,
    total_ref,
    mixed_sems,
):
    samples, reach, feature_dim = merged_ref.shape
    chunk_count, (_, width, _) = len(mixed_refs), mixed_refs[0].shape
    halves = piece_refs[0].shape[-2] // width
    arrived_directly = len(piece_refs) > 1
    depth = piece_refs[0].shape[-1] // samples
    rows = WLAT * width

    def place(n):
        window_row, half, s = n // (halves * samples), n // samples % halves, n % samples
        lines, columns = pl.ds(window_row * WLAT, WLAT), pl.ds(half * width, width)
        return window_row, half, s, (s, lines, columns)

    stores = [
        pltpu.make_async_copy(mixed_refs[n], mixed_hbm_ref.at[place(n)[3]], mixed_sems.at[n])
        for n in range(chunk_count)
    ]
    def arrange(half):
        me = lax.axis_index("band")
        for distance, piece_ref in zip(ORDER, piece_refs):
            within = slice(half * width, (half + 1) * width)
            arrived_refs[half][jnp.bitwise_xor(me, distance)] = piece_ref[within, :]

    def pixels_of(n, lanes):
        window_row, half, _, _ = place(n)
        if arrived_directly:
            block = arrived_refs[half][:, :, lanes]
        else:
            lines = slice(window_row * WLAT, (window_row + 1) * WLAT)
            block = piece_refs[0][lines, half * width : (half + 1) * width, lanes]
        return block.reshape(rows, lanes.stop - lanes.start)

    def turn(n):
        def part(lanes):
            turned_refs[n // samples][lanes, :] = pixels_of(n, lanes).T

        starts = range(0, samples * depth, LANE)
        return [functools.partial(part, slice(start, start + LANE)) for start in starts]

    def forward(n, columns):
        s = n % samples
        lane = s * depth // LANE * LANE

        def embed():
            pixels = pixels_of(n, slice(lane, lane + reach))
            tokens_refs[n][:, columns] = dot_nn(pixels, merged_ref[s, :, columns]).astype(BF16)

        def mixing():
            pre_refs[n][:, columns] = dot_nn(mix_ref[...], tokens_refs[n][:, columns])

        return [embed, mixing]

    def grad_line(n, line, within, columns):
        _, _, s, (_, lines, first) = place(n)
        return grad_ref[s, lines.start + line, pl.ds(first.start + within.start, within.size), columns]

    def pointwise(n, columns):
        def part(line):
            for start in range(0, width, SUB):
                at, within = pl.ds(line * width + start, SUB), pl.ds(start, SUB)
                pre = pre_refs[n][at, columns]
                cdf, pdf = normal_parts(pre)
                tokens = tokens_refs[n][at, columns].astype(F32)
                mixed_refs[n][line, within, columns] = (tokens + pre * cdf).astype(BF16)
                grad = grad_line(n, line, within, columns).astype(F32)
                grad_pre_refs[n][at, columns] = (grad * (cdf + pre * pdf)).astype(BF16)

        return [functools.partial(part, line) for line in range(WLAT)]

    def backward(n, columns):
        def spread():
            _, _, s, (_, lines, within) = place(n)
            direct = grad_ref[s, lines, within, columns].reshape(rows, COLUMNS).astype(F32)
            through = dot_nn(mix_t_ref[...], grad_pre_refs[n][:, columns])
            grad_tokens_refs[n][:, columns] = (through + direct).astype(BF16)

        def share():
            s = n % samples
            turned = turned_refs[n // samples][s * depth : (s + 1) * depth, :]
            part = dot_nn(turned, grad_tokens_refs[n][:, columns])
            total_ref[:, columns] = part if n == 0 else total_ref[:, columns] + part

        return [spread, share]

    units = [
        (n, slice(start, start + COLUMNS))
        for n in range(chunk_count)
        for start in range(0, feature_dim, COLUMNS)
    ]
    if arrived_directly:
        arrange(0)
    for step in forward(*units[0]):
        step()
    for i, unit in enumerate(units):
        n, columns = unit
        others = []
        if i + 1 < len(units):
            others += forward(*units[i + 1])
        if columns.start == 0 and n % samples == 0:
            others += turn(n)
            if arrived_directly and n // samples + 1 < halves:
                others.append(functools.partial(arrange, n // samples + 1))
        if i > 0:
            others += backward(*units[i - 1])
        lines = pointwise(*unit)
        for line, vector_step in enumerate(lines):
            vector_step()
            for step in others[line * len(others) // len(lines) : (line + 1) * len(others) // len(lines)]:
                step()
        if columns.stop == feature_dim:
            stores[n].start()
    for step in backward(*units[-1]):
        step()

    first, second = factor_shares(total_ref[...], up_ref, down_ref, level_ref)
    rank, channels = down_ref.shape
    columns = share_ref.shape[2]
    reps = feature_dim // columns
    folds = rank // (share_ref.shape[1] - rank)
    depth_rows, fold_lanes, row_share = rank // folds, columns // folds, channels // reps
    packed = jnp.zeros((depth_rows, feature_dim), F32)
    row, lane = iota2((channels, feature_dim), 0), iota2((1, feature_dim), 1)
    rep, lane = lane // columns, lane % columns
    for fold in range(folds):
        inside = lane - fold * fold_lanes
        target = jnp.where((inside >= 0) & (inside < row_share), inside + rep * row_share, -1)
        pick = jnp.where(row == target, 1.0, 0.0).astype(BF16)
        part = first[fold * depth_rows : (fold + 1) * depth_rows].astype(BF16)
        packed = packed + dot_nn(part, pick)
    payload = jnp.concatenate([second, packed], axis=0).astype(BF16)
    for slot in range(share_ref.shape[0]):
        at = slot % reps * columns
        share_ref[slot] = payload[:, at : at + columns]
    for store in stores:
        store.wait()


def mix_blocks(halves, arrived, merged, mix, mix_t, grad, up_through, down_t, level_weight, band_count, reps):
    samples, lat_rows, block_width, feature_dim = grad.shape
    width = block_width // halves
    lanes = arrived[0].shape[-1]
    reach = merged.shape[1]
    rows = WLAT * width
    rank = down_t.shape[0]
    chunks = lat_rows // WLAT * halves * samples
    share_shape = (band_count * reps, rank + rank // FOLDS, feature_dim // reps)
    flops = 2 * samples * lat_rows * block_width * feature_dim * (2 * reach + 2 * rows)
    vmem = pl.BlockSpec(memory_space=pltpu.VMEM)
    any_space = pl.BlockSpec(memory_space=pl.ANY)
    local = [*arrived, merged, mix, mix_t, up_through, down_t]
    return pl.pallas_call(
        lambda *refs: mix_kernel(refs[: len(arrived)], *refs[len(arrived) :]),
        out_shape=[
            jax.ShapeDtypeStruct(grad.shape, BF16),
            jax.ShapeDtypeStruct(share_shape, BF16),
        ],
        in_specs=[vmem] * (len(local) + 2),
        out_specs=[any_space, vmem],
        scratch_shapes=[
            [pltpu.VMEM((WLAT, width, lanes), BF16)] * halves,
            [pltpu.VMEM((lanes, rows), BF16)] * (chunks // samples),
            [pltpu.VMEM((WLAT, width, feature_dim), BF16)] * chunks,
            [pltpu.VMEM((rows, feature_dim), F32)] * chunks,
            [pltpu.VMEM((rows, feature_dim), BF16)] * chunks,
            [pltpu.VMEM((rows, feature_dim), BF16)] * chunks,
            [pltpu.VMEM((rows, feature_dim), BF16)] * chunks,
            pltpu.VMEM((lanes // samples, feature_dim), F32),
            pltpu.SemaphoreType.DMA((chunks,)),
        ],
        compiler_params=params(),
        cost_estimate=pl.CostEstimate(
            flops=flops,
            bytes_accessed=12 * 2**20,
            transcendentals=samples * lat_rows * block_width * feature_dim,
        ),
        name="mix_blocks",
    )(*local, grad, level_weight)


def sum_kernel(parts_ref, first_ref, second_ref):
    rank, row_share = first_ref.shape
    total = parts_ref[0].astype(F32)
    for n in range(1, parts_ref.shape[0]):
        total = total + parts_ref[n].astype(F32)
    second_ref[...] = total[:rank]
    depth_rows = total.shape[0] - rank
    for fold in range(rank // depth_rows):
        lane = fold * depth_rows * total.shape[1] // rank
        first_ref[fold * depth_rows : (fold + 1) * depth_rows, :] = total[rank:, lane : lane + row_share]


def sum_shares(shares, rank, row_share):
    parts = lax.all_to_all(shares, ("band", "rep"), split_axis=0, concat_axis=0, tiled=True)
    return pl.pallas_call(
        sum_kernel,
        out_shape=[
            jax.ShapeDtypeStruct((rank, row_share), F32),
            jax.ShapeDtypeStruct((rank, shares.shape[2]), F32),
        ],
        compiler_params=params(),
        name="sum_shares",
    )(parts)


def on_device(
    patches,
    variable_group_index,
    frozen_patch_weight,
    adapter_down,
    adapter_up,
    level_merge_weight,
    window_patch_mixer,
    column_block_owner,
    mixed_token_gradient,
):
    band_count, reps = lax.axis_size("band"), lax.axis_size("rep")
    samples, levels, channels, row_count, col_count = patches.shape
    feature_dim = frozen_patch_weight.shape[2]
    rank, col_share = adapter_up.shape
    row_share = adapter_down.shape[0]
    lat_rows = band_count * row_count
    block_width = col_count // band_count
    halves = 2 if block_width % (2 * SUB * WLON // 4) == 0 else 1
    half_width = block_width // halves
    half_padded = round_up(half_width, SUB)
    padded_width = halves * half_padded
    features = samples * levels * channels

    pixels = patches.reshape(features, col_count)
    pack_shape = (2, rank, round_up(max(row_share, col_share), LANE))
    direct = band_count == BANDS and lat_rows == WLAT and half_padded == half_width
    if direct and features % LANE == 0 and col_count % LANE == 0:
        blocks, pack = send_blocks(
            pixels, column_block_owner, adapter_up, adapter_down.T, block_width, pack_shape
        )
        arrived = exchange(blocks)
    else:
        block_ids = jnp.arange(band_count, dtype=jnp.int32)
        inverse = jnp.sum(
            jnp.where(column_block_owner[None, :] == block_ids[:, None], block_ids[None, :], 0), axis=1
        )
        outgoing = jnp.take(pixels.T.reshape(band_count, block_width, features), inverse, axis=0)
        outgoing = jnp.pad(outgoing, ((0, 0), (0, padded_width - block_width), (0, 0)))
        arrived = [lax.all_to_all(outgoing, "band", split_axis=0, concat_axis=0, tiled=True)]
        pack = jnp.stack(
            [
                jnp.pad(array, ((0, 0), (0, pack_shape[2] - array.shape[1])))
                for array in (adapter_up, adapter_down.T)
            ]
        )
    factors = lax.all_gather(pack, "rep", axis=0, tiled=False)

    grad = mixed_token_gradient.reshape(samples, lat_rows, block_width, feature_dim)
    if padded_width != block_width:
        grad = jnp.pad(grad, ((0, 0), (0, 0), (0, padded_width - block_width), (0, 0)))
    merged, up_through, down_t, mix, mix_t, level_copy, grad_copy = prepare(
        variable_group_index,
        frozen_patch_weight,
        factors,
        level_merge_weight,
        window_patch_mixer,
        grad,
        row_share,
        half_width,
        half_padded,
    )
    mixed, shares = mix_blocks(
        halves, arrived, merged, mix, mix_t, grad_copy, up_through, down_t, level_copy, band_count, reps
    )
    if padded_width != block_width:
        mixed = mixed[:, :, :block_width]
    first_t, second = sum_shares(shares, rank, row_share)
    return mixed.reshape(mixed_token_gradient.shape), first_t.T, second


def solution(mesh):
    in_specs = (
        P("rep", None, None, "band", None),
        P(),
        P(),
        P("rep", None),
        P(None, "rep"),
        P(),
        P(),
        P(),
        P("rep", "band", None, None, None),
    )
    out_specs = (P("rep", "band", None, None, None), P("rep", None), P(None, "rep"))
    return jax.shard_map(
        on_device, mesh=mesh, in_specs=in_specs, out_specs=out_specs, check_vma=False
    )
```

```python
import functools

import jax
import jax.numpy as jnp
from jax import lax
from jax.experimental import pallas as pl
from jax.experimental.pallas import tpu as pltpu
from jax.sharding import PartitionSpec as P

WLAT = 8
WLON = 12
LANE = 128
SUB = 16
VMEM_LIMIT = 24 * 1024 * 1024
BANDS = 8
ORDER = (0, 4, 1, 5, 2, 6, 7, 3)
FOLDS = 2
COLUMNS = 256
BF16 = jnp.bfloat16
F32 = jnp.float32


def round_up(value, step):
    return -(-value // step) * step


def dot_nn(a, b):
    return lax.dot_general(a, b, (((1,), (0,)), ((), ())), preferred_element_type=F32)


def dot_nt(a, b):
    return lax.dot_general(a, b, (((1,), (1,)), ((), ())), preferred_element_type=F32)


def dot_tn(a, b):
    return lax.dot_general(a, b, (((0,), (0,)), ((), ())), preferred_element_type=F32)


def split_hi_lo(values):
    high = values.astype(BF16)
    low = (values - high.astype(F32)).astype(BF16)
    return high, low


def iota2(shape, axis):
    return lax.broadcasted_iota(jnp.int32, shape, axis)


def params(**extra):
    return pltpu.CompilerParams(vmem_limit_bytes=VMEM_LIMIT, **extra)


def in_hbm(values):
    return pltpu.with_memory_space_constraint(values, pltpu.HBM)


def swap(values, axis, distance):
    count = lax.axis_size(axis)
    return lax.ppermute(values, axis, [(source, source ^ distance) for source in range(count)])


def send_kernel(owner_hbm_ref, up_hbm_ref, down_hbm_ref, x_hbm_ref, *refs):
    block_refs, pack_ref, scratch = refs[:-8], refs[-8], refs[-7:]
    owner_ref, up_ref, down_ref, x_ref, turned_ref, small_sems, x_sems = scratch
    width = block_refs[0].shape[0]
    features, columns = x_ref.shape
    small = [
        pltpu.make_async_copy(source, target, small_sems.at[n])
        for n, (source, target) in enumerate(
            [(owner_hbm_ref, owner_ref), (up_hbm_ref, up_ref), (down_hbm_ref, down_ref)]
        )
    ]
    parts = [slice(start, start + LANE) for start in range(0, features, LANE)]
    large = [
        pltpu.make_async_copy(x_hbm_ref.at[part, :], x_ref.at[part, :], x_sems.at[n])
        for n, part in enumerate(parts)
    ]
    for copy in large + small:
        copy.start()
    for copy, part in zip(large, parts):
        copy.wait()
        for start in range(0, columns, LANE):
            at = slice(start, start + LANE)
            turned_ref[at, part] = x_ref[part, at].T
    for copy in small:
        copy.wait()
    pack_ref[...] = jnp.zeros_like(pack_ref)
    pack_ref[0, :, : up_ref.shape[1]] = up_ref[...]
    pack_ref[1, :, : down_ref.shape[1]] = down_ref[...]
    me = lax.axis_index("band")
    for distance, block_ref in zip(ORDER, block_refs):
        target = jnp.bitwise_xor(me, distance)
        block = 0
        for j in range(1, owner_ref.shape[0]):
            block = jnp.where(owner_ref[j] == target, j, block)
        block_ref[...] = turned_ref[pl.ds(pl.multiple_of(block * width, SUB), width), :]


def send_blocks(pixels, owner, up, down_t, width, pack_shape):
    features, columns = pixels.shape
    any_space = pl.BlockSpec(memory_space=pl.ANY)
    vmem = pl.BlockSpec(memory_space=pltpu.VMEM)
    blocks = [(width, features)] * BANDS
    *blocks, pack = pl.pallas_call(
        send_kernel,
        out_shape=[jax.ShapeDtypeStruct(shape, BF16) for shape in [*blocks, pack_shape]],
        in_specs=[any_space] * 4,
        out_specs=[vmem] * (len(blocks) + 1),
        scratch_shapes=[
            pltpu.SMEM(owner.shape, jnp.int32),
            pltpu.VMEM(up.shape, BF16),
            pltpu.VMEM(down_t.shape, BF16),
            pltpu.VMEM((features, columns), BF16),
            pltpu.VMEM((columns, features), BF16),
            pltpu.SemaphoreType.DMA((3,)),
            pltpu.SemaphoreType.DMA((features // LANE,)),
        ],
        compiler_params=params(),
        name="send_blocks",
    )(in_hbm(owner), in_hbm(up), in_hbm(down_t), in_hbm(pixels))
    return blocks, pack


def exchange(blocks):
    arrived = dict(zip(ORDER, blocks))
    for distance in ORDER[1:-2]:
        arrived[distance] = swap(arrived[distance], "band", distance)
    for distance, before in zip(ORDER[-2:], (1, 2)):
        block, arrived[before] = lax.optimization_barrier((arrived[distance], arrived[before]))
        arrived[distance] = swap(block, "band", distance)
    return [arrived[distance] for distance in ORDER]


def expand_table(table, rows, half_width_padded, half_width, transpose):
    position = iota2((rows, WLAT * WLON), 0)
    line, col = position // half_width_padded, position % half_width_padded
    target = iota2((rows, WLAT * WLON), 1)
    pick = jnp.where((target == line * WLON + col % WLON) & (col < half_width), 1.0, 0.0).astype(BF16)
    left = (dot_nt if transpose else dot_nn)(pick, table).astype(BF16)
    full = dot_nt(left, pick)
    row_window = (iota2((rows, 1), 0) % half_width_padded) // WLON
    col_window = (iota2((1, rows), 1) % half_width_padded) // WLON
    return jnp.where(row_window == col_window, full, 0.0).astype(BF16)


def prep_kernel(
    row_share,
    half_width,
    half_width_padded,
    group_hbm_ref,
    level_hbm_ref,
    grad_hbm_ref,
    frozen_ref,
    factors_ref,
    mixer_ref,
    merged_ref,
    up_ref,
    down_ref,
    mix_ref,
    mix_t_ref,
    level_ref,
    grad_ref,
    group_ref,
    sems,
):
    sources = [group_hbm_ref, level_hbm_ref, grad_hbm_ref]
    loads = [
        pltpu.make_async_copy(source, target, sems.at[n])
        for n, (source, target) in enumerate(zip(sources, [group_ref, level_ref, grad_ref]))
    ]
    for load in loads:
        load.start()
    rows = mix_ref.shape[0]
    mix_ref[...] = expand_table(mixer_ref[...], rows, half_width_padded, half_width, False)
    mix_t_ref[...] = expand_table(mixer_ref[...], rows, half_width_padded, half_width, True)
    reps, _, rank, share = factors_ref.shape
    levels = level_ref.shape[0]
    variables = group_ref.shape[0]
    channels = variables * frozen_ref.shape[1]
    up = jnp.concatenate([factors_ref[r, 0] for r in range(reps)], axis=1)
    source, target = iota2((share, channels), 0), iota2((share, channels), 1)
    down_t = jnp.zeros((rank, channels), F32)
    for r in range(reps):
        place = jnp.where((target == source + r * row_share) & (source < row_share), 1.0, 0.0)
        down_t = down_t + dot_nn(factors_ref[r, 1], place.astype(BF16))
    down_t = down_t.astype(BF16)
    down_ref[...] = down_t
    loads[0].wait()
    base = jnp.concatenate([frozen_ref[group_ref[v]].astype(F32) for v in range(variables)], axis=0)
    merged = (base + dot_tn(down_t, up)).astype(BF16)
    stacked = jnp.concatenate([merged, up], axis=0)
    merged_ref[...] = jnp.zeros_like(merged_ref)
    loads[1].wait()
    for level in range(levels):
        through = dot_nn(stacked, level_ref[level])
        weights = through[:channels].astype(BF16)
        for s in range(merged_ref.shape[0]):
            offset = (s * levels * channels) % LANE + level * channels
            merged_ref[s, offset : offset + channels, :] = weights
        up_high, up_low = split_hi_lo(through[channels:])
        up_ref[level, :rank, :] = up_high
        up_ref[level, rank:, :] = up_low
    loads[2].wait()


def prepare(groups, frozen, factors, level_weight, mixer, grad, row_share, half_width, half_width_padded):
    reps, _, rank, _ = factors.shape
    levels, feature_dim, _ = level_weight.shape
    channels = groups.shape[0] * frozen.shape[1]
    reach = round_up(levels * channels + LANE // 2, LANE)
    rows = WLAT * half_width_padded
    vmem = pl.BlockSpec(memory_space=pltpu.VMEM)
    flops = 2 * levels * (channels + rank) * feature_dim * feature_dim + 4 * rows * rows * WLAT * WLON
    shapes = [
        (grad.shape[0], reach, feature_dim),
        (levels, 2 * rank, feature_dim),
        (rank, channels),
        (rows, rows),
        (rows, rows),
        level_weight.shape,
        grad.shape,
    ]
    return pl.pallas_call(
        functools.partial(prep_kernel, row_share, half_width, half_width_padded),
        out_shape=[jax.ShapeDtypeStruct(shape, BF16) for shape in shapes],
        in_specs=[pl.BlockSpec(memory_space=pl.ANY)] * 3 + [vmem] * 3,
        out_specs=[vmem] * len(shapes),
        scratch_shapes=[pltpu.SMEM(groups.shape, jnp.int32), pltpu.SemaphoreType.DMA((3,))],
        compiler_params=params(),
        cost_estimate=pl.CostEstimate(flops=flops, bytes_accessed=6 * 2**20, transcendentals=0),
        name="prepare",
    )(in_hbm(groups), in_hbm(level_weight), in_hbm(grad), in_hbm(frozen), factors, in_hbm(mixer))


def normal_parts(values):
    cdf = 0.5 + 0.5 * lax.erf(values * 0.7071067811865476)
    return cdf, 0.3989422804014327 * jnp.exp2(values * values * -0.7213475204444817)


def factor_shares(total, up_ref, down_ref, level_ref):
    levels, two_rank, feature_dim = up_ref.shape
    rank, channels = down_ref.shape
    high, low = split_hi_lo(total)
    down = down_ref[...]
    first = jnp.zeros((rank, channels), F32)
    second = jnp.zeros((two_rank, feature_dim), F32)
    for level in range(levels):
        at = slice(level * channels, (level + 1) * channels)
        both = dot_nt(up_ref[level], high[at])
        first = first + both[:rank] + both[rank:] + dot_nt(up_ref[level, :rank, :], low[at])
        through = dot_nn(down, high[at]) + dot_nn(down, low[at])
        through = jnp.concatenate(split_hi_lo(through), axis=0)
        second = second + dot_nt(through, level_ref[level])
    return first, second[:rank] + second[rank:]


def mix_kernel(
    piece_refs,
    merged_ref,
    mix_ref,
    mix_t_ref,
    up_ref,
    down_ref,
    grad_ref,
    level_ref,
    mixed_hbm_ref,
    share_ref,
    arrived_refs,
    turned_refs,
    mixed_refs,
    pre_refs,
    tokens_refs,
    grad_pre_refs,
    grad_tokens_refs,
    total_ref,
    mixed_sems,
):
    samples, reach, feature_dim = merged_ref.shape
    chunk_count, (_, width, _) = len(mixed_refs), mixed_refs[0].shape
    halves = piece_refs[0].shape[-2] // width
    arrived_directly = len(piece_refs) > 1
    depth = piece_refs[0].shape[-1] // samples
    rows = WLAT * width

    group_rows = mix_ref.shape[0]
    group = group_rows // WLAT
    groups = [
        (slice(start, start + group), slice(start * WLAT, start * WLAT + group_rows))
        for start in range(0, width, group)
    ]
    pair = 1 if group % SUB == 0 else 2

    def place(n):
        window_row, half, s = n // (halves * samples), n // samples % halves, n % samples
        lines, columns = pl.ds(window_row * WLAT, WLAT), pl.ds(half * width, width)
        return window_row, half, s, (s, lines, columns)

    stores = [
        pltpu.make_async_copy(mixed_refs[n], mixed_hbm_ref.at[place(n)[3]], mixed_sems.at[n])
        for n in range(chunk_count)
    ]
    def arrange(half):
        me = lax.axis_index("band")
        for distance, piece_ref in zip(ORDER, piece_refs):
            within = slice(half * width, (half + 1) * width)
            arrived_refs[half][jnp.bitwise_xor(me, distance)] = piece_ref[within, :]

    def pixels_of(n, lanes):
        window_row, half, _, _ = place(n)
        if arrived_directly:
            block = arrived_refs[half][:, :, lanes]
        else:
            lines = slice(window_row * WLAT, (window_row + 1) * WLAT)
            block = piece_refs[0][lines, half * width : (half + 1) * width, lanes]
        return block.reshape(rows, lanes.stop - lanes.start)

    def turn(n):
        def part(lanes):
            turned_refs[n // samples][lanes, :] = pixels_of(n, lanes).T

        starts = range(0, samples * depth, LANE)
        return [functools.partial(part, slice(start, start + LANE)) for start in starts]

    def forward(n, columns):
        s = n % samples
        lane = s * depth // LANE * LANE

        def embed():
            pixels = pixels_of(n, slice(lane, lane + reach))
            tokens = dot_nn(pixels, merged_ref[s, :, columns]).reshape(WLAT, width, COLUMNS)
            for within, at in groups:
                tokens_refs[n][at, columns] = tokens[:, within].reshape(group_rows, COLUMNS).astype(BF16)

        def mixing():
            for _, at in groups:
                pre_refs[n][at, columns] = dot_nn(mix_ref[...], tokens_refs[n][at, columns])

        return [embed, mixing]

    def pointwise(n, columns):
        _, _, s, (_, lines, across) = place(n)

        def part(line, lanes):
            grads = [grad_ref[s, lines.start + line + k, across, lanes].astype(F32) for k in range(pair)]
            mixed = []
            for within, at in groups:
                at = pl.ds(at.start + line * group, pair * group)
                pre = pre_refs[n][at, lanes]
                cdf, pdf = normal_parts(pre)
                mixed.append(tokens_refs[n][at, lanes].astype(F32) + pre * cdf)
                grad = jnp.concatenate([values[within] for values in grads], axis=0)
                grad_pre_refs[n][at, lanes] = (grad * (cdf + pre * pdf)).astype(BF16)
            for k in range(pair):
                parts = [values[k * group : (k + 1) * group] for values in mixed]
                mixed_refs[n][line + k, :, lanes] = jnp.concatenate(parts, axis=0).astype(BF16)

        return [
            functools.partial(part, line, slice(start, start + LANE))
            for line in range(0, WLAT, pair)
            for start in range(columns.start, columns.stop, LANE)
        ]

    def backward(n, columns):
        def spread():
            _, _, s, (_, lines, within) = place(n)
            through = [
                dot_nn(mix_t_ref[...], grad_pre_refs[n][at, columns]).reshape(WLAT, group, COLUMNS)
                for _, at in groups
            ]
            total = jnp.concatenate(through, axis=1) + grad_ref[s, lines, within, columns].astype(F32)
            grad_tokens_refs[n][:, columns] = total.reshape(rows, COLUMNS).astype(BF16)

        def share():
            s = n % samples
            turned = turned_refs[n // samples][s * depth : (s + 1) * depth, :]
            part = dot_nn(turned, grad_tokens_refs[n][:, columns])
            total_ref[:, columns] = part if n == 0 else total_ref[:, columns] + part

        return [spread, share]

    units = [
        (n, slice(start, start + COLUMNS))
        for n in range(chunk_count)
        for start in range(0, feature_dim, COLUMNS)
    ]
    if arrived_directly:
        arrange(0)
    for step in forward(*units[0]):
        step()
    for i, unit in enumerate(units):
        n, columns = unit
        others = []
        if i + 1 < len(units):
            others += forward(*units[i + 1])
        if columns.start == 0 and n % samples == 0:
            others += turn(n)
            if arrived_directly and n // samples + 1 < halves:
                others.append(functools.partial(arrange, n // samples + 1))
        if i > 0:
            others += backward(*units[i - 1])
        lines = pointwise(*unit)
        for line, vector_step in enumerate(lines):
            vector_step()
            for step in others[line * len(others) // len(lines) : (line + 1) * len(others) // len(lines)]:
                step()
        if columns.stop == feature_dim:
            stores[n].start()
    for step in backward(*units[-1]):
        step()

    first, second = factor_shares(total_ref[...], up_ref, down_ref, level_ref)
    rank, channels = down_ref.shape
    columns = share_ref.shape[2]
    reps = feature_dim // columns
    folds = rank // (share_ref.shape[1] - rank)
    depth_rows, fold_lanes, row_share = rank // folds, columns // folds, channels // reps
    packed = jnp.zeros((depth_rows, feature_dim), F32)
    row, lane = iota2((channels, feature_dim), 0), iota2((1, feature_dim), 1)
    rep, lane = lane // columns, lane % columns
    for fold in range(folds):
        inside = lane - fold * fold_lanes
        target = jnp.where((inside >= 0) & (inside < row_share), inside + rep * row_share, -1)
        pick = jnp.where(row == target, 1.0, 0.0).astype(BF16)
        part = first[fold * depth_rows : (fold + 1) * depth_rows].astype(BF16)
        packed = packed + dot_nn(part, pick)
    payload = jnp.concatenate([second, packed], axis=0).astype(BF16)
    for slot in range(share_ref.shape[0]):
        at = slot % reps * columns
        share_ref[slot] = payload[:, at : at + columns]
    for store in stores:
        store.wait()


def mix_blocks(halves, arrived, merged, mix, mix_t, grad, up_through, down_t, level_weight, band_count, reps):
    samples, lat_rows, block_width, feature_dim = grad.shape
    width = block_width // halves
    lanes = arrived[0].shape[-1]
    reach = merged.shape[1]
    rows = WLAT * width
    rank = down_t.shape[0]
    chunks = lat_rows // WLAT * halves * samples
    share_shape = (band_count * reps, rank + rank // FOLDS, feature_dim // reps)
    flops = 2 * samples * lat_rows * block_width * feature_dim * (2 * reach + 2 * rows)
    vmem = pl.BlockSpec(memory_space=pltpu.VMEM)
    any_space = pl.BlockSpec(memory_space=pl.ANY)
    local = [*arrived, merged, mix, mix_t, up_through, down_t]
    return pl.pallas_call(
        lambda *refs: mix_kernel(refs[: len(arrived)], *refs[len(arrived) :]),
        out_shape=[
            jax.ShapeDtypeStruct(grad.shape, BF16),
            jax.ShapeDtypeStruct(share_shape, BF16),
        ],
        in_specs=[vmem] * (len(local) + 2),
        out_specs=[any_space, vmem],
        scratch_shapes=[
            [pltpu.VMEM((WLAT, width, lanes), BF16)] * halves,
            [pltpu.VMEM((lanes, rows), BF16)] * (chunks // samples),
            [pltpu.VMEM((WLAT, width, feature_dim), BF16)] * chunks,
            [pltpu.VMEM((rows, feature_dim), F32)] * chunks,
            [pltpu.VMEM((rows, feature_dim), BF16)] * chunks,
            [pltpu.VMEM((rows, feature_dim), BF16)] * chunks,
            [pltpu.VMEM((rows, feature_dim), BF16)] * chunks,
            pltpu.VMEM((lanes // samples, feature_dim), F32),
            pltpu.SemaphoreType.DMA((chunks,)),
        ],
        compiler_params=params(),
        cost_estimate=pl.CostEstimate(
            flops=flops,
            bytes_accessed=12 * 2**20,
            transcendentals=samples * lat_rows * block_width * feature_dim,
        ),
        name="mix_blocks",
    )(*local, grad, level_weight)


def sum_kernel(parts_ref, first_ref, second_ref):
    rank, row_share = first_ref.shape
    total = parts_ref[0].astype(F32)
    for n in range(1, parts_ref.shape[0]):
        total = total + parts_ref[n].astype(F32)
    second_ref[...] = total[:rank]
    depth_rows = total.shape[0] - rank
    for fold in range(rank // depth_rows):
        lane = fold * depth_rows * total.shape[1] // rank
        first_ref[fold * depth_rows : (fold + 1) * depth_rows, :] = total[rank:, lane : lane + row_share]


def sum_shares(shares, rank, row_share):
    parts = lax.all_to_all(shares, ("band", "rep"), split_axis=0, concat_axis=0, tiled=True)
    return pl.pallas_call(
        sum_kernel,
        out_shape=[
            jax.ShapeDtypeStruct((rank, row_share), F32),
            jax.ShapeDtypeStruct((rank, shares.shape[2]), F32),
        ],
        compiler_params=params(),
        name="sum_shares",
    )(parts)


def on_device(
    patches,
    variable_group_index,
    frozen_patch_weight,
    adapter_down,
    adapter_up,
    level_merge_weight,
    window_patch_mixer,
    column_block_owner,
    mixed_token_gradient,
):
    band_count, reps = lax.axis_size("band"), lax.axis_size("rep")
    samples, levels, channels, row_count, col_count = patches.shape
    feature_dim = frozen_patch_weight.shape[2]
    rank, col_share = adapter_up.shape
    row_share = adapter_down.shape[0]
    lat_rows = band_count * row_count
    block_width = col_count // band_count
    halves = 2 if block_width % (2 * SUB * WLON // 4) == 0 else 1
    half_width = block_width // halves
    half_padded = round_up(half_width, SUB)
    padded_width = halves * half_padded
    group = 2 * WLON if half_width % (2 * WLON) == 0 else half_padded
    features = samples * levels * channels

    pixels = patches.reshape(features, col_count)
    pack_shape = (2, rank, round_up(max(row_share, col_share), LANE))
    direct = band_count == BANDS and lat_rows == WLAT and half_padded == half_width
    if direct and features % LANE == 0 and col_count % LANE == 0:
        blocks, pack = send_blocks(
            pixels, column_block_owner, adapter_up, adapter_down.T, block_width, pack_shape
        )
        arrived = exchange(blocks)
    else:
        block_ids = jnp.arange(band_count, dtype=jnp.int32)
        inverse = jnp.sum(
            jnp.where(column_block_owner[None, :] == block_ids[:, None], block_ids[None, :], 0), axis=1
        )
        outgoing = jnp.take(pixels.T.reshape(band_count, block_width, features), inverse, axis=0)
        outgoing = jnp.pad(outgoing, ((0, 0), (0, padded_width - block_width), (0, 0)))
        arrived = [lax.all_to_all(outgoing, "band", split_axis=0, concat_axis=0, tiled=True)]
        pack = jnp.stack(
            [
                jnp.pad(array, ((0, 0), (0, pack_shape[2] - array.shape[1])))
                for array in (adapter_up, adapter_down.T)
            ]
        )
    factors = lax.all_gather(pack, "rep", axis=0, tiled=False)

    grad = mixed_token_gradient.reshape(samples, lat_rows, block_width, feature_dim)
    if padded_width != block_width:
        grad = jnp.pad(grad, ((0, 0), (0, 0), (0, padded_width - block_width), (0, 0)))
    merged, up_through, down_t, mix, mix_t, level_copy, grad_copy = prepare(
        variable_group_index,
        frozen_patch_weight,
        factors,
        level_merge_weight,
        window_patch_mixer,
        grad,
        row_share,
        min(half_width, group),
        group,
    )
    mixed, shares = mix_blocks(
        halves, arrived, merged, mix, mix_t, grad_copy, up_through, down_t, level_copy, band_count, reps
    )
    if padded_width != block_width:
        mixed = mixed[:, :, :block_width]
    first_t, second = sum_shares(shares, rank, row_share)
    return mixed.reshape(mixed_token_gradient.shape), first_t.T, second


def solution(mesh):
    in_specs = (
        P("rep", None, None, "band", None),
        P(),
        P(),
        P("rep", None),
        P(None, "rep"),
        P(),
        P(),
        P(),
        P("rep", "band", None, None, None),
    )
    out_specs = (P("rep", "band", None, None, None), P("rep", None), P(None, "rep"))
    return jax.shard_map(
        on_device, mesh=mesh, in_specs=in_specs, out_specs=out_specs, check_vma=False
    )
```

```python
import functools

import jax
import jax.numpy as jnp
from jax import lax
from jax.experimental import pallas as pl
from jax.experimental.pallas import tpu as pltpu
from jax.sharding import PartitionSpec as P

WLAT = 8
WLON = 12
LANE = 128
SUB = 16
VMEM_LIMIT = 24 * 1024 * 1024
BANDS = 8
ORDER = (0, 4, 1, 5, 2, 6, 7, 3)
FOLDS = 2
COLUMNS = 256
BF16 = jnp.bfloat16
F32 = jnp.float32


def round_up(value, step):
    return -(-value // step) * step


def dot_nn(a, b):
    return lax.dot_general(a, b, (((1,), (0,)), ((), ())), preferred_element_type=F32)


def dot_nt(a, b):
    return lax.dot_general(a, b, (((1,), (1,)), ((), ())), preferred_element_type=F32)


def dot_tn(a, b):
    return lax.dot_general(a, b, (((0,), (0,)), ((), ())), preferred_element_type=F32)


def split_hi_lo(values):
    high = values.astype(BF16)
    low = (values - high.astype(F32)).astype(BF16)
    return high, low


def iota2(shape, axis):
    return lax.broadcasted_iota(jnp.int32, shape, axis)


def params(**extra):
    return pltpu.CompilerParams(vmem_limit_bytes=VMEM_LIMIT, **extra)


def in_hbm(values):
    return pltpu.with_memory_space_constraint(values, pltpu.HBM)


def swap(values, axis, distance):
    count = lax.axis_size(axis)
    return lax.ppermute(values, axis, [(source, source ^ distance) for source in range(count)])


def send_kernel(owner_hbm_ref, up_hbm_ref, down_hbm_ref, x_hbm_ref, *refs):
    block_refs, pack_ref, scratch = refs[:-8], refs[-8], refs[-7:]
    owner_ref, up_ref, down_ref, x_ref, turned_ref, small_sems, x_sems = scratch
    width = block_refs[0].shape[0]
    features, columns = x_ref.shape
    small = [
        pltpu.make_async_copy(source, target, small_sems.at[n])
        for n, (source, target) in enumerate(
            [(owner_hbm_ref, owner_ref), (up_hbm_ref, up_ref), (down_hbm_ref, down_ref)]
        )
    ]
    parts = [slice(start, start + LANE) for start in range(0, features, LANE)]
    large = [
        pltpu.make_async_copy(x_hbm_ref.at[part, :], x_ref.at[part, :], x_sems.at[n])
        for n, part in enumerate(parts)
    ]
    for copy in large + small:
        copy.start()
    for copy, part in zip(large, parts):
        copy.wait()
        for start in range(0, columns, LANE):
            at = slice(start, start + LANE)
            turned_ref[at, part] = x_ref[part, at].T
    for copy in small:
        copy.wait()
    pack_ref[...] = jnp.zeros_like(pack_ref)
    pack_ref[0, :, : up_ref.shape[1]] = up_ref[...]
    pack_ref[1, :, : down_ref.shape[1]] = down_ref[...]
    me = lax.axis_index("band")
    for distance, block_ref in zip(ORDER, block_refs):
        target = jnp.bitwise_xor(me, distance)
        block = 0
        for j in range(1, owner_ref.shape[0]):
            block = jnp.where(owner_ref[j] == target, j, block)
        block_ref[...] = turned_ref[pl.ds(pl.multiple_of(block * width, SUB), width), :]


def send_blocks(pixels, owner, up, down_t, width, pack_shape):
    features, columns = pixels.shape
    any_space = pl.BlockSpec(memory_space=pl.ANY)
    vmem = pl.BlockSpec(memory_space=pltpu.VMEM)
    blocks = [(width, features)] * BANDS
    *blocks, pack = pl.pallas_call(
        send_kernel,
        out_shape=[jax.ShapeDtypeStruct(shape, BF16) for shape in [*blocks, pack_shape]],
        in_specs=[any_space] * 4,
        out_specs=[vmem] * (len(blocks) + 1),
        scratch_shapes=[
            pltpu.SMEM(owner.shape, jnp.int32),
            pltpu.VMEM(up.shape, BF16),
            pltpu.VMEM(down_t.shape, BF16),
            pltpu.VMEM((features, columns), BF16),
            pltpu.VMEM((columns, features), BF16),
            pltpu.SemaphoreType.DMA((3,)),
            pltpu.SemaphoreType.DMA((features // LANE,)),
        ],
        compiler_params=params(),
        name="send_blocks",
    )(in_hbm(owner), in_hbm(up), in_hbm(down_t), in_hbm(pixels))
    return blocks, pack


def exchange(blocks):
    arrived = dict(zip(ORDER, blocks))
    for distance in ORDER[1:-2]:
        arrived[distance] = swap(arrived[distance], "band", distance)
    for distance, before in zip(ORDER[-2:], (1, 2)):
        block, arrived[before] = lax.optimization_barrier((arrived[distance], arrived[before]))
        arrived[distance] = swap(block, "band", distance)
    return [arrived[distance] for distance in ORDER]


def expand_table(table, rows, half_width_padded, half_width, flip, transpose):
    position = iota2((rows, WLAT * WLON), 0)
    line, col = jnp.bitwise_xor(position // half_width_padded, flip), position % half_width_padded
    target = iota2((rows, WLAT * WLON), 1)
    pick = jnp.where((target == line * WLON + col % WLON) & (col < half_width), 1.0, 0.0).astype(BF16)
    left = (dot_nt if transpose else dot_nn)(pick, table).astype(BF16)
    full = dot_nt(left, pick)
    row_window = (iota2((rows, 1), 0) % half_width_padded) // WLON
    col_window = (iota2((1, rows), 1) % half_width_padded) // WLON
    return jnp.where(row_window == col_window, full, 0.0).astype(BF16)


def prep_kernel(
    direct,
    row_share,
    half_width,
    half_width_padded,
    group_hbm_ref,
    level_hbm_ref,
    grad_hbm_ref,
    frozen_ref,
    factors_ref,
    mixer_ref,
    merged_ref,
    up_ref,
    down_ref,
    mix_ref,
    mix_t_ref,
    level_ref,
    grad_ref,
    group_ref,
    sems,
):
    pairs = [(group_hbm_ref, group_ref), (level_hbm_ref, level_ref)]
    flip = lax.axis_index("band") if direct else 0
    if direct:
        pairs += [
            (grad_hbm_ref.at[:, jnp.bitwise_xor(flip, line)], grad_ref.at[:, line]) for line in range(WLAT)
        ]
    else:
        pairs.append((grad_hbm_ref, grad_ref))
    loads = [
        pltpu.make_async_copy(source, target, sems.at[n]) for n, (source, target) in enumerate(pairs)
    ]
    for load in loads:
        load.start()
    rows = mix_ref.shape[0]
    mix_ref[...] = expand_table(mixer_ref[...], rows, half_width_padded, half_width, flip, False)
    mix_t_ref[...] = expand_table(mixer_ref[...], rows, half_width_padded, half_width, flip, True)
    reps, _, rank, share = factors_ref.shape
    levels = level_ref.shape[0]
    variables = group_ref.shape[0]
    channels = variables * frozen_ref.shape[1]
    up = jnp.concatenate([factors_ref[r, 0] for r in range(reps)], axis=1)
    source, target = iota2((share, channels), 0), iota2((share, channels), 1)
    down_t = jnp.zeros((rank, channels), F32)
    for r in range(reps):
        place = jnp.where((target == source + r * row_share) & (source < row_share), 1.0, 0.0)
        down_t = down_t + dot_nn(factors_ref[r, 1], place.astype(BF16))
    down_t = down_t.astype(BF16)
    down_ref[...] = down_t
    loads[0].wait()
    base = jnp.concatenate([frozen_ref[group_ref[v]].astype(F32) for v in range(variables)], axis=0)
    merged = (base + dot_tn(down_t, up)).astype(BF16)
    stacked = jnp.concatenate([merged, up], axis=0)
    merged_ref[...] = jnp.zeros_like(merged_ref)
    loads[1].wait()
    for level in range(levels):
        through = dot_nn(stacked, level_ref[level])
        weights = through[:channels].astype(BF16)
        for s in range(merged_ref.shape[0]):
            offset = (s * levels * channels) % LANE + level * channels
            merged_ref[s, offset : offset + channels, :] = weights
        up_high, up_low = split_hi_lo(through[channels:])
        up_ref[level, :rank, :] = up_high
        up_ref[level, rank:, :] = up_low
    for load in loads[2:]:
        load.wait()


def prepare(direct, groups, frozen, factors, level_weight, mixer, grad, row_share, half_width, half_width_padded):
    reps, _, rank, _ = factors.shape
    levels, feature_dim, _ = level_weight.shape
    channels = groups.shape[0] * frozen.shape[1]
    reach = round_up(levels * channels + LANE // 2, LANE)
    rows = WLAT * half_width_padded
    vmem = pl.BlockSpec(memory_space=pltpu.VMEM)
    flops = 2 * levels * (channels + rank) * feature_dim * feature_dim + 4 * rows * rows * WLAT * WLON
    shapes = [
        (grad.shape[0], reach, feature_dim),
        (levels, 2 * rank, feature_dim),
        (rank, channels),
        (rows, rows),
        (rows, rows),
        level_weight.shape,
        grad.shape,
    ]
    return pl.pallas_call(
        functools.partial(prep_kernel, direct, row_share, half_width, half_width_padded),
        out_shape=[jax.ShapeDtypeStruct(shape, BF16) for shape in shapes],
        in_specs=[pl.BlockSpec(memory_space=pl.ANY)] * 3 + [vmem] * 3,
        out_specs=[vmem] * len(shapes),
        scratch_shapes=[pltpu.SMEM(groups.shape, jnp.int32), pltpu.SemaphoreType.DMA((2 + WLAT,))],
        compiler_params=params(),
        cost_estimate=pl.CostEstimate(flops=flops, bytes_accessed=6 * 2**20, transcendentals=0),
        name="prepare",
    )(in_hbm(groups), in_hbm(level_weight), in_hbm(grad), in_hbm(frozen), factors, in_hbm(mixer))


def normal_parts(values):
    cdf = 0.5 + 0.5 * lax.erf(values * 0.7071067811865476)
    return cdf, 0.3989422804014327 * jnp.exp2(values * values * -0.7213475204444817)


def factor_shares(total, up_ref, down_ref, level_ref):
    levels, two_rank, feature_dim = up_ref.shape
    rank, channels = down_ref.shape
    high, low = split_hi_lo(total)
    down = down_ref[...]
    first = jnp.zeros((rank, channels), F32)
    second = jnp.zeros((two_rank, feature_dim), F32)
    for level in range(levels):
        at = slice(level * channels, (level + 1) * channels)
        both = dot_nt(up_ref[level], high[at])
        first = first + both[:rank] + both[rank:] + dot_nt(up_ref[level, :rank, :], low[at])
        through = dot_nn(down, high[at]) + dot_nn(down, low[at])
        through = jnp.concatenate(split_hi_lo(through), axis=0)
        second = second + dot_nt(through, level_ref[level])
    return first, second[:rank] + second[rank:]


def mix_kernel(
    direct,
    piece_refs,
    merged_ref,
    mix_ref,
    mix_t_ref,
    up_ref,
    down_ref,
    grad_ref,
    level_ref,
    mixed_hbm_ref,
    share_ref,
    turned_refs,
    mixed_refs,
    pre_refs,
    tokens_refs,
    grad_pre_refs,
    grad_tokens_refs,
    total_ref,
    mixed_sems,
):
    samples, reach, feature_dim = merged_ref.shape
    chunk_count, (_, width, _) = len(mixed_refs), mixed_refs[0].shape
    depth = piece_refs[0].shape[-1] // samples
    rows = WLAT * width

    group_rows = mix_ref.shape[0]
    group = group_rows // WLAT
    groups = [
        (slice(start, start + group), slice(start * WLAT, start * WLAT + group_rows))
        for start in range(0, width, group)
    ]
    pair = 1 if group % SUB == 0 else 2

    def lines_of(n):
        return pl.ds(n // samples * WLAT, WLAT)

    if direct:
        me = lax.axis_index("band")
        targets = [
            (mixed_refs[n].at[line], mixed_hbm_ref.at[n, jnp.bitwise_xor(me, line)])
            for n in range(chunk_count)
            for line in range(WLAT)
        ]
    else:
        targets = [
            (mixed_refs[n], mixed_hbm_ref.at[n % samples, lines_of(n)]) for n in range(chunk_count)
        ]
    stores = [
        pltpu.make_async_copy(source, target, mixed_sems.at[n]) for n, (source, target) in enumerate(targets)
    ]

    def pixels_of(n, lanes):
        if direct:
            by_distance = dict(zip(ORDER, piece_refs))
            return jnp.concatenate([by_distance[line][:, lanes] for line in range(WLAT)], axis=0)
        return piece_refs[0][lines_of(n), :, lanes].reshape(rows, lanes.stop - lanes.start)

    def turn(n):
        def part(lanes):
            turned_refs[n // samples][lanes, :] = pixels_of(n, lanes).T

        starts = range(0, samples * depth, LANE)
        return [functools.partial(part, slice(start, start + LANE)) for start in starts]

    def forward(n, columns):
        s = n % samples
        lane = s * depth // LANE * LANE

        def embed():
            pixels = pixels_of(n, slice(lane, lane + reach))
            tokens = dot_nn(pixels, merged_ref[s, :, columns]).reshape(WLAT, width, COLUMNS)
            for within, at in groups:
                tokens_refs[n][at, columns] = tokens[:, within].reshape(group_rows, COLUMNS).astype(BF16)

        def mixing():
            for _, at in groups:
                pre_refs[n][at, columns] = dot_nn(mix_ref[...], tokens_refs[n][at, columns])

        return [embed, mixing]

    def pointwise(n, columns):
        s, first_line = n % samples, n // samples * WLAT

        def part(line, across, lanes):
            grads = [grad_ref[s, first_line + line + k, across, lanes].astype(F32) for k in range(pair)]
            mixed = []
            for within, at in groups:
                if within.start < across.start or within.stop > across.stop:
                    continue
                at = pl.ds(at.start + line * group, pair * group)
                pre = pre_refs[n][at, lanes]
                cdf, pdf = normal_parts(pre)
                mixed.append(tokens_refs[n][at, lanes].astype(F32) + pre * cdf)
                first = within.start - across.start
                grad = jnp.concatenate([values[first : first + group] for values in grads], axis=0)
                grad_pre_refs[n][at, lanes] = (grad * (cdf + pre * pdf)).astype(BF16)
            for k in range(pair):
                parts = [values[k * group : (k + 1) * group] for values in mixed]
                mixed_refs[n][line + k, across, lanes] = jnp.concatenate(parts, axis=0).astype(BF16)

        return [
            functools.partial(part, line, slice(across, across + pair * group), slice(start, start + LANE))
            for line in range(0, WLAT, pair)
            for across in range(0, width, pair * group)
            for start in range(columns.start, columns.stop, LANE)
        ]

    def backward(n, columns):
        def spread():
            direct_part = grad_ref[n % samples, lines_of(n), :, columns].astype(F32)
            through = [
                dot_nn(mix_t_ref[...], grad_pre_refs[n][at, columns]).reshape(WLAT, group, COLUMNS)
                for _, at in groups
            ]
            total = jnp.concatenate(through, axis=1) + direct_part
            grad_tokens_refs[n][:, columns] = total.reshape(rows, COLUMNS).astype(BF16)

        def share():
            s = n % samples
            turned = turned_refs[n // samples][s * depth : (s + 1) * depth, :]
            part = dot_nn(turned, grad_tokens_refs[n][:, columns])
            total_ref[:, columns] = part if n == 0 else total_ref[:, columns] + part

        return [spread, share]

    units = [
        (n, slice(start, start + COLUMNS))
        for n in range(chunk_count)
        for start in range(0, feature_dim, COLUMNS)
    ]
    for step in forward(*units[0]):
        step()
    for i, unit in enumerate(units):
        n, columns = unit
        others = []
        if i + 1 < len(units):
            others += forward(*units[i + 1])
        if columns.start == 0 and n % samples == 0:
            others += turn(n)
        if i > 0:
            others += backward(*units[i - 1])
        lines = pointwise(*unit)
        for line, vector_step in enumerate(lines):
            vector_step()
            for step in others[line * len(others) // len(lines) : (line + 1) * len(others) // len(lines)]:
                step()
        if columns.stop == feature_dim:
            each = len(stores) // chunk_count
            for store in stores[n * each : (n + 1) * each]:
                store.start()
    for step in backward(*units[-1]):
        step()

    first, second = factor_shares(total_ref[...], up_ref, down_ref, level_ref)
    rank, channels = down_ref.shape
    columns = share_ref.shape[2]
    reps = feature_dim // columns
    folds = rank // (share_ref.shape[1] - rank)
    depth_rows, fold_lanes, row_share = rank // folds, columns // folds, channels // reps
    packed = jnp.zeros((depth_rows, feature_dim), F32)
    row, lane = iota2((channels, feature_dim), 0), iota2((1, feature_dim), 1)
    rep, lane = lane // columns, lane % columns
    for fold in range(folds):
        inside = lane - fold * fold_lanes
        target = jnp.where((inside >= 0) & (inside < row_share), inside + rep * row_share, -1)
        pick = jnp.where(row == target, 1.0, 0.0).astype(BF16)
        part = first[fold * depth_rows : (fold + 1) * depth_rows].astype(BF16)
        packed = packed + dot_nn(part, pick)
    payload = jnp.concatenate([second, packed], axis=0).astype(BF16)
    for slot in range(share_ref.shape[0]):
        at = slot % reps * columns
        share_ref[slot] = payload[:, at : at + columns]
    for store in stores:
        store.wait()


def mix_blocks(direct, arrived, merged, mix, mix_t, grad, up_through, down_t, level_weight, band_count, reps):
    samples, lat_rows, block_width, feature_dim = grad.shape
    width = block_width
    lanes = arrived[0].shape[-1]
    reach = merged.shape[1]
    rows = WLAT * width
    rank = down_t.shape[0]
    chunks = lat_rows // WLAT * samples
    share_shape = (band_count * reps, rank + rank // FOLDS, feature_dim // reps)
    flops = 2 * samples * lat_rows * block_width * feature_dim * (2 * reach + 2 * rows)
    vmem = pl.BlockSpec(memory_space=pltpu.VMEM)
    any_space = pl.BlockSpec(memory_space=pl.ANY)
    local = [*arrived, merged, mix, mix_t, up_through, down_t]
    return pl.pallas_call(
        lambda *refs: mix_kernel(direct, refs[: len(arrived)], *refs[len(arrived) :]),
        out_shape=[
            jax.ShapeDtypeStruct(grad.shape, BF16),
            jax.ShapeDtypeStruct(share_shape, BF16),
        ],
        in_specs=[vmem] * (len(local) + 2),
        out_specs=[any_space, vmem],
        scratch_shapes=[
            [pltpu.VMEM((lanes, rows), BF16)] * (chunks // samples),
            [pltpu.VMEM((WLAT, width, feature_dim), BF16)] * chunks,
            [pltpu.VMEM((rows, feature_dim), F32)] * chunks,
            [pltpu.VMEM((rows, feature_dim), BF16)] * chunks,
            [pltpu.VMEM((rows, feature_dim), BF16)] * chunks,
            [pltpu.VMEM((rows, feature_dim), BF16)] * chunks,
            pltpu.VMEM((lanes // samples, feature_dim), F32),
            pltpu.SemaphoreType.DMA((chunks * WLAT,)),
        ],
        compiler_params=params(),
        cost_estimate=pl.CostEstimate(
            flops=flops,
            bytes_accessed=12 * 2**20,
            transcendentals=samples * lat_rows * block_width * feature_dim,
        ),
        name="mix_blocks",
    )(*local, grad, level_weight)


def sum_kernel(parts_ref, first_ref, second_ref):
    rank, row_share = first_ref.shape
    total = parts_ref[0].astype(F32)
    for n in range(1, parts_ref.shape[0]):
        total = total + parts_ref[n].astype(F32)
    second_ref[...] = total[:rank]
    depth_rows = total.shape[0] - rank
    for fold in range(rank // depth_rows):
        lane = fold * depth_rows * total.shape[1] // rank
        first_ref[fold * depth_rows : (fold + 1) * depth_rows, :] = total[rank:, lane : lane + row_share]


def sum_shares(shares, rank, row_share):
    parts = lax.all_to_all(shares, ("band", "rep"), split_axis=0, concat_axis=0, tiled=True)
    return pl.pallas_call(
        sum_kernel,
        out_shape=[
            jax.ShapeDtypeStruct((rank, row_share), F32),
            jax.ShapeDtypeStruct((rank, shares.shape[2]), F32),
        ],
        compiler_params=params(),
        name="sum_shares",
    )(parts)


def on_device(
    patches,
    variable_group_index,
    frozen_patch_weight,
    adapter_down,
    adapter_up,
    level_merge_weight,
    window_patch_mixer,
    column_block_owner,
    mixed_token_gradient,
):
    band_count, reps = lax.axis_size("band"), lax.axis_size("rep")
    samples, levels, channels, row_count, col_count = patches.shape
    feature_dim = frozen_patch_weight.shape[2]
    rank, col_share = adapter_up.shape
    row_share = adapter_down.shape[0]
    lat_rows = band_count * row_count
    block_width = col_count // band_count
    padded_width = round_up(block_width, SUB)
    group = 2 * WLON if block_width % (2 * WLON) == 0 else padded_width
    features = samples * levels * channels

    pixels = patches.reshape(features, col_count)
    pack_shape = (2, rank, round_up(max(row_share, col_share), LANE))
    direct = band_count == BANDS and lat_rows == WLAT and padded_width == block_width
    direct = direct and features % LANE == 0 and col_count % LANE == 0
    if direct:
        blocks, pack = send_blocks(
            pixels, column_block_owner, adapter_up, adapter_down.T, block_width, pack_shape
        )
        arrived = exchange(blocks)
    else:
        block_ids = jnp.arange(band_count, dtype=jnp.int32)
        inverse = jnp.sum(
            jnp.where(column_block_owner[None, :] == block_ids[:, None], block_ids[None, :], 0), axis=1
        )
        outgoing = jnp.take(pixels.T.reshape(band_count, block_width, features), inverse, axis=0)
        outgoing = jnp.pad(outgoing, ((0, 0), (0, padded_width - block_width), (0, 0)))
        arrived = [lax.all_to_all(outgoing, "band", split_axis=0, concat_axis=0, tiled=True)]
        pack = jnp.stack(
            [
                jnp.pad(array, ((0, 0), (0, pack_shape[2] - array.shape[1])))
                for array in (adapter_up, adapter_down.T)
            ]
        )
    factors = lax.all_gather(pack, "rep", axis=0, tiled=False)

    grad = mixed_token_gradient.reshape(samples, lat_rows, block_width, feature_dim)
    if padded_width != block_width:
        grad = jnp.pad(grad, ((0, 0), (0, 0), (0, padded_width - block_width), (0, 0)))
    merged, up_through, down_t, mix, mix_t, level_copy, grad_copy = prepare(
        direct,
        variable_group_index,
        frozen_patch_weight,
        factors,
        level_merge_weight,
        window_patch_mixer,
        grad,
        row_share,
        min(block_width, group),
        group,
    )
    mixed, shares = mix_blocks(
        direct, arrived, merged, mix, mix_t, grad_copy, up_through, down_t, level_copy, band_count, reps
    )
    if padded_width != block_width:
        mixed = mixed[:, :, :block_width]
    first_t, second = sum_shares(shares, rank, row_share)
    return mixed.reshape(mixed_token_gradient.shape), first_t.T, second


def solution(mesh):
    in_specs = (
        P("rep", None, None, "band", None),
        P(),
        P(),
        P("rep", None),
        P(None, "rep"),
        P(),
        P(),
        P(),
        P("rep", "band", None, None, None),
    )
    out_specs = (P("rep", "band", None, None, None), P("rep", None), P(None, "rep"))
    return jax.shard_map(
        on_device, mesh=mesh, in_specs=in_specs, out_specs=out_specs, check_vma=False
    )
```

```python
import functools

import jax
import jax.numpy as jnp
from jax import lax
from jax.experimental import pallas as pl
from jax.experimental.pallas import tpu as pltpu
from jax.sharding import PartitionSpec as P

WLAT = 8
WLON = 12
LANE = 128
SUB = 16
VMEM_LIMIT = 24 * 1024 * 1024
BANDS = 8
ORDER = (0, 4, 1, 5, 2, 6, 7, 3)
EARLY = 6
FOLDS = 2
COLUMNS = 256
BF16 = jnp.bfloat16
F32 = jnp.float32


def round_up(value, step):
    return -(-value // step) * step


def dot_nn(a, b):
    return lax.dot_general(a, b, (((1,), (0,)), ((), ())), preferred_element_type=F32)


def dot_nt(a, b):
    return lax.dot_general(a, b, (((1,), (1,)), ((), ())), preferred_element_type=F32)


def dot_tn(a, b):
    return lax.dot_general(a, b, (((0,), (0,)), ((), ())), preferred_element_type=F32)


def split_hi_lo(values):
    high = values.astype(BF16)
    low = (values - high.astype(F32)).astype(BF16)
    return high, low


def iota2(shape, axis):
    return lax.broadcasted_iota(jnp.int32, shape, axis)


def params(**extra):
    return pltpu.CompilerParams(vmem_limit_bytes=VMEM_LIMIT, **extra)


def in_hbm(values):
    return pltpu.with_memory_space_constraint(values, pltpu.HBM)


def swap(values, axis, distance):
    count = lax.axis_size(axis)
    return lax.ppermute(values, axis, [(source, source ^ distance) for source in range(count)])


def send_kernel(owner_hbm_ref, up_hbm_ref, down_hbm_ref, x_hbm_ref, *refs):
    block_refs, pack_ref, scratch = refs[:-8], refs[-8], refs[-7:]
    owner_ref, up_ref, down_ref, x_ref, turned_ref, small_sems, x_sems = scratch
    width = block_refs[0].shape[0]
    features, columns = x_ref.shape
    small = [
        pltpu.make_async_copy(source, target, small_sems.at[n])
        for n, (source, target) in enumerate(
            [(owner_hbm_ref, owner_ref), (up_hbm_ref, up_ref), (down_hbm_ref, down_ref)]
        )
    ]
    parts = [slice(start, start + LANE) for start in range(0, features, LANE)]
    large = [
        pltpu.make_async_copy(x_hbm_ref.at[part, :], x_ref.at[part, :], x_sems.at[n])
        for n, part in enumerate(parts)
    ]
    for copy in large + small:
        copy.start()
    for copy, part in zip(large, parts):
        copy.wait()
        for start in range(0, columns, LANE):
            at = slice(start, start + LANE)
            turned_ref[at, part] = x_ref[part, at].T
    for copy in small:
        copy.wait()
    pack_ref[...] = jnp.zeros_like(pack_ref)
    pack_ref[0, :, : up_ref.shape[1]] = up_ref[...]
    pack_ref[1, :, : down_ref.shape[1]] = down_ref[...]
    me = lax.axis_index("band")
    for distance, block_ref in zip(ORDER, block_refs):
        target = jnp.bitwise_xor(me, distance)
        block = 0
        for j in range(1, owner_ref.shape[0]):
            block = jnp.where(owner_ref[j] == target, j, block)
        block_ref[...] = turned_ref[pl.ds(pl.multiple_of(block * width, SUB), width), :]


def send_blocks(pixels, owner, up, down_t, width, pack_shape):
    features, columns = pixels.shape
    any_space = pl.BlockSpec(memory_space=pl.ANY)
    vmem = pl.BlockSpec(memory_space=pltpu.VMEM)
    blocks = [(width, features)] * BANDS
    *blocks, pack = pl.pallas_call(
        send_kernel,
        out_shape=[jax.ShapeDtypeStruct(shape, BF16) for shape in [*blocks, pack_shape]],
        in_specs=[any_space] * 4,
        out_specs=[vmem] * (len(blocks) + 1),
        scratch_shapes=[
            pltpu.SMEM(owner.shape, jnp.int32),
            pltpu.VMEM(up.shape, BF16),
            pltpu.VMEM(down_t.shape, BF16),
            pltpu.VMEM((features, columns), BF16),
            pltpu.VMEM((columns, features), BF16),
            pltpu.SemaphoreType.DMA((3,)),
            pltpu.SemaphoreType.DMA((features // LANE,)),
        ],
        compiler_params=params(),
        name="send_blocks",
    )(in_hbm(owner), in_hbm(up), in_hbm(down_t), in_hbm(pixels))
    return blocks, pack


def exchange(blocks):
    arrived = dict(zip(ORDER, blocks))
    for distance in ORDER[1:-2]:
        arrived[distance] = swap(arrived[distance], "band", distance)
    for distance, before in zip(ORDER[-2:], (1, 2)):
        block, arrived[before] = lax.optimization_barrier((arrived[distance], arrived[before]))
        arrived[distance] = swap(block, "band", distance)
    return [arrived[distance] for distance in range(BANDS)]


def expand_table(table, rows, half_width_padded, half_width, flip, transpose):
    position = iota2((rows, WLAT * WLON), 0)
    line, col = jnp.bitwise_xor(position // half_width_padded, flip), position % half_width_padded
    target = iota2((rows, WLAT * WLON), 1)
    pick = jnp.where((target == line * WLON + col % WLON) & (col < half_width), 1.0, 0.0).astype(BF16)
    left = (dot_nt if transpose else dot_nn)(pick, table).astype(BF16)
    full = dot_nt(left, pick)
    row_window = (iota2((rows, 1), 0) % half_width_padded) // WLON
    col_window = (iota2((1, rows), 1) % half_width_padded) // WLON
    return jnp.where(row_window == col_window, full, 0.0).astype(BF16)


def prep_kernel(
    direct,
    row_share,
    half_width,
    half_width_padded,
    group_hbm_ref,
    level_hbm_ref,
    grad_hbm_ref,
    frozen_ref,
    factors_ref,
    mixer_ref,
    merged_ref,
    up_ref,
    down_ref,
    mix_ref,
    mix_t_ref,
    level_ref,
    grad_ref,
    group_ref,
    sems,
):
    pairs = [(group_hbm_ref, group_ref), (level_hbm_ref, level_ref)]
    flip = lax.axis_index("band") if direct else 0
    if direct:
        pairs += [
            (grad_hbm_ref.at[:, jnp.bitwise_xor(flip, line)], grad_ref.at[:, line]) for line in range(WLAT)
        ]
    else:
        pairs.append((grad_hbm_ref, grad_ref))
    loads = [
        pltpu.make_async_copy(source, target, sems.at[n]) for n, (source, target) in enumerate(pairs)
    ]
    for load in loads:
        load.start()
    rows = mix_ref.shape[0]
    mix_ref[...] = expand_table(mixer_ref[...], rows, half_width_padded, half_width, flip, False)
    mix_t_ref[...] = expand_table(mixer_ref[...], rows, half_width_padded, half_width, flip, True)
    reps, _, rank, share = factors_ref.shape
    levels = level_ref.shape[0]
    variables = group_ref.shape[0]
    channels = variables * frozen_ref.shape[1]
    up = jnp.concatenate([factors_ref[r, 0] for r in range(reps)], axis=1)
    source, target = iota2((share, channels), 0), iota2((share, channels), 1)
    down_t = jnp.zeros((rank, channels), F32)
    for r in range(reps):
        place = jnp.where((target == source + r * row_share) & (source < row_share), 1.0, 0.0)
        down_t = down_t + dot_nn(factors_ref[r, 1], place.astype(BF16))
    down_t = down_t.astype(BF16)
    down_ref[...] = down_t
    loads[0].wait()
    base = jnp.concatenate([frozen_ref[group_ref[v]].astype(F32) for v in range(variables)], axis=0)
    merged = (base + dot_tn(down_t, up)).astype(BF16)
    stacked = jnp.concatenate([merged, up], axis=0)
    merged_ref[...] = jnp.zeros_like(merged_ref)
    loads[1].wait()
    for level in range(levels):
        through = dot_nn(stacked, level_ref[level])
        weights = through[:channels].astype(BF16)
        for s in range(merged_ref.shape[0]):
            offset = (s * levels * channels) % LANE + level * channels
            merged_ref[s, offset : offset + channels, :] = weights
        up_high, up_low = split_hi_lo(through[channels:])
        up_ref[level, :rank, :] = up_high
        up_ref[level, rank:, :] = up_low
    for load in loads[2:]:
        load.wait()


def prepare(direct, groups, frozen, factors, level_weight, mixer, grad, row_share, half_width, half_width_padded):
    reps, _, rank, _ = factors.shape
    levels, feature_dim, _ = level_weight.shape
    channels = groups.shape[0] * frozen.shape[1]
    reach = round_up(levels * channels + LANE // 2, LANE)
    rows = WLAT * half_width_padded
    vmem = pl.BlockSpec(memory_space=pltpu.VMEM)
    flops = 2 * levels * (channels + rank) * feature_dim * feature_dim + 4 * rows * rows * WLAT * WLON
    shapes = [
        (grad.shape[0], reach, feature_dim),
        (levels, 2 * rank, feature_dim),
        (rank, channels),
        (rows, rows),
        (rows, rows),
        level_weight.shape,
        grad.shape,
    ]
    return pl.pallas_call(
        functools.partial(prep_kernel, direct, row_share, half_width, half_width_padded),
        out_shape=[jax.ShapeDtypeStruct(shape, BF16) for shape in shapes],
        in_specs=[pl.BlockSpec(memory_space=pl.ANY)] * 3 + [vmem] * 3,
        out_specs=[vmem] * len(shapes),
        scratch_shapes=[pltpu.SMEM(groups.shape, jnp.int32), pltpu.SemaphoreType.DMA((2 + WLAT,))],
        compiler_params=params(),
        cost_estimate=pl.CostEstimate(flops=flops, bytes_accessed=6 * 2**20, transcendentals=0),
        name="prepare",
    )(in_hbm(groups), in_hbm(level_weight), in_hbm(grad), in_hbm(frozen), factors, in_hbm(mixer))


def normal_parts(values):
    cdf = 0.5 + 0.5 * lax.erf(values * 0.7071067811865476)
    return cdf, 0.3989422804014327 * jnp.exp2(values * values * -0.7213475204444817)


def factor_shares(total, up_ref, down_ref, level_ref):
    levels, two_rank, feature_dim = up_ref.shape
    rank, channels = down_ref.shape
    high, low = split_hi_lo(total)
    down = down_ref[...]
    first = jnp.zeros((rank, channels), F32)
    second = jnp.zeros((two_rank, feature_dim), F32)
    for level in range(levels):
        at = slice(level * channels, (level + 1) * channels)
        both = dot_nt(up_ref[level], high[at])
        first = first + both[:rank] + both[rank:] + dot_nt(up_ref[level, :rank, :], low[at])
        through = dot_nn(down, high[at]) + dot_nn(down, low[at])
        through = jnp.concatenate(split_hi_lo(through), axis=0)
        second = second + dot_nt(through, level_ref[level])
    return first, second[:rank] + second[rank:]


def turned_whole(lines, width):
    return lines * width // LANE * LANE


def embed_kernel(*refs):
    piece_refs, (merged_ref, tokens_ref, turned_ref) = refs[:-3], refs[-3:]
    samples, reach, feature_dim = merged_ref.shape
    width, features = piece_refs[0].shape
    depth = features // samples
    group = 2 * WLON
    rows = len(piece_refs) * group
    positions = turned_ref.shape[1]
    for s in range(samples):
        lane = s * depth // LANE * LANE
        pixels = jnp.concatenate([piece_ref[:, lane : lane + reach] for piece_ref in piece_refs], axis=0)
        for start in range(0, feature_dim, COLUMNS):
            columns = slice(start, start + COLUMNS)
            tokens = dot_nn(pixels, merged_ref[s, :, columns]).reshape(len(piece_refs), width, COLUMNS)
            for n in range(width // group):
                part = tokens[:, n * group : (n + 1) * group].reshape(rows, COLUMNS)
                tokens_ref[s, n * rows : (n + 1) * rows, columns] = part.astype(BF16)
    for start in range(0, features, LANE):
        lanes = slice(start, start + LANE)
        pixels = jnp.concatenate([piece_ref[:, lanes] for piece_ref in piece_refs], axis=0)
        turned_ref[lanes, :] = pixels[:positions].T


def embed_early(pieces, merged):
    samples, _, feature_dim = merged.shape
    width, features = pieces[0].shape
    count = len(pieces) * width
    return pl.pallas_call(
        embed_kernel,
        out_shape=[
            jax.ShapeDtypeStruct((samples, count, feature_dim), BF16),
            jax.ShapeDtypeStruct((features, turned_whole(len(pieces), width)), BF16),
        ],
        in_specs=[pl.BlockSpec(memory_space=pltpu.VMEM)] * (len(pieces) + 1),
        out_specs=[pl.BlockSpec(memory_space=pltpu.VMEM)] * 2,
        compiler_params=params(),
        cost_estimate=pl.CostEstimate(
            flops=2 * count * features * feature_dim, bytes_accessed=4 * 2**20, transcendentals=0
        ),
        name="embed_early",
    )(*pieces, merged)


def mix_kernel(
    direct,
    piece_refs,
    merged_ref,
    mix_ref,
    mix_t_ref,
    up_ref,
    down_ref,
    grad_ref,
    level_ref,
    mixed_hbm_ref,
    share_ref,
    turned_refs,
    mixed_refs,
    pre_refs,
    tokens_refs,
    grad_pre_refs,
    grad_tokens_refs,
    total_ref,
    mixed_sems,
):
    samples, reach, feature_dim = merged_ref.shape
    chunk_count, (_, width, _) = len(mixed_refs), mixed_refs[0].shape
    depth = piece_refs[0].shape[-1] // samples
    rows = WLAT * width

    group_rows = mix_ref.shape[0]
    group = group_rows // WLAT
    groups = [
        (slice(start, start + group), slice(start * WLAT, start * WLAT + group_rows))
        for start in range(0, width, group)
    ]
    pair = 1 if group % SUB == 0 else 2

    early = EARLY if direct else 0
    early_rows, late_rows = early * group, (WLAT - early) * group
    if direct:
        *line_refs, early_tokens_ref, early_turned_ref = piece_refs
        early_positions = early_turned_ref.shape[1]

    def lines_of(n):
        return pl.ds(n // samples * WLAT, WLAT)

    if direct:
        me = lax.axis_index("band")
        targets = [
            (mixed_refs[n].at[line], mixed_hbm_ref.at[n, jnp.bitwise_xor(me, line)])
            for n in range(chunk_count)
            for line in range(WLAT)
        ]
    else:
        targets = [
            (mixed_refs[n], mixed_hbm_ref.at[n % samples, lines_of(n)]) for n in range(chunk_count)
        ]
    stores = [
        pltpu.make_async_copy(source, target, mixed_sems.at[n]) for n, (source, target) in enumerate(targets)
    ]

    def pixels_of(n, lanes):
        if direct:
            return jnp.concatenate([line_ref[:, lanes] for line_ref in line_refs], axis=0)
        return piece_refs[0][lines_of(n), :, lanes].reshape(rows, lanes.stop - lanes.start)

    def turn(n):
        def part(lanes):
            pixels = pixels_of(n, lanes)
            if direct:
                before = early_positions - (early - 1) * width
                pixels = pixels[before:]
            turned_refs[n // samples][lanes, :] = pixels.T

        starts = range(0, samples * depth, LANE)
        return [functools.partial(part, slice(start, start + LANE)) for start in starts]

    def tokens_at(n, block, line, count, columns):
        if line < early:
            at = pl.ds(block * early_rows + line * group, count * group)
            return early_tokens_ref[n % samples, at, columns]
        return tokens_refs[n][pl.ds(block * late_rows + (line - early) * group, count * group), columns]

    def forward(n, columns):
        s = n % samples
        lane = s * depth // LANE * LANE

        def embed():
            pixels = pixels_of(n, slice(lane, lane + reach))
            if direct:
                pixels = pixels[width:]
            tokens = dot_nn(pixels, merged_ref[s, :, columns]).reshape(WLAT - early, width, COLUMNS)
            for block, (within, _) in enumerate(groups):
                part = tokens[:, within].reshape(late_rows, COLUMNS).astype(BF16)
                tokens_refs[n][block * late_rows : (block + 1) * late_rows, columns] = part

        def mixing():
            for block, (_, at) in enumerate(groups):
                tokens = tokens_at(n, block, early, WLAT - early, columns)
                if direct:
                    tokens = jnp.concatenate([tokens_at(n, block, 0, early, columns), tokens], axis=0)
                pre_refs[n][at, columns] = dot_nn(mix_ref[...], tokens)

        return [embed, mixing]

    def pointwise(n, columns):
        s, first_line = n % samples, n // samples * WLAT

        def part(line, across, lanes):
            grads = [grad_ref[s, first_line + line + k, across, lanes].astype(F32) for k in range(pair)]
            mixed = []
            for block, (within, at) in enumerate(groups):
                if within.start < across.start or within.stop > across.stop:
                    continue
                at = pl.ds(at.start + line * group, pair * group)
                pre = pre_refs[n][at, lanes]
                cdf, pdf = normal_parts(pre)
                mixed.append(tokens_at(n, block, line, pair, lanes).astype(F32) + pre * cdf)
                first = within.start - across.start
                grad = jnp.concatenate([values[first : first + group] for values in grads], axis=0)
                grad_pre_refs[n][at, lanes] = (grad * (cdf + pre * pdf)).astype(BF16)
            for k in range(pair):
                parts = [values[k * group : (k + 1) * group] for values in mixed]
                mixed_refs[n][line + k, across, lanes] = jnp.concatenate(parts, axis=0).astype(BF16)

        return [
            functools.partial(part, line, slice(across, across + pair * group), slice(start, start + LANE))
            for line in range(0, WLAT, pair)
            for across in range(0, width, pair * group)
            for start in range(columns.start, columns.stop, LANE)
        ]

    def backward(n, columns):
        def spread():
            direct_part = grad_ref[n % samples, lines_of(n), :, columns].astype(F32)
            through = [
                dot_nn(mix_t_ref[...], grad_pre_refs[n][at, columns]).reshape(WLAT, group, COLUMNS)
                for _, at in groups
            ]
            total = jnp.concatenate(through, axis=1) + direct_part
            grad_tokens_refs[n][:, columns] = total.reshape(rows, COLUMNS).astype(BF16)

        def share():
            s = n % samples
            features = slice(s * depth, (s + 1) * depth)
            late = rows - turned_refs[0].shape[1]
            part = dot_nn(turned_refs[n // samples][features, :], grad_tokens_refs[n][late:, columns])
            if direct:
                part = part + dot_nn(early_turned_ref[features, :], grad_tokens_refs[n][:late, columns])
            total_ref[:, columns] = part if n == 0 else total_ref[:, columns] + part

        return [spread, share]

    units = [
        (n, slice(start, start + COLUMNS))
        for n in range(chunk_count)
        for start in range(0, feature_dim, COLUMNS)
    ]
    for step in forward(*units[0]):
        step()
    for i, unit in enumerate(units):
        n, columns = unit
        others = []
        if i + 1 < len(units):
            others += forward(*units[i + 1])
        if columns.start == 0 and n % samples == 0:
            others += turn(n)
        if i > 0:
            others += backward(*units[i - 1])
        lines = pointwise(*unit)
        for line, vector_step in enumerate(lines):
            vector_step()
            for step in others[line * len(others) // len(lines) : (line + 1) * len(others) // len(lines)]:
                step()
        if columns.stop == feature_dim:
            each = len(stores) // chunk_count
            for store in stores[n * each : (n + 1) * each]:
                store.start()
    for step in backward(*units[-1]):
        step()

    first, second = factor_shares(total_ref[...], up_ref, down_ref, level_ref)
    rank, channels = down_ref.shape
    columns = share_ref.shape[2]
    reps = feature_dim // columns
    folds = rank // (share_ref.shape[1] - rank)
    depth_rows, fold_lanes, row_share = rank // folds, columns // folds, channels // reps
    packed = jnp.zeros((depth_rows, feature_dim), F32)
    row, lane = iota2((channels, feature_dim), 0), iota2((1, feature_dim), 1)
    rep, lane = lane // columns, lane % columns
    for fold in range(folds):
        inside = lane - fold * fold_lanes
        target = jnp.where((inside >= 0) & (inside < row_share), inside + rep * row_share, -1)
        pick = jnp.where(row == target, 1.0, 0.0).astype(BF16)
        part = first[fold * depth_rows : (fold + 1) * depth_rows].astype(BF16)
        packed = packed + dot_nn(part, pick)
    payload = jnp.concatenate([second, packed], axis=0).astype(BF16)
    for slot in range(share_ref.shape[0]):
        at = slot % reps * columns
        share_ref[slot] = payload[:, at : at + columns]
    for store in stores:
        store.wait()


def mix_blocks(direct, arrived, merged, mix, mix_t, grad, up_through, down_t, level_weight, band_count, reps):
    samples, lat_rows, block_width, feature_dim = grad.shape
    width = block_width
    lanes = arrived[0].shape[-1]
    early = EARLY if direct else 0
    turned_early = turned_whole(early, width)
    reach = merged.shape[1]
    rows = WLAT * width
    rank = down_t.shape[0]
    chunks = lat_rows // WLAT * samples
    share_shape = (band_count * reps, rank + rank // FOLDS, feature_dim // reps)
    flops = 2 * samples * lat_rows * block_width * feature_dim * (2 * reach + 2 * rows)
    vmem = pl.BlockSpec(memory_space=pltpu.VMEM)
    any_space = pl.BlockSpec(memory_space=pl.ANY)
    local = [*arrived, merged, mix, mix_t, up_through, down_t]
    return pl.pallas_call(
        lambda *refs: mix_kernel(direct, refs[: len(arrived)], *refs[len(arrived) :]),
        out_shape=[
            jax.ShapeDtypeStruct(grad.shape, BF16),
            jax.ShapeDtypeStruct(share_shape, BF16),
        ],
        in_specs=[vmem] * (len(local) + 2),
        out_specs=[any_space, vmem],
        scratch_shapes=[
            [pltpu.VMEM((lanes, rows - turned_early), BF16)] * (chunks // samples),
            [pltpu.VMEM((WLAT, width, feature_dim), BF16)] * chunks,
            [pltpu.VMEM((rows, feature_dim), F32)] * chunks,
            [pltpu.VMEM((rows - early * width, feature_dim), BF16)] * chunks,
            [pltpu.VMEM((rows, feature_dim), BF16)] * chunks,
            [pltpu.VMEM((rows, feature_dim), BF16)] * chunks,
            pltpu.VMEM((lanes // samples, feature_dim), F32),
            pltpu.SemaphoreType.DMA((chunks * WLAT,)),
        ],
        compiler_params=params(),
        cost_estimate=pl.CostEstimate(
            flops=flops,
            bytes_accessed=12 * 2**20,
            transcendentals=samples * lat_rows * block_width * feature_dim,
        ),
        name="mix_blocks",
    )(*local, grad, level_weight)


def sum_kernel(parts_ref, first_ref, second_ref):
    rank, row_share = first_ref.shape
    total = parts_ref[0].astype(F32)
    for n in range(1, parts_ref.shape[0]):
        total = total + parts_ref[n].astype(F32)
    second_ref[...] = total[:rank]
    depth_rows = total.shape[0] - rank
    for fold in range(rank // depth_rows):
        lane = fold * depth_rows * total.shape[1] // rank
        first_ref[fold * depth_rows : (fold + 1) * depth_rows, :] = total[rank:, lane : lane + row_share]


def sum_shares(shares, rank, row_share):
    parts = lax.all_to_all(shares, ("band", "rep"), split_axis=0, concat_axis=0, tiled=True)
    return pl.pallas_call(
        sum_kernel,
        out_shape=[
            jax.ShapeDtypeStruct((rank, row_share), F32),
            jax.ShapeDtypeStruct((rank, shares.shape[2]), F32),
        ],
        compiler_params=params(),
        name="sum_shares",
    )(parts)


def on_device(
    patches,
    variable_group_index,
    frozen_patch_weight,
    adapter_down,
    adapter_up,
    level_merge_weight,
    window_patch_mixer,
    column_block_owner,
    mixed_token_gradient,
):
    band_count, reps = lax.axis_size("band"), lax.axis_size("rep")
    samples, levels, channels, row_count, col_count = patches.shape
    feature_dim = frozen_patch_weight.shape[2]
    rank, col_share = adapter_up.shape
    row_share = adapter_down.shape[0]
    lat_rows = band_count * row_count
    block_width = col_count // band_count
    padded_width = round_up(block_width, SUB)
    group = 2 * WLON if block_width % (2 * WLON) == 0 else padded_width
    features = samples * levels * channels

    pixels = patches.reshape(features, col_count)
    pack_shape = (2, rank, round_up(max(row_share, col_share), LANE))
    direct = band_count == BANDS and lat_rows == WLAT and padded_width == block_width
    direct = direct and features % LANE == 0 and col_count % LANE == 0
    if direct:
        blocks, pack = send_blocks(
            pixels, column_block_owner, adapter_up, adapter_down.T, block_width, pack_shape
        )
        arrived = exchange(blocks)
    else:
        block_ids = jnp.arange(band_count, dtype=jnp.int32)
        inverse = jnp.sum(
            jnp.where(column_block_owner[None, :] == block_ids[:, None], block_ids[None, :], 0), axis=1
        )
        outgoing = jnp.take(pixels.T.reshape(band_count, block_width, features), inverse, axis=0)
        outgoing = jnp.pad(outgoing, ((0, 0), (0, padded_width - block_width), (0, 0)))
        arrived = [lax.all_to_all(outgoing, "band", split_axis=0, concat_axis=0, tiled=True)]
        pack = jnp.stack(
            [
                jnp.pad(array, ((0, 0), (0, pack_shape[2] - array.shape[1])))
                for array in (adapter_up, adapter_down.T)
            ]
        )
    factors = lax.all_gather(pack, "rep", axis=0, tiled=False)

    grad = mixed_token_gradient.reshape(samples, lat_rows, block_width, feature_dim)
    if padded_width != block_width:
        grad = jnp.pad(grad, ((0, 0), (0, 0), (0, padded_width - block_width), (0, 0)))
    merged, up_through, down_t, mix, mix_t, level_copy, grad_copy = prepare(
        direct,
        variable_group_index,
        frozen_patch_weight,
        factors,
        level_merge_weight,
        window_patch_mixer,
        grad,
        row_share,
        min(block_width, group),
        group,
    )
    if direct:
        arrived = [*arrived[EARLY - 1 :], *embed_early(arrived[:EARLY], merged)]
    mixed, shares = mix_blocks(
        direct, arrived, merged, mix, mix_t, grad_copy, up_through, down_t, level_copy, band_count, reps
    )
    if padded_width != block_width:
        mixed = mixed[:, :, :block_width]
    first_t, second = sum_shares(shares, rank, row_share)
    return mixed.reshape(mixed_token_gradient.shape), first_t.T, second


def solution(mesh):
    in_specs = (
        P("rep", None, None, "band", None),
        P(),
        P(),
        P("rep", None),
        P(None, "rep"),
        P(),
        P(),
        P(),
        P("rep", "band", None, None, None),
    )
    out_specs = (P("rep", "band", None, None, None), P("rep", None), P(None, "rep"))
    return jax.shard_map(
        on_device, mesh=mesh, in_specs=in_specs, out_specs=out_specs, check_vma=False
    )
```

```python
import functools

import jax
import jax.numpy as jnp
from jax import lax
from jax.experimental import pallas as pl
from jax.experimental.pallas import tpu as pltpu
from jax.sharding import PartitionSpec as P

WLAT = 8
WLON = 12
LANE = 128
SUB = 16
VMEM_LIMIT = 24 * 1024 * 1024
BANDS = 8
ORDER = (0, 4, 1, 5, 2, 6, 7, 3)
EARLY = 6
SLOTS = (0, 1, 4, 5, 6, 2, 3, 7)
FOLDS = 2
COLUMNS = 256
BF16 = jnp.bfloat16
F32 = jnp.float32


def round_up(value, step):
    return -(-value // step) * step


def dot_nn(a, b):
    return lax.dot_general(a, b, (((1,), (0,)), ((), ())), preferred_element_type=F32)


def dot_nt(a, b):
    return lax.dot_general(a, b, (((1,), (1,)), ((), ())), preferred_element_type=F32)


def dot_tn(a, b):
    return lax.dot_general(a, b, (((0,), (0,)), ((), ())), preferred_element_type=F32)


def split_hi_lo(values):
    high = values.astype(BF16)
    low = (values - high.astype(F32)).astype(BF16)
    return high, low


def iota2(shape, axis):
    return lax.broadcasted_iota(jnp.int32, shape, axis)


def params(**extra):
    return pltpu.CompilerParams(vmem_limit_bytes=VMEM_LIMIT, **extra)


def in_hbm(values):
    return pltpu.with_memory_space_constraint(values, pltpu.HBM)


def swap(values, axis, distance):
    count = lax.axis_size(axis)
    return lax.ppermute(values, axis, [(source, source ^ distance) for source in range(count)])


def send_kernel(owner_hbm_ref, up_hbm_ref, down_hbm_ref, x_hbm_ref, *refs):
    block_refs, pack_ref, scratch = refs[:-8], refs[-8], refs[-7:]
    owner_ref, up_ref, down_ref, x_ref, turned_ref, small_sems, x_sems = scratch
    width = block_refs[0].shape[0]
    features, columns = x_ref.shape
    small = [
        pltpu.make_async_copy(source, target, small_sems.at[n])
        for n, (source, target) in enumerate(
            [(owner_hbm_ref, owner_ref), (up_hbm_ref, up_ref), (down_hbm_ref, down_ref)]
        )
    ]
    parts = [slice(start, start + LANE) for start in range(0, features, LANE)]
    large = [
        pltpu.make_async_copy(x_hbm_ref.at[part, :], x_ref.at[part, :], x_sems.at[n])
        for n, part in enumerate(parts)
    ]
    for copy in large + small:
        copy.start()
    for copy, part in zip(large, parts):
        copy.wait()
        for start in range(0, columns, LANE):
            at = slice(start, start + LANE)
            turned_ref[at, part] = x_ref[part, at].T
    for copy in small:
        copy.wait()
    pack_ref[...] = jnp.zeros_like(pack_ref)
    pack_ref[0, :, : up_ref.shape[1]] = up_ref[...]
    pack_ref[1, :, : down_ref.shape[1]] = down_ref[...]
    me = lax.axis_index("band")
    for distance, block_ref in zip(ORDER, block_refs):
        target = jnp.bitwise_xor(me, distance)
        block = 0
        for j in range(1, owner_ref.shape[0]):
            block = jnp.where(owner_ref[j] == target, j, block)
        block_ref[...] = turned_ref[pl.ds(pl.multiple_of(block * width, SUB), width), :]


def send_blocks(pixels, owner, up, down_t, width, pack_shape):
    features, columns = pixels.shape
    any_space = pl.BlockSpec(memory_space=pl.ANY)
    vmem = pl.BlockSpec(memory_space=pltpu.VMEM)
    blocks = [(width, features)] * BANDS
    *blocks, pack = pl.pallas_call(
        send_kernel,
        out_shape=[jax.ShapeDtypeStruct(shape, BF16) for shape in [*blocks, pack_shape]],
        in_specs=[any_space] * 4,
        out_specs=[vmem] * (len(blocks) + 1),
        scratch_shapes=[
            pltpu.SMEM(owner.shape, jnp.int32),
            pltpu.VMEM(up.shape, BF16),
            pltpu.VMEM(down_t.shape, BF16),
            pltpu.VMEM((features, columns), BF16),
            pltpu.VMEM((columns, features), BF16),
            pltpu.SemaphoreType.DMA((3,)),
            pltpu.SemaphoreType.DMA((features // LANE,)),
        ],
        compiler_params=params(),
        name="send_blocks",
    )(in_hbm(owner), in_hbm(up), in_hbm(down_t), in_hbm(pixels))
    return blocks, pack


def exchange(blocks, pack):
    arrived = dict(zip(ORDER, blocks))
    for distance in (1, 4, 5, 6, 2):
        arrived[distance] = swap(arrived[distance], "band", distance)
    arrived[1], pack = lax.optimization_barrier((arrived[1], pack))
    factors = lax.all_gather(pack, "rep", axis=0, tiled=False)
    arrived[7], factors = lax.optimization_barrier((arrived[7], factors))
    arrived[7] = swap(arrived[7], "band", 7)
    arrived[3], factors = lax.optimization_barrier((arrived[3], factors))
    arrived[3] = swap(arrived[3], "band", 3)
    return [arrived[distance] for distance in SLOTS], factors


def expand_table(table, rows, half_width_padded, half_width, flip, transpose):
    position = iota2((rows, WLAT * WLON), 0)
    line, col = position // half_width_padded, position % half_width_padded
    if flip is not None:
        distance = sum(jnp.where(line == slot, far, 0) for slot, far in enumerate(SLOTS))
        line = jnp.bitwise_xor(distance, flip)
    target = iota2((rows, WLAT * WLON), 1)
    pick = jnp.where((target == line * WLON + col % WLON) & (col < half_width), 1.0, 0.0).astype(BF16)
    left = (dot_nt if transpose else dot_nn)(pick, table).astype(BF16)
    full = dot_nt(left, pick)
    row_window = (iota2((rows, 1), 0) % half_width_padded) // WLON
    col_window = (iota2((1, rows), 1) % half_width_padded) // WLON
    return jnp.where(row_window == col_window, full, 0.0).astype(BF16)


def prep_kernel(
    direct,
    row_share,
    half_width,
    half_width_padded,
    group_hbm_ref,
    level_hbm_ref,
    grad_hbm_ref,
    frozen_ref,
    factors_ref,
    mixer_ref,
    merged_ref,
    up_ref,
    down_ref,
    mix_ref,
    mix_t_ref,
    level_ref,
    grad_ref,
    group_ref,
    sems,
):
    pairs = [(group_hbm_ref, group_ref), (level_hbm_ref, level_ref)]
    flip = lax.axis_index("band") if direct else None
    if direct:
        pairs += [
            (grad_hbm_ref.at[:, jnp.bitwise_xor(flip, far)], grad_ref.at[:, slot])
            for slot, far in enumerate(SLOTS)
        ]
    else:
        pairs.append((grad_hbm_ref, grad_ref))
    loads = [
        pltpu.make_async_copy(source, target, sems.at[n]) for n, (source, target) in enumerate(pairs)
    ]
    for load in loads:
        load.start()
    rows = mix_ref.shape[0]
    mix_ref[...] = expand_table(mixer_ref[...], rows, half_width_padded, half_width, flip, False)
    mix_t_ref[...] = expand_table(mixer_ref[...], rows, half_width_padded, half_width, flip, True)
    reps, _, rank, share = factors_ref.shape
    levels = level_ref.shape[0]
    variables = group_ref.shape[0]
    channels = variables * frozen_ref.shape[1]
    up = jnp.concatenate([factors_ref[r, 0] for r in range(reps)], axis=1)
    source, target = iota2((share, channels), 0), iota2((share, channels), 1)
    down_t = jnp.zeros((rank, channels), F32)
    for r in range(reps):
        place = jnp.where((target == source + r * row_share) & (source < row_share), 1.0, 0.0)
        down_t = down_t + dot_nn(factors_ref[r, 1], place.astype(BF16))
    down_t = down_t.astype(BF16)
    down_ref[...] = down_t
    loads[0].wait()
    base = jnp.concatenate([frozen_ref[group_ref[v]].astype(F32) for v in range(variables)], axis=0)
    merged = (base + dot_tn(down_t, up)).astype(BF16)
    stacked = jnp.concatenate([merged, up], axis=0)
    merged_ref[...] = jnp.zeros_like(merged_ref)
    loads[1].wait()
    for level in range(levels):
        through = dot_nn(stacked, level_ref[level])
        weights = through[:channels].astype(BF16)
        for s in range(merged_ref.shape[0]):
            offset = (s * levels * channels) % LANE + level * channels
            merged_ref[s, offset : offset + channels, :] = weights
        up_high, up_low = split_hi_lo(through[channels:])
        up_ref[level, :rank, :] = up_high
        up_ref[level, rank:, :] = up_low
    for load in loads[2:]:
        load.wait()


def prepare(direct, groups, frozen, factors, level_weight, mixer, grad, row_share, half_width, half_width_padded):
    reps, _, rank, _ = factors.shape
    levels, feature_dim, _ = level_weight.shape
    channels = groups.shape[0] * frozen.shape[1]
    reach = round_up(levels * channels + LANE // 2, LANE)
    rows = WLAT * half_width_padded
    vmem = pl.BlockSpec(memory_space=pltpu.VMEM)
    flops = 2 * levels * (channels + rank) * feature_dim * feature_dim + 4 * rows * rows * WLAT * WLON
    shapes = [
        (grad.shape[0], reach, feature_dim),
        (levels, 2 * rank, feature_dim),
        (rank, channels),
        (rows, rows),
        (rows, rows),
        level_weight.shape,
        grad.shape,
    ]
    return pl.pallas_call(
        functools.partial(prep_kernel, direct, row_share, half_width, half_width_padded),
        out_shape=[jax.ShapeDtypeStruct(shape, BF16) for shape in shapes],
        in_specs=[pl.BlockSpec(memory_space=pl.ANY)] * 3 + [vmem] * 3,
        out_specs=[vmem] * len(shapes),
        scratch_shapes=[pltpu.SMEM(groups.shape, jnp.int32), pltpu.SemaphoreType.DMA((2 + WLAT,))],
        compiler_params=params(),
        cost_estimate=pl.CostEstimate(flops=flops, bytes_accessed=6 * 2**20, transcendentals=0),
        name="prepare",
    )(in_hbm(groups), in_hbm(level_weight), in_hbm(grad), in_hbm(frozen), factors, in_hbm(mixer))


def normal_parts(values):
    cdf = 0.5 + 0.5 * lax.erf(values * 0.7071067811865476)
    return cdf, 0.3989422804014327 * jnp.exp2(values * values * -0.7213475204444817)


def factor_shares(total, up_ref, down_ref, level_ref):
    levels, two_rank, feature_dim = up_ref.shape
    rank, channels = down_ref.shape
    high, low = split_hi_lo(total)
    down = down_ref[...]
    first = jnp.zeros((rank, channels), F32)
    second = jnp.zeros((two_rank, feature_dim), F32)
    for level in range(levels):
        at = slice(level * channels, (level + 1) * channels)
        both = dot_nt(up_ref[level], high[at])
        first = first + both[:rank] + both[rank:] + dot_nt(up_ref[level, :rank, :], low[at])
        through = dot_nn(down, high[at]) + dot_nn(down, low[at])
        through = jnp.concatenate(split_hi_lo(through), axis=0)
        second = second + dot_nt(through, level_ref[level])
    return first, second[:rank] + second[rank:]


def turned_whole(lines, width):
    return lines * width // LANE * LANE


def embed_kernel(*refs):
    piece_refs, (merged_ref, tokens_ref, turned_ref) = refs[:-3], refs[-3:]
    samples, reach, feature_dim = merged_ref.shape
    width, features = piece_refs[0].shape
    depth = features // samples
    group = 2 * WLON
    rows = len(piece_refs) * group
    positions = turned_ref.shape[1]
    for s in range(samples):
        lane = s * depth // LANE * LANE
        pixels = jnp.concatenate([piece_ref[:, lane : lane + reach] for piece_ref in piece_refs], axis=0)
        for start in range(0, feature_dim, COLUMNS):
            columns = slice(start, start + COLUMNS)
            tokens = dot_nn(pixels, merged_ref[s, :, columns]).reshape(len(piece_refs), width, COLUMNS)
            for n in range(width // group):
                part = tokens[:, n * group : (n + 1) * group].reshape(rows, COLUMNS)
                tokens_ref[s, n * rows : (n + 1) * rows, columns] = part.astype(BF16)
    for start in range(0, features, LANE):
        lanes = slice(start, start + LANE)
        pixels = jnp.concatenate([piece_ref[:, lanes] for piece_ref in piece_refs], axis=0)
        turned_ref[lanes, :] = pixels[:positions].T


def embed_early(pieces, merged):
    samples, _, feature_dim = merged.shape
    width, features = pieces[0].shape
    count = len(pieces) * width
    return pl.pallas_call(
        embed_kernel,
        out_shape=[
            jax.ShapeDtypeStruct((samples, count, feature_dim), BF16),
            jax.ShapeDtypeStruct((features, turned_whole(len(pieces), width)), BF16),
        ],
        in_specs=[pl.BlockSpec(memory_space=pltpu.VMEM)] * (len(pieces) + 1),
        out_specs=[pl.BlockSpec(memory_space=pltpu.VMEM)] * 2,
        compiler_params=params(),
        cost_estimate=pl.CostEstimate(
            flops=2 * count * features * feature_dim, bytes_accessed=4 * 2**20, transcendentals=0
        ),
        name="embed_early",
    )(*pieces, merged)


def mix_kernel(
    direct,
    piece_refs,
    merged_ref,
    mix_ref,
    mix_t_ref,
    up_ref,
    down_ref,
    grad_ref,
    level_ref,
    mixed_hbm_ref,
    share_ref,
    turned_refs,
    mixed_refs,
    pre_refs,
    tokens_refs,
    grad_pre_refs,
    grad_tokens_refs,
    total_ref,
    mixed_sems,
):
    samples, reach, feature_dim = merged_ref.shape
    chunk_count, (_, width, _) = len(mixed_refs), mixed_refs[0].shape
    depth = piece_refs[-1].shape[-1] // samples
    rows = WLAT * width

    group_rows = mix_ref.shape[0]
    group = group_rows // WLAT
    groups = [
        (slice(start, start + group), slice(start * WLAT, start * WLAT + group_rows))
        for start in range(0, width, group)
    ]
    pair = 1 if group % SUB == 0 else 2

    early = EARLY if direct else 0
    early_rows, late_rows = early * group, (WLAT - early) * group
    if direct:
        early_tokens_ref, early_turned_ref, *line_refs = piece_refs
        early_positions = early_turned_ref.shape[1]

    def lines_of(n):
        return pl.ds(n // samples * WLAT, WLAT)

    if direct:
        me = lax.axis_index("band")
        targets = [
            (mixed_refs[n].at[slot], mixed_hbm_ref.at[n, jnp.bitwise_xor(me, far)])
            for n in range(chunk_count)
            for slot, far in enumerate(SLOTS)
        ]
    else:
        targets = [
            (mixed_refs[n], mixed_hbm_ref.at[n % samples, lines_of(n)]) for n in range(chunk_count)
        ]
    stores = [
        pltpu.make_async_copy(source, target, mixed_sems.at[n]) for n, (source, target) in enumerate(targets)
    ]

    def pixels_of(n, lanes):
        if direct:
            return jnp.concatenate([line_ref[:, lanes] for line_ref in line_refs], axis=0)
        return piece_refs[0][lines_of(n), :, lanes].reshape(rows, lanes.stop - lanes.start)

    def turn(n):
        def part(lanes):
            pixels = pixels_of(n, lanes)
            if direct:
                before = early_positions - (early - 1) * width
                pixels = pixels[before:]
            turned_refs[n // samples][lanes, :] = pixels.T

        starts = range(0, samples * depth, LANE)
        return [functools.partial(part, slice(start, start + LANE)) for start in starts]

    def tokens_at(n, block, line, count, columns):
        if line < early:
            at = pl.ds(block * early_rows + line * group, count * group)
            return early_tokens_ref[n % samples, at, columns]
        return tokens_refs[n][pl.ds(block * late_rows + (line - early) * group, count * group), columns]

    def forward(n, columns):
        s = n % samples
        lane = s * depth // LANE * LANE

        def embed():
            pixels = pixels_of(n, slice(lane, lane + reach))
            if direct:
                pixels = pixels[width:]
            tokens = dot_nn(pixels, merged_ref[s, :, columns]).reshape(WLAT - early, width, COLUMNS)
            for block, (within, _) in enumerate(groups):
                part = tokens[:, within].reshape(late_rows, COLUMNS).astype(BF16)
                tokens_refs[n][block * late_rows : (block + 1) * late_rows, columns] = part

        def mixing():
            for block, (_, at) in enumerate(groups):
                tokens = tokens_at(n, block, early, WLAT - early, columns)
                if direct:
                    tokens = jnp.concatenate([tokens_at(n, block, 0, early, columns), tokens], axis=0)
                pre_refs[n][at, columns] = dot_nn(mix_ref[...], tokens)

        return [embed, mixing]

    def pointwise(n, columns):
        s, first_line = n % samples, n // samples * WLAT

        def part(line, across, lanes):
            grads = [grad_ref[s, first_line + line + k, across, lanes].astype(F32) for k in range(pair)]
            mixed = []
            for block, (within, at) in enumerate(groups):
                if within.start < across.start or within.stop > across.stop:
                    continue
                at = pl.ds(at.start + line * group, pair * group)
                pre = pre_refs[n][at, lanes]
                cdf, pdf = normal_parts(pre)
                mixed.append(tokens_at(n, block, line, pair, lanes).astype(F32) + pre * cdf)
                first = within.start - across.start
                grad = jnp.concatenate([values[first : first + group] for values in grads], axis=0)
                grad_pre_refs[n][at, lanes] = (grad * (cdf + pre * pdf)).astype(BF16)
            for k in range(pair):
                parts = [values[k * group : (k + 1) * group] for values in mixed]
                mixed_refs[n][line + k, across, lanes] = jnp.concatenate(parts, axis=0).astype(BF16)

        return [
            functools.partial(part, line, slice(across, across + pair * group), slice(start, start + LANE))
            for line in range(0, WLAT, pair)
            for across in range(0, width, pair * group)
            for start in range(columns.start, columns.stop, LANE)
        ]

    def backward(n, columns):
        def spread():
            direct_part = grad_ref[n % samples, lines_of(n), :, columns].astype(F32)
            through = [
                dot_nn(mix_t_ref[...], grad_pre_refs[n][at, columns]).reshape(WLAT, group, COLUMNS)
                for _, at in groups
            ]
            total = jnp.concatenate(through, axis=1) + direct_part
            grad_tokens_refs[n][:, columns] = total.reshape(rows, COLUMNS).astype(BF16)

        def share():
            s = n % samples
            features = slice(s * depth, (s + 1) * depth)
            late = rows - turned_refs[0].shape[1]
            part = dot_nn(turned_refs[n // samples][features, :], grad_tokens_refs[n][late:, columns])
            if direct:
                part = part + dot_nn(early_turned_ref[features, :], grad_tokens_refs[n][:late, columns])
            total_ref[:, columns] = part if n == 0 else total_ref[:, columns] + part

        return [spread, share]

    units = [
        (n, slice(start, start + COLUMNS))
        for n in range(chunk_count)
        for start in range(0, feature_dim, COLUMNS)
    ]
    for step in forward(*units[0]):
        step()
    for i, unit in enumerate(units):
        n, columns = unit
        others = []
        if i + 1 < len(units):
            others += forward(*units[i + 1])
        if columns.start == 0 and n % samples == 0:
            others += turn(n)
        if i > 0:
            others += backward(*units[i - 1])
        lines = pointwise(*unit)
        for line, vector_step in enumerate(lines):
            vector_step()
            for step in others[line * len(others) // len(lines) : (line + 1) * len(others) // len(lines)]:
                step()
        if columns.stop == feature_dim:
            each = len(stores) // chunk_count
            for store in stores[n * each : (n + 1) * each]:
                store.start()
    for step in backward(*units[-1]):
        step()

    first, second = factor_shares(total_ref[...], up_ref, down_ref, level_ref)
    rank, channels = down_ref.shape
    columns = share_ref.shape[2]
    reps = feature_dim // columns
    folds = rank // (share_ref.shape[1] - rank)
    depth_rows, fold_lanes, row_share = rank // folds, columns // folds, channels // reps
    packed = jnp.zeros((depth_rows, feature_dim), F32)
    row, lane = iota2((channels, feature_dim), 0), iota2((1, feature_dim), 1)
    rep, lane = lane // columns, lane % columns
    for fold in range(folds):
        inside = lane - fold * fold_lanes
        target = jnp.where((inside >= 0) & (inside < row_share), inside + rep * row_share, -1)
        pick = jnp.where(row == target, 1.0, 0.0).astype(BF16)
        part = first[fold * depth_rows : (fold + 1) * depth_rows].astype(BF16)
        packed = packed + dot_nn(part, pick)
    payload = jnp.concatenate([second, packed], axis=0).astype(BF16)
    for slot in range(share_ref.shape[0]):
        at = slot % reps * columns
        share_ref[slot] = payload[:, at : at + columns]
    for store in stores:
        store.wait()


def mix_blocks(direct, arrived, merged, mix, mix_t, grad, up_through, down_t, level_weight, band_count, reps):
    samples, lat_rows, block_width, feature_dim = grad.shape
    width = block_width
    lanes = arrived[-1].shape[-1]
    early = EARLY if direct else 0
    turned_early = turned_whole(early, width)
    reach = merged.shape[1]
    rows = WLAT * width
    rank = down_t.shape[0]
    chunks = lat_rows // WLAT * samples
    share_shape = (band_count * reps, rank + rank // FOLDS, feature_dim // reps)
    flops = 2 * samples * lat_rows * block_width * feature_dim * (2 * reach + 2 * rows)
    vmem = pl.BlockSpec(memory_space=pltpu.VMEM)
    any_space = pl.BlockSpec(memory_space=pl.ANY)
    local = [*arrived, merged, mix, mix_t, up_through, down_t]
    return pl.pallas_call(
        lambda *refs: mix_kernel(direct, refs[: len(arrived)], *refs[len(arrived) :]),
        out_shape=[
            jax.ShapeDtypeStruct(grad.shape, BF16),
            jax.ShapeDtypeStruct(share_shape, BF16),
        ],
        in_specs=[vmem] * (len(local) + 2),
        out_specs=[any_space, vmem],
        scratch_shapes=[
            [pltpu.VMEM((lanes, rows - turned_early), BF16)] * (chunks // samples),
            [pltpu.VMEM((WLAT, width, feature_dim), BF16)] * chunks,
            [pltpu.VMEM((rows, feature_dim), F32)] * chunks,
            [pltpu.VMEM((rows - early * width, feature_dim), BF16)] * chunks,
            [pltpu.VMEM((rows, feature_dim), BF16)] * chunks,
            [pltpu.VMEM((rows, feature_dim), BF16)] * chunks,
            pltpu.VMEM((lanes // samples, feature_dim), F32),
            pltpu.SemaphoreType.DMA((chunks * WLAT,)),
        ],
        compiler_params=params(),
        cost_estimate=pl.CostEstimate(
            flops=flops,
            bytes_accessed=12 * 2**20,
            transcendentals=samples * lat_rows * block_width * feature_dim,
        ),
        name="mix_blocks",
    )(*local, grad, level_weight)


def sum_kernel(parts_ref, first_ref, second_ref):
    rank, row_share = first_ref.shape
    total = parts_ref[0].astype(F32)
    for n in range(1, parts_ref.shape[0]):
        total = total + parts_ref[n].astype(F32)
    second_ref[...] = total[:rank]
    depth_rows = total.shape[0] - rank
    for fold in range(rank // depth_rows):
        lane = fold * depth_rows * total.shape[1] // rank
        first_ref[fold * depth_rows : (fold + 1) * depth_rows, :] = total[rank:, lane : lane + row_share]


def sum_shares(shares, rank, row_share):
    parts = lax.all_to_all(shares, ("band", "rep"), split_axis=0, concat_axis=0, tiled=True)
    return pl.pallas_call(
        sum_kernel,
        out_shape=[
            jax.ShapeDtypeStruct((rank, row_share), F32),
            jax.ShapeDtypeStruct((rank, shares.shape[2]), F32),
        ],
        compiler_params=params(),
        name="sum_shares",
    )(parts)


def on_device(
    patches,
    variable_group_index,
    frozen_patch_weight,
    adapter_down,
    adapter_up,
    level_merge_weight,
    window_patch_mixer,
    column_block_owner,
    mixed_token_gradient,
):
    band_count, reps = lax.axis_size("band"), lax.axis_size("rep")
    samples, levels, channels, row_count, col_count = patches.shape
    feature_dim = frozen_patch_weight.shape[2]
    rank, col_share = adapter_up.shape
    row_share = adapter_down.shape[0]
    lat_rows = band_count * row_count
    block_width = col_count // band_count
    padded_width = round_up(block_width, SUB)
    group = 2 * WLON if block_width % (2 * WLON) == 0 else padded_width
    features = samples * levels * channels

    pixels = patches.reshape(features, col_count)
    pack_shape = (2, rank, round_up(max(row_share, col_share), LANE))
    direct = band_count == BANDS and lat_rows == WLAT and padded_width == block_width
    direct = direct and features % LANE == 0 and col_count % LANE == 0
    if direct:
        blocks, pack = send_blocks(
            pixels, column_block_owner, adapter_up, adapter_down.T, block_width, pack_shape
        )
        arrived, factors = exchange(blocks, pack)
    else:
        block_ids = jnp.arange(band_count, dtype=jnp.int32)
        inverse = jnp.sum(
            jnp.where(column_block_owner[None, :] == block_ids[:, None], block_ids[None, :], 0), axis=1
        )
        outgoing = jnp.take(pixels.T.reshape(band_count, block_width, features), inverse, axis=0)
        outgoing = jnp.pad(outgoing, ((0, 0), (0, padded_width - block_width), (0, 0)))
        arrived = [lax.all_to_all(outgoing, "band", split_axis=0, concat_axis=0, tiled=True)]
        pack = jnp.stack(
            [
                jnp.pad(array, ((0, 0), (0, pack_shape[2] - array.shape[1])))
                for array in (adapter_up, adapter_down.T)
            ]
        )
        factors = lax.all_gather(pack, "rep", axis=0, tiled=False)

    grad = mixed_token_gradient.reshape(samples, lat_rows, block_width, feature_dim)
    if padded_width != block_width:
        grad = jnp.pad(grad, ((0, 0), (0, 0), (0, padded_width - block_width), (0, 0)))
    merged, up_through, down_t, mix, mix_t, level_copy, grad_copy = prepare(
        direct,
        variable_group_index,
        frozen_patch_weight,
        factors,
        level_merge_weight,
        window_patch_mixer,
        grad,
        row_share,
        min(block_width, group),
        group,
    )
    if direct:
        arrived = [*embed_early(arrived[:EARLY], merged), *arrived[EARLY - 1 :]]
    mixed, shares = mix_blocks(
        direct, arrived, merged, mix, mix_t, grad_copy, up_through, down_t, level_copy, band_count, reps
    )
    if padded_width != block_width:
        mixed = mixed[:, :, :block_width]
    first_t, second = sum_shares(shares, rank, row_share)
    return mixed.reshape(mixed_token_gradient.shape), first_t.T, second


def solution(mesh):
    in_specs = (
        P("rep", None, None, "band", None),
        P(),
        P(),
        P("rep", None),
        P(None, "rep"),
        P(),
        P(),
        P(),
        P("rep", "band", None, None, None),
    )
    out_specs = (P("rep", "band", None, None, None), P("rep", None), P(None, "rep"))
    return jax.shard_map(
        on_device, mesh=mesh, in_specs=in_specs, out_specs=out_specs, check_vma=False
    )
```

```python
import functools

import jax
import jax.numpy as jnp
from jax import lax
from jax.experimental import pallas as pl
from jax.experimental.pallas import tpu as pltpu
from jax.sharding import PartitionSpec as P

WLAT = 8
WLON = 12
LANE = 128
SUB = 16
VMEM_LIMIT = 24 * 1024 * 1024
BANDS = 8
ORDER = (0, 4, 1, 5, 2, 6, 7, 3)
EARLY = 6
SLOTS = (0, 1, 4, 5, 6, 2, 3, 7)
FOLDS = 2
COLUMNS = 256
BF16 = jnp.bfloat16
F32 = jnp.float32


def round_up(value, step):
    return -(-value // step) * step


def dot_nn(a, b):
    return lax.dot_general(a, b, (((1,), (0,)), ((), ())), preferred_element_type=F32)


def dot_nt(a, b):
    return lax.dot_general(a, b, (((1,), (1,)), ((), ())), preferred_element_type=F32)


def dot_tn(a, b):
    return lax.dot_general(a, b, (((0,), (0,)), ((), ())), preferred_element_type=F32)


def split_hi_lo(values):
    high = values.astype(BF16)
    low = (values - high.astype(F32)).astype(BF16)
    return high, low


def iota2(shape, axis):
    return lax.broadcasted_iota(jnp.int32, shape, axis)


def params(**extra):
    return pltpu.CompilerParams(vmem_limit_bytes=VMEM_LIMIT, **extra)


def in_hbm(values):
    return pltpu.with_memory_space_constraint(values, pltpu.HBM)


def swap(values, axis, distance):
    count = lax.axis_size(axis)
    return lax.ppermute(values, axis, [(source, source ^ distance) for source in range(count)])


def send_kernel(owner_hbm_ref, up_hbm_ref, down_hbm_ref, x_hbm_ref, *refs):
    block_refs, pack_ref, scratch = refs[:-8], refs[-8], refs[-7:]
    owner_ref, up_ref, down_ref, x_ref, turned_ref, small_sems, x_sems = scratch
    width = block_refs[0].shape[0]
    features, columns = x_ref.shape
    small = [
        pltpu.make_async_copy(source, target, small_sems.at[n])
        for n, (source, target) in enumerate(
            [(owner_hbm_ref, owner_ref), (up_hbm_ref, up_ref), (down_hbm_ref, down_ref)]
        )
    ]
    parts = [slice(start, start + LANE) for start in range(0, features, LANE)]
    large = [
        pltpu.make_async_copy(x_hbm_ref.at[part, :], x_ref.at[part, :], x_sems.at[n])
        for n, part in enumerate(parts)
    ]
    for copy in large + small:
        copy.start()
    for copy, part in zip(large, parts):
        copy.wait()
        for start in range(0, columns, LANE):
            at = slice(start, start + LANE)
            turned_ref[at, part] = x_ref[part, at].T
    for copy in small:
        copy.wait()
    pack_ref[...] = jnp.zeros_like(pack_ref)
    pack_ref[0, :, : up_ref.shape[1]] = up_ref[...]
    pack_ref[1, :, : down_ref.shape[1]] = down_ref[...]
    me = lax.axis_index("band")
    for distance, block_ref in zip(ORDER, block_refs):
        target = jnp.bitwise_xor(me, distance)
        block = 0
        for j in range(1, owner_ref.shape[0]):
            block = jnp.where(owner_ref[j] == target, j, block)
        block_ref[...] = turned_ref[pl.ds(pl.multiple_of(block * width, SUB), width), :]


def send_blocks(pixels, owner, up, down_t, width, pack_shape):
    features, columns = pixels.shape
    any_space = pl.BlockSpec(memory_space=pl.ANY)
    vmem = pl.BlockSpec(memory_space=pltpu.VMEM)
    blocks = [(width, features)] * BANDS
    *blocks, pack = pl.pallas_call(
        send_kernel,
        out_shape=[jax.ShapeDtypeStruct(shape, BF16) for shape in [*blocks, pack_shape]],
        in_specs=[any_space] * 4,
        out_specs=[vmem] * (len(blocks) + 1),
        scratch_shapes=[
            pltpu.SMEM(owner.shape, jnp.int32),
            pltpu.VMEM(up.shape, BF16),
            pltpu.VMEM(down_t.shape, BF16),
            pltpu.VMEM((features, columns), BF16),
            pltpu.VMEM((columns, features), BF16),
            pltpu.SemaphoreType.DMA((3,)),
            pltpu.SemaphoreType.DMA((features // LANE,)),
        ],
        compiler_params=params(),
        name="send_blocks",
    )(in_hbm(owner), in_hbm(up), in_hbm(down_t), in_hbm(pixels))
    return blocks, pack


def exchange(blocks, pack):
    arrived = dict(zip(ORDER, blocks))
    for distance in (1, 4, 5, 6, 2):
        arrived[distance] = swap(arrived[distance], "band", distance)
    arrived[1], pack = lax.optimization_barrier((arrived[1], pack))
    factors = lax.all_gather(pack, "rep", axis=0, tiled=False)
    arrived[7], factors = lax.optimization_barrier((arrived[7], factors))
    arrived[7] = swap(arrived[7], "band", 7)
    arrived[3], factors = lax.optimization_barrier((arrived[3], factors))
    arrived[3] = swap(arrived[3], "band", 3)
    return [arrived[distance] for distance in SLOTS], factors


def expand_table(table, rows, half_width_padded, half_width, flip, transpose):
    position = iota2((rows, WLAT * WLON), 0)
    line, col = position // half_width_padded, position % half_width_padded
    if flip is not None:
        distance = sum(jnp.where(line == slot, far, 0) for slot, far in enumerate(SLOTS))
        line = jnp.bitwise_xor(distance, flip)
    target = iota2((rows, WLAT * WLON), 1)
    pick = jnp.where((target == line * WLON + col % WLON) & (col < half_width), 1.0, 0.0).astype(BF16)
    left = (dot_nt if transpose else dot_nn)(pick, table).astype(BF16)
    full = dot_nt(left, pick)
    row_window = (iota2((rows, 1), 0) % half_width_padded) // WLON
    col_window = (iota2((1, rows), 1) % half_width_padded) // WLON
    return jnp.where(row_window == col_window, full, 0.0).astype(BF16)


def prep_kernel(
    direct,
    row_share,
    half_width,
    half_width_padded,
    group_hbm_ref,
    level_hbm_ref,
    grad_hbm_ref,
    frozen_ref,
    factors_ref,
    mixer_ref,
    merged_ref,
    up_ref,
    down_ref,
    mix_ref,
    mix_t_ref,
    level_ref,
    grad_ref,
    group_ref,
    sems,
):
    pairs = [(group_hbm_ref, group_ref), (level_hbm_ref, level_ref)]
    flip = lax.axis_index("band") if direct else None
    if direct:
        pairs += [
            (grad_hbm_ref.at[:, jnp.bitwise_xor(flip, far)], grad_ref.at[:, slot])
            for slot, far in enumerate(SLOTS)
        ]
    else:
        pairs.append((grad_hbm_ref, grad_ref))
    loads = [
        pltpu.make_async_copy(source, target, sems.at[n]) for n, (source, target) in enumerate(pairs)
    ]
    for load in loads:
        load.start()
    rows = mix_ref.shape[0]
    mix_ref[...] = expand_table(mixer_ref[...], rows, half_width_padded, half_width, flip, False)
    mix_t_ref[...] = expand_table(mixer_ref[...], rows, half_width_padded, half_width, flip, True)
    reps, _, rank, share = factors_ref.shape
    levels = level_ref.shape[0]
    variables = group_ref.shape[0]
    channels = variables * frozen_ref.shape[1]
    up = jnp.concatenate([factors_ref[r, 0] for r in range(reps)], axis=1)
    source, target = iota2((share, channels), 0), iota2((share, channels), 1)
    down_t = jnp.zeros((rank, channels), F32)
    for r in range(reps):
        place = jnp.where((target == source + r * row_share) & (source < row_share), 1.0, 0.0)
        down_t = down_t + dot_nn(factors_ref[r, 1], place.astype(BF16))
    down_t = down_t.astype(BF16)
    down_ref[...] = down_t
    loads[0].wait()
    base = jnp.concatenate([frozen_ref[group_ref[v]].astype(F32) for v in range(variables)], axis=0)
    merged = (base + dot_tn(down_t, up)).astype(BF16)
    stacked = jnp.concatenate([merged, up], axis=0)
    merged_ref[...] = jnp.zeros_like(merged_ref)
    loads[1].wait()
    for level in range(levels):
        through = dot_nn(stacked, level_ref[level])
        weights = through[:channels].astype(BF16)
        for s in range(merged_ref.shape[0]):
            offset = (s * levels * channels) % LANE + level * channels
            merged_ref[s, offset : offset + channels, :] = weights
        up_high, up_low = split_hi_lo(through[channels:])
        up_ref[level, :rank, :] = up_high
        up_ref[level, rank:, :] = up_low
    for load in loads[2:]:
        load.wait()


def prepare(direct, groups, frozen, factors, level_weight, mixer, grad, row_share, half_width, half_width_padded):
    reps, _, rank, _ = factors.shape
    levels, feature_dim, _ = level_weight.shape
    channels = groups.shape[0] * frozen.shape[1]
    reach = round_up(levels * channels + LANE // 2, LANE)
    rows = WLAT * half_width_padded
    vmem = pl.BlockSpec(memory_space=pltpu.VMEM)
    flops = 2 * levels * (channels + rank) * feature_dim * feature_dim + 4 * rows * rows * WLAT * WLON
    shapes = [
        (grad.shape[0], reach, feature_dim),
        (levels, 2 * rank, feature_dim),
        (rank, channels),
        (rows, rows),
        (rows, rows),
        level_weight.shape,
        grad.shape,
    ]
    return pl.pallas_call(
        functools.partial(prep_kernel, direct, row_share, half_width, half_width_padded),
        out_shape=[jax.ShapeDtypeStruct(shape, BF16) for shape in shapes],
        in_specs=[pl.BlockSpec(memory_space=pl.ANY)] * 3 + [vmem] * 3,
        out_specs=[vmem] * len(shapes),
        scratch_shapes=[pltpu.SMEM(groups.shape, jnp.int32), pltpu.SemaphoreType.DMA((2 + WLAT,))],
        compiler_params=params(),
        cost_estimate=pl.CostEstimate(flops=flops, bytes_accessed=6 * 2**20, transcendentals=0),
        name="prepare",
    )(in_hbm(groups), in_hbm(level_weight), in_hbm(grad), in_hbm(frozen), factors, in_hbm(mixer))


def normal_parts(values):
    cdf = 0.5 + 0.5 * lax.erf(values * 0.7071067811865476)
    return cdf, 0.3989422804014327 * jnp.exp2(values * values * -0.7213475204444817)


def factor_shares(total, up_ref, down_ref, level_ref):
    levels, two_rank, feature_dim = up_ref.shape
    rank, channels = down_ref.shape
    total = total.astype(BF16)
    first = jnp.zeros((two_rank, channels), F32)
    second = jnp.zeros((two_rank, feature_dim), F32)
    for level in range(levels):
        part = total[level * channels : (level + 1) * channels]
        first = first + dot_nt(up_ref[level], part)
        through = jnp.concatenate(split_hi_lo(dot_nn(down_ref[...], part)), axis=0)
        second = second + dot_nt(through, level_ref[level])
    first = first[:rank] + first[rank:]
    return first, second[:rank] + second[rank:]


def turned_whole(lines, width):
    return lines * width // LANE * LANE


def embed_kernel(*refs):
    piece_refs, (merged_ref, tokens_ref, turned_ref) = refs[:-3], refs[-3:]
    samples, reach, feature_dim = merged_ref.shape
    width, features = piece_refs[0].shape
    depth = features // samples
    group = 2 * WLON
    rows = len(piece_refs) * group
    positions = turned_ref.shape[1]
    for s in range(samples):
        lane = s * depth // LANE * LANE
        pixels = jnp.concatenate([piece_ref[:, lane : lane + reach] for piece_ref in piece_refs], axis=0)
        for start in range(0, feature_dim, COLUMNS):
            columns = slice(start, start + COLUMNS)
            tokens = dot_nn(pixels, merged_ref[s, :, columns]).reshape(len(piece_refs), width, COLUMNS)
            for n in range(width // group):
                part = tokens[:, n * group : (n + 1) * group].reshape(rows, COLUMNS)
                tokens_ref[s, n * rows : (n + 1) * rows, columns] = part.astype(BF16)
    for start in range(0, features, LANE):
        lanes = slice(start, start + LANE)
        pixels = jnp.concatenate([piece_ref[:, lanes] for piece_ref in piece_refs], axis=0)
        turned_ref[lanes, :] = pixels[:positions].T


def embed_early(pieces, merged):
    samples, _, feature_dim = merged.shape
    width, features = pieces[0].shape
    count = len(pieces) * width
    return pl.pallas_call(
        embed_kernel,
        out_shape=[
            jax.ShapeDtypeStruct((samples, count, feature_dim), BF16),
            jax.ShapeDtypeStruct((features, turned_whole(len(pieces), width)), BF16),
        ],
        in_specs=[pl.BlockSpec(memory_space=pltpu.VMEM)] * (len(pieces) + 1),
        out_specs=[pl.BlockSpec(memory_space=pltpu.VMEM)] * 2,
        compiler_params=params(),
        cost_estimate=pl.CostEstimate(
            flops=2 * count * features * feature_dim, bytes_accessed=4 * 2**20, transcendentals=0
        ),
        name="embed_early",
    )(*pieces, merged)


def mix_kernel(
    direct,
    piece_refs,
    merged_ref,
    mix_ref,
    mix_t_ref,
    up_ref,
    down_ref,
    grad_ref,
    level_ref,
    mixed_hbm_ref,
    share_ref,
    turned_refs,
    mixed_refs,
    pre_refs,
    tokens_refs,
    grad_pre_refs,
    grad_tokens_refs,
    total_ref,
    mixed_sems,
):
    samples, reach, feature_dim = merged_ref.shape
    chunk_count, (_, width, _) = len(mixed_refs), mixed_refs[0].shape
    depth = piece_refs[-1].shape[-1] // samples
    rows = WLAT * width

    group_rows = mix_ref.shape[0]
    group = group_rows // WLAT
    groups = [
        (slice(start, start + group), slice(start * WLAT, start * WLAT + group_rows))
        for start in range(0, width, group)
    ]
    pair = 1 if group % SUB == 0 else 2

    early = EARLY if direct else 0
    early_rows, late_rows = early * group, (WLAT - early) * group
    if direct:
        early_tokens_ref, early_turned_ref, *line_refs = piece_refs
        early_positions = early_turned_ref.shape[1]

    def lines_of(n):
        return pl.ds(n // samples * WLAT, WLAT)

    if direct:
        me = lax.axis_index("band")
        targets = [
            (mixed_refs[n].at[slot], mixed_hbm_ref.at[n, jnp.bitwise_xor(me, far)])
            for n in range(chunk_count)
            for slot, far in enumerate(SLOTS)
        ]
    else:
        targets = [
            (mixed_refs[n], mixed_hbm_ref.at[n % samples, lines_of(n)]) for n in range(chunk_count)
        ]
    stores = [
        pltpu.make_async_copy(source, target, mixed_sems.at[n]) for n, (source, target) in enumerate(targets)
    ]

    def pixels_of(n, lanes):
        if direct:
            return jnp.concatenate([line_ref[:, lanes] for line_ref in line_refs], axis=0)
        return piece_refs[0][lines_of(n), :, lanes].reshape(rows, lanes.stop - lanes.start)

    def turn(n):
        def part(lanes):
            pixels = pixels_of(n, lanes)
            if direct:
                before = early_positions - (early - 1) * width
                pixels = pixels[before:]
            turned_refs[n // samples][lanes, :] = pixels.T

        starts = range(0, samples * depth, LANE)
        return [functools.partial(part, slice(start, start + LANE)) for start in starts]

    def tokens_at(n, block, line, count, columns):
        if line < early:
            at = pl.ds(block * early_rows + line * group, count * group)
            return early_tokens_ref[n % samples, at, columns]
        return tokens_refs[n][pl.ds(block * late_rows + (line - early) * group, count * group), columns]

    def forward(n, columns):
        s = n % samples
        lane = s * depth // LANE * LANE

        def embed():
            pixels = pixels_of(n, slice(lane, lane + reach))
            if direct:
                pixels = pixels[width:]
            tokens = dot_nn(pixels, merged_ref[s, :, columns]).reshape(WLAT - early, width, COLUMNS)
            for block, (within, _) in enumerate(groups):
                part = tokens[:, within].reshape(late_rows, COLUMNS).astype(BF16)
                tokens_refs[n][block * late_rows : (block + 1) * late_rows, columns] = part

        def mixing():
            for block, (_, at) in enumerate(groups):
                tokens = tokens_at(n, block, early, WLAT - early, columns)
                if direct:
                    tokens = jnp.concatenate([tokens_at(n, block, 0, early, columns), tokens], axis=0)
                pre_refs[n][at, columns] = dot_nn(mix_ref[...], tokens)

        return [embed, mixing]

    def pointwise(n, columns):
        s, first_line = n % samples, n // samples * WLAT

        def part(line, across, lanes):
            grads = [grad_ref[s, first_line + line + k, across, lanes].astype(F32) for k in range(pair)]
            mixed = []
            for block, (within, at) in enumerate(groups):
                if within.start < across.start or within.stop > across.stop:
                    continue
                at = pl.ds(at.start + line * group, pair * group)
                pre = pre_refs[n][at, lanes]
                cdf, pdf = normal_parts(pre)
                mixed.append(tokens_at(n, block, line, pair, lanes).astype(F32) + pre * cdf)
                first = within.start - across.start
                grad = jnp.concatenate([values[first : first + group] for values in grads], axis=0)
                grad_pre_refs[n][at, lanes] = (grad * (cdf + pre * pdf)).astype(BF16)
            for k in range(pair):
                parts = [values[k * group : (k + 1) * group] for values in mixed]
                mixed_refs[n][line + k, across, lanes] = jnp.concatenate(parts, axis=0).astype(BF16)

        return [
            functools.partial(part, line, slice(across, across + pair * group), slice(start, start + LANE))
            for line in range(0, WLAT, pair)
            for across in range(0, width, pair * group)
            for start in range(columns.start, columns.stop, LANE)
        ]

    def backward(n, columns):
        def spread():
            direct_part = grad_ref[n % samples, lines_of(n), :, columns].astype(F32)
            through = [
                dot_nn(mix_t_ref[...], grad_pre_refs[n][at, columns]).reshape(WLAT, group, COLUMNS)
                for _, at in groups
            ]
            total = jnp.concatenate(through, axis=1) + direct_part
            grad_tokens_refs[n][:, columns] = total.reshape(rows, COLUMNS).astype(BF16)

        def share():
            s = n % samples
            features = slice(s * depth, (s + 1) * depth)
            late = rows - turned_refs[0].shape[1]
            part = dot_nn(turned_refs[n // samples][features, :], grad_tokens_refs[n][late:, columns])
            if direct:
                part = part + dot_nn(early_turned_ref[features, :], grad_tokens_refs[n][:late, columns])
            total_ref[:, columns] = part if n == 0 else total_ref[:, columns] + part

        return [spread, share]

    units = [
        (n, slice(start, start + COLUMNS))
        for n in range(chunk_count)
        for start in range(0, feature_dim, COLUMNS)
    ]
    for step in forward(*units[0]):
        step()
    for i, unit in enumerate(units):
        n, columns = unit
        others = []
        if i + 1 < len(units):
            others += forward(*units[i + 1])
        if columns.start == 0 and n % samples == 0:
            others += turn(n)
        if i > 0:
            others += backward(*units[i - 1])
        lines = pointwise(*unit)
        for line, vector_step in enumerate(lines):
            vector_step()
            for step in others[line * len(others) // len(lines) : (line + 1) * len(others) // len(lines)]:
                step()
        if columns.stop == feature_dim:
            each = len(stores) // chunk_count
            for store in stores[n * each : (n + 1) * each]:
                store.start()
    for step in backward(*units[-1]):
        step()

    first, second = factor_shares(total_ref[...], up_ref, down_ref, level_ref)
    rank, channels = down_ref.shape
    columns = share_ref.shape[2]
    reps = feature_dim // columns
    folds = rank // (share_ref.shape[1] - rank)
    depth_rows, fold_lanes, row_share = rank // folds, columns // folds, channels // reps
    packed = jnp.zeros((depth_rows, feature_dim), F32)
    row, lane = iota2((channels, feature_dim), 0), iota2((1, feature_dim), 1)
    rep, lane = lane // columns, lane % columns
    for fold in range(folds):
        inside = lane - fold * fold_lanes
        target = jnp.where((inside >= 0) & (inside < row_share), inside + rep * row_share, -1)
        pick = jnp.where(row == target, 1.0, 0.0).astype(BF16)
        part = first[fold * depth_rows : (fold + 1) * depth_rows].astype(BF16)
        packed = packed + dot_nn(part, pick)
    payload = jnp.concatenate([second, packed], axis=0).astype(BF16)
    for slot in range(share_ref.shape[0]):
        at = slot % reps * columns
        share_ref[slot] = payload[:, at : at + columns]
    for store in stores:
        store.wait()


def mix_blocks(direct, arrived, merged, mix, mix_t, grad, up_through, down_t, level_weight, band_count, reps):
    samples, lat_rows, block_width, feature_dim = grad.shape
    width = block_width
    lanes = arrived[-1].shape[-1]
    early = EARLY if direct else 0
    turned_early = turned_whole(early, width)
    reach = merged.shape[1]
    rows = WLAT * width
    rank = down_t.shape[0]
    chunks = lat_rows // WLAT * samples
    share_shape = (band_count * reps, rank + rank // FOLDS, feature_dim // reps)
    flops = 2 * samples * lat_rows * block_width * feature_dim * (2 * reach + 2 * rows)
    vmem = pl.BlockSpec(memory_space=pltpu.VMEM)
    any_space = pl.BlockSpec(memory_space=pl.ANY)
    local = [*arrived, merged, mix, mix_t, up_through, down_t]
    return pl.pallas_call(
        lambda *refs: mix_kernel(direct, refs[: len(arrived)], *refs[len(arrived) :]),
        out_shape=[
            jax.ShapeDtypeStruct(grad.shape, BF16),
            jax.ShapeDtypeStruct(share_shape, BF16),
        ],
        in_specs=[vmem] * (len(local) + 2),
        out_specs=[any_space, vmem],
        scratch_shapes=[
            [pltpu.VMEM((lanes, rows - turned_early), BF16)] * (chunks // samples),
            [pltpu.VMEM((WLAT, width, feature_dim), BF16)] * chunks,
            [pltpu.VMEM((rows, feature_dim), F32)] * chunks,
            [pltpu.VMEM((rows - early * width, feature_dim), BF16)] * chunks,
            [pltpu.VMEM((rows, feature_dim), BF16)] * chunks,
            [pltpu.VMEM((rows, feature_dim), BF16)] * chunks,
            pltpu.VMEM((lanes // samples, feature_dim), F32),
            pltpu.SemaphoreType.DMA((chunks * WLAT,)),
        ],
        compiler_params=params(),
        cost_estimate=pl.CostEstimate(
            flops=flops,
            bytes_accessed=12 * 2**20,
            transcendentals=samples * lat_rows * block_width * feature_dim,
        ),
        name="mix_blocks",
    )(*local, grad, level_weight)


def sum_kernel(parts_ref, first_ref, second_ref):
    rank, row_share = first_ref.shape
    total = parts_ref[0].astype(F32)
    for n in range(1, parts_ref.shape[0]):
        total = total + parts_ref[n].astype(F32)
    second_ref[...] = total[:rank]
    depth_rows = total.shape[0] - rank
    for fold in range(rank // depth_rows):
        lane = fold * depth_rows * total.shape[1] // rank
        first_ref[fold * depth_rows : (fold + 1) * depth_rows, :] = total[rank:, lane : lane + row_share]


def sum_shares(shares, rank, row_share):
    parts = lax.all_to_all(shares, ("band", "rep"), split_axis=0, concat_axis=0, tiled=True)
    return pl.pallas_call(
        sum_kernel,
        out_shape=[
            jax.ShapeDtypeStruct((rank, row_share), F32),
            jax.ShapeDtypeStruct((rank, shares.shape[2]), F32),
        ],
        compiler_params=params(),
        name="sum_shares",
    )(parts)


def on_device(
    patches,
    variable_group_index,
    frozen_patch_weight,
    adapter_down,
    adapter_up,
    level_merge_weight,
    window_patch_mixer,
    column_block_owner,
    mixed_token_gradient,
):
    band_count, reps = lax.axis_size("band"), lax.axis_size("rep")
    samples, levels, channels, row_count, col_count = patches.shape
    feature_dim = frozen_patch_weight.shape[2]
    rank, col_share = adapter_up.shape
    row_share = adapter_down.shape[0]
    lat_rows = band_count * row_count
    block_width = col_count // band_count
    padded_width = round_up(block_width, SUB)
    group = 2 * WLON if block_width % (2 * WLON) == 0 else padded_width
    features = samples * levels * channels

    pixels = patches.reshape(features, col_count)
    pack_shape = (2, rank, round_up(max(row_share, col_share), LANE))
    direct = band_count == BANDS and lat_rows == WLAT and padded_width == block_width
    direct = direct and features % LANE == 0 and col_count % LANE == 0
    if direct:
        blocks, pack = send_blocks(
            pixels, column_block_owner, adapter_up, adapter_down.T, block_width, pack_shape
        )
        arrived, factors = exchange(blocks, pack)
    else:
        block_ids = jnp.arange(band_count, dtype=jnp.int32)
        inverse = jnp.sum(
            jnp.where(column_block_owner[None, :] == block_ids[:, None], block_ids[None, :], 0), axis=1
        )
        outgoing = jnp.take(pixels.T.reshape(band_count, block_width, features), inverse, axis=0)
        outgoing = jnp.pad(outgoing, ((0, 0), (0, padded_width - block_width), (0, 0)))
        arrived = [lax.all_to_all(outgoing, "band", split_axis=0, concat_axis=0, tiled=True)]
        pack = jnp.stack(
            [
                jnp.pad(array, ((0, 0), (0, pack_shape[2] - array.shape[1])))
                for array in (adapter_up, adapter_down.T)
            ]
        )
        factors = lax.all_gather(pack, "rep", axis=0, tiled=False)

    grad = mixed_token_gradient.reshape(samples, lat_rows, block_width, feature_dim)
    if padded_width != block_width:
        grad = jnp.pad(grad, ((0, 0), (0, 0), (0, padded_width - block_width), (0, 0)))
    merged, up_through, down_t, mix, mix_t, level_copy, grad_copy = prepare(
        direct,
        variable_group_index,
        frozen_patch_weight,
        factors,
        level_merge_weight,
        window_patch_mixer,
        grad,
        row_share,
        min(block_width, group),
        group,
    )
    if direct:
        arrived = [*embed_early(arrived[:EARLY], merged), *arrived[EARLY - 1 :]]
    mixed, shares = mix_blocks(
        direct, arrived, merged, mix, mix_t, grad_copy, up_through, down_t, level_copy, band_count, reps
    )
    if padded_width != block_width:
        mixed = mixed[:, :, :block_width]
    first_t, second = sum_shares(shares, rank, row_share)
    return mixed.reshape(mixed_token_gradient.shape), first_t.T, second


def solution(mesh):
    in_specs = (
        P("rep", None, None, "band", None),
        P(),
        P(),
        P("rep", None),
        P(None, "rep"),
        P(),
        P(),
        P(),
        P("rep", "band", None, None, None),
    )
    out_specs = (P("rep", "band", None, None, None), P("rep", None), P(None, "rep"))
    return jax.shard_map(
        on_device, mesh=mesh, in_specs=in_specs, out_specs=out_specs, check_vma=False
    )
```

```python
import functools

import jax
import jax.numpy as jnp
from jax import lax
from jax.experimental import pallas as pl
from jax.experimental.pallas import tpu as pltpu
from jax.sharding import PartitionSpec as P

WLAT = 8
WLON = 12
LANE = 128
SUB = 16
VMEM_LIMIT = 24 * 1024 * 1024
BANDS = 8
ORDER = (0, 4, 1, 5, 2, 6, 7, 3)
EARLY = 6
SLOTS = (0, 1, 4, 5, 6, 2, 3, 7)
FOLDS = 2
COLUMNS = 512
BF16 = jnp.bfloat16
F32 = jnp.float32


def round_up(value, step):
    return -(-value // step) * step


def dot_nn(a, b):
    return lax.dot_general(a, b, (((1,), (0,)), ((), ())), preferred_element_type=F32)


def dot_nt(a, b):
    return lax.dot_general(a, b, (((1,), (1,)), ((), ())), preferred_element_type=F32)


def dot_tn(a, b):
    return lax.dot_general(a, b, (((0,), (0,)), ((), ())), preferred_element_type=F32)


def split_hi_lo(values):
    high = values.astype(BF16)
    low = (values - high.astype(F32)).astype(BF16)
    return high, low


def iota2(shape, axis):
    return lax.broadcasted_iota(jnp.int32, shape, axis)


def params(**extra):
    return pltpu.CompilerParams(vmem_limit_bytes=VMEM_LIMIT, **extra)


def in_hbm(values):
    return pltpu.with_memory_space_constraint(values, pltpu.HBM)


def swap(values, axis, distance):
    count = lax.axis_size(axis)
    return lax.ppermute(values, axis, [(source, source ^ distance) for source in range(count)])


def send_kernel(owner_hbm_ref, up_hbm_ref, down_hbm_ref, x_hbm_ref, *refs):
    block_refs, pack_ref, scratch = refs[:-8], refs[-8], refs[-7:]
    owner_ref, up_ref, down_ref, x_ref, turned_ref, small_sems, x_sems = scratch
    width = block_refs[0].shape[0]
    features, columns = x_ref.shape
    small = [
        pltpu.make_async_copy(source, target, small_sems.at[n])
        for n, (source, target) in enumerate(
            [(owner_hbm_ref, owner_ref), (up_hbm_ref, up_ref), (down_hbm_ref, down_ref)]
        )
    ]
    parts = [slice(start, start + LANE) for start in range(0, features, LANE)]
    large = [
        pltpu.make_async_copy(x_hbm_ref.at[part, :], x_ref.at[part, :], x_sems.at[n])
        for n, part in enumerate(parts)
    ]
    for copy in large + small:
        copy.start()
    for copy, part in zip(large, parts):
        copy.wait()
        for start in range(0, columns, LANE):
            at = slice(start, start + LANE)
            turned_ref[at, part] = x_ref[part, at].T
    for copy in small:
        copy.wait()
    pack_ref[...] = jnp.zeros_like(pack_ref)
    pack_ref[0, :, : up_ref.shape[1]] = up_ref[...]
    pack_ref[1, :, : down_ref.shape[1]] = down_ref[...]
    me = lax.axis_index("band")
    for distance, block_ref in zip(ORDER, block_refs):
        target = jnp.bitwise_xor(me, distance)
        block = 0
        for j in range(1, owner_ref.shape[0]):
            block = jnp.where(owner_ref[j] == target, j, block)
        block_ref[...] = turned_ref[pl.ds(pl.multiple_of(block * width, SUB), width), :]


def send_blocks(pixels, owner, up, down_t, width, pack_shape):
    features, columns = pixels.shape
    any_space = pl.BlockSpec(memory_space=pl.ANY)
    vmem = pl.BlockSpec(memory_space=pltpu.VMEM)
    blocks = [(width, features)] * BANDS
    *blocks, pack = pl.pallas_call(
        send_kernel,
        out_shape=[jax.ShapeDtypeStruct(shape, BF16) for shape in [*blocks, pack_shape]],
        in_specs=[any_space] * 4,
        out_specs=[vmem] * (len(blocks) + 1),
        scratch_shapes=[
            pltpu.SMEM(owner.shape, jnp.int32),
            pltpu.VMEM(up.shape, BF16),
            pltpu.VMEM(down_t.shape, BF16),
            pltpu.VMEM((features, columns), BF16),
            pltpu.VMEM((columns, features), BF16),
            pltpu.SemaphoreType.DMA((3,)),
            pltpu.SemaphoreType.DMA((features // LANE,)),
        ],
        compiler_params=params(),
        name="send_blocks",
    )(in_hbm(owner), in_hbm(up), in_hbm(down_t), in_hbm(pixels))
    return blocks, pack


def exchange(blocks, pack):
    arrived = dict(zip(ORDER, blocks))
    for distance in (1, 4, 5, 6, 2):
        arrived[distance] = swap(arrived[distance], "band", distance)
    arrived[1], pack = lax.optimization_barrier((arrived[1], pack))
    factors = lax.all_gather(pack, "rep", axis=0, tiled=False)
    arrived[7], factors = lax.optimization_barrier((arrived[7], factors))
    arrived[7] = swap(arrived[7], "band", 7)
    arrived[3], factors = lax.optimization_barrier((arrived[3], factors))
    arrived[3] = swap(arrived[3], "band", 3)
    return [arrived[distance] for distance in SLOTS], factors


def expand_table(table, rows, half_width_padded, half_width, flip, transpose):
    position = iota2((rows, WLAT * WLON), 0)
    line, col = position // half_width_padded, position % half_width_padded
    if flip is not None:
        distance = sum(jnp.where(line == slot, far, 0) for slot, far in enumerate(SLOTS))
        line = jnp.bitwise_xor(distance, flip)
    target = iota2((rows, WLAT * WLON), 1)
    pick = jnp.where((target == line * WLON + col % WLON) & (col < half_width), 1.0, 0.0).astype(BF16)
    left = (dot_nt if transpose else dot_nn)(pick, table).astype(BF16)
    full = dot_nt(left, pick)
    row_window = (iota2((rows, 1), 0) % half_width_padded) // WLON
    col_window = (iota2((1, rows), 1) % half_width_padded) // WLON
    return jnp.where(row_window == col_window, full, 0.0).astype(BF16)


def prep_kernel(
    direct,
    row_share,
    half_width,
    half_width_padded,
    group_hbm_ref,
    level_hbm_ref,
    grad_hbm_ref,
    frozen_ref,
    factors_ref,
    mixer_ref,
    merged_ref,
    up_ref,
    down_ref,
    mix_ref,
    mix_t_ref,
    level_ref,
    grad_ref,
    group_ref,
    sems,
):
    pairs = [(group_hbm_ref, group_ref), (level_hbm_ref, level_ref)]
    flip = lax.axis_index("band") if direct else None
    if direct:
        pairs += [
            (grad_hbm_ref.at[:, jnp.bitwise_xor(flip, far)], grad_ref.at[:, slot])
            for slot, far in enumerate(SLOTS)
        ]
    else:
        pairs.append((grad_hbm_ref, grad_ref))
    loads = [
        pltpu.make_async_copy(source, target, sems.at[n]) for n, (source, target) in enumerate(pairs)
    ]
    for load in loads:
        load.start()
    rows = mix_ref.shape[0]
    mix_ref[...] = expand_table(mixer_ref[...], rows, half_width_padded, half_width, flip, False)
    mix_t_ref[...] = expand_table(mixer_ref[...], rows, half_width_padded, half_width, flip, True)
    reps, _, rank, share = factors_ref.shape
    levels = level_ref.shape[0]
    variables = group_ref.shape[0]
    channels = variables * frozen_ref.shape[1]
    up = jnp.concatenate([factors_ref[r, 0] for r in range(reps)], axis=1)
    source, target = iota2((share, channels), 0), iota2((share, channels), 1)
    down_t = jnp.zeros((rank, channels), F32)
    for r in range(reps):
        place = jnp.where((target == source + r * row_share) & (source < row_share), 1.0, 0.0)
        down_t = down_t + dot_nn(factors_ref[r, 1], place.astype(BF16))
    down_t = down_t.astype(BF16)
    down_ref[...] = down_t
    loads[0].wait()
    base = jnp.concatenate([frozen_ref[group_ref[v]].astype(F32) for v in range(variables)], axis=0)
    merged = (base + dot_tn(down_t, up)).astype(BF16)
    stacked = jnp.concatenate([merged, up], axis=0)
    merged_ref[...] = jnp.zeros_like(merged_ref)
    loads[1].wait()
    for level in range(levels):
        through = dot_nn(stacked, level_ref[level])
        weights = through[:channels].astype(BF16)
        for s in range(merged_ref.shape[0]):
            offset = (s * levels * channels) % LANE + level * channels
            merged_ref[s, offset : offset + channels, :] = weights
        up_high, up_low = split_hi_lo(through[channels:])
        up_ref[level, :rank, :] = up_high
        up_ref[level, rank:, :] = up_low
    for load in loads[2:]:
        load.wait()


def prepare(direct, groups, frozen, factors, level_weight, mixer, grad, row_share, half_width, half_width_padded):
    reps, _, rank, _ = factors.shape
    levels, feature_dim, _ = level_weight.shape
    channels = groups.shape[0] * frozen.shape[1]
    reach = round_up(levels * channels + LANE // 2, LANE)
    rows = WLAT * half_width_padded
    vmem = pl.BlockSpec(memory_space=pltpu.VMEM)
    flops = 2 * levels * (channels + rank) * feature_dim * feature_dim + 4 * rows * rows * WLAT * WLON
    shapes = [
        (grad.shape[0], reach, feature_dim),
        (levels, 2 * rank, feature_dim),
        (rank, channels),
        (rows, rows),
        (rows, rows),
        level_weight.shape,
        grad.shape,
    ]
    return pl.pallas_call(
        functools.partial(prep_kernel, direct, row_share, half_width, half_width_padded),
        out_shape=[jax.ShapeDtypeStruct(shape, BF16) for shape in shapes],
        in_specs=[pl.BlockSpec(memory_space=pl.ANY)] * 3 + [vmem] * 3,
        out_specs=[vmem] * len(shapes),
        scratch_shapes=[pltpu.SMEM(groups.shape, jnp.int32), pltpu.SemaphoreType.DMA((2 + WLAT,))],
        compiler_params=params(),
        cost_estimate=pl.CostEstimate(flops=flops, bytes_accessed=6 * 2**20, transcendentals=0),
        name="prepare",
    )(in_hbm(groups), in_hbm(level_weight), in_hbm(grad), in_hbm(frozen), factors, in_hbm(mixer))


def normal_parts(values):
    cdf = 0.5 + 0.5 * lax.erf(values * 0.7071067811865476)
    return cdf, 0.3989422804014327 * jnp.exp2(values * values * -0.7213475204444817)


def factor_shares(total, up_ref, down_ref, level_ref):
    levels, two_rank, feature_dim = up_ref.shape
    rank, channels = down_ref.shape
    high, low = split_hi_lo(total)
    down = down_ref[...]
    first = jnp.zeros((rank, channels), F32)
    second = jnp.zeros((two_rank, feature_dim), F32)
    for level in range(levels):
        at = slice(level * channels, (level + 1) * channels)
        both = dot_nt(up_ref[level], high[at])
        first = first + both[:rank] + both[rank:] + dot_nt(up_ref[level, :rank, :], low[at])
        through = dot_nn(down, high[at]) + dot_nn(down, low[at])
        through = jnp.concatenate(split_hi_lo(through), axis=0)
        second = second + dot_nt(through, level_ref[level])
    return first, second[:rank] + second[rank:]


def turned_whole(lines, width):
    return lines * width // LANE * LANE


def embed_kernel(*refs):
    piece_refs, (merged_ref, tokens_ref, turned_ref) = refs[:-3], refs[-3:]
    samples, reach, feature_dim = merged_ref.shape
    width, features = piece_refs[0].shape
    depth = features // samples
    group = 2 * WLON
    rows = len(piece_refs) * group
    positions = turned_ref.shape[1]
    for s in range(samples):
        lane = s * depth // LANE * LANE
        pixels = jnp.concatenate([piece_ref[:, lane : lane + reach] for piece_ref in piece_refs], axis=0)
        for start in range(0, feature_dim, COLUMNS):
            columns = slice(start, start + COLUMNS)
            tokens = dot_nn(pixels, merged_ref[s, :, columns]).reshape(len(piece_refs), width, COLUMNS)
            for n in range(width // group):
                part = tokens[:, n * group : (n + 1) * group].reshape(rows, COLUMNS)
                tokens_ref[s, n * rows : (n + 1) * rows, columns] = part.astype(BF16)
    for start in range(0, features, LANE):
        lanes = slice(start, start + LANE)
        pixels = jnp.concatenate([piece_ref[:, lanes] for piece_ref in piece_refs], axis=0)
        turned_ref[lanes, :] = pixels[:positions].T


def embed_early(pieces, merged):
    samples, _, feature_dim = merged.shape
    width, features = pieces[0].shape
    count = len(pieces) * width
    return pl.pallas_call(
        embed_kernel,
        out_shape=[
            jax.ShapeDtypeStruct((samples, count, feature_dim), BF16),
            jax.ShapeDtypeStruct((features, turned_whole(len(pieces), width)), BF16),
        ],
        in_specs=[pl.BlockSpec(memory_space=pltpu.VMEM)] * (len(pieces) + 1),
        out_specs=[pl.BlockSpec(memory_space=pltpu.VMEM)] * 2,
        compiler_params=params(),
        cost_estimate=pl.CostEstimate(
            flops=2 * count * features * feature_dim, bytes_accessed=4 * 2**20, transcendentals=0
        ),
        name="embed_early",
    )(*pieces, merged)


def mix_kernel(
    direct,
    piece_refs,
    merged_ref,
    mix_ref,
    mix_t_ref,
    up_ref,
    down_ref,
    grad_ref,
    level_ref,
    mixed_hbm_ref,
    share_ref,
    turned_refs,
    mixed_refs,
    pre_refs,
    tokens_refs,
    grad_pre_refs,
    grad_tokens_refs,
    total_ref,
    mixed_sems,
):
    samples, reach, feature_dim = merged_ref.shape
    chunk_count, (_, width, _) = len(mixed_refs), mixed_refs[0].shape
    depth = piece_refs[-1].shape[-1] // samples
    rows = WLAT * width

    group_rows = mix_ref.shape[0]
    group = group_rows // WLAT
    groups = [
        (slice(start, start + group), slice(start * WLAT, start * WLAT + group_rows))
        for start in range(0, width, group)
    ]
    pair = 1 if group % SUB == 0 else 2

    early = EARLY if direct else 0
    early_rows, late_rows = early * group, (WLAT - early) * group
    if direct:
        early_tokens_ref, early_turned_ref, *line_refs = piece_refs
        early_positions = early_turned_ref.shape[1]

    def lines_of(n):
        return pl.ds(n // samples * WLAT, WLAT)

    if direct:
        me = lax.axis_index("band")
        targets = [
            (mixed_refs[n].at[slot], mixed_hbm_ref.at[n, jnp.bitwise_xor(me, far)])
            for n in range(chunk_count)
            for slot, far in enumerate(SLOTS)
        ]
    else:
        targets = [
            (mixed_refs[n], mixed_hbm_ref.at[n % samples, lines_of(n)]) for n in range(chunk_count)
        ]
    stores = [
        pltpu.make_async_copy(source, target, mixed_sems.at[n]) for n, (source, target) in enumerate(targets)
    ]

    def pixels_of(n, lanes):
        if direct:
            return jnp.concatenate([line_ref[:, lanes] for line_ref in line_refs], axis=0)
        return piece_refs[0][lines_of(n), :, lanes].reshape(rows, lanes.stop - lanes.start)

    def turn(n):
        def part(lanes):
            pixels = pixels_of(n, lanes)
            if direct:
                before = early_positions - (early - 1) * width
                pixels = pixels[before:]
            turned_refs[n // samples][lanes, :] = pixels.T

        starts = range(0, samples * depth, LANE)
        return [functools.partial(part, slice(start, start + LANE)) for start in starts]

    def tokens_at(n, block, line, count, columns):
        if line < early:
            at = pl.ds(block * early_rows + line * group, count * group)
            return early_tokens_ref[n % samples, at, columns]
        return tokens_refs[n][pl.ds(block * late_rows + (line - early) * group, count * group), columns]

    def forward(n, columns):
        s = n % samples
        lane = s * depth // LANE * LANE

        def embed():
            pixels = pixels_of(n, slice(lane, lane + reach))
            if direct:
                pixels = pixels[width:]
            tokens = dot_nn(pixels, merged_ref[s, :, columns]).reshape(WLAT - early, width, COLUMNS)
            for block, (within, _) in enumerate(groups):
                part = tokens[:, within].reshape(late_rows, COLUMNS).astype(BF16)
                tokens_refs[n][block * late_rows : (block + 1) * late_rows, columns] = part

        def mixing(block, at):
            tokens = tokens_at(n, block, early, WLAT - early, columns)
            if direct:
                tokens = jnp.concatenate([tokens_at(n, block, 0, early, columns), tokens], axis=0)
            pre_refs[n][at, columns] = dot_nn(mix_ref[...], tokens)

        return [embed] + [functools.partial(mixing, block, at) for block, (_, at) in enumerate(groups)]

    def pointwise(n, columns):
        s, first_line = n % samples, n // samples * WLAT

        def part(line, across, lanes):
            grads = [grad_ref[s, first_line + line + k, across, lanes].astype(F32) for k in range(pair)]
            mixed = []
            for block, (within, at) in enumerate(groups):
                if within.start < across.start or within.stop > across.stop:
                    continue
                at = pl.ds(at.start + line * group, pair * group)
                pre = pre_refs[n][at, lanes]
                cdf, pdf = normal_parts(pre)
                mixed.append(tokens_at(n, block, line, pair, lanes).astype(F32) + pre * cdf)
                first = within.start - across.start
                grad = jnp.concatenate([values[first : first + group] for values in grads], axis=0)
                grad_pre_refs[n][at, lanes] = (grad * (cdf + pre * pdf)).astype(BF16)
            for k in range(pair):
                parts = [values[k * group : (k + 1) * group] for values in mixed]
                mixed_refs[n][line + k, across, lanes] = jnp.concatenate(parts, axis=0).astype(BF16)

        return [
            functools.partial(part, line, slice(across, across + pair * group), slice(start, start + LANE))
            for line in range(0, WLAT, pair)
            for across in range(0, width, pair * group)
            for start in range(columns.start, columns.stop, LANE)
        ]

    def backward(n, columns):
        def spread():
            direct_part = grad_ref[n % samples, lines_of(n), :, columns].astype(F32)
            through = [
                dot_nn(mix_t_ref[...], grad_pre_refs[n][at, columns]).reshape(WLAT, group, COLUMNS)
                for _, at in groups
            ]
            total = jnp.concatenate(through, axis=1) + direct_part
            grad_tokens_refs[n][:, columns] = total.reshape(rows, COLUMNS).astype(BF16)

        def share():
            s = n % samples
            features = slice(s * depth, (s + 1) * depth)
            late = rows - turned_refs[0].shape[1]
            part = dot_nn(turned_refs[n // samples][features, :], grad_tokens_refs[n][late:, columns])
            if direct:
                part = part + dot_nn(early_turned_ref[features, :], grad_tokens_refs[n][:late, columns])
            total_ref[:, columns] = part if n == 0 else total_ref[:, columns] + part

        return [spread, share]

    units = [
        (n, slice(start, start + COLUMNS))
        for n in range(chunk_count)
        for start in range(0, feature_dim, COLUMNS)
    ]
    for step in forward(*units[0]):
        step()
    for i, unit in enumerate(units):
        n, columns = unit
        others = []
        if i + 1 < len(units):
            others += forward(*units[i + 1])
        if columns.start == 0 and n % samples == 0:
            others += turn(n)
        if i > 0:
            others += backward(*units[i - 1])
        lines = pointwise(*unit)
        for line, vector_step in enumerate(lines):
            vector_step()
            for step in others[line * len(others) // len(lines) : (line + 1) * len(others) // len(lines)]:
                step()
        if columns.stop == feature_dim:
            each = len(stores) // chunk_count
            for store in stores[n * each : (n + 1) * each]:
                store.start()
    for step in backward(*units[-1]):
        step()

    first, second = factor_shares(total_ref[...], up_ref, down_ref, level_ref)
    rank, channels = down_ref.shape
    columns = share_ref.shape[2]
    reps = feature_dim // columns
    folds = rank // (share_ref.shape[1] - rank)
    depth_rows, fold_lanes, row_share = rank // folds, columns // folds, channels // reps
    packed = jnp.zeros((depth_rows, feature_dim), F32)
    row, lane = iota2((channels, feature_dim), 0), iota2((1, feature_dim), 1)
    rep, lane = lane // columns, lane % columns
    for fold in range(folds):
        inside = lane - fold * fold_lanes
        target = jnp.where((inside >= 0) & (inside < row_share), inside + rep * row_share, -1)
        pick = jnp.where(row == target, 1.0, 0.0).astype(BF16)
        part = first[fold * depth_rows : (fold + 1) * depth_rows].astype(BF16)
        packed = packed + dot_nn(part, pick)
    payload = jnp.concatenate([second, packed], axis=0).astype(BF16)
    for slot in range(share_ref.shape[0]):
        at = slot % reps * columns
        share_ref[slot] = payload[:, at : at + columns]
    for store in stores:
        store.wait()


def mix_blocks(direct, arrived, merged, mix, mix_t, grad, up_through, down_t, level_weight, band_count, reps):
    samples, lat_rows, block_width, feature_dim = grad.shape
    width = block_width
    lanes = arrived[-1].shape[-1]
    early = EARLY if direct else 0
    turned_early = turned_whole(early, width)
    reach = merged.shape[1]
    rows = WLAT * width
    rank = down_t.shape[0]
    chunks = lat_rows // WLAT * samples
    share_shape = (band_count * reps, rank + rank // FOLDS, feature_dim // reps)
    flops = 2 * samples * lat_rows * block_width * feature_dim * (2 * reach + 2 * rows)
    vmem = pl.BlockSpec(memory_space=pltpu.VMEM)
    any_space = pl.BlockSpec(memory_space=pl.ANY)
    local = [*arrived, merged, mix, mix_t, up_through, down_t]
    return pl.pallas_call(
        lambda *refs: mix_kernel(direct, refs[: len(arrived)], *refs[len(arrived) :]),
        out_shape=[
            jax.ShapeDtypeStruct(grad.shape, BF16),
            jax.ShapeDtypeStruct(share_shape, BF16),
        ],
        in_specs=[vmem] * (len(local) + 2),
        out_specs=[any_space, vmem],
        scratch_shapes=[
            [pltpu.VMEM((lanes, rows - turned_early), BF16)] * (chunks // samples),
            [pltpu.VMEM((WLAT, width, feature_dim), BF16)] * chunks,
            [pltpu.VMEM((rows, feature_dim), F32)] * chunks,
            [pltpu.VMEM((rows - early * width, feature_dim), BF16)] * chunks,
            [pltpu.VMEM((rows, feature_dim), BF16)] * chunks,
            [pltpu.VMEM((rows, feature_dim), BF16)] * chunks,
            pltpu.VMEM((lanes // samples, feature_dim), F32),
            pltpu.SemaphoreType.DMA((chunks * WLAT,)),
        ],
        compiler_params=params(),
        cost_estimate=pl.CostEstimate(
            flops=flops,
            bytes_accessed=12 * 2**20,
            transcendentals=samples * lat_rows * block_width * feature_dim,
        ),
        name="mix_blocks",
    )(*local, grad, level_weight)


def sum_kernel(parts_ref, first_ref, second_ref):
    rank, row_share = first_ref.shape
    total = parts_ref[0].astype(F32)
    for n in range(1, parts_ref.shape[0]):
        total = total + parts_ref[n].astype(F32)
    second_ref[...] = total[:rank]
    depth_rows = total.shape[0] - rank
    for fold in range(rank // depth_rows):
        lane = fold * depth_rows * total.shape[1] // rank
        first_ref[fold * depth_rows : (fold + 1) * depth_rows, :] = total[rank:, lane : lane + row_share]


def sum_shares(shares, rank, row_share):
    parts = lax.all_to_all(shares, ("band", "rep"), split_axis=0, concat_axis=0, tiled=True)
    return pl.pallas_call(
        sum_kernel,
        out_shape=[
            jax.ShapeDtypeStruct((rank, row_share), F32),
            jax.ShapeDtypeStruct((rank, shares.shape[2]), F32),
        ],
        compiler_params=params(),
        name="sum_shares",
    )(parts)


def on_device(
    patches,
    variable_group_index,
    frozen_patch_weight,
    adapter_down,
    adapter_up,
    level_merge_weight,
    window_patch_mixer,
    column_block_owner,
    mixed_token_gradient,
):
    band_count, reps = lax.axis_size("band"), lax.axis_size("rep")
    samples, levels, channels, row_count, col_count = patches.shape
    feature_dim = frozen_patch_weight.shape[2]
    rank, col_share = adapter_up.shape
    row_share = adapter_down.shape[0]
    lat_rows = band_count * row_count
    block_width = col_count // band_count
    padded_width = round_up(block_width, SUB)
    group = 2 * WLON if block_width % (2 * WLON) == 0 else padded_width
    features = samples * levels * channels

    pixels = patches.reshape(features, col_count)
    pack_shape = (2, rank, round_up(max(row_share, col_share), LANE))
    direct = band_count == BANDS and lat_rows == WLAT and padded_width == block_width
    direct = direct and features % LANE == 0 and col_count % LANE == 0
    if direct:
        blocks, pack = send_blocks(
            pixels, column_block_owner, adapter_up, adapter_down.T, block_width, pack_shape
        )
        arrived, factors = exchange(blocks, pack)
    else:
        block_ids = jnp.arange(band_count, dtype=jnp.int32)
        inverse = jnp.sum(
            jnp.where(column_block_owner[None, :] == block_ids[:, None], block_ids[None, :], 0), axis=1
        )
        outgoing = jnp.take(pixels.T.reshape(band_count, block_width, features), inverse, axis=0)
        outgoing = jnp.pad(outgoing, ((0, 0), (0, padded_width - block_width), (0, 0)))
        arrived = [lax.all_to_all(outgoing, "band", split_axis=0, concat_axis=0, tiled=True)]
        pack = jnp.stack(
            [
                jnp.pad(array, ((0, 0), (0, pack_shape[2] - array.shape[1])))
                for array in (adapter_up, adapter_down.T)
            ]
        )
        factors = lax.all_gather(pack, "rep", axis=0, tiled=False)

    grad = mixed_token_gradient.reshape(samples, lat_rows, block_width, feature_dim)
    if padded_width != block_width:
        grad = jnp.pad(grad, ((0, 0), (0, 0), (0, padded_width - block_width), (0, 0)))
    merged, up_through, down_t, mix, mix_t, level_copy, grad_copy = prepare(
        direct,
        variable_group_index,
        frozen_patch_weight,
        factors,
        level_merge_weight,
        window_patch_mixer,
        grad,
        row_share,
        min(block_width, group),
        group,
    )
    if direct:
        arrived = [*embed_early(arrived[:EARLY], merged), *arrived[EARLY - 1 :]]
    mixed, shares = mix_blocks(
        direct, arrived, merged, mix, mix_t, grad_copy, up_through, down_t, level_copy, band_count, reps
    )
    if padded_width != block_width:
        mixed = mixed[:, :, :block_width]
    first_t, second = sum_shares(shares, rank, row_share)
    return mixed.reshape(mixed_token_gradient.shape), first_t.T, second


def solution(mesh):
    in_specs = (
        P("rep", None, None, "band", None),
        P(),
        P(),
        P("rep", None),
        P(None, "rep"),
        P(),
        P(),
        P(),
        P("rep", "band", None, None, None),
    )
    out_specs = (P("rep", "band", None, None, None), P("rep", None), P(None, "rep"))
    return jax.shard_map(
        on_device, mesh=mesh, in_specs=in_specs, out_specs=out_specs, check_vma=False
    )
```

```python
import functools

import jax
import jax.numpy as jnp
from jax import lax
from jax.experimental import pallas as pl
from jax.experimental.pallas import tpu as pltpu
from jax.sharding import PartitionSpec as P

WLAT = 8
WLON = 12
LANE = 128
SUB = 16
VMEM_LIMIT = 24 * 1024 * 1024
BANDS = 8
ORDER = (0, 4, 1, 5, 2, 6, 7, 3)
EARLY = 6
SLOTS = (0, 1, 4, 5, 6, 2, 3, 7)
FOLDS = 2
COLUMNS = 256
BF16 = jnp.bfloat16
F32 = jnp.float32


def round_up(value, step):
    return -(-value // step) * step


def dot_nn(a, b):
    return lax.dot_general(a, b, (((1,), (0,)), ((), ())), preferred_element_type=F32)


def dot_nt(a, b):
    return lax.dot_general(a, b, (((1,), (1,)), ((), ())), preferred_element_type=F32)


def dot_tn(a, b):
    return lax.dot_general(a, b, (((0,), (0,)), ((), ())), preferred_element_type=F32)


def split_hi_lo(values):
    high = values.astype(BF16)
    low = (values - high.astype(F32)).astype(BF16)
    return high, low


def iota2(shape, axis):
    return lax.broadcasted_iota(jnp.int32, shape, axis)


def params(**extra):
    return pltpu.CompilerParams(vmem_limit_bytes=VMEM_LIMIT, **extra)


def in_hbm(values):
    return pltpu.with_memory_space_constraint(values, pltpu.HBM)


def swap(values, axis, distance):
    count = lax.axis_size(axis)
    return lax.ppermute(values, axis, [(source, source ^ distance) for source in range(count)])


def send_kernel(owner_hbm_ref, up_hbm_ref, down_hbm_ref, x_hbm_ref, *refs):
    block_refs, pack_ref, scratch = refs[:-8], refs[-8], refs[-7:]
    owner_ref, up_ref, down_ref, x_ref, turned_ref, small_sems, x_sems = scratch
    width = block_refs[0].shape[0]
    features, columns = x_ref.shape
    small = [
        pltpu.make_async_copy(source, target, small_sems.at[n])
        for n, (source, target) in enumerate(
            [(owner_hbm_ref, owner_ref), (up_hbm_ref, up_ref), (down_hbm_ref, down_ref)]
        )
    ]
    parts = [slice(start, start + LANE) for start in range(0, features, LANE)]
    large = [
        pltpu.make_async_copy(x_hbm_ref.at[part, :], x_ref.at[part, :], x_sems.at[n])
        for n, part in enumerate(parts)
    ]
    for copy in large + small:
        copy.start()
    for copy, part in zip(large, parts):
        copy.wait()
        for start in range(0, columns, LANE):
            at = slice(start, start + LANE)
            turned_ref[at, part] = x_ref[part, at].T
    for copy in small:
        copy.wait()
    pack_ref[...] = jnp.zeros_like(pack_ref)
    pack_ref[0, :, : up_ref.shape[1]] = up_ref[...]
    pack_ref[1, :, : down_ref.shape[1]] = down_ref[...]
    me = lax.axis_index("band")
    for distance, block_ref in zip(ORDER, block_refs):
        target = jnp.bitwise_xor(me, distance)
        block = 0
        for j in range(1, owner_ref.shape[0]):
            block = jnp.where(owner_ref[j] == target, j, block)
        block_ref[...] = turned_ref[pl.ds(pl.multiple_of(block * width, SUB), width), :]


def send_blocks(pixels, owner, up, down_t, width, pack_shape):
    features, columns = pixels.shape
    any_space = pl.BlockSpec(memory_space=pl.ANY)
    vmem = pl.BlockSpec(memory_space=pltpu.VMEM)
    blocks = [(width, features)] * BANDS
    *blocks, pack = pl.pallas_call(
        send_kernel,
        out_shape=[jax.ShapeDtypeStruct(shape, BF16) for shape in [*blocks, pack_shape]],
        in_specs=[any_space] * 4,
        out_specs=[vmem] * (len(blocks) + 1),
        scratch_shapes=[
            pltpu.SMEM(owner.shape, jnp.int32),
            pltpu.VMEM(up.shape, BF16),
            pltpu.VMEM(down_t.shape, BF16),
            pltpu.VMEM((features, columns), BF16),
            pltpu.VMEM((columns, features), BF16),
            pltpu.SemaphoreType.DMA((3,)),
            pltpu.SemaphoreType.DMA((features // LANE,)),
        ],
        compiler_params=params(),
        name="send_blocks",
    )(in_hbm(owner), in_hbm(up), in_hbm(down_t), in_hbm(pixels))
    return blocks, pack


def exchange(blocks, pack):
    arrived = dict(zip(ORDER, blocks))
    for distance in (1, 4, 5, 6, 2):
        arrived[distance] = swap(arrived[distance], "band", distance)
    arrived[1], pack = lax.optimization_barrier((arrived[1], pack))
    factors = lax.all_gather(pack, "rep", axis=0, tiled=False)
    arrived[7], factors = lax.optimization_barrier((arrived[7], factors))
    arrived[7] = swap(arrived[7], "band", 7)
    arrived[3], factors = lax.optimization_barrier((arrived[3], factors))
    arrived[3] = swap(arrived[3], "band", 3)
    return [arrived[distance] for distance in SLOTS], factors


def expand_table(table, rows, half_width_padded, half_width, flip, transpose):
    position = iota2((rows, WLAT * WLON), 0)
    line, col = position // half_width_padded, position % half_width_padded
    if flip is not None:
        distance = sum(jnp.where(line == slot, far, 0) for slot, far in enumerate(SLOTS))
        line = jnp.bitwise_xor(distance, flip)
    target = iota2((rows, WLAT * WLON), 1)
    pick = jnp.where((target == line * WLON + col % WLON) & (col < half_width), 1.0, 0.0).astype(BF16)
    left = (dot_nt if transpose else dot_nn)(pick, table).astype(BF16)
    full = dot_nt(left, pick)
    row_window = (iota2((rows, 1), 0) % half_width_padded) // WLON
    col_window = (iota2((1, rows), 1) % half_width_padded) // WLON
    return jnp.where(row_window == col_window, full, 0.0).astype(BF16)


def prep_kernel(
    direct,
    row_share,
    half_width,
    half_width_padded,
    group_hbm_ref,
    level_hbm_ref,
    grad_hbm_ref,
    frozen_ref,
    factors_ref,
    mixer_ref,
    merged_ref,
    up_ref,
    down_ref,
    mix_ref,
    mix_t_ref,
    level_ref,
    grad_ref,
    group_ref,
    sems,
):
    pairs = [(group_hbm_ref, group_ref), (level_hbm_ref, level_ref)]
    flip = lax.axis_index("band") if direct else None
    if direct:
        pairs += [
            (grad_hbm_ref.at[:, jnp.bitwise_xor(flip, far)], grad_ref.at[:, slot])
            for slot, far in enumerate(SLOTS)
        ]
    else:
        pairs.append((grad_hbm_ref, grad_ref))
    loads = [
        pltpu.make_async_copy(source, target, sems.at[n]) for n, (source, target) in enumerate(pairs)
    ]
    for load in loads:
        load.start()
    rows = mix_ref.shape[0]
    mix_ref[...] = expand_table(mixer_ref[...], rows, half_width_padded, half_width, flip, False)
    mix_t_ref[...] = expand_table(mixer_ref[...], rows, half_width_padded, half_width, flip, True)
    reps, _, rank, share = factors_ref.shape
    levels = level_ref.shape[0]
    variables = group_ref.shape[0]
    channels = variables * frozen_ref.shape[1]
    up = jnp.concatenate([factors_ref[r, 0] for r in range(reps)], axis=1)
    source, target = iota2((share, channels), 0), iota2((share, channels), 1)
    down_t = jnp.zeros((rank, channels), F32)
    for r in range(reps):
        place = jnp.where((target == source + r * row_share) & (source < row_share), 1.0, 0.0)
        down_t = down_t + dot_nn(factors_ref[r, 1], place.astype(BF16))
    down_t = down_t.astype(BF16)
    down_ref[...] = down_t
    loads[0].wait()
    base = jnp.concatenate([frozen_ref[group_ref[v]].astype(F32) for v in range(variables)], axis=0)
    merged = (base + dot_tn(down_t, up)).astype(BF16)
    stacked = jnp.concatenate([merged, up], axis=0)
    merged_ref[...] = jnp.zeros_like(merged_ref)
    loads[1].wait()
    for level in range(levels):
        through = dot_nn(stacked, level_ref[level])
        weights = through[:channels].astype(BF16)
        for s in range(merged_ref.shape[0]):
            offset = (s * levels * channels) % LANE + level * channels
            merged_ref[s, offset : offset + channels, :] = weights
        up_high, up_low = split_hi_lo(through[channels:])
        up_ref[level, :rank, :] = up_high
        up_ref[level, rank:, :] = up_low
    for load in loads[2:]:
        load.wait()


def prepare(direct, groups, frozen, factors, level_weight, mixer, grad, row_share, half_width, half_width_padded):
    reps, _, rank, _ = factors.shape
    levels, feature_dim, _ = level_weight.shape
    channels = groups.shape[0] * frozen.shape[1]
    reach = round_up(levels * channels + LANE // 2, LANE)
    rows = WLAT * half_width_padded
    vmem = pl.BlockSpec(memory_space=pltpu.VMEM)
    flops = 2 * levels * (channels + rank) * feature_dim * feature_dim + 4 * rows * rows * WLAT * WLON
    shapes = [
        (grad.shape[0], reach, feature_dim),
        (levels, 2 * rank, feature_dim),
        (rank, channels),
        (rows, rows),
        (rows, rows),
        level_weight.shape,
        grad.shape,
    ]
    return pl.pallas_call(
        functools.partial(prep_kernel, direct, row_share, half_width, half_width_padded),
        out_shape=[jax.ShapeDtypeStruct(shape, BF16) for shape in shapes],
        in_specs=[pl.BlockSpec(memory_space=pl.ANY)] * 3 + [vmem] * 3,
        out_specs=[vmem] * len(shapes),
        scratch_shapes=[pltpu.SMEM(groups.shape, jnp.int32), pltpu.SemaphoreType.DMA((2 + WLAT,))],
        compiler_params=params(),
        cost_estimate=pl.CostEstimate(flops=flops, bytes_accessed=6 * 2**20, transcendentals=0),
        name="prepare",
    )(in_hbm(groups), in_hbm(level_weight), in_hbm(grad), in_hbm(frozen), factors, in_hbm(mixer))


def normal_parts(values):
    cdf = 0.5 + 0.5 * lax.erf(values * 0.7071067811865476)
    return cdf, 0.3989422804014327 * jnp.exp2(values * values * -0.7213475204444817)


def factor_shares(total, up_ref, down_ref, level_ref):
    levels, two_rank, feature_dim = up_ref.shape
    rank, channels = down_ref.shape
    high, low = split_hi_lo(total)
    down = down_ref[...]
    first = jnp.zeros((rank, channels), F32)
    second = jnp.zeros((two_rank, feature_dim), F32)
    for level in range(levels):
        at = slice(level * channels, (level + 1) * channels)
        both = dot_nt(up_ref[level], high[at])
        first = first + both[:rank] + both[rank:] + dot_nt(up_ref[level, :rank, :], low[at])
        through = dot_nn(down, high[at]) + dot_nn(down, low[at])
        through = jnp.concatenate(split_hi_lo(through), axis=0)
        second = second + dot_nt(through, level_ref[level])
    return first, second[:rank] + second[rank:]


def turned_whole(lines, width):
    return lines * width // LANE * LANE


def embed_kernel(*refs):
    piece_refs, (merged_ref, tokens_ref, turned_ref) = refs[:-3], refs[-3:]
    samples, reach, feature_dim = merged_ref.shape
    width, features = piece_refs[0].shape
    depth = features // samples
    group = 2 * WLON
    rows = len(piece_refs) * group
    positions = turned_ref.shape[1]
    for s in range(samples):
        lane = s * depth // LANE * LANE
        pixels = jnp.concatenate([piece_ref[:, lane : lane + reach] for piece_ref in piece_refs], axis=0)
        tokens = dot_nn(pixels, merged_ref[s]).reshape(len(piece_refs), width, feature_dim)
        for n in range(width // group):
            part = tokens[:, n * group : (n + 1) * group].reshape(rows, feature_dim)
            tokens_ref[s, n * rows : (n + 1) * rows, :] = part.astype(BF16)
    for start in range(0, features, LANE):
        lanes = slice(start, start + LANE)
        pixels = jnp.concatenate([piece_ref[:, lanes] for piece_ref in piece_refs], axis=0)
        turned_ref[lanes, :] = pixels[:positions].T


def embed_early(pieces, merged):
    samples, _, feature_dim = merged.shape
    width, features = pieces[0].shape
    count = len(pieces) * width
    return pl.pallas_call(
        embed_kernel,
        out_shape=[
            jax.ShapeDtypeStruct((samples, count, feature_dim), BF16),
            jax.ShapeDtypeStruct((features, turned_whole(len(pieces), width)), BF16),
        ],
        in_specs=[pl.BlockSpec(memory_space=pltpu.VMEM)] * (len(pieces) + 1),
        out_specs=[pl.BlockSpec(memory_space=pltpu.VMEM)] * 2,
        compiler_params=params(),
        cost_estimate=pl.CostEstimate(
            flops=2 * count * features * feature_dim, bytes_accessed=4 * 2**20, transcendentals=0
        ),
        name="embed_early",
    )(*pieces, merged)


def mix_kernel(
    direct,
    piece_refs,
    merged_ref,
    mix_ref,
    mix_t_ref,
    up_ref,
    down_ref,
    grad_ref,
    level_ref,
    mixed_hbm_ref,
    share_ref,
    turned_refs,
    mixed_refs,
    pre_refs,
    tokens_refs,
    grad_pre_refs,
    grad_tokens_refs,
    total_ref,
    mixed_sems,
):
    samples, reach, feature_dim = merged_ref.shape
    chunk_count, (_, width, _) = len(mixed_refs), mixed_refs[0].shape
    depth = piece_refs[-1].shape[-1] // samples
    rows = WLAT * width

    group_rows = mix_ref.shape[0]
    group = group_rows // WLAT
    groups = [
        (slice(start, start + group), slice(start * WLAT, start * WLAT + group_rows))
        for start in range(0, width, group)
    ]
    pair = 1 if group % SUB == 0 else 2

    early = EARLY if direct else 0
    early_rows, late_rows = early * group, (WLAT - early) * group
    if direct:
        early_tokens_ref, early_turned_ref, *line_refs = piece_refs
        early_positions = early_turned_ref.shape[1]

    def lines_of(n):
        return pl.ds(n // samples * WLAT, WLAT)

    if direct:
        me = lax.axis_index("band")
        targets = [
            (mixed_refs[n].at[slot], mixed_hbm_ref.at[n, jnp.bitwise_xor(me, far)])
            for n in range(chunk_count)
            for slot, far in enumerate(SLOTS)
        ]
    else:
        targets = [
            (mixed_refs[n], mixed_hbm_ref.at[n % samples, lines_of(n)]) for n in range(chunk_count)
        ]
    stores = [
        pltpu.make_async_copy(source, target, mixed_sems.at[n]) for n, (source, target) in enumerate(targets)
    ]

    def pixels_of(n, lanes):
        if direct:
            return jnp.concatenate([line_ref[:, lanes] for line_ref in line_refs], axis=0)
        return piece_refs[0][lines_of(n), :, lanes].reshape(rows, lanes.stop - lanes.start)

    def turn(n):
        def part(lanes):
            pixels = pixels_of(n, lanes)
            if direct:
                before = early_positions - (early - 1) * width
                pixels = pixels[before:]
            turned_refs[n // samples][lanes, :] = pixels.T

        starts = range(0, samples * depth, LANE)
        return [functools.partial(part, slice(start, start + LANE)) for start in starts]

    def tokens_at(n, block, line, count, columns):
        if line < early:
            at = pl.ds(block * early_rows + line * group, count * group)
            return early_tokens_ref[n % samples, at, columns]
        return tokens_refs[n][pl.ds(block * late_rows + (line - early) * group, count * group), columns]

    def forward(n, columns):
        s = n % samples
        lane = s * depth // LANE * LANE

        def embed():
            pixels = pixels_of(n, slice(lane, lane + reach))
            if direct:
                pixels = pixels[width:]
            tokens = dot_nn(pixels, merged_ref[s, :, columns]).reshape(WLAT - early, width, -1)
            for block, (within, _) in enumerate(groups):
                part = tokens[:, within].reshape(late_rows, -1).astype(BF16)
                tokens_refs[n][block * late_rows : (block + 1) * late_rows, columns] = part

        def mixing(block, at):
            tokens = tokens_at(n, block, early, WLAT - early, columns)
            if direct:
                tokens = jnp.concatenate([tokens_at(n, block, 0, early, columns), tokens], axis=0)
            pre_refs[n][at, columns] = dot_nn(mix_ref[...], tokens)

        return [embed] + [functools.partial(mixing, block, at) for block, (_, at) in enumerate(groups)]

    def pointwise(n, columns):
        s, first_line = n % samples, n // samples * WLAT

        def part(line, across, lanes):
            grads = [grad_ref[s, first_line + line + k, across, lanes].astype(F32) for k in range(pair)]
            mixed = []
            for block, (within, at) in enumerate(groups):
                if within.start < across.start or within.stop > across.stop:
                    continue
                at = pl.ds(at.start + line * group, pair * group)
                pre = pre_refs[n][at, lanes]
                cdf, pdf = normal_parts(pre)
                mixed.append(tokens_at(n, block, line, pair, lanes).astype(F32) + pre * cdf)
                first = within.start - across.start
                grad = jnp.concatenate([values[first : first + group] for values in grads], axis=0)
                grad_pre_refs[n][at, lanes] = (grad * (cdf + pre * pdf)).astype(BF16)
            for k in range(pair):
                parts = [values[k * group : (k + 1) * group] for values in mixed]
                mixed_refs[n][line + k, across, lanes] = jnp.concatenate(parts, axis=0).astype(BF16)

        return [
            functools.partial(part, line, slice(across, across + pair * group), slice(start, start + LANE))
            for line in range(0, WLAT, pair)
            for across in range(0, width, pair * group)
            for start in range(columns.start, columns.stop, LANE)
        ]

    def backward(n, columns):
        def spread():
            direct_part = grad_ref[n % samples, lines_of(n), :, columns].astype(F32)
            through = [
                dot_nn(mix_t_ref[...], grad_pre_refs[n][at, columns]).reshape(WLAT, group, -1)
                for _, at in groups
            ]
            total = jnp.concatenate(through, axis=1) + direct_part
            grad_tokens_refs[n][:, columns] = total.reshape(rows, -1).astype(BF16)

        def share():
            s = n % samples
            features = slice(s * depth, (s + 1) * depth)
            late = rows - turned_refs[0].shape[1]
            part = dot_nn(turned_refs[n // samples][features, :], grad_tokens_refs[n][late:, columns])
            if direct:
                part = part + dot_nn(early_turned_ref[features, :], grad_tokens_refs[n][:late, columns])
            total_ref[:, columns] = part if n == 0 else total_ref[:, columns] + part

        return [spread, share]

    units = [(n, slice(0, feature_dim)) for n in range(chunk_count - 1)]
    units += [
        (chunk_count - 1, slice(start, start + COLUMNS)) for start in range(0, feature_dim, COLUMNS)
    ]
    for step in forward(*units[0]):
        step()
    for i, unit in enumerate(units):
        n, columns = unit
        others = []
        if i + 1 < len(units):
            others += forward(*units[i + 1])
        if columns.start == 0 and n % samples == 0:
            others += turn(n)
        if i > 0:
            others += backward(*units[i - 1])
        lines = pointwise(*unit)
        for line, vector_step in enumerate(lines):
            vector_step()
            for step in others[line * len(others) // len(lines) : (line + 1) * len(others) // len(lines)]:
                step()
        if columns.stop == feature_dim:
            each = len(stores) // chunk_count
            for store in stores[n * each : (n + 1) * each]:
                store.start()
    for step in backward(*units[-1]):
        step()

    first, second = factor_shares(total_ref[...], up_ref, down_ref, level_ref)
    rank, channels = down_ref.shape
    columns = share_ref.shape[2]
    reps = feature_dim // columns
    folds = rank // (share_ref.shape[1] - rank)
    depth_rows, fold_lanes, row_share = rank // folds, columns // folds, channels // reps
    packed = jnp.zeros((depth_rows, feature_dim), F32)
    row, lane = iota2((channels, feature_dim), 0), iota2((1, feature_dim), 1)
    rep, lane = lane // columns, lane % columns
    for fold in range(folds):
        inside = lane - fold * fold_lanes
        target = jnp.where((inside >= 0) & (inside < row_share), inside + rep * row_share, -1)
        pick = jnp.where(row == target, 1.0, 0.0).astype(BF16)
        part = first[fold * depth_rows : (fold + 1) * depth_rows].astype(BF16)
        packed = packed + dot_nn(part, pick)
    payload = jnp.concatenate([second, packed], axis=0).astype(BF16)
    for slot in range(share_ref.shape[0]):
        at = slot % reps * columns
        share_ref[slot] = payload[:, at : at + columns]
    for store in stores:
        store.wait()


def mix_blocks(direct, arrived, merged, mix, mix_t, grad, up_through, down_t, level_weight, band_count, reps):
    samples, lat_rows, block_width, feature_dim = grad.shape
    width = block_width
    lanes = arrived[-1].shape[-1]
    early = EARLY if direct else 0
    turned_early = turned_whole(early, width)
    reach = merged.shape[1]
    rows = WLAT * width
    rank = down_t.shape[0]
    chunks = lat_rows // WLAT * samples
    share_shape = (band_count * reps, rank + rank // FOLDS, feature_dim // reps)
    flops = 2 * samples * lat_rows * block_width * feature_dim * (2 * reach + 2 * rows)
    vmem = pl.BlockSpec(memory_space=pltpu.VMEM)
    any_space = pl.BlockSpec(memory_space=pl.ANY)
    local = [*arrived, merged, mix, mix_t, up_through, down_t]
    return pl.pallas_call(
        lambda *refs: mix_kernel(direct, refs[: len(arrived)], *refs[len(arrived) :]),
        out_shape=[
            jax.ShapeDtypeStruct(grad.shape, BF16),
            jax.ShapeDtypeStruct(share_shape, BF16),
        ],
        in_specs=[vmem] * (len(local) + 2),
        out_specs=[any_space, vmem],
        scratch_shapes=[
            [pltpu.VMEM((lanes, rows - turned_early), BF16)] * (chunks // samples),
            [pltpu.VMEM((WLAT, width, feature_dim), BF16)] * chunks,
            [pltpu.VMEM((rows, feature_dim), F32)] * chunks,
            [pltpu.VMEM((rows - early * width, feature_dim), BF16)] * chunks,
            [pltpu.VMEM((rows, feature_dim), BF16)] * chunks,
            [pltpu.VMEM((rows, feature_dim), BF16)] * chunks,
            pltpu.VMEM((lanes // samples, feature_dim), F32),
            pltpu.SemaphoreType.DMA((chunks * WLAT,)),
        ],
        compiler_params=params(),
        cost_estimate=pl.CostEstimate(
            flops=flops,
            bytes_accessed=12 * 2**20,
            transcendentals=samples * lat_rows * block_width * feature_dim,
        ),
        name="mix_blocks",
    )(*local, grad, level_weight)


def sum_kernel(parts_ref, first_ref, second_ref):
    rank, row_share = first_ref.shape
    total = parts_ref[0].astype(F32)
    for n in range(1, parts_ref.shape[0]):
        total = total + parts_ref[n].astype(F32)
    second_ref[...] = total[:rank]
    depth_rows = total.shape[0] - rank
    for fold in range(rank // depth_rows):
        lane = fold * depth_rows * total.shape[1] // rank
        first_ref[fold * depth_rows : (fold + 1) * depth_rows, :] = total[rank:, lane : lane + row_share]


def sum_shares(shares, rank, row_share):
    parts = lax.all_to_all(shares, ("band", "rep"), split_axis=0, concat_axis=0, tiled=True)
    return pl.pallas_call(
        sum_kernel,
        out_shape=[
            jax.ShapeDtypeStruct((rank, row_share), F32),
            jax.ShapeDtypeStruct((rank, shares.shape[2]), F32),
        ],
        compiler_params=params(),
        name="sum_shares",
    )(parts)


def on_device(
    patches,
    variable_group_index,
    frozen_patch_weight,
    adapter_down,
    adapter_up,
    level_merge_weight,
    window_patch_mixer,
    column_block_owner,
    mixed_token_gradient,
):
    band_count, reps = lax.axis_size("band"), lax.axis_size("rep")
    samples, levels, channels, row_count, col_count = patches.shape
    feature_dim = frozen_patch_weight.shape[2]
    rank, col_share = adapter_up.shape
    row_share = adapter_down.shape[0]
    lat_rows = band_count * row_count
    block_width = col_count // band_count
    padded_width = round_up(block_width, SUB)
    group = 2 * WLON if block_width % (2 * WLON) == 0 else padded_width
    features = samples * levels * channels

    pixels = patches.reshape(features, col_count)
    pack_shape = (2, rank, round_up(max(row_share, col_share), LANE))
    direct = band_count == BANDS and lat_rows == WLAT and padded_width == block_width
    direct = direct and features % LANE == 0 and col_count % LANE == 0
    if direct:
        blocks, pack = send_blocks(
            pixels, column_block_owner, adapter_up, adapter_down.T, block_width, pack_shape
        )
        arrived, factors = exchange(blocks, pack)
    else:
        block_ids = jnp.arange(band_count, dtype=jnp.int32)
        inverse = jnp.sum(
            jnp.where(column_block_owner[None, :] == block_ids[:, None], block_ids[None, :], 0), axis=1
        )
        outgoing = jnp.take(pixels.T.reshape(band_count, block_width, features), inverse, axis=0)
        outgoing = jnp.pad(outgoing, ((0, 0), (0, padded_width - block_width), (0, 0)))
        arrived = [lax.all_to_all(outgoing, "band", split_axis=0, concat_axis=0, tiled=True)]
        pack = jnp.stack(
            [
                jnp.pad(array, ((0, 0), (0, pack_shape[2] - array.shape[1])))
                for array in (adapter_up, adapter_down.T)
            ]
        )
        factors = lax.all_gather(pack, "rep", axis=0, tiled=False)

    grad = mixed_token_gradient.reshape(samples, lat_rows, block_width, feature_dim)
    if padded_width != block_width:
        grad = jnp.pad(grad, ((0, 0), (0, 0), (0, padded_width - block_width), (0, 0)))
    merged, up_through, down_t, mix, mix_t, level_copy, grad_copy = prepare(
        direct,
        variable_group_index,
        frozen_patch_weight,
        factors,
        level_merge_weight,
        window_patch_mixer,
        grad,
        row_share,
        min(block_width, group),
        group,
    )
    if direct:
        arrived = [*embed_early(arrived[:EARLY], merged), *arrived[EARLY - 1 :]]
    mixed, shares = mix_blocks(
        direct, arrived, merged, mix, mix_t, grad_copy, up_through, down_t, level_copy, band_count, reps
    )
    if padded_width != block_width:
        mixed = mixed[:, :, :block_width]
    first_t, second = sum_shares(shares, rank, row_share)
    return mixed.reshape(mixed_token_gradient.shape), first_t.T, second


def solution(mesh):
    in_specs = (
        P("rep", None, None, "band", None),
        P(),
        P(),
        P("rep", None),
        P(None, "rep"),
        P(),
        P(),
        P(),
        P("rep", "band", None, None, None),
    )
    out_specs = (P("rep", "band", None, None, None), P("rep", None), P(None, "rep"))
    return jax.shard_map(
        on_device, mesh=mesh, in_specs=in_specs, out_specs=out_specs, check_vma=False
    )
```

```python
import functools

import jax
import jax.numpy as jnp
from jax import lax
from jax.experimental import pallas as pl
from jax.experimental.pallas import tpu as pltpu
from jax.sharding import PartitionSpec as P

WLAT = 8
WLON = 12
LANE = 128
SUB = 16
VMEM_LIMIT = 24 * 1024 * 1024
BANDS = 8
ORDER = (0, 4, 1, 5, 2, 6, 7, 3)
EARLY = 6
SLOTS = (0, 1, 4, 5, 6, 2, 3, 7)
FOLDS = 2
COLUMNS = 512
BF16 = jnp.bfloat16
F32 = jnp.float32


def round_up(value, step):
    return -(-value // step) * step


def dot_nn(a, b):
    return lax.dot_general(a, b, (((1,), (0,)), ((), ())), preferred_element_type=F32)


def dot_nt(a, b):
    return lax.dot_general(a, b, (((1,), (1,)), ((), ())), preferred_element_type=F32)


def dot_tn(a, b):
    return lax.dot_general(a, b, (((0,), (0,)), ((), ())), preferred_element_type=F32)


def split_hi_lo(values):
    high = values.astype(BF16)
    low = (values - high.astype(F32)).astype(BF16)
    return high, low


def iota2(shape, axis):
    return lax.broadcasted_iota(jnp.int32, shape, axis)


def params(**extra):
    return pltpu.CompilerParams(vmem_limit_bytes=VMEM_LIMIT, **extra)


def in_hbm(values):
    return pltpu.with_memory_space_constraint(values, pltpu.HBM)


def swap(values, axis, distance):
    count = lax.axis_size(axis)
    return lax.ppermute(values, axis, [(source, source ^ distance) for source in range(count)])


def send_kernel(owner_hbm_ref, up_hbm_ref, down_hbm_ref, x_hbm_ref, *refs):
    block_refs, pack_ref, scratch = refs[:-8], refs[-8], refs[-7:]
    owner_ref, up_ref, down_ref, x_ref, turned_ref, small_sems, x_sems = scratch
    width = block_refs[0].shape[0]
    features, columns = x_ref.shape
    small = [
        pltpu.make_async_copy(source, target, small_sems.at[n])
        for n, (source, target) in enumerate(
            [(owner_hbm_ref, owner_ref), (up_hbm_ref, up_ref), (down_hbm_ref, down_ref)]
        )
    ]
    parts = [slice(start, start + LANE) for start in range(0, features, LANE)]
    large = [
        pltpu.make_async_copy(x_hbm_ref.at[part, :], x_ref.at[part, :], x_sems.at[n])
        for n, part in enumerate(parts)
    ]
    for copy in large + small:
        copy.start()
    for copy, part in zip(large, parts):
        copy.wait()
        for start in range(0, columns, LANE):
            at = slice(start, start + LANE)
            turned_ref[at, part] = x_ref[part, at].T
    for copy in small:
        copy.wait()
    pack_ref[...] = jnp.zeros_like(pack_ref)
    pack_ref[0, :, : up_ref.shape[1]] = up_ref[...]
    pack_ref[1, :, : down_ref.shape[1]] = down_ref[...]
    me = lax.axis_index("band")
    for distance, block_ref in zip(ORDER, block_refs):
        target = jnp.bitwise_xor(me, distance)
        block = 0
        for j in range(1, owner_ref.shape[0]):
            block = jnp.where(owner_ref[j] == target, j, block)
        block_ref[...] = turned_ref[pl.ds(pl.multiple_of(block * width, SUB), width), :]


def send_blocks(pixels, owner, up, down_t, width, pack_shape):
    features, columns = pixels.shape
    any_space = pl.BlockSpec(memory_space=pl.ANY)
    vmem = pl.BlockSpec(memory_space=pltpu.VMEM)
    blocks = [(width, features)] * BANDS
    *blocks, pack = pl.pallas_call(
        send_kernel,
        out_shape=[jax.ShapeDtypeStruct(shape, BF16) for shape in [*blocks, pack_shape]],
        in_specs=[any_space] * 4,
        out_specs=[vmem] * (len(blocks) + 1),
        scratch_shapes=[
            pltpu.SMEM(owner.shape, jnp.int32),
            pltpu.VMEM(up.shape, BF16),
            pltpu.VMEM(down_t.shape, BF16),
            pltpu.VMEM((features, columns), BF16),
            pltpu.VMEM((columns, features), BF16),
            pltpu.SemaphoreType.DMA((3,)),
            pltpu.SemaphoreType.DMA((features // LANE,)),
        ],
        compiler_params=params(),
        name="send_blocks",
    )(in_hbm(owner), in_hbm(up), in_hbm(down_t), in_hbm(pixels))
    return blocks, pack


def exchange(blocks, pack):
    arrived = dict(zip(ORDER, blocks))
    for distance in (1, 4, 5, 6, 2):
        arrived[distance] = swap(arrived[distance], "band", distance)
    arrived[1], pack = lax.optimization_barrier((arrived[1], pack))
    factors = lax.all_gather(pack, "rep", axis=0, tiled=False)
    arrived[7], factors = lax.optimization_barrier((arrived[7], factors))
    arrived[7] = swap(arrived[7], "band", 7)
    arrived[3], factors = lax.optimization_barrier((arrived[3], factors))
    arrived[3] = swap(arrived[3], "band", 3)
    return [arrived[distance] for distance in SLOTS], factors


def expand_table(table, rows, half_width_padded, half_width, flip, transpose):
    position = iota2((rows, WLAT * WLON), 0)
    line, col = position // half_width_padded, position % half_width_padded
    if flip is not None:
        distance = sum(jnp.where(line == slot, far, 0) for slot, far in enumerate(SLOTS))
        line = jnp.bitwise_xor(distance, flip)
    target = iota2((rows, WLAT * WLON), 1)
    pick = jnp.where((target == line * WLON + col % WLON) & (col < half_width), 1.0, 0.0).astype(BF16)
    left = (dot_nt if transpose else dot_nn)(pick, table).astype(BF16)
    full = dot_nt(left, pick)
    row_window = (iota2((rows, 1), 0) % half_width_padded) // WLON
    col_window = (iota2((1, rows), 1) % half_width_padded) // WLON
    return jnp.where(row_window == col_window, full, 0.0).astype(BF16)


def prep_kernel(
    direct,
    row_share,
    half_width,
    half_width_padded,
    group_hbm_ref,
    level_hbm_ref,
    grad_hbm_ref,
    frozen_ref,
    factors_ref,
    mixer_ref,
    merged_ref,
    up_ref,
    down_ref,
    mix_ref,
    mix_t_ref,
    level_ref,
    grad_ref,
    group_ref,
    sems,
):
    pairs = [(group_hbm_ref, group_ref), (level_hbm_ref, level_ref)]
    flip = lax.axis_index("band") if direct else None
    if direct:
        pairs += [
            (grad_hbm_ref.at[:, jnp.bitwise_xor(flip, far)], grad_ref.at[:, slot])
            for slot, far in enumerate(SLOTS)
        ]
    else:
        pairs.append((grad_hbm_ref, grad_ref))
    loads = [
        pltpu.make_async_copy(source, target, sems.at[n]) for n, (source, target) in enumerate(pairs)
    ]
    for load in loads:
        load.start()
    rows = mix_ref.shape[0]
    mix_ref[...] = expand_table(mixer_ref[...], rows, half_width_padded, half_width, flip, False)
    mix_t_ref[...] = expand_table(mixer_ref[...], rows, half_width_padded, half_width, flip, True)
    reps, _, rank, share = factors_ref.shape
    levels = level_ref.shape[0]
    variables = group_ref.shape[0]
    channels = variables * frozen_ref.shape[1]
    up = jnp.concatenate([factors_ref[r, 0] for r in range(reps)], axis=1)
    source, target = iota2((share, channels), 0), iota2((share, channels), 1)
    down_t = jnp.zeros((rank, channels), F32)
    for r in range(reps):
        place = jnp.where((target == source + r * row_share) & (source < row_share), 1.0, 0.0)
        down_t = down_t + dot_nn(factors_ref[r, 1], place.astype(BF16))
    down_t = down_t.astype(BF16)
    down_ref[...] = down_t
    loads[0].wait()
    base = jnp.concatenate([frozen_ref[group_ref[v]].astype(F32) for v in range(variables)], axis=0)
    merged = (base + dot_tn(down_t, up)).astype(BF16)
    stacked = jnp.concatenate([merged, up], axis=0)
    merged_ref[...] = jnp.zeros_like(merged_ref)
    loads[1].wait()
    for level in range(levels):
        through = dot_nn(stacked, level_ref[level])
        weights = through[:channels].astype(BF16)
        for s in range(merged_ref.shape[0]):
            offset = (s * levels * channels) % LANE + level * channels
            merged_ref[s, offset : offset + channels, :] = weights
        up_high, up_low = split_hi_lo(through[channels:])
        up_ref[level, :rank, :] = up_high
        up_ref[level, rank:, :] = up_low
    for load in loads[2:]:
        load.wait()


def prepare(direct, groups, frozen, factors, level_weight, mixer, grad, row_share, half_width, half_width_padded):
    reps, _, rank, _ = factors.shape
    levels, feature_dim, _ = level_weight.shape
    channels = groups.shape[0] * frozen.shape[1]
    reach = round_up(levels * channels + LANE // 2, LANE)
    rows = WLAT * half_width_padded
    vmem = pl.BlockSpec(memory_space=pltpu.VMEM)
    flops = 2 * levels * (channels + rank) * feature_dim * feature_dim + 4 * rows * rows * WLAT * WLON
    shapes = [
        (grad.shape[0], reach, feature_dim),
        (levels, 2 * rank, feature_dim),
        (rank, channels),
        (rows, rows),
        (rows, rows),
        level_weight.shape,
        grad.shape,
    ]
    return pl.pallas_call(
        functools.partial(prep_kernel, direct, row_share, half_width, half_width_padded),
        out_shape=[jax.ShapeDtypeStruct(shape, BF16) for shape in shapes],
        in_specs=[pl.BlockSpec(memory_space=pl.ANY)] * 3 + [vmem] * 3,
        out_specs=[vmem] * len(shapes),
        scratch_shapes=[pltpu.SMEM(groups.shape, jnp.int32), pltpu.SemaphoreType.DMA((2 + WLAT,))],
        compiler_params=params(),
        cost_estimate=pl.CostEstimate(flops=flops, bytes_accessed=6 * 2**20, transcendentals=0),
        name="prepare",
    )(in_hbm(groups), in_hbm(level_weight), in_hbm(grad), in_hbm(frozen), factors, in_hbm(mixer))


def normal_parts(values):
    cdf = 0.5 + 0.5 * lax.erf(values * 0.7071067811865476)
    return cdf, 0.3989422804014327 * jnp.exp2(values * values * -0.7213475204444817)


def factor_shares(total, up_ref, down_ref, level_ref):
    levels, two_rank, feature_dim = up_ref.shape
    rank, channels = down_ref.shape
    high, low = split_hi_lo(total)
    down = down_ref[...]
    first = jnp.zeros((rank, channels), F32)
    second = jnp.zeros((two_rank, feature_dim), F32)
    for level in range(levels):
        at = slice(level * channels, (level + 1) * channels)
        both = dot_nt(up_ref[level], high[at])
        first = first + both[:rank] + both[rank:] + dot_nt(up_ref[level, :rank, :], low[at])
        through = dot_nn(down, high[at]) + dot_nn(down, low[at])
        through = jnp.concatenate(split_hi_lo(through), axis=0)
        second = second + dot_nt(through, level_ref[level])
    return first, second[:rank] + second[rank:]


def turned_whole(lines, width):
    return lines * width // LANE * LANE


def embed_kernel(*refs):
    piece_refs, (merged_ref, tokens_ref, turned_ref) = refs[:-3], refs[-3:]
    samples, reach, feature_dim = merged_ref.shape
    width, features = piece_refs[0].shape
    depth = features // samples
    group = 2 * WLON
    rows = len(piece_refs) * group
    positions = turned_ref.shape[1]
    for s in range(samples):
        lane = s * depth // LANE * LANE
        pixels = jnp.concatenate([piece_ref[:, lane : lane + reach] for piece_ref in piece_refs], axis=0)
        for start in range(0, feature_dim, COLUMNS):
            columns = slice(start, start + COLUMNS)
            tokens = dot_nn(pixels, merged_ref[s, :, columns]).reshape(len(piece_refs), width, COLUMNS)
            for n in range(width // group):
                part = tokens[:, n * group : (n + 1) * group].reshape(rows, COLUMNS)
                tokens_ref[s, n * rows : (n + 1) * rows, columns] = part.astype(BF16)
    for start in range(0, features, LANE):
        lanes = slice(start, start + LANE)
        pixels = jnp.concatenate([piece_ref[:, lanes] for piece_ref in piece_refs], axis=0)
        turned_ref[lanes, :] = pixels[:positions].T


def embed_early(pieces, merged):
    samples, _, feature_dim = merged.shape
    width, features = pieces[0].shape
    count = len(pieces) * width
    return pl.pallas_call(
        embed_kernel,
        out_shape=[
            jax.ShapeDtypeStruct((samples, count, feature_dim), BF16),
            jax.ShapeDtypeStruct((features, turned_whole(len(pieces), width)), BF16),
        ],
        in_specs=[pl.BlockSpec(memory_space=pltpu.VMEM)] * (len(pieces) + 1),
        out_specs=[pl.BlockSpec(memory_space=pltpu.VMEM)] * 2,
        compiler_params=params(),
        cost_estimate=pl.CostEstimate(
            flops=2 * count * features * feature_dim, bytes_accessed=4 * 2**20, transcendentals=0
        ),
        name="embed_early",
    )(*pieces, merged)


def mix_kernel(
    direct,
    piece_refs,
    merged_ref,
    mix_ref,
    mix_t_ref,
    up_ref,
    down_ref,
    grad_ref,
    level_ref,
    mixed_hbm_ref,
    share_ref,
    turned_refs,
    mixed_refs,
    pre_refs,
    tokens_refs,
    grad_pre_refs,
    grad_tokens_refs,
    total_ref,
    mixed_sems,
):
    samples, reach, feature_dim = merged_ref.shape
    chunk_count, (_, width, _) = len(mixed_refs), mixed_refs[0].shape
    depth = piece_refs[-1].shape[-1] // samples
    rows = WLAT * width

    group_rows = mix_ref.shape[0]
    group = group_rows // WLAT
    groups = [
        (slice(start, start + group), slice(start * WLAT, start * WLAT + group_rows))
        for start in range(0, width, group)
    ]
    pair = 1 if group % SUB == 0 else 2

    early = EARLY if direct else 0
    early_rows, late_rows = early * group, (WLAT - early) * group
    if direct:
        early_tokens_ref, early_turned_ref, *line_refs = piece_refs
        early_positions = early_turned_ref.shape[1]

    def lines_of(n):
        return pl.ds(n // samples * WLAT, WLAT)

    if direct:
        me = lax.axis_index("band")
        targets = [
            (mixed_refs[n].at[slot], mixed_hbm_ref.at[n, jnp.bitwise_xor(me, far)])
            for n in range(chunk_count)
            for slot, far in enumerate(SLOTS)
        ]
    else:
        targets = [
            (mixed_refs[n], mixed_hbm_ref.at[n % samples, lines_of(n)]) for n in range(chunk_count)
        ]
    stores = [
        pltpu.make_async_copy(source, target, mixed_sems.at[n]) for n, (source, target) in enumerate(targets)
    ]

    def pixels_of(n, lanes):
        if direct:
            return jnp.concatenate([line_ref[:, lanes] for line_ref in line_refs], axis=0)
        return piece_refs[0][lines_of(n), :, lanes].reshape(rows, lanes.stop - lanes.start)

    def turn(n):
        def part(lanes):
            pixels = pixels_of(n, lanes)
            if direct:
                before = early_positions - (early - 1) * width
                pixels = pixels[before:]
            turned_refs[n // samples][lanes, :] = pixels.T

        starts = range(0, samples * depth, LANE)
        return [functools.partial(part, slice(start, start + LANE)) for start in starts]

    def tokens_at(n, block, line, count, columns):
        if line < early:
            at = pl.ds(block * early_rows + line * group, count * group)
            return early_tokens_ref[n % samples, at, columns]
        return tokens_refs[n][pl.ds(block * late_rows + (line - early) * group, count * group), columns]

    def forward(n, columns):
        s = n % samples
        lane = s * depth // LANE * LANE

        def embed():
            pixels = pixels_of(n, slice(lane, lane + reach))
            if direct:
                pixels = pixels[width:]
            tokens = dot_nn(pixels, merged_ref[s, :, columns]).reshape(WLAT - early, width, COLUMNS)
            for block, (within, _) in enumerate(groups):
                part = tokens[:, within].reshape(late_rows, COLUMNS).astype(BF16)
                tokens_refs[n][block * late_rows : (block + 1) * late_rows, columns] = part

        def mixing(block, at):
            tokens = tokens_at(n, block, early, WLAT - early, columns)
            if direct:
                tokens = jnp.concatenate([tokens_at(n, block, 0, early, columns), tokens], axis=0)
            pre_refs[n][at, columns] = dot_nn(mix_ref[...], tokens)

        return [embed] + [functools.partial(mixing, block, at) for block, (_, at) in enumerate(groups)]

    def pointwise(n, columns):
        s, first_line = n % samples, n // samples * WLAT

        def part(line, across, lanes):
            grads = [grad_ref[s, first_line + line + k, across, lanes].astype(F32) for k in range(pair)]
            mixed = []
            for block, (within, at) in enumerate(groups):
                if within.start < across.start or within.stop > across.stop:
                    continue
                at = pl.ds(at.start + line * group, pair * group)
                pre = pre_refs[n][at, lanes]
                cdf, pdf = normal_parts(pre)
                mixed.append(tokens_at(n, block, line, pair, lanes).astype(F32) + pre * cdf)
                first = within.start - across.start
                grad = jnp.concatenate([values[first : first + group] for values in grads], axis=0)
                grad_pre_refs[n][at, lanes] = (grad * (cdf + pre * pdf)).astype(BF16)
            for k in range(pair):
                parts = [values[k * group : (k + 1) * group] for values in mixed]
                mixed_refs[n][line + k, across, lanes] = jnp.concatenate(parts, axis=0).astype(BF16)

        return [
            functools.partial(part, line, slice(across, across + pair * group), slice(start, start + LANE))
            for line in range(0, WLAT, pair)
            for across in range(0, width, pair * group)
            for start in range(columns.start, columns.stop, LANE)
        ]

    def backward(n, columns):
        def spread():
            direct_part = grad_ref[n % samples, lines_of(n), :, columns].astype(F32)
            through = [
                dot_nn(mix_t_ref[...], grad_pre_refs[n][at, columns]).reshape(WLAT, group, COLUMNS)
                for _, at in groups
            ]
            total = jnp.concatenate(through, axis=1) + direct_part
            grad_tokens_refs[n][:, columns] = total.reshape(rows, COLUMNS).astype(BF16)

        def share():
            s = n % samples
            features = slice(s * depth, (s + 1) * depth)
            late = rows - turned_refs[0].shape[1]
            part = dot_nn(turned_refs[n // samples][features, :], grad_tokens_refs[n][late:, columns])
            if direct:
                part = part + dot_nn(early_turned_ref[features, :], grad_tokens_refs[n][:late, columns])
            total_ref[:, columns] = part if n == 0 else total_ref[:, columns] + part

        return [spread, share]

    units = [
        (n, slice(start, start + COLUMNS))
        for n in range(chunk_count)
        for start in range(0, feature_dim, COLUMNS)
    ]
    for step in forward(*units[0]):
        step()
    for i, unit in enumerate(units):
        n, columns = unit
        others = []
        if i + 1 < len(units):
            others += forward(*units[i + 1])
        if columns.start == 0 and n % samples == 0:
            others += turn(n)
        if i > 0:
            others += backward(*units[i - 1])
        for step in others + pointwise(*unit):
            step()
        if columns.stop == feature_dim:
            each = len(stores) // chunk_count
            for store in stores[n * each : (n + 1) * each]:
                store.start()
    for step in backward(*units[-1]):
        step()

    first, second = factor_shares(total_ref[...], up_ref, down_ref, level_ref)
    rank, channels = down_ref.shape
    columns = share_ref.shape[2]
    reps = feature_dim // columns
    folds = rank // (share_ref.shape[1] - rank)
    depth_rows, fold_lanes, row_share = rank // folds, columns // folds, channels // reps
    packed = jnp.zeros((depth_rows, feature_dim), F32)
    row, lane = iota2((channels, feature_dim), 0), iota2((1, feature_dim), 1)
    rep, lane = lane // columns, lane % columns
    for fold in range(folds):
        inside = lane - fold * fold_lanes
        target = jnp.where((inside >= 0) & (inside < row_share), inside + rep * row_share, -1)
        pick = jnp.where(row == target, 1.0, 0.0).astype(BF16)
        part = first[fold * depth_rows : (fold + 1) * depth_rows].astype(BF16)
        packed = packed + dot_nn(part, pick)
    payload = jnp.concatenate([second, packed], axis=0).astype(BF16)
    for slot in range(share_ref.shape[0]):
        at = slot % reps * columns
        share_ref[slot] = payload[:, at : at + columns]
    for store in stores:
        store.wait()


def mix_blocks(direct, arrived, merged, mix, mix_t, grad, up_through, down_t, level_weight, band_count, reps):
    samples, lat_rows, block_width, feature_dim = grad.shape
    width = block_width
    lanes = arrived[-1].shape[-1]
    early = EARLY if direct else 0
    turned_early = turned_whole(early, width)
    reach = merged.shape[1]
    rows = WLAT * width
    rank = down_t.shape[0]
    chunks = lat_rows // WLAT * samples
    share_shape = (band_count * reps, rank + rank // FOLDS, feature_dim // reps)
    flops = 2 * samples * lat_rows * block_width * feature_dim * (2 * reach + 2 * rows)
    vmem = pl.BlockSpec(memory_space=pltpu.VMEM)
    any_space = pl.BlockSpec(memory_space=pl.ANY)
    local = [*arrived, merged, mix, mix_t, up_through, down_t]
    return pl.pallas_call(
        lambda *refs: mix_kernel(direct, refs[: len(arrived)], *refs[len(arrived) :]),
        out_shape=[
            jax.ShapeDtypeStruct(grad.shape, BF16),
            jax.ShapeDtypeStruct(share_shape, BF16),
        ],
        in_specs=[vmem] * (len(local) + 2),
        out_specs=[any_space, vmem],
        scratch_shapes=[
            [pltpu.VMEM((lanes, rows - turned_early), BF16)] * (chunks // samples),
            [pltpu.VMEM((WLAT, width, feature_dim), BF16)] * chunks,
            [pltpu.VMEM((rows, feature_dim), F32)] * chunks,
            [pltpu.VMEM((rows - early * width, feature_dim), BF16)] * chunks,
            [pltpu.VMEM((rows, feature_dim), BF16)] * chunks,
            [pltpu.VMEM((rows, feature_dim), BF16)] * chunks,
            pltpu.VMEM((lanes // samples, feature_dim), F32),
            pltpu.SemaphoreType.DMA((chunks * WLAT,)),
        ],
        compiler_params=params(),
        cost_estimate=pl.CostEstimate(
            flops=flops,
            bytes_accessed=12 * 2**20,
            transcendentals=samples * lat_rows * block_width * feature_dim,
        ),
        name="mix_blocks",
    )(*local, grad, level_weight)


def sum_kernel(parts_ref, first_ref, second_ref):
    rank, row_share = first_ref.shape
    total = parts_ref[0].astype(F32)
    for n in range(1, parts_ref.shape[0]):
        total = total + parts_ref[n].astype(F32)
    second_ref[...] = total[:rank]
    depth_rows = total.shape[0] - rank
    for fold in range(rank // depth_rows):
        lane = fold * depth_rows * total.shape[1] // rank
        first_ref[fold * depth_rows : (fold + 1) * depth_rows, :] = total[rank:, lane : lane + row_share]


def sum_shares(shares, rank, row_share):
    parts = lax.all_to_all(shares, ("band", "rep"), split_axis=0, concat_axis=0, tiled=True)
    return pl.pallas_call(
        sum_kernel,
        out_shape=[
            jax.ShapeDtypeStruct((rank, row_share), F32),
            jax.ShapeDtypeStruct((rank, shares.shape[2]), F32),
        ],
        compiler_params=params(),
        name="sum_shares",
    )(parts)


def on_device(
    patches,
    variable_group_index,
    frozen_patch_weight,
    adapter_down,
    adapter_up,
    level_merge_weight,
    window_patch_mixer,
    column_block_owner,
    mixed_token_gradient,
):
    band_count, reps = lax.axis_size("band"), lax.axis_size("rep")
    samples, levels, channels, row_count, col_count = patches.shape
    feature_dim = frozen_patch_weight.shape[2]
    rank, col_share = adapter_up.shape
    row_share = adapter_down.shape[0]
    lat_rows = band_count * row_count
    block_width = col_count // band_count
    padded_width = round_up(block_width, SUB)
    group = 2 * WLON if block_width % (2 * WLON) == 0 else padded_width
    features = samples * levels * channels

    pixels = patches.reshape(features, col_count)
    pack_shape = (2, rank, round_up(max(row_share, col_share), LANE))
    direct = band_count == BANDS and lat_rows == WLAT and padded_width == block_width
    direct = direct and features % LANE == 0 and col_count % LANE == 0
    if direct:
        blocks, pack = send_blocks(
            pixels, column_block_owner, adapter_up, adapter_down.T, block_width, pack_shape
        )
        arrived, factors = exchange(blocks, pack)
    else:
        block_ids = jnp.arange(band_count, dtype=jnp.int32)
        inverse = jnp.sum(
            jnp.where(column_block_owner[None, :] == block_ids[:, None], block_ids[None, :], 0), axis=1
        )
        outgoing = jnp.take(pixels.T.reshape(band_count, block_width, features), inverse, axis=0)
        outgoing = jnp.pad(outgoing, ((0, 0), (0, padded_width - block_width), (0, 0)))
        arrived = [lax.all_to_all(outgoing, "band", split_axis=0, concat_axis=0, tiled=True)]
        pack = jnp.stack(
            [
                jnp.pad(array, ((0, 0), (0, pack_shape[2] - array.shape[1])))
                for array in (adapter_up, adapter_down.T)
            ]
        )
        factors = lax.all_gather(pack, "rep", axis=0, tiled=False)

    grad = mixed_token_gradient.reshape(samples, lat_rows, block_width, feature_dim)
    if padded_width != block_width:
        grad = jnp.pad(grad, ((0, 0), (0, 0), (0, padded_width - block_width), (0, 0)))
    merged, up_through, down_t, mix, mix_t, level_copy, grad_copy = prepare(
        direct,
        variable_group_index,
        frozen_patch_weight,
        factors,
        level_merge_weight,
        window_patch_mixer,
        grad,
        row_share,
        min(block_width, group),
        group,
    )
    if direct:
        arrived = [*embed_early(arrived[:EARLY], merged), *arrived[EARLY - 1 :]]
    mixed, shares = mix_blocks(
        direct, arrived, merged, mix, mix_t, grad_copy, up_through, down_t, level_copy, band_count, reps
    )
    if padded_width != block_width:
        mixed = mixed[:, :, :block_width]
    first_t, second = sum_shares(shares, rank, row_share)
    return mixed.reshape(mixed_token_gradient.shape), first_t.T, second


def solution(mesh):
    in_specs = (
        P("rep", None, None, "band", None),
        P(),
        P(),
        P("rep", None),
        P(None, "rep"),
        P(),
        P(),
        P(),
        P("rep", "band", None, None, None),
    )
    out_specs = (P("rep", "band", None, None, None), P("rep", None), P(None, "rep"))
    return jax.shard_map(
        on_device, mesh=mesh, in_specs=in_specs, out_specs=out_specs, check_vma=False
    )
```

```python
import functools

import jax
import jax.numpy as jnp
from jax import lax
from jax.experimental import pallas as pl
from jax.experimental.pallas import tpu as pltpu
from jax.sharding import PartitionSpec as P

WLAT = 8
WLON = 12
LANE = 128
SUB = 16
VMEM_LIMIT = 24 * 1024 * 1024
BANDS = 8
ORDER = (0, 4, 1, 5, 2, 6, 7, 3)
EARLY = 6
SLOTS = (0, 1, 4, 5, 6, 2, 3, 7)
FOLDS = 2
COLUMNS = 512
BF16 = jnp.bfloat16
F32 = jnp.float32


def round_up(value, step):
    return -(-value // step) * step


def dot_nn(a, b):
    return lax.dot_general(a, b, (((1,), (0,)), ((), ())), preferred_element_type=F32)


def dot_nt(a, b):
    return lax.dot_general(a, b, (((1,), (1,)), ((), ())), preferred_element_type=F32)


def dot_tn(a, b):
    return lax.dot_general(a, b, (((0,), (0,)), ((), ())), preferred_element_type=F32)


def split_hi_lo(values):
    high = values.astype(BF16)
    low = (values - high.astype(F32)).astype(BF16)
    return high, low


def iota2(shape, axis):
    return lax.broadcasted_iota(jnp.int32, shape, axis)


def params(**extra):
    return pltpu.CompilerParams(vmem_limit_bytes=VMEM_LIMIT, **extra)


def in_hbm(values):
    return pltpu.with_memory_space_constraint(values, pltpu.HBM)


def swap(values, axis, distance):
    count = lax.axis_size(axis)
    return lax.ppermute(values, axis, [(source, source ^ distance) for source in range(count)])


def send_kernel(owner_hbm_ref, up_hbm_ref, down_hbm_ref, x_hbm_ref, *refs):
    block_refs, pack_ref, scratch = refs[:-8], refs[-8], refs[-7:]
    owner_ref, up_ref, down_ref, x_ref, turned_ref, small_sems, x_sems = scratch
    width = block_refs[0].shape[0]
    features, columns = x_ref.shape
    small = [
        pltpu.make_async_copy(source, target, small_sems.at[n])
        for n, (source, target) in enumerate(
            [(owner_hbm_ref, owner_ref), (up_hbm_ref, up_ref), (down_hbm_ref, down_ref)]
        )
    ]
    parts = [slice(start, start + LANE) for start in range(0, features, LANE)]
    large = [
        pltpu.make_async_copy(x_hbm_ref.at[part, :], x_ref.at[part, :], x_sems.at[n])
        for n, part in enumerate(parts)
    ]
    for copy in large + small:
        copy.start()
    for copy, part in zip(large, parts):
        copy.wait()
        for start in range(0, columns, LANE):
            at = slice(start, start + LANE)
            turned_ref[at, part] = x_ref[part, at].T
    for copy in small:
        copy.wait()
    pack_ref[...] = jnp.zeros_like(pack_ref)
    pack_ref[0, :, : up_ref.shape[1]] = up_ref[...]
    pack_ref[1, :, : down_ref.shape[1]] = down_ref[...]
    me = lax.axis_index("band")
    for distance, block_ref in zip(ORDER, block_refs):
        target = jnp.bitwise_xor(me, distance)
        block = 0
        for j in range(1, owner_ref.shape[0]):
            block = jnp.where(owner_ref[j] == target, j, block)
        block_ref[...] = turned_ref[pl.ds(pl.multiple_of(block * width, SUB), width), :]


def send_blocks(pixels, owner, up, down_t, width, pack_shape):
    features, columns = pixels.shape
    any_space = pl.BlockSpec(memory_space=pl.ANY)
    vmem = pl.BlockSpec(memory_space=pltpu.VMEM)
    blocks = [(width, features)] * BANDS
    *blocks, pack = pl.pallas_call(
        send_kernel,
        out_shape=[jax.ShapeDtypeStruct(shape, BF16) for shape in [*blocks, pack_shape]],
        in_specs=[any_space] * 4,
        out_specs=[vmem] * (len(blocks) + 1),
        scratch_shapes=[
            pltpu.SMEM(owner.shape, jnp.int32),
            pltpu.VMEM(up.shape, BF16),
            pltpu.VMEM(down_t.shape, BF16),
            pltpu.VMEM((features, columns), BF16),
            pltpu.VMEM((columns, features), BF16),
            pltpu.SemaphoreType.DMA((3,)),
            pltpu.SemaphoreType.DMA((features // LANE,)),
        ],
        compiler_params=params(),
        name="send_blocks",
    )(in_hbm(owner), in_hbm(up), in_hbm(down_t), in_hbm(pixels))
    return blocks, pack


def exchange(blocks, pack):
    arrived = dict(zip(ORDER, blocks))
    for distance in (1, 4, 5, 6, 2):
        arrived[distance] = swap(arrived[distance], "band", distance)
    arrived[1], pack = lax.optimization_barrier((arrived[1], pack))
    factors = lax.all_gather(pack, "rep", axis=0, tiled=False)
    arrived[7], factors = lax.optimization_barrier((arrived[7], factors))
    arrived[7] = swap(arrived[7], "band", 7)
    arrived[3], factors = lax.optimization_barrier((arrived[3], factors))
    arrived[3] = swap(arrived[3], "band", 3)
    return [arrived[distance] for distance in SLOTS], factors


def expand_table(table, rows, half_width_padded, half_width, flip, transpose):
    position = iota2((rows, WLAT * WLON), 0)
    line, col = position // half_width_padded, position % half_width_padded
    if flip is not None:
        distance = sum(jnp.where(line == slot, far, 0) for slot, far in enumerate(SLOTS))
        line = jnp.bitwise_xor(distance, flip)
    target = iota2((rows, WLAT * WLON), 1)
    pick = jnp.where((target == line * WLON + col % WLON) & (col < half_width), 1.0, 0.0).astype(BF16)
    left = (dot_nt if transpose else dot_nn)(pick, table).astype(BF16)
    full = dot_nt(left, pick)
    row_window = (iota2((rows, 1), 0) % half_width_padded) // WLON
    col_window = (iota2((1, rows), 1) % half_width_padded) // WLON
    return jnp.where(row_window == col_window, full, 0.0).astype(BF16)


def prep_kernel(
    direct,
    row_share,
    half_width,
    half_width_padded,
    group_hbm_ref,
    level_hbm_ref,
    grad_hbm_ref,
    frozen_ref,
    factors_ref,
    mixer_ref,
    merged_ref,
    up_ref,
    down_ref,
    mix_ref,
    mix_t_ref,
    level_ref,
    grad_ref,
    group_ref,
    sems,
):
    pairs = [(group_hbm_ref, group_ref), (level_hbm_ref, level_ref)]
    flip = lax.axis_index("band") if direct else None
    if direct:
        pairs += [
            (grad_hbm_ref.at[:, jnp.bitwise_xor(flip, far)], grad_ref.at[:, slot])
            for slot, far in enumerate(SLOTS)
        ]
    else:
        pairs.append((grad_hbm_ref, grad_ref))
    loads = [
        pltpu.make_async_copy(source, target, sems.at[n]) for n, (source, target) in enumerate(pairs)
    ]
    for load in loads:
        load.start()
    rows = mix_ref.shape[0]
    mix_ref[...] = expand_table(mixer_ref[...], rows, half_width_padded, half_width, flip, False)
    mix_t_ref[...] = expand_table(mixer_ref[...], rows, half_width_padded, half_width, flip, True)
    reps, _, rank, share = factors_ref.shape
    levels = level_ref.shape[0]
    variables = group_ref.shape[0]
    channels = variables * frozen_ref.shape[1]
    up = jnp.concatenate([factors_ref[r, 0] for r in range(reps)], axis=1)
    source, target = iota2((share, channels), 0), iota2((share, channels), 1)
    down_t = jnp.zeros((rank, channels), F32)
    for r in range(reps):
        place = jnp.where((target == source + r * row_share) & (source < row_share), 1.0, 0.0)
        down_t = down_t + dot_nn(factors_ref[r, 1], place.astype(BF16))
    down_t = down_t.astype(BF16)
    down_ref[...] = down_t
    loads[0].wait()
    base = jnp.concatenate([frozen_ref[group_ref[v]].astype(F32) for v in range(variables)], axis=0)
    merged = (base + dot_tn(down_t, up)).astype(BF16)
    stacked = jnp.concatenate([merged, up], axis=0)
    merged_ref[...] = jnp.zeros_like(merged_ref)
    loads[1].wait()
    for level in range(levels):
        through = dot_nn(stacked, level_ref[level])
        weights = through[:channels].astype(BF16)
        for s in range(merged_ref.shape[0]):
            offset = (s * levels * channels) % LANE + level * channels
            merged_ref[s, offset : offset + channels, :] = weights
        up_high, up_low = split_hi_lo(through[channels:])
        up_ref[level, :rank, :] = up_high
        up_ref[level, rank:, :] = up_low
    for load in loads[2:]:
        load.wait()


def prepare(direct, groups, frozen, factors, level_weight, mixer, grad, row_share, half_width, half_width_padded):
    reps, _, rank, _ = factors.shape
    levels, feature_dim, _ = level_weight.shape
    channels = groups.shape[0] * frozen.shape[1]
    reach = round_up(levels * channels + LANE // 2, LANE)
    rows = WLAT * half_width_padded
    vmem = pl.BlockSpec(memory_space=pltpu.VMEM)
    flops = 2 * levels * (channels + rank) * feature_dim * feature_dim + 4 * rows * rows * WLAT * WLON
    shapes = [
        (grad.shape[0], reach, feature_dim),
        (levels, 2 * rank, feature_dim),
        (rank, channels),
        (rows, rows),
        (rows, rows),
        level_weight.shape,
        grad.shape,
    ]
    return pl.pallas_call(
        functools.partial(prep_kernel, direct, row_share, half_width, half_width_padded),
        out_shape=[jax.ShapeDtypeStruct(shape, BF16) for shape in shapes],
        in_specs=[pl.BlockSpec(memory_space=pl.ANY)] * 3 + [vmem] * 3,
        out_specs=[vmem] * len(shapes),
        scratch_shapes=[pltpu.SMEM(groups.shape, jnp.int32), pltpu.SemaphoreType.DMA((2 + WLAT,))],
        compiler_params=params(),
        cost_estimate=pl.CostEstimate(flops=flops, bytes_accessed=6 * 2**20, transcendentals=0),
        name="prepare",
    )(in_hbm(groups), in_hbm(level_weight), in_hbm(grad), in_hbm(frozen), factors, in_hbm(mixer))


def normal_parts(values):
    cdf = 0.5 + 0.5 * lax.erf(values * 0.7071067811865476)
    return cdf, 0.3989422804014327 * jnp.exp2(values * values * -0.7213475204444817)


def factor_shares(total, up_ref, down_ref, level_ref):
    levels, two_rank, feature_dim = up_ref.shape
    rank, channels = down_ref.shape
    total = total.astype(BF16)
    first = jnp.zeros((two_rank, channels), F32)
    second = jnp.zeros((two_rank, feature_dim), F32)
    for level in range(levels):
        part = total[level * channels : (level + 1) * channels]
        first = first + dot_nt(up_ref[level], part)
        through = jnp.concatenate(split_hi_lo(dot_nn(down_ref[...], part)), axis=0)
        second = second + dot_nt(through, level_ref[level])
    first = first[:rank] + first[rank:]
    return first, second[:rank] + second[rank:]


def turned_whole(lines, width):
    return lines * width // LANE * LANE


def embed_kernel(*refs):
    piece_refs, (merged_ref, tokens_ref, turned_ref) = refs[:-3], refs[-3:]
    samples, reach, feature_dim = merged_ref.shape
    width, features = piece_refs[0].shape
    depth = features // samples
    group = 2 * WLON
    rows = len(piece_refs) * group
    positions = turned_ref.shape[1]
    for s in range(samples):
        lane = s * depth // LANE * LANE
        pixels = jnp.concatenate([piece_ref[:, lane : lane + reach] for piece_ref in piece_refs], axis=0)
        for start in range(0, feature_dim, COLUMNS):
            columns = slice(start, start + COLUMNS)
            tokens = dot_nn(pixels, merged_ref[s, :, columns]).reshape(len(piece_refs), width, COLUMNS)
            for n in range(width // group):
                part = tokens[:, n * group : (n + 1) * group].reshape(rows, COLUMNS)
                tokens_ref[s, n * rows : (n + 1) * rows, columns] = part.astype(BF16)
    for start in range(0, features, LANE):
        lanes = slice(start, start + LANE)
        pixels = jnp.concatenate([piece_ref[:, lanes] for piece_ref in piece_refs], axis=0)
        turned_ref[lanes, :] = pixels[:positions].T


def embed_early(pieces, merged):
    samples, _, feature_dim = merged.shape
    width, features = pieces[0].shape
    count = len(pieces) * width
    return pl.pallas_call(
        embed_kernel,
        out_shape=[
            jax.ShapeDtypeStruct((samples, count, feature_dim), BF16),
            jax.ShapeDtypeStruct((features, turned_whole(len(pieces), width)), BF16),
        ],
        in_specs=[pl.BlockSpec(memory_space=pltpu.VMEM)] * (len(pieces) + 1),
        out_specs=[pl.BlockSpec(memory_space=pltpu.VMEM)] * 2,
        compiler_params=params(),
        cost_estimate=pl.CostEstimate(
            flops=2 * count * features * feature_dim, bytes_accessed=4 * 2**20, transcendentals=0
        ),
        name="embed_early",
    )(*pieces, merged)


def mix_kernel(
    direct,
    piece_refs,
    merged_ref,
    mix_ref,
    mix_t_ref,
    up_ref,
    down_ref,
    grad_ref,
    level_ref,
    mixed_hbm_ref,
    share_ref,
    turned_refs,
    mixed_refs,
    pre_refs,
    tokens_refs,
    grad_pre_refs,
    grad_tokens_refs,
    total_ref,
    mixed_sems,
):
    samples, reach, feature_dim = merged_ref.shape
    chunk_count, (_, width, _) = len(mixed_refs), mixed_refs[0].shape
    depth = piece_refs[-1].shape[-1] // samples
    rows = WLAT * width

    group_rows = mix_ref.shape[0]
    group = group_rows // WLAT
    groups = [
        (slice(start, start + group), slice(start * WLAT, start * WLAT + group_rows))
        for start in range(0, width, group)
    ]
    pair = 1 if group % SUB == 0 else 2

    early = EARLY if direct else 0
    early_rows, late_rows = early * group, (WLAT - early) * group
    if direct:
        early_tokens_ref, early_turned_ref, *line_refs = piece_refs
        early_positions = early_turned_ref.shape[1]

    def lines_of(n):
        return pl.ds(n // samples * WLAT, WLAT)

    if direct:
        me = lax.axis_index("band")
        targets = [
            (mixed_refs[n].at[slot], mixed_hbm_ref.at[n, jnp.bitwise_xor(me, far)])
            for n in range(chunk_count)
            for slot, far in enumerate(SLOTS)
        ]
    else:
        targets = [
            (mixed_refs[n], mixed_hbm_ref.at[n % samples, lines_of(n)]) for n in range(chunk_count)
        ]
    stores = [
        pltpu.make_async_copy(source, target, mixed_sems.at[n]) for n, (source, target) in enumerate(targets)
    ]

    def pixels_of(n, lanes):
        if direct:
            return jnp.concatenate([line_ref[:, lanes] for line_ref in line_refs], axis=0)
        return piece_refs[0][lines_of(n), :, lanes].reshape(rows, lanes.stop - lanes.start)

    def turn(n):
        def part(lanes):
            pixels = pixels_of(n, lanes)
            if direct:
                before = early_positions - (early - 1) * width
                pixels = pixels[before:]
            turned_refs[n // samples][lanes, :] = pixels.T

        starts = range(0, samples * depth, LANE)
        return [functools.partial(part, slice(start, start + LANE)) for start in starts]

    def tokens_at(n, block, line, count, columns):
        if line < early:
            at = pl.ds(block * early_rows + line * group, count * group)
            return early_tokens_ref[n % samples, at, columns]
        return tokens_refs[n][pl.ds(block * late_rows + (line - early) * group, count * group), columns]

    def forward(n, columns):
        s = n % samples
        lane = s * depth // LANE * LANE

        def embed():
            pixels = pixels_of(n, slice(lane, lane + reach))
            if direct:
                pixels = pixels[width:]
            tokens = dot_nn(pixels, merged_ref[s, :, columns]).reshape(WLAT - early, width, COLUMNS)
            for block, (within, _) in enumerate(groups):
                part = tokens[:, within].reshape(late_rows, COLUMNS).astype(BF16)
                tokens_refs[n][block * late_rows : (block + 1) * late_rows, columns] = part

        def mixing(block, at):
            tokens = tokens_at(n, block, early, WLAT - early, columns)
            if direct:
                tokens = jnp.concatenate([tokens_at(n, block, 0, early, columns), tokens], axis=0)
            pre_refs[n][at, columns] = dot_nn(mix_ref[...], tokens)

        return [embed] + [functools.partial(mixing, block, at) for block, (_, at) in enumerate(groups)]

    def pointwise(n, columns):
        s, first_line = n % samples, n // samples * WLAT

        def part(line, across, lanes):
            grads = [grad_ref[s, first_line + line + k, across, lanes].astype(F32) for k in range(pair)]
            mixed = []
            for block, (within, at) in enumerate(groups):
                if within.start < across.start or within.stop > across.stop:
                    continue
                at = pl.ds(at.start + line * group, pair * group)
                pre = pre_refs[n][at, lanes]
                cdf, pdf = normal_parts(pre)
                mixed.append(tokens_at(n, block, line, pair, lanes).astype(F32) + pre * cdf)
                first = within.start - across.start
                grad = jnp.concatenate([values[first : first + group] for values in grads], axis=0)
                grad_pre_refs[n][at, lanes] = (grad * (cdf + pre * pdf)).astype(BF16)
            for k in range(pair):
                parts = [values[k * group : (k + 1) * group] for values in mixed]
                mixed_refs[n][line + k, across, lanes] = jnp.concatenate(parts, axis=0).astype(BF16)

        return [
            functools.partial(part, line, slice(across, across + pair * group), slice(start, start + LANE))
            for line in range(0, WLAT, pair)
            for across in range(0, width, pair * group)
            for start in range(columns.start, columns.stop, LANE)
        ]

    def backward(n, columns):
        def spread():
            direct_part = grad_ref[n % samples, lines_of(n), :, columns].astype(F32)
            through = [
                dot_nn(mix_t_ref[...], grad_pre_refs[n][at, columns]).reshape(WLAT, group, COLUMNS)
                for _, at in groups
            ]
            total = jnp.concatenate(through, axis=1) + direct_part
            grad_tokens_refs[n][:, columns] = total.reshape(rows, COLUMNS).astype(BF16)

        def share():
            s = n % samples
            features = slice(s * depth, (s + 1) * depth)
            late = rows - turned_refs[0].shape[1]
            part = dot_nn(turned_refs[n // samples][features, :], grad_tokens_refs[n][late:, columns])
            if direct:
                part = part + dot_nn(early_turned_ref[features, :], grad_tokens_refs[n][:late, columns])
            total_ref[:, columns] = part if n == 0 else total_ref[:, columns] + part

        return [spread, share]

    units = [
        (n, slice(start, start + COLUMNS))
        for n in range(chunk_count)
        for start in range(0, feature_dim, COLUMNS)
    ]
    for step in forward(*units[0]):
        step()
    for i, unit in enumerate(units):
        n, columns = unit
        others = []
        if i + 1 < len(units):
            others += forward(*units[i + 1])
        if columns.start == 0 and n % samples == 0:
            others += turn(n)
        if i > 0:
            others += backward(*units[i - 1])
        lines = pointwise(*unit)
        for line, vector_step in enumerate(lines):
            vector_step()
            for step in others[line * len(others) // len(lines) : (line + 1) * len(others) // len(lines)]:
                step()
        if columns.stop == feature_dim:
            each = len(stores) // chunk_count
            for store in stores[n * each : (n + 1) * each]:
                store.start()
    for step in backward(*units[-1]):
        step()

    first, second = factor_shares(total_ref[...], up_ref, down_ref, level_ref)
    rank, channels = down_ref.shape
    columns = share_ref.shape[2]
    reps = feature_dim // columns
    folds = rank // (share_ref.shape[1] - rank)
    depth_rows, fold_lanes, row_share = rank // folds, columns // folds, channels // reps
    packed = jnp.zeros((depth_rows, feature_dim), F32)
    row, lane = iota2((channels, feature_dim), 0), iota2((1, feature_dim), 1)
    rep, lane = lane // columns, lane % columns
    for fold in range(folds):
        inside = lane - fold * fold_lanes
        target = jnp.where((inside >= 0) & (inside < row_share), inside + rep * row_share, -1)
        pick = jnp.where(row == target, 1.0, 0.0).astype(BF16)
        part = first[fold * depth_rows : (fold + 1) * depth_rows].astype(BF16)
        packed = packed + dot_nn(part, pick)
    payload = jnp.concatenate([second, packed], axis=0).astype(BF16)
    for slot in range(share_ref.shape[0]):
        at = slot % reps * columns
        share_ref[slot] = payload[:, at : at + columns]
    for store in stores:
        store.wait()


def mix_blocks(direct, arrived, merged, mix, mix_t, grad, up_through, down_t, level_weight, band_count, reps):
    samples, lat_rows, block_width, feature_dim = grad.shape
    width = block_width
    lanes = arrived[-1].shape[-1]
    early = EARLY if direct else 0
    turned_early = turned_whole(early, width)
    reach = merged.shape[1]
    rows = WLAT * width
    rank = down_t.shape[0]
    chunks = lat_rows // WLAT * samples
    share_shape = (band_count * reps, rank + rank // FOLDS, feature_dim // reps)
    flops = 2 * samples * lat_rows * block_width * feature_dim * (2 * reach + 2 * rows)
    vmem = pl.BlockSpec(memory_space=pltpu.VMEM)
    any_space = pl.BlockSpec(memory_space=pl.ANY)
    local = [*arrived, merged, mix, mix_t, up_through, down_t]
    return pl.pallas_call(
        lambda *refs: mix_kernel(direct, refs[: len(arrived)], *refs[len(arrived) :]),
        out_shape=[
            jax.ShapeDtypeStruct(grad.shape, BF16),
            jax.ShapeDtypeStruct(share_shape, BF16),
        ],
        in_specs=[vmem] * (len(local) + 2),
        out_specs=[any_space, vmem],
        scratch_shapes=[
            [pltpu.VMEM((lanes, rows - turned_early), BF16)] * (chunks // samples),
            [pltpu.VMEM((WLAT, width, feature_dim), BF16)] * chunks,
            [pltpu.VMEM((rows, feature_dim), F32)] * chunks,
            [pltpu.VMEM((rows - early * width, feature_dim), BF16)] * chunks,
            [pltpu.VMEM((rows, feature_dim), BF16)] * chunks,
            [pltpu.VMEM((rows, feature_dim), BF16)] * chunks,
            pltpu.VMEM((lanes // samples, feature_dim), F32),
            pltpu.SemaphoreType.DMA((chunks * WLAT,)),
        ],
        compiler_params=params(),
        cost_estimate=pl.CostEstimate(
            flops=flops,
            bytes_accessed=12 * 2**20,
            transcendentals=samples * lat_rows * block_width * feature_dim,
        ),
        name="mix_blocks",
    )(*local, grad, level_weight)


def sum_kernel(parts_ref, first_ref, second_ref):
    rank, row_share = first_ref.shape
    total = parts_ref[0].astype(F32)
    for n in range(1, parts_ref.shape[0]):
        total = total + parts_ref[n].astype(F32)
    second_ref[...] = total[:rank]
    depth_rows = total.shape[0] - rank
    for fold in range(rank // depth_rows):
        lane = fold * depth_rows * total.shape[1] // rank
        first_ref[fold * depth_rows : (fold + 1) * depth_rows, :] = total[rank:, lane : lane + row_share]


def sum_shares(shares, rank, row_share):
    parts = lax.all_to_all(shares, ("band", "rep"), split_axis=0, concat_axis=0, tiled=True)
    return pl.pallas_call(
        sum_kernel,
        out_shape=[
            jax.ShapeDtypeStruct((rank, row_share), F32),
            jax.ShapeDtypeStruct((rank, shares.shape[2]), F32),
        ],
        compiler_params=params(),
        name="sum_shares",
    )(parts)


def on_device(
    patches,
    variable_group_index,
    frozen_patch_weight,
    adapter_down,
    adapter_up,
    level_merge_weight,
    window_patch_mixer,
    column_block_owner,
    mixed_token_gradient,
):
    band_count, reps = lax.axis_size("band"), lax.axis_size("rep")
    samples, levels, channels, row_count, col_count = patches.shape
    feature_dim = frozen_patch_weight.shape[2]
    rank, col_share = adapter_up.shape
    row_share = adapter_down.shape[0]
    lat_rows = band_count * row_count
    block_width = col_count // band_count
    padded_width = round_up(block_width, SUB)
    group = 2 * WLON if block_width % (2 * WLON) == 0 else padded_width
    features = samples * levels * channels

    pixels = patches.reshape(features, col_count)
    pack_shape = (2, rank, round_up(max(row_share, col_share), LANE))
    direct = band_count == BANDS and lat_rows == WLAT and padded_width == block_width
    direct = direct and features % LANE == 0 and col_count % LANE == 0
    if direct:
        blocks, pack = send_blocks(
            pixels, column_block_owner, adapter_up, adapter_down.T, block_width, pack_shape
        )
        arrived, factors = exchange(blocks, pack)
    else:
        block_ids = jnp.arange(band_count, dtype=jnp.int32)
        inverse = jnp.sum(
            jnp.where(column_block_owner[None, :] == block_ids[:, None], block_ids[None, :], 0), axis=1
        )
        outgoing = jnp.take(pixels.T.reshape(band_count, block_width, features), inverse, axis=0)
        outgoing = jnp.pad(outgoing, ((0, 0), (0, padded_width - block_width), (0, 0)))
        arrived = [lax.all_to_all(outgoing, "band", split_axis=0, concat_axis=0, tiled=True)]
        pack = jnp.stack(
            [
                jnp.pad(array, ((0, 0), (0, pack_shape[2] - array.shape[1])))
                for array in (adapter_up, adapter_down.T)
            ]
        )
        factors = lax.all_gather(pack, "rep", axis=0, tiled=False)

    grad = mixed_token_gradient.reshape(samples, lat_rows, block_width, feature_dim)
    if padded_width != block_width:
        grad = jnp.pad(grad, ((0, 0), (0, 0), (0, padded_width - block_width), (0, 0)))
    merged, up_through, down_t, mix, mix_t, level_copy, grad_copy = prepare(
        direct,
        variable_group_index,
        frozen_patch_weight,
        factors,
        level_merge_weight,
        window_patch_mixer,
        grad,
        row_share,
        min(block_width, group),
        group,
    )
    if direct:
        arrived = [*embed_early(arrived[:EARLY], merged), *arrived[EARLY - 1 :]]
    mixed, shares = mix_blocks(
        direct, arrived, merged, mix, mix_t, grad_copy, up_through, down_t, level_copy, band_count, reps
    )
    if padded_width != block_width:
        mixed = mixed[:, :, :block_width]
    first_t, second = sum_shares(shares, rank, row_share)
    return mixed.reshape(mixed_token_gradient.shape), first_t.T, second


def solution(mesh):
    in_specs = (
        P("rep", None, None, "band", None),
        P(),
        P(),
        P("rep", None),
        P(None, "rep"),
        P(),
        P(),
        P(),
        P("rep", "band", None, None, None),
    )
    out_specs = (P("rep", "band", None, None, None), P("rep", None), P(None, "rep"))
    return jax.shard_map(
        on_device, mesh=mesh, in_specs=in_specs, out_specs=out_specs, check_vma=False
    )
```
